32 devices in a mesh: dp: 32 (over z, y, x, core).
Axes of the slice: x: 2, y: 2, z: 4, core: 2. Of those that a mesh axis runs over, the one named last changes fastest.
Arguments:
- query_tokens: bfloat16 [1024, 768], P('dp'), may hold values from -6 to 6
- passage_tokens: bfloat16 [14080, 768], P('dp'), may hold values from -6 to 6
- query_lengths: int32 [32], P('dp'), may hold values from 5 to 32, as said below
- passage_lengths: int32 [64], P('dp'), may hold values from 28 to 220, as said below
- passage_valid: int32 [64], P('dp'), may hold values 0 or 1
- positives: int32 [32], P('dp'), may hold values from 0 to 63
- negatives: int32 [32], P('dp'), may hold values from 0 to 63
- teacher_margins: float32 [32], P('dp'), may hold values from -8 to 8
- query_grad: bfloat16 [1024, 768], P('dp'), may hold values from -6 to 6
- passage_grad: bfloat16 [14080, 768], P('dp'), may hold values from -6 to 6
- weight_query: bfloat16 [768, 768], replicated, may hold values from -0.21875 to 0.21875
- bias_query: bfloat16 [768], replicated, may hold values from -1.75 to 1.75
- weight_key: bfloat16 [768, 768], replicated, may hold values from -0.21875 to 0.21875
- weight_value: bfloat16 [768, 768], replicated, may hold values from -0.21875 to 0.21875
- bias_value: bfloat16 [768], replicated, may hold values from -0.625 to 0.625
- weight_out: bfloat16 [768, 768], replicated, may hold values from -1.25 to 1.25
- bias_out: bfloat16 [768], replicated, may hold values from -1.75 to 1.75
- gain_attn: bfloat16 [768], replicated, may hold values from 0.5 to 1.5
- shift_attn: bfloat16 [768], replicated, may hold values from -1.25 to 1.25
- weight_in: bfloat16 [768, 3072], replicated, may hold values from -0.21875 to 0.21875
- bias_in: bfloat16 [3072], replicated, may hold values from -1.75 to 1.75
- weight_back: bfloat16 [3072, 768], replicated, may hold values from -0.109375 to 0.109375
- bias_back: bfloat16 [768], replicated, may hold values from -1.75 to 1.75
- gain_ffn: bfloat16 [768], replicated, may hold values from 0.5 to 1.5
- shift_ffn: bfloat16 [768], replicated, may hold values from -1.25 to 1.25
Outputs:
- query_out: bfloat16 [1024, 768], P('dp')
- passage_out: bfloat16 [14080, 768], P('dp')
- query_loss: float32 [32], P('dp')
- query_tokens_grad: float32 [1024, 768], P('dp')
- passage_tokens_grad: float32 [14080, 768], P('dp')
- weight_query_grad: float32 [768, 768], P('dp')
- bias_query_grad: float32 [768], P('dp')
- weight_key_grad: float32 [768, 768], P('dp')
- weight_value_grad: float32 [768, 768], P('dp')
- bias_value_grad: float32 [768], P('dp')
- weight_out_grad: float32 [768, 768], P('dp')
- bias_out_grad: float32 [768], P('dp')
- gain_attn_grad: float32 [768], P('dp')
- shift_attn_grad: float32 [768], P('dp')
- weight_in_grad: float32 [768, 3072], P('dp')
- bias_in_grad: float32 [3072], P('dp')
- weight_back_grad: float32 [3072, 768], P('dp')
- bias_back_grad: float32 [768], P('dp')
- gain_ffn_grad: float32 [768], P('dp')
- shift_ffn_grad: float32 [768], P('dp')
The draws below stay inside these ranges and needn't reach their ends.
Inputs may be any that keep to these rules, and one draw needn't show every extreme that they name: `query_lengths`: some query slot in every draw uses all 32 tokens. `passage_lengths`: some passage slot in every draw uses all 220 tokens.
All inputs are finite; a program needn't handle non-finite values. No bound on the sum of `passage_valid` on one device may be relied on, other than what follows from the above.
Results may differ from the reference program's by a relative error of at most 0.014.
Values may be sent and summed in bfloat16 or wider, within the bound.
A program may use at most 192 MiB of HBM per device.

```python
import jax
import jax.numpy as jnp
from jax import lax

D = 768
HEADS = 12
HEAD_DIM = 64
FF = 3072
LQ = 32
LP = 220
NQ = 32
NP = 64


def lengths_with_full(key, slot_count, least, most):
    key_pick, key_rest = jax.random.split(key)
    drawn = jax.random.randint(key_rest, (slot_count,), least, most + 1)
    full_slot = jax.random.randint(key_pick, (), 0, slot_count)
    return jnp.where(jnp.arange(slot_count) == full_slot, most, drawn).astype(jnp.int32)


def draw_query_lengths(key, part):
    key = jax.random.fold_in(key, 11)
    return lengths_with_full(key, NQ, LQ // 8 + 1, LQ)


def draw_passage_lengths(key, part):
    key = jax.random.fold_in(key, 23)
    return lengths_with_full(key, NP, LP // 8 + 1, LP)


def plant(array, stream_key, low, largest):
    spot = [jax.random.randint(jax.random.fold_in(stream_key, axis), (), 0, length) for axis, length in enumerate(array.shape)]
    longest = array.shape.index(max(array.shape))
    next_to = spot[:longest] + [(spot[longest] + 1) % array.shape[longest]] + spot[longest + 1:]
    return array.at[tuple(spot)].set(low).at[tuple(next_to)].set(largest)


def block_scale(rng, shape, pieces, low, largest):
    level = 1.0
    for axis_at, parts in pieces:
        draws = jax.random.uniform(jax.random.fold_in(jax.random.fold_in(rng, 6), axis_at), (parts,), jnp.float32, low / len(pieces), largest / len(pieces))
        level = level * jnp.repeat(jnp.exp(draws), shape[axis_at] // parts).reshape((-1,) + (1,) * (len(shape) - 1 - axis_at))
    return level


def scatter_about(rng, shape, deviation, most, cuts=(), held_as=jnp.bfloat16):
    array = deviation * jax.random.normal(rng, shape, jnp.float32)
    if cuts:
        array = array * block_scale(rng, shape, cuts, -0.22, 0.18)
    return jnp.clip(array, -most, most).astype(held_as)


def setup_inputs(seed: int = 0) -> dict:
    key_of = jax.random.split(jax.random.key(seed), 26)
    query_tokens = scatter_about(key_of[0], (NQ * LQ, D), 1.0, 6.0, ((0, 32),))
    passage_tokens = scatter_about(key_of[1], (NP * LP, D), 1.0, 6.0, ((0, 32),))
    query_lengths = draw_query_lengths(jax.random.fold_in(key_of[25], 71), 0)
    passage_lengths = draw_passage_lengths(jax.random.fold_in(key_of[25], 71), 0)
    passage_valid = plant((jax.random.randint(key_of[4], (NP,), 0, 4) < 3).astype(jnp.int32), jax.random.fold_in(key_of[4], 1), 0, 1)
    positives = plant(jax.random.randint(key_of[5], (NQ,), 0, NP), jax.random.fold_in(key_of[5], 1), 0, NP - 1).astype(jnp.int32)
    negatives = plant(jax.random.randint(key_of[6], (NQ,), 0, NP), jax.random.fold_in(key_of[6], 1), 0, NP - 1).astype(jnp.int32)
    teacher_margins = scatter_about(key_of[7], (NQ,), 2.0, 8.0, ((0, 32),), jnp.float32)
    query_grad = scatter_about(key_of[8], (NQ * LQ, D), 1.0, 6.0, ((0, 32),))
    passage_grad = scatter_about(key_of[9], (NP * LP, D), 1.0, 6.0, ((0, 32),))
    weight_query = scatter_about(key_of[10], (D, D), D ** -0.5, 0.21875)
    bias_query = scatter_about(key_of[11], (D,), 0.3, 1.75)
    weight_key = scatter_about(key_of[12], (D, D), D ** -0.5, 0.21875)
    weight_value = scatter_about(key_of[13], (D, D), D ** -0.5, 0.21875)
    bias_value = scatter_about(key_of[14], (D,), 0.1, 0.625)
    weight_out = scatter_about(key_of[15], (D, D), (D // 32) ** -0.5, 1.25)
    bias_out = scatter_about(key_of[16], (D,), 0.3, 1.75)
    gain_attn = jnp.clip(1.0 + 0.1 * jax.random.normal(key_of[17], (D,), jnp.float32), 0.5, 1.5).astype(jnp.bfloat16)
    shift_attn = scatter_about(key_of[18], (D,), 0.2, 1.25)
    weight_in = scatter_about(key_of[19], (D, FF), D ** -0.5, 0.21875)
    bias_in = scatter_about(key_of[20], (FF,), 0.3, 1.75)
    weight_back = scatter_about(key_of[21], (FF, D), FF ** -0.5, 0.109375)
    bias_back = scatter_about(key_of[22], (D,), 0.3, 1.75)
    gain_ffn = jnp.clip(1.0 + 0.1 * jax.random.normal(key_of[23], (D,), jnp.float32), 0.5, 1.5).astype(jnp.bfloat16)
    shift_ffn = scatter_about(key_of[24], (D,), 0.2, 1.25)
    return {"query_tokens": query_tokens, "passage_tokens": passage_tokens, "query_lengths": query_lengths, "passage_lengths": passage_lengths, "passage_valid": passage_valid, "positives": positives, "negatives": negatives, "teacher_margins": teacher_margins, "query_grad": query_grad, "passage_grad": passage_grad, "weight_query": weight_query, "bias_query": bias_query, "weight_key": weight_key, "weight_value": weight_value, "bias_value": bias_value, "weight_out": weight_out, "bias_out": bias_out, "gain_attn": gain_attn, "shift_attn": shift_attn, "weight_in": weight_in, "bias_in": bias_in, "weight_back": weight_back, "bias_back": bias_back, "gain_ffn": gain_ffn, "shift_ffn": shift_ffn}


@jax.custom_vjp
def low(v):
    return lax.optimization_barrier(v.astype(jnp.bfloat16)).astype(jnp.float32)

@jax.custom_vjp
def low_back(v):
    return v

def low_keep(v):
    return (low(v), None)

def low_pass(kept, grad):
    return (grad,)

def back_keep(v):
    return (v, None)

def back_low(kept, grad):
    return (low(grad),)
low.defvjp(low_keep, low_pass)
low_back.defvjp(back_keep, back_low)
highest = lax.Precision.HIGHEST
ln_eps = 1e-12
score_scale = 0.0625
margin_weight = 0.5
root_half = 0.7071067811865476

def layer_norm(hidden, gain, shift):
    centered = hidden - lax.optimization_barrier(jnp.mean(hidden, axis=-1, keepdims=True))
    variance = lax.optimization_barrier(jnp.mean(centered * centered, axis=-1, keepdims=True))
    return centered * lax.rsqrt(variance + ln_eps) * gain + shift

def gelu_exact(inputs):
    return 0.5 * inputs * (1.0 + lax.erf(inputs * root_half))

def both_ways(inputs):
    return low(low_back(inputs))

def project(left, right):
    return jnp.einsum('bld,de->ble', left, right, precision=highest)

def encode(tokens, lengths, params):
    weight_query, bias_query, weight_key, weight_value, bias_value, weight_out, bias_out, gain_attn, shift_attn, weight_in, bias_in, weight_back, bias_back, gain_ffn, shift_ffn = params
    slot_count, slot_length = (tokens.shape[0], tokens.shape[1])
    split_heads = (slot_count, slot_length, HEADS, HEAD_DIM)
    queries = both_ways(project(tokens, weight_query) + bias_query).reshape(split_heads)
    keys_all = both_ways(project(tokens, weight_key)).reshape(split_heads)
    values_all = both_ways(project(tokens, weight_value) + bias_value).reshape(split_heads)
    raw_scores = 0.125 * jnp.einsum('bqhd,bkhd->bhqk', queries, keys_all, precision=highest)
    allowed = (jnp.arange(slot_length, dtype=jnp.int32)[None, :] < lengths[:, None])[:, None, None, :]
    scores = jnp.where(allowed, low_back(raw_scores), -1000000000.0)
    peak_score = lax.optimization_barrier(jnp.max(scores, axis=-1, keepdims=True))
    exp_scores = jnp.exp(scores - peak_score)
    soft_scores = exp_scores / lax.optimization_barrier(jnp.sum(exp_scores, axis=-1, keepdims=True))
    context = jnp.einsum('bhqk,bkhd->bqhd', low(soft_scores), values_all, precision=highest)
    context = both_ways(context).reshape(slot_count, slot_length, D)
    attended = low_back(project(context, weight_out) + bias_out)
    middle = layer_norm(tokens + attended, gain_attn, shift_attn)
    inner_act = low_back(project(low(middle), weight_in) + bias_in)
    branch = low_back(project(low(gelu_exact(inner_act)), weight_back) + bias_back)
    return layer_norm(middle + branch, gain_ffn, shift_ffn)

def group_size(slot_count, slot_length):
    chosen = 1
    for option in (2, 4, 8, 16, 32, 64, 128):
        if slot_count % option == 0 and option * slot_length <= 4096:
            chosen = option
    return chosen

def encode_all(tokens, lengths, slot_count, slot_length, params):
    chosen = group_size(slot_count, slot_length)
    blocks = tokens.reshape(slot_count // chosen, chosen, slot_length, D)
    block_lengths = lengths.reshape(slot_count // chosen, chosen)
    one_block = jax.checkpoint(lambda item: encode(item[0], item[1], params))
    return lax.map(one_block, (blocks, block_lengths)).reshape(slot_count * slot_length, D)

def forward(query_in, passage_in, query_lengths, passage_lengths, passage_valid, positives, negatives, teacher_margins, params):
    query_out = encode_all(query_in, query_lengths, NQ, LQ, params)
    passage_out = encode_all(passage_in, passage_lengths, NP, LP, params)
    cls_query = low(query_out.reshape(NQ, LQ, D)[:, 0])
    cls_passage = low(passage_out.reshape(NP, LP, D)[:, 0])
    scores = low_back(score_scale * jnp.dot(cls_query, cls_passage.T, precision=highest))
    position = jnp.arange(NP, dtype=jnp.int32)
    is_positive = position[None, :] == positives[:, None]
    is_negative = position[None, :] == negatives[:, None]
    allowed = (passage_valid[None, :] == 1) | is_positive
    masked = jnp.where(allowed, scores, -1e+30)
    peak_score = lax.optimization_barrier(jnp.max(masked, axis=1, keepdims=True))
    log_total = peak_score[:, 0] + jnp.log(lax.optimization_barrier(jnp.sum(jnp.where(allowed, jnp.exp(masked - peak_score), 0.0), axis=1)))
    positive_score = lax.optimization_barrier(jnp.sum(jnp.where(is_positive, scores, 0.0), axis=1))
    negative_score = lax.optimization_barrier(jnp.sum(jnp.where(is_negative, scores, 0.0), axis=1))
    shortfall = positive_score - negative_score - teacher_margins
    return (query_out, passage_out, log_total - positive_score + margin_weight * shortfall * shortfall)

def reference(query_tokens, passage_tokens, query_lengths, passage_lengths, passage_valid, positives, negatives, teacher_margins, query_grad, passage_grad, weight_query, bias_query, weight_key, weight_value, bias_value, weight_out, bias_out, gain_attn, shift_attn, weight_in, bias_in, weight_back, bias_back, gain_ffn, shift_ffn):
    params = tuple((item.astype(jnp.float32) for item in (weight_query, bias_query, weight_key, weight_value, bias_value, weight_out, bias_out, gain_attn, shift_attn, weight_in, bias_in, weight_back, bias_back, gain_ffn, shift_ffn)))

    def whole(query_in, passage_in, *weights):
        return forward(query_in, passage_in, query_lengths, passage_lengths, passage_valid, positives, negatives, teacher_margins, weights)
    (query_out, passage_out, query_loss), pull = jax.vjp(whole, query_tokens.astype(jnp.float32), passage_tokens.astype(jnp.float32), *params)
    grads = pull((query_grad.astype(jnp.float32), passage_grad.astype(jnp.float32), jnp.ones_like(query_loss)))
    return (query_out.astype(jnp.bfloat16), passage_out.astype(jnp.bfloat16), query_loss, grads[0], grads[1], grads[2], grads[3], grads[4], grads[5], grads[6], grads[7], grads[8], grads[9], grads[10], grads[11], grads[12], grads[13], grads[14], grads[15], grads[16])
```

```python
import jax
import jax.numpy as jnp
from jax import lax
from jax.experimental import pallas as pl
from jax.experimental.pallas import tpu as pltpu
from jax.sharding import PartitionSpec as P

D = 768
HEADS = 12
HEAD_DIM = 64


ln_eps = 1e-12
score_scale = 0.0625
margin_weight = 0.5
root_half = 0.7071067811865476
inv_root_tau = 0.3989422804014327


def matmul(left, right):
    return jnp.dot(left, right, preferred_element_type=jnp.float32)


def left_across(left, right):
    return lax.dot_general(
        left, right, (((0,), (0,)), ((), ())), preferred_element_type=jnp.float32
    )


def right_across(left, right):
    return lax.dot_general(
        left, right, (((1,), (1,)), ((), ())), preferred_element_type=jnp.float32
    )


def normalize(hidden, gain, shift):
    centered = hidden - jnp.mean(hidden, axis=-1, keepdims=True)
    inv_std = lax.rsqrt(jnp.mean(centered * centered, axis=-1, keepdims=True) + ln_eps)
    unit_rows = centered * inv_std
    return (unit_rows * gain.astype(jnp.float32) + shift.astype(jnp.float32), unit_rows, inv_std)


def normalize_back(upstream, unit_rows, inv_std, gain):
    scaled = upstream * gain.astype(jnp.float32)
    hidden_grad = inv_std * (
        scaled
        - jnp.mean(scaled, axis=-1, keepdims=True)
        - unit_rows * jnp.mean(scaled * unit_rows, axis=-1, keepdims=True)
    )
    return (hidden_grad, jnp.sum(upstream * unit_rows, axis=0), jnp.sum(upstream, axis=0))


def gelu_exact(inputs):
    return 0.5 * inputs * (1.0 + lax.erf(inputs * root_half))


def gelu_slope(inputs):
    return 0.5 * (1.0 + lax.erf(inputs * root_half)) + inputs * inv_root_tau * jnp.exp(
        -0.5 * inputs * inputs
    )


def head_scores(query_heads, key_heads, lengths):
    slot_length = query_heads.shape[1]
    allowed = (lax.iota(jnp.int32, slot_length)[None, :] < lengths[:, None])[:, None, None, :]
    raw_scores = 0.125 * jnp.einsum(
        "bqhd,bkhd->bhqk", query_heads, key_heads, preferred_element_type=jnp.float32
    )
    return jnp.where(allowed, raw_scores, -1000000000.0)


def encode_forward(tokens, lengths, params):
    (
        weight_query,
        bias_query,
        weight_key,
        weight_value,
        bias_value,
        weight_out,
        bias_out,
        gain_attn,
        shift_attn,
        weight_in,
        bias_in,
        weight_back,
        bias_back,
        gain_ffn,
        shift_ffn,
    ) = params
    slot_count = lengths.shape[0]
    row_count = tokens.shape[0]
    split_heads = (slot_count, row_count // slot_count, HEADS, HEAD_DIM)
    queries = (matmul(tokens, weight_query) + bias_query.astype(jnp.float32)).astype(jnp.bfloat16)
    keys_all = matmul(tokens, weight_key).astype(jnp.bfloat16)
    values_all = (matmul(tokens, weight_value) + bias_value.astype(jnp.float32)).astype(
        jnp.bfloat16
    )
    scores = head_scores(queries.reshape(split_heads), keys_all.reshape(split_heads), lengths)
    peak_score = jnp.max(scores, axis=-1, keepdims=True)
    exp_scores = jnp.exp(scores - peak_score)
    row_total = jnp.sum(exp_scores, axis=-1, keepdims=True)
    soft_low = (exp_scores / row_total).astype(jnp.bfloat16)
    log_total = peak_score + jnp.log(row_total)
    context = jnp.einsum(
        "bhqk,bkhd->bqhd",
        soft_low,
        values_all.reshape(split_heads),
        preferred_element_type=jnp.float32,
    )
    context = context.reshape(row_count, D).astype(jnp.bfloat16)
    attn_sum = (
        tokens.astype(jnp.float32) + matmul(context, weight_out) + bias_out.astype(jnp.float32)
    )
    middle, unit_attn, inv_attn = normalize(attn_sum, gain_attn, shift_attn)
    middle_low = middle.astype(jnp.bfloat16)
    inner_act = matmul(middle_low, weight_in) + bias_in.astype(jnp.float32)
    gelu_low = gelu_exact(inner_act).astype(jnp.bfloat16)
    ffn_sum = middle + matmul(gelu_low, weight_back) + bias_back.astype(jnp.float32)
    output, unit_ffn, inv_ffn = normalize(ffn_sum, gain_ffn, shift_ffn)
    kept = (
        queries,
        keys_all,
        values_all,
        log_total,
        context,
        unit_attn,
        inv_attn,
        middle_low,
        inner_act,
        gelu_low,
        unit_ffn,
        inv_ffn,
    )
    return (output.astype(jnp.bfloat16), kept)


def ffn_backward(upstream, kept, params):
    (
        queries,
        keys_all,
        values_all,
        log_total,
        context,
        unit_attn,
        inv_attn,
        middle_low,
        inner_act,
        gelu_low,
        unit_ffn,
        inv_ffn,
    ) = kept
    weight_in, weight_back, gain_ffn = (params[9], params[11], params[13])
    ffn_grad, gain_grad, shift_grad = normalize_back(upstream, unit_ffn, inv_ffn, gain_ffn)
    branch_low = ffn_grad.astype(jnp.bfloat16)
    back_weight_grad = left_across(gelu_low, branch_low)
    back_bias_grad = jnp.sum(branch_low, axis=0, dtype=jnp.float32)
    inner_low = (right_across(branch_low, weight_back) * gelu_slope(inner_act)).astype(jnp.bfloat16)
    in_weight_grad = left_across(middle_low, inner_low)
    in_bias_grad = jnp.sum(inner_low, axis=0, dtype=jnp.float32)
    middle_grad = ffn_grad + right_across(inner_low, weight_in)
    return (
        middle_grad,
        (in_weight_grad, in_bias_grad, back_weight_grad, back_bias_grad, gain_grad, shift_grad),
    )


def attention_backward(middle_grad, tokens, lengths, kept, params):
    (
        queries,
        keys_all,
        values_all,
        log_total,
        context,
        unit_attn,
        inv_attn,
        middle_low,
        inner_act,
        gelu_low,
        unit_ffn,
        inv_ffn,
    ) = kept
    weight_query, weight_key, weight_value, weight_out, gain_attn = (
        params[0],
        params[2],
        params[3],
        params[5],
        params[7],
    )
    slot_count = lengths.shape[0]
    row_count = tokens.shape[0]
    split_heads = (slot_count, row_count // slot_count, HEADS, HEAD_DIM)
    attn_grad, gain_grad, shift_grad = normalize_back(middle_grad, unit_attn, inv_attn, gain_attn)
    attn_low = attn_grad.astype(jnp.bfloat16)
    out_weight_grad = left_across(context, attn_low)
    out_bias_grad = jnp.sum(attn_low, axis=0, dtype=jnp.float32)
    context_grad = right_across(attn_low, weight_out).astype(jnp.bfloat16).reshape(split_heads)
    query_heads = queries.reshape(split_heads)
    key_heads = keys_all.reshape(split_heads)
    value_heads = values_all.reshape(split_heads)
    soft_full = jnp.exp(head_scores(query_heads, key_heads, lengths) - log_total)
    soft_grad = jnp.einsum(
        "bqhd,bkhd->bhqk", context_grad, value_heads, preferred_element_type=jnp.float32
    )
    value_grad = jnp.einsum(
        "bhqk,bqhd->bkhd",
        soft_full.astype(jnp.bfloat16),
        context_grad,
        preferred_element_type=jnp.float32,
    )
    value_grad = value_grad.reshape(row_count, D).astype(jnp.bfloat16)
    score_low = (
        soft_full * (soft_grad - jnp.sum(soft_full * soft_grad, axis=-1, keepdims=True))
    ).astype(jnp.bfloat16)
    query_grad_low = 0.125 * jnp.einsum(
        "bhqk,bkhd->bqhd", score_low, key_heads, preferred_element_type=jnp.float32
    )
    query_grad_low = query_grad_low.reshape(row_count, D).astype(jnp.bfloat16)
    key_grad_low = 0.125 * jnp.einsum(
        "bhqk,bqhd->bkhd", score_low, query_heads, preferred_element_type=jnp.float32
    )
    key_grad_low = key_grad_low.reshape(row_count, D).astype(jnp.bfloat16)
    token_grad = (
        attn_grad
        + right_across(query_grad_low, weight_query)
        + right_across(key_grad_low, weight_key)
        + right_across(value_grad, weight_value)
    )
    grads = (
        left_across(tokens, query_grad_low),
        jnp.sum(query_grad_low, axis=0, dtype=jnp.float32),
        left_across(tokens, key_grad_low),
        left_across(tokens, value_grad),
        jnp.sum(value_grad, axis=0, dtype=jnp.float32),
        out_weight_grad,
        out_bias_grad,
        gain_grad,
        shift_grad,
    )
    return (token_grad, grads)


def on_device(
    query_tokens,
    passage_tokens,
    query_lengths,
    passage_lengths,
    passage_valid,
    positives,
    negatives,
    teacher_margins,
    query_grad,
    passage_grad,
    weight_query,
    bias_query,
    weight_key,
    weight_value,
    bias_value,
    weight_out,
    bias_out,
    gain_attn,
    shift_attn,
    weight_in,
    bias_in,
    weight_back,
    bias_back,
    gain_ffn,
    shift_ffn,
):
    params = (
        weight_query,
        bias_query,
        weight_key,
        weight_value,
        bias_value,
        weight_out,
        bias_out,
        gain_attn,
        shift_attn,
        weight_in,
        bias_in,
        weight_back,
        bias_back,
        gain_ffn,
        shift_ffn,
    )
    query_out, query_kept = encode_forward(query_tokens, query_lengths, params)
    passage_out, passage_kept = encode_forward(passage_tokens, passage_lengths, params)
    query_slots = query_lengths.shape[0]
    passage_slots = passage_lengths.shape[0]
    cls_query = query_out.reshape(query_slots, -1, D)[:, 0]
    cls_passage = passage_out.reshape(passage_slots, -1, D)[:, 0]
    valid_low = passage_valid.astype(jnp.bfloat16)

    def score_piece(cls_piece, valid_piece):
        scores = score_scale * right_across(cls_query, cls_piece)
        position = lax.iota(jnp.int32, cls_piece.shape[0])
        is_positive = position[None, :] == positives[:, None]
        is_negative = position[None, :] == negatives[:, None]
        allowed = (valid_piece[None, :] > 0.5) | is_positive
        return (scores, allowed, is_positive, is_negative)

    peak_score = jnp.full((query_slots,), -1e30, jnp.float32)
    scores, allowed, is_positive, is_negative = score_piece(
        lax.all_gather(cls_passage, "dp", axis=0, tiled=True),
        lax.all_gather(valid_low, "dp", axis=0, tiled=True),
    )
    masked = jnp.where(allowed, scores, -1e30)
    new_peak = jnp.maximum(peak_score, jnp.max(masked, axis=1))
    row_total = jnp.sum(jnp.where(allowed, jnp.exp(masked - new_peak[:, None]), 0.0), axis=1)
    positive_score = jnp.sum(jnp.where(is_positive, scores, 0.0), axis=1)
    negative_score = jnp.sum(jnp.where(is_negative, scores, 0.0), axis=1)
    peak_score, row_total, positive_score, negative_score = (
        new_peak,
        row_total,
        positive_score,
        negative_score,
    )
    all_cls, all_valid = (
        lax.all_gather(cls_passage, "dp", axis=0, tiled=True),
        lax.all_gather(valid_low, "dp", axis=0, tiled=True),
    )
    log_total = peak_score + jnp.log(row_total)
    shortfall = positive_score - negative_score - teacher_margins
    query_loss = log_total - positive_score + margin_weight * shortfall * shortfall
    scores, allowed, is_positive, is_negative = score_piece(all_cls, all_valid)
    soft_scores = jnp.where(allowed, jnp.exp(scores - log_total[:, None]), 0.0)
    positive_hit = is_positive.astype(jnp.float32)
    negative_hit = is_negative.astype(jnp.float32)
    score_grad = (
        soft_scores
        - positive_hit
        + 2.0 * margin_weight * shortfall[:, None] * (positive_hit - negative_hit)
    ).astype(jnp.bfloat16)
    cls_query_grad = score_scale * matmul(score_grad, all_cls)
    cls_passage_grad = lax.psum_scatter(
        score_scale * left_across(score_grad, cls_query), "dp", scatter_dimension=0, tiled=True
    )
    query_upstream = (
        query_grad.astype(jnp.float32)
        .reshape(query_slots, -1, D)
        .at[:, 0]
        .add(cls_query_grad)
        .reshape(-1, D)
    )
    passage_upstream = (
        passage_grad.astype(jnp.float32)
        .reshape(passage_slots, -1, D)
        .at[:, 0]
        .add(cls_passage_grad)
        .reshape(-1, D)
    )
    query_middle_grad, query_ffn = ffn_backward(query_upstream, query_kept, params)
    passage_middle_grad, passage_ffn = ffn_backward(passage_upstream, passage_kept, params)
    (
        in_weight_grad,
        in_bias_grad,
        back_weight_grad,
        back_bias_grad,
        ffn_gain_grad,
        ffn_shift_grad,
    ) = tuple((first + second for first, second in zip(query_ffn, passage_ffn)))
    query_tokens_grad, query_attn = attention_backward(
        query_middle_grad, query_tokens, query_lengths, query_kept, params
    )
    passage_tokens_grad, passage_attn = attention_backward(
        passage_middle_grad, passage_tokens, passage_lengths, passage_kept, params
    )
    (
        query_weight_grad,
        query_bias_grad,
        key_weight_grad,
        value_weight_grad,
        value_bias_grad,
        out_weight_grad,
        out_bias_grad,
        attn_gain_grad,
        attn_shift_grad,
    ) = tuple((first + second for first, second in zip(query_attn, passage_attn)))
    (
        query_weight_grad,
        query_bias_grad,
        key_weight_grad,
        value_weight_grad,
        value_bias_grad,
        out_weight_grad,
        out_bias_grad,
        attn_gain_grad,
        attn_shift_grad,
        in_weight_grad,
        in_bias_grad,
        back_weight_grad,
        back_bias_grad,
        ffn_gain_grad,
        ffn_shift_grad,
    ) = (
        lax.psum_scatter(query_weight_grad, "dp", scatter_dimension=0, tiled=True),
        lax.psum_scatter(query_bias_grad, "dp", scatter_dimension=0, tiled=True),
        lax.psum_scatter(key_weight_grad, "dp", scatter_dimension=0, tiled=True),
        lax.psum_scatter(value_weight_grad, "dp", scatter_dimension=0, tiled=True),
        lax.psum_scatter(value_bias_grad, "dp", scatter_dimension=0, tiled=True),
        lax.psum_scatter(out_weight_grad, "dp", scatter_dimension=0, tiled=True),
        lax.psum_scatter(out_bias_grad, "dp", scatter_dimension=0, tiled=True),
        lax.psum_scatter(attn_gain_grad, "dp", scatter_dimension=0, tiled=True),
        lax.psum_scatter(attn_shift_grad, "dp", scatter_dimension=0, tiled=True),
        lax.psum_scatter(in_weight_grad, "dp", scatter_dimension=0, tiled=True),
        lax.psum_scatter(in_bias_grad, "dp", scatter_dimension=0, tiled=True),
        lax.psum_scatter(back_weight_grad, "dp", scatter_dimension=0, tiled=True),
        lax.psum_scatter(back_bias_grad, "dp", scatter_dimension=0, tiled=True),
        lax.psum_scatter(ffn_gain_grad, "dp", scatter_dimension=0, tiled=True),
        lax.psum_scatter(ffn_shift_grad, "dp", scatter_dimension=0, tiled=True),
    )
    return (
        query_out,
        passage_out,
        query_loss,
        query_tokens_grad,
        passage_tokens_grad,
        query_weight_grad,
        query_bias_grad,
        key_weight_grad,
        value_weight_grad,
        value_bias_grad,
        out_weight_grad,
        out_bias_grad,
        attn_gain_grad,
        attn_shift_grad,
        in_weight_grad,
        in_bias_grad,
        back_weight_grad,
        back_bias_grad,
        ffn_gain_grad,
        ffn_shift_grad,
    )


F32 = jnp.float32
BF16 = jnp.bfloat16
MESH = pl.DeviceIdType.MESH
FF = 3072
ROWS = 480
WIN = 240
SLOT = 220
NEG = -1000000000.0


def dot_nn(left, right):
    return jnp.dot(left, right, preferred_element_type=F32)


def dot_nt(left, right):
    return lax.dot_general(left, right, (((1,), (1,)), ((), ())), preferred_element_type=F32)


def dot_tn(left, right):
    return lax.dot_general(left, right, (((0,), (0,)), ((), ())), preferred_element_type=F32)


def row_of(ref, start=0, size=D):
    return ref[pl.ds(start, size)].astype(F32).reshape(1, size)


def iota(shape, dim):
    return lax.broadcasted_iota(jnp.int32, shape, dim)


def fold8(block):
    return jnp.sum(block.reshape(-1, 8, block.shape[-1]), axis=0)


def layer_kernel(
    qtok, ptok, qlen, plen, pvalid, pos, neg, margin, qgrad, pgrad,
    wq_h, bq, wk_h, wv_h, bv, wo_h, bo, ga, sa, wi_h, bi, wb_h, bb, gf, sf,
    qout_h, pout_h, loss_o, qtg_h, ptg_h, wqg, bqg, wkg, wvg, bvg, wog, bog, gag, sag,
    wig, big, wbg, bbg, gfg, sfg,
    wq, wk, wv, wo, wi, wb, pstage, x_s, xT, q_s, k_s, v_s, p_s, pq_s, c_s, cT, n1, n2, r1, r2,
    ml, mlT, act_s, actT, tmp, gp, qg_s, pg_s, qo_s, po_s, ex, dcls, vec, vecr, vecz,
    g_s, rc, ra, rb, rz,
    load_sem, out_sem, ex_send, ex_recv, c_send, c_recv, a_send, a_recv, b_send, b_recv,
    z_send, z_recv, v_send, v_recv, credit,
):
    me = lax.axis_index("dp")
    core = lax.rem(me, 2)
    xx = lax.rem(lax.div(me, 2), 2)
    yy = lax.rem(lax.div(me, 4), 2)
    zz = lax.div(me, 8)
    chip = lax.div(me, 2)
    partner = me + 1 - 2 * core
    x_peer = me + 2 - 4 * xx
    y_peer = me + 4 - 8 * yy
    plane = lax.rem(me, 8)

    loads = {}
    for at, (name, source, target) in enumerate((
        ("ptok", ptok, pstage), ("qtok", qtok, qo_s), ("wq", wq_h, wq), ("wk", wk_h, wk), ("wv", wv_h, wv),
        ("wo", wo_h, wo), ("wi", wi_h, wi), ("wb", wb_h, wb), ("qg", qgrad, qg_s), ("pg", pgrad, pg_s),
    )):
        loads[name] = pltpu.make_async_copy(source, target, load_sem.at[at])
        loads[name].start()

    barrier = pltpu.get_barrier_semaphore()
    for hop in range(1, 16):
        other = 2 * lax.rem(chip + hop, 16) + core
        pl.semaphore_signal(barrier, inc=1, device_id=(other,), device_id_type=MESH)
    pl.semaphore_signal(barrier, inc=1, device_id=(partner,), device_id_type=MESH)

    loads["ptok"].wait()
    loads["qtok"].wait()
    x_s[0:32, :] = qo_s[...]

    def copy_tokens(i, carry):
        x_s[pl.ds(pl.multiple_of(32 + i * 16, 16), 16), :] = pstage[pl.ds(pl.multiple_of(i * 16, 16), 16), :]
        return carry

    lax.fori_loop(0, 27, copy_tokens, 0)
    x_s[464:480, :] = jnp.concatenate(
        [pstage[432:440, :].astype(F32), jnp.zeros((8, D), F32)], axis=0
    ).astype(BF16)

    loads["wq"].wait()
    q_s[...] = ((dot_nn(x_s[...], wq[...]) + row_of(bq)).astype(BF16) * 0.125).astype(BF16)
    loads["wk"].wait()
    k_s[...] = dot_nn(x_s[...], wk[...]).astype(BF16)
    loads["wv"].wait()
    v_s[...] = (dot_nn(x_s[...], wv[...]) + row_of(bv)).astype(BF16)

    head_of = iota((12, 1, D), 2) // 64
    head_mask = (head_of == iota((12, 1, D), 0)).astype(F32)

    def spread(rows):
        return (rows.astype(F32)[None] * head_mask).astype(BF16).reshape(384, D)

    def gather_heads(stacked):
        return jnp.sum(stacked.reshape(12, 32, D) * head_mask, axis=0)

    raw = dot_nt(k_s[0:32, :], spread(q_s[0:32, :]))
    raw = jnp.where(iota((32, 384), 0) < qlen[0], raw, NEG)
    soft = jnp.exp(raw - jnp.max(raw, axis=0, keepdims=True))
    soft = (soft * (1.0 / jnp.sum(soft, axis=0, keepdims=True))).astype(BF16)
    pq_s[...] = soft
    c_s[0:32, :] = gather_heads(dot_tn(soft, v_s[0:32, :])).astype(BF16)

    lane = iota((1, 128), 1)
    half = ((lane < 64).astype(BF16), (lane >= 64).astype(BF16))
    key_at = iota((WIN, 1), 0)

    def attend(pair, carry):
        lanes = pl.ds(pl.multiple_of(pair * 128, 128), 128)
        for slot in range(2):
            low_at = 12 * slot
            rows = pl.ds(32 + 208 * slot, WIN)
            keys, queries = k_s[rows, lanes], q_s[rows, lanes]
            values_t = v_s[rows, lanes].T
            allowed = (key_at >= low_at) & (key_at < low_at + plen[slot])
            parts = []
            for h in range(2):
                scores = jnp.where(allowed, dot_nt(keys, queries * half[h]), NEG)
                e = jnp.exp(scores - jnp.max(scores, axis=0, keepdims=True))
                p = (e * (1.0 / jnp.sum(e, axis=0, keepdims=True))).astype(BF16)
                p_s[slot, 2 * pair + h] = p
                parts.append(dot_nn(values_t, p)[64 * h:64 * h + 64, :])
            context = jnp.concatenate(parts, axis=0).T
            if slot == 0:
                c_s[rows, lanes] = context.astype(BF16)
            else:
                old = c_s[240:256, lanes].astype(F32)
                c_s[240:256, lanes] = jnp.where(iota((16, 128), 0) >= 12, context[0:16], old).astype(BF16)
                c_s[256:480, lanes] = context[16:240].astype(BF16)
        return carry

    lax.fori_loop(0, 6, attend, 0)

    loads["wo"].wait()
    tmp[...] = dot_nn(c_s[...], wo[...])
    gain1, shift1, bias1 = row_of(ga), row_of(sa), row_of(bo)

    def norm_attn(i, carry):
        rows = pl.ds(pl.multiple_of(i * 16, 16), 16)
        hidden = tmp[rows, :] + x_s[rows, :].astype(F32) + bias1
        centered = hidden - jnp.mean(hidden, axis=-1, keepdims=True)
        inv = lax.rsqrt(jnp.mean(centered * centered, axis=-1, keepdims=True) + ln_eps)
        unit = centered * inv
        n1[rows, :] = unit
        r1[rows, :] = inv
        ml[rows, :] = (unit * gain1 + shift1).astype(BF16)
        return carry

    lax.fori_loop(0, 30, norm_attn, 0)

    loads["wi"].wait()
    loads["wb"].wait()

    def wb_tile(t):
        return wb[lax.div(t, 2), lax.rem(t, 2)].reshape(D, D)

    for t in range(4):
        cols = pl.ds(t * D, D)
        tmp[...] = dot_nn(ml[...], wi[:, cols])
        bias_t = row_of(bi, t * D)

        def activate(i, carry):
            rows = pl.ds(pl.multiple_of(i * 16, 16), 16)
            u = tmp[rows, :] + bias_t
            cdf = 0.5 * (1.0 + lax.erf(u * root_half))
            act_s[rows, :] = (u * cdf).astype(BF16)
            gp[rows, cols] = (cdf + u * inv_root_tau * jnp.exp(-0.5 * u * u)).astype(BF16)
            return carry

        lax.fori_loop(0, 30, activate, 0)
        if t == 0:
            n2[...] = dot_nn(act_s[...], wb_tile(t))
        else:
            n2[...] += dot_nn(act_s[...], wb_tile(t))
        actT[cols, :] = act_s[...].T

    gain2, shift2, bias2 = row_of(gf), row_of(sf), row_of(bb)

    def norm_ffn_at(r0, size):
        rows = pl.ds(r0, size)
        hidden = n2[rows, :] + (n1[rows, :] * gain1 + shift1) + bias2
        centered = hidden - jnp.mean(hidden, axis=-1, keepdims=True)
        inv = lax.rsqrt(jnp.mean(centered * centered, axis=-1, keepdims=True) + ln_eps)
        unit = centered * inv
        n2[rows, :] = unit
        r2[rows, :] = inv
        return (unit * gain2 + shift2).astype(BF16)

    qo_s[0:16, :] = norm_ffn_at(0, 16)
    qo_s[16:32, :] = norm_ffn_at(16, 16)

    def norm_ffn(i, carry):
        po_s[pl.ds(pl.multiple_of(i * 16, 16), 16), :] = norm_ffn_at(pl.multiple_of(32 + i * 16, 16), 16)
        return carry

    lax.fori_loop(0, 27, norm_ffn, 0)
    po_s[432:440, :] = norm_ffn_at(464, 16)[0:8]

    slot_me = core * 16 + chip
    base = pl.multiple_of(slot_me * 24, 8)
    first_rows = (
        qo_s[0:16, :].astype(F32)[0:1],
        po_s[0:16, :].astype(F32)[0:1],
        po_s[208:224, :].astype(F32)[12:13],
    )
    lane_row = iota((1, 128), 1)
    meta = jnp.zeros((1, 128), F32)
    for at, value in enumerate((
        pvalid[0].astype(F32), pvalid[1].astype(F32), pos[0].astype(F32), neg[0].astype(F32), margin[0],
    )):
        meta = jnp.where(lane_row == at, value, meta)
    pieces = [row[:, 128 * i:128 * i + 128] for row in first_rows for i in range(6)]
    ex[pl.ds(base, 24), :] = jnp.concatenate(pieces + [meta, jnp.zeros((5, 128), F32)], axis=0)

    pl.semaphore_wait(barrier, 16)
    sends = []
    for hop in range(1, 16):
        block = ex.at[pl.ds(base, 24), :]
        sends.append(pltpu.make_async_remote_copy(
            src_ref=block, dst_ref=block, send_sem=ex_send.at[hop], recv_sem=ex_recv.at[hop],
            device_id=(2 * lax.rem(chip + hop, 16) + core,), device_id_type=MESH,
        ))
        sends[-1].start()

    out_q = pltpu.make_async_copy(qo_s, qout_h, out_sem.at[0])
    out_p = pltpu.make_async_copy(po_s, pout_h, out_sem.at[1])
    out_q.start()
    out_p.start()

    mlT[...] = ml[...].T
    xT[...] = x_s[...].T
    cT[...] = c_s[...].T
    loads["qg"].wait()
    loads["pg"].wait()

    def ffn_norm_back(r0, upstream, sums):
        rows = pl.ds(r0, 16)
        unit = n2[rows, :]
        scaled = upstream * gain2
        hidden_grad = r2[rows, :] * (
            scaled
            - jnp.mean(scaled, axis=-1, keepdims=True)
            - unit * jnp.mean(scaled * unit, axis=-1, keepdims=True)
        )
        n2[rows, :] = hidden_grad
        rounded = hidden_grad.astype(BF16)
        ml[rows, :] = rounded
        return (
            sums[0] + fold8(upstream * unit), sums[1] + fold8(upstream), sums[2] + fold8(rounded.astype(F32)),
        )

    def middle_block(i, sums):
        upstream = pg_s[pl.ds(pl.multiple_of(i * 16, 16), 16), :].astype(F32)
        return ffn_norm_back(pl.multiple_of(32 + i * 16, 16), upstream, sums)

    zero8 = jnp.zeros((8, D), F32)
    sums = (zero8, zero8, zero8)
    sums = ffn_norm_back(16, qg_s[16:32, :].astype(F32), sums)
    sums = lax.fori_loop(1, 13, middle_block, sums)
    sums = lax.fori_loop(14, 27, middle_block, sums)
    last = jnp.concatenate([pg_s[432:440, :].astype(F32), jnp.zeros((8, D), F32)], axis=0)
    sums = ffn_norm_back(464, last, sums)

    for send in sends:
        send.wait()
    same_core = ex.at[pl.ds(pl.multiple_of(core * 384, 8), 384), :]
    across = pltpu.make_async_remote_copy(
        src_ref=same_core, dst_ref=same_core, send_sem=ex_send.at[0], recv_sem=ex_recv.at[0],
        device_id=(partner,), device_id_type=MESH,
    )
    across.start()
    across.wait()

    def first(r):
        return ex[pl.ds(r, 32, stride=24), :]

    cls_q = jnp.concatenate([first(i) for i in range(6)], axis=1)
    cls_0 = jnp.concatenate([first(6 + i) for i in range(6)], axis=1).astype(BF16)
    cls_1 = jnp.concatenate([first(12 + i) for i in range(6)], axis=1).astype(BF16)
    metas = first(18)
    metas_t = metas.T
    s0 = score_scale * dot_nt(cls_q.astype(BF16), cls_0)
    s1 = score_scale * dot_nt(cls_q.astype(BF16), cls_1)
    col = iota((1, 32), 1)
    passage = (4 * lax.rem(col, 16) + 2 * lax.div(col, 16)).astype(F32)
    at_pos, at_neg, wanted = metas[:, 2:3], metas[:, 3:4], metas[:, 4:5]
    pos0, pos1 = at_pos == passage, at_pos == passage + 1.0
    neg0, neg1 = at_neg == passage, at_neg == passage + 1.0
    m0 = jnp.where((metas_t[0:1, :] > 0.5) | pos0, s0, -1e30)
    m1 = jnp.where((metas_t[1:2, :] > 0.5) | pos1, s1, -1e30)
    peak = jnp.maximum(jnp.max(m0, axis=1, keepdims=True), jnp.max(m1, axis=1, keepdims=True))
    total = jnp.sum(jnp.exp(m0 - peak), axis=1, keepdims=True) + jnp.sum(jnp.exp(m1 - peak), axis=1, keepdims=True)
    lse = peak + jnp.log(total)

    def picked(where0, where1):
        return jnp.sum(jnp.where(where0, s0, 0.0), axis=1, keepdims=True) + jnp.sum(
            jnp.where(where1, s1, 0.0), axis=1, keepdims=True
        )

    at_positive = picked(pos0, pos1)
    miss = at_positive - picked(neg0, neg1) - wanted
    losses = lse - at_positive + margin_weight * miss * miss
    pos0, pos1, neg0, neg1 = (hit.astype(F32) for hit in (pos0, pos1, neg0, neg1))
    ds0 = (jnp.exp(m0 - lse) - pos0 + 2.0 * margin_weight * miss * (pos0 - neg0)).astype(BF16)
    ds1 = (jnp.exp(m1 - lse) - pos1 + 2.0 * margin_weight * miss * (pos1 - neg1)).astype(BF16)
    mine = iota((32, 1), 0) == slot_me
    mine_col = iota((1, 32), 1) == slot_me
    loss_o[...] = jnp.sum(jnp.where(mine, losses, 0.0), axis=0, keepdims=True)
    dq_all = score_scale * (dot_nn(ds0, cls_0) + dot_nn(ds1, cls_1))
    d_query = jnp.sum(jnp.where(mine, dq_all, 0.0), axis=0, keepdims=True)

    def passage_grad_row(ds):
        column = jnp.sum(jnp.where(mine_col, ds.astype(F32), 0.0), axis=1, keepdims=True)
        return score_scale * jnp.sum(column * cls_q, axis=0, keepdims=True)

    d_first = (d_query, passage_grad_row(ds0), passage_grad_row(ds1))

    row16 = iota((16, 1), 0)
    for r0, at, source, add in (
        (0, 0, qg_s[0:16, :], d_first[0]), (32, 0, pg_s[0:16, :], d_first[1]), (240, 12, pg_s[208:224, :], d_first[2]),
    ):
        upstream = source.astype(F32) + jnp.where(row16 == at, add, 0.0)
        sums = ffn_norm_back(r0, upstream, sums)
    vec[...] = jnp.zeros_like(vec)
    vec[5:6, :] = jnp.sum(sums[2], axis=0, keepdims=True)
    vec[6:7, :] = jnp.sum(sums[0], axis=0, keepdims=True)
    vec[7:8, :] = jnp.sum(sums[1], axis=0, keepdims=True)

    def chunk(k):
        return g_s.at[k] if k < 4 else wb.at[k - 4]

    def x_first(k):
        return k % 2 == 0

    def remote(source, target, send, recv, device):
        return pltpu.make_async_remote_copy(
            src_ref=source, dst_ref=target, send_sem=send, recv_sem=recv, device_id=(device,), device_id_type=MESH,
        )

    def step_c(k):
        return remote(chunk(k).at[1 - core], rc.at[k % 2], c_send.at[k], c_recv.at[k], partner)

    def step_a(k):
        half_away = chunk(k).at[core, :, :, 1 - xx] if x_first(k) else chunk(k).at[core, :, 1 - yy]
        return remote(half_away, ra.at[k], a_send.at[k], a_recv.at[k], x_peer if x_first(k) else y_peer)

    def step_b(k):
        away = chunk(k).at[core, :, 1 - yy, xx] if x_first(k) else chunk(k).at[core, :, yy, 1 - xx]
        return remote(away, rb.at[k], b_send.at[k], b_recv.at[k], y_peer if x_first(k) else x_peer)

    def step_z(k, hop):
        to = lax.rem(zz + hop, 4)
        return remote(
            chunk(k).at[core, to, yy, xx], rz.at[k, hop - 1], z_send.at[k, hop - 1], z_recv.at[k, hop - 1],
            to * 8 + plane,
        )

    def start_c(k):
        if k >= 2:
            pl.semaphore_wait(credit, 1)
        step_c(k).start()

    def end_c(k):
        step_c(k).wait()

        def add(z, carry):
            for y in range(2):
                for x in range(2):
                    chunk(k)[core, z, y, x] += rc[k % 2, z, y, x]
            return carry

        lax.fori_loop(0, 4, add, 0)
        if k < 4:
            pl.semaphore_signal(credit, inc=1, device_id=(partner,), device_id_type=MESH)
        step_a(k).start()

    def end_a(k):
        step_a(k).wait()

        def add(z, carry):
            for i in range(2):
                if x_first(k):
                    chunk(k)[core, z, i, xx] += ra[k, z, i]
                else:
                    chunk(k)[core, z, yy, i] += ra[k, z, i]
            return carry

        lax.fori_loop(0, 4, add, 0)
        step_b(k).start()

    def end_b(k):
        step_b(k).wait()

        def add(z, carry):
            chunk(k)[core, z, yy, xx] += rb[k, z]
            return carry

        lax.fori_loop(0, 4, add, 0)
        for hop in range(1, 4):
            step_z(k, hop).start()

    def end_z(k):
        for hop in range(1, 4):
            step_z(k, hop).wait()
        total = chunk(k)[core, zz, yy, xx].astype(F32)
        for hop in range(3):
            total += rz[k, hop].astype(F32)
        if k < 2:
            wbg[48 * k:48 * k + 48, :] = total
        elif k < 4:
            at = (k - 2) * 1536
            wig[:, at:at + 768] = total[0:24]
            wig[:, at + 768:at + 1536] = total[24:48]
        elif k == 4:
            wvg[...] = total[0:24]
            wog[...] = total[24:48]
        else:
            wqg[...] = total[0:24]
            wkg[...] = total[24:48]

    for h in range(2):
        def back_grad(t, carry):
            left = jnp.concatenate(
                [actT[pl.ds(pl.multiple_of(t * D + 96 * i + 48 * h, 16), 48), :] for i in range(8)], axis=0
            )
            grad = dot_nn(left, ml[...]).astype(BF16)
            for i in range(8):
                chunk(h)[i % 2, t, i // 4, (i // 2) % 2] = grad[48 * i:48 * i + 48]
            return carry

        lax.fori_loop(0, 4, back_grad, 0)
        start_c(h)

    for t in range(4):
        cols = pl.ds(t * D, D)
        tmp[...] = dot_nt(ml[...], wb_tile(t))

        def inner_back(i, total):
            rows = pl.ds(pl.multiple_of(i * 16, 16), 16)
            rounded = (tmp[rows, :] * gp[rows, cols].astype(F32)).astype(BF16)
            gp[rows, cols] = rounded
            return total + fold8(rounded.astype(F32))

        total = lax.fori_loop(0, 30, inner_back, zero8)
        vec[8 + t:9 + t, :] = jnp.sum(total, axis=0, keepdims=True)
        n2[...] += dot_nt(gp[:, cols], wi[:, cols])
        if t == 0:
            end_c(0)
        if t == 1:
            end_c(1)

    def pair_grad(k, left_0, right_0, left_1, right_1):
        def group(t, carry):
            rows = pl.ds(pl.multiple_of(t * 192, 16), 192)
            grad_0 = dot_nn(left_0[rows, :], right_0[...]).reshape(8, 24, D)
            grad_1 = dot_nn(left_1[rows, :], right_1[...]).reshape(8, 24, D)
            both = jnp.concatenate([grad_0, grad_1], axis=1).astype(BF16)
            for i in range(8):
                chunk(k)[i % 2, t, i // 4, (i // 2) % 2] = both[i]
            return carry

        lax.fori_loop(0, 4, group, 0)
        start_c(k)

    for j in range(2):
        pair_grad(2 + j, mlT, gp.at[:, pl.ds(2 * j * D, D)], mlT, gp.at[:, pl.ds((2 * j + 1) * D, D)])

    def attn_norm_back(i, sums):
        rows = pl.ds(pl.multiple_of(i * 16, 16), 16)
        upstream, unit = n2[rows, :], n1[rows, :]
        scaled = upstream * gain1
        hidden_grad = r1[rows, :] * (
            scaled
            - jnp.mean(scaled, axis=-1, keepdims=True)
            - unit * jnp.mean(scaled * unit, axis=-1, keepdims=True)
        )
        n1[rows, :] = hidden_grad
        rounded = hidden_grad.astype(BF16)
        ml[rows, :] = rounded
        return (
            sums[0] + fold8(upstream * unit), sums[1] + fold8(upstream), sums[2] + fold8(rounded.astype(F32)),
        )

    sums = lax.fori_loop(0, 30, attn_norm_back, (zero8, zero8, zero8))
    vec[2:3, :] = jnp.sum(sums[2], axis=0, keepdims=True)
    vec[3:4, :] = jnp.sum(sums[0], axis=0, keepdims=True)
    vec[4:5, :] = jnp.sum(sums[1], axis=0, keepdims=True)
    c_s[...] = dot_nt(ml[...], wo[...]).astype(BF16)
    end_c(2)
    end_c(3)

    q_rows, k_rows, v_rows = spread(q_s[0:32, :]), k_s[0:32, :], v_s[0:32, :]
    dc_rows = spread(c_s[0:32, :])
    soft = pq_s[...]
    dp = dot_nt(v_rows, dc_rows)
    soft_f = soft.astype(F32)
    ds = (soft_f * (dp - jnp.sum(soft_f * dp, axis=0, keepdims=True))).astype(BF16)
    v_s[0:32, :] = dot_nn(soft, dc_rows).astype(BF16)
    k_s[0:32, :] = dot_nn(ds, q_rows).astype(BF16)
    q_s[0:32, :] = (0.125 * gather_heads(dot_tn(ds, k_rows))).astype(BF16)

    def attend_back(pair, carry):
        lanes = pl.ds(pl.multiple_of(pair * 128, 128), 128)
        for slot in range(2):
            low_at = 12 * slot
            rows = pl.ds(32 + 208 * slot, WIN)
            keys, queries, values = k_s[rows, lanes], q_s[rows, lanes], v_s[rows, lanes]
            inside = ((key_at >= low_at) & (key_at < low_at + SLOT)).astype(BF16)
            upstream = c_s[rows, lanes] * inside
            keys_t = keys.T
            parts, dv, dk = [], 0.0, 0.0
            for h in range(2):
                p = p_s[slot, 2 * pair + h]
                dc = upstream * half[h]
                dp = dot_nt(values, dc)
                pf = p.astype(F32)
                ds = (pf * (dp - jnp.sum(pf * dp, axis=0, keepdims=True))).astype(BF16)
                dv += dot_nn(p, dc)
                dk += dot_nn(ds, queries * half[h])
                parts.append(dot_nn(keys_t, ds)[64 * h:64 * h + 64, :])
            dq = 0.125 * jnp.concatenate(parts, axis=0).T
            for ref, new in ((q_s, dq), (k_s, dk), (v_s, dv)):
                if slot == 0:
                    ref[32:240, lanes] = new[0:208].astype(BF16)
                    old = ref[240:272, lanes].astype(F32)
                    ref[240:272, lanes] = jnp.where(iota((32, 128), 0) < 12, new[208:240], old).astype(BF16)
                else:
                    old = ref[240:256, lanes].astype(F32)
                    ref[240:256, lanes] = jnp.where(iota((16, 128), 0) >= 12, new[0:16], old).astype(BF16)
                    ref[256:480, lanes] = new[16:240].astype(BF16)
        return carry

    lax.fori_loop(0, 3, attend_back, 0)
    end_a(0)
    end_a(1)
    lax.fori_loop(3, 6, attend_back, 0)

    def column_sum(ref):
        def step(i, total):
            return total + fold8(ref[pl.ds(pl.multiple_of(i * 16, 16), 16), :].astype(F32))

        return jnp.sum(lax.fori_loop(0, 30, step, zero8), axis=0, keepdims=True)

    vec[0:1, :] = column_sum(q_s)
    vec[1:2, :] = column_sum(v_s)
    end_b(0)
    end_b(1)
    pair_grad(4, xT, v_s, cT, ml)
    pair_grad(5, xT, q_s, xT, k_s)

    def vec_step(i, device):
        return remote(vec, vecr.at[i], v_send.at[i], v_recv.at[i], device)

    vec_step(0, partner).start()
    end_c(4)
    end_c(5)
    n1[...] += dot_nt(q_s[...], wq[...])
    vec_step(0, partner).wait()
    vec[...] += vecr[0]
    vec_step(1, x_peer).start()
    n1[...] += dot_nt(k_s[...], wk[...])
    vec_step(1, x_peer).wait()
    vec[...] += vecr[1]
    vec_step(2, y_peer).start()
    n1[...] += dot_nt(v_s[...], wv[...])
    vec_step(2, y_peer).wait()
    vec[...] += vecr[2]

    def vec_z(hop):
        return remote(
            vec, vecz.at[hop - 1], v_send.at[2 + hop], v_recv.at[2 + hop], lax.rem(zz + hop, 4) * 8 + plane
        )

    for hop in range(1, 4):
        vec_z(hop).start()
    out_qg = pltpu.make_async_copy(n1.at[0:32, :], qtg_h, out_sem.at[2])
    out_pg = pltpu.make_async_copy(n1.at[32:472, :], ptg_h, out_sem.at[3])
    out_qg.start()
    out_pg.start()
    end_z(0)
    end_z(1)
    for hop in range(1, 4):
        vec_z(hop).wait()
    whole = vec[...] + vecz[0] + vecz[1] + vecz[2]
    small = pltpu.roll(whole, D - 24 * me, 1)
    for at, ref in enumerate((bqg, bvg, bog, gag, sag, bbg, gfg, sfg)):
        ref[...] = small[at:at + 1, 0:24]
    wide = pltpu.roll(whole[8:16], D - 96 * plane, 1)
    big[...] = jnp.sum(jnp.where(iota((8, D), 0) == zz, wide, 0.0), axis=0, keepdims=True)[:, 0:96]

    end_a(2)
    end_a(3)
    end_b(2)
    end_b(3)
    end_a(4)
    end_a(5)
    end_z(2)
    end_z(3)
    end_b(4)
    end_b(5)
    end_z(4)
    end_z(5)
    out_q.wait()
    out_p.wait()
    out_qg.wait()
    out_pg.wait()


def on_device_small(*operands):
    (
        query_tokens, passage_tokens, query_lengths, passage_lengths, passage_valid, positives, negatives,
        teacher_margins, query_grad, passage_grad, weight_query, bias_query, weight_key, weight_value, bias_value,
        weight_out, bias_out, gain_attn, shift_attn, weight_in, bias_in, weight_back, bias_back, gain_ffn, shift_ffn,
    ) = operands
    hbm, vmem, smem = (pl.BlockSpec(memory_space=space) for space in (pl.ANY, pltpu.VMEM, pltpu.SMEM))
    shape = jax.ShapeDtypeStruct
    slabs = (2, 2, 4, 2, 2, 48, D)
    outs = pl.pallas_call(
        layer_kernel,
        out_shape=(
            shape((32, D), BF16), shape((440, D), BF16), shape((1, 1), F32), shape((32, D), F32), shape((440, D), F32),
            shape((24, D), F32), shape((1, 24), F32), shape((24, D), F32), shape((24, D), F32), shape((1, 24), F32),
            shape((24, D), F32), shape((1, 24), F32), shape((1, 24), F32), shape((1, 24), F32),
            shape((24, FF), F32), shape((1, 96), F32), shape((96, D), F32), shape((1, 24), F32), shape((1, 24), F32),
            shape((1, 24), F32),
        ),
        in_specs=[
            hbm, hbm, smem, smem, smem, smem, smem, smem, hbm, hbm,
            hbm, vmem, hbm, hbm, vmem, hbm, vmem, vmem, vmem, hbm, vmem, hbm, vmem, vmem, vmem,
        ],
        out_specs=(hbm, hbm, vmem, hbm, hbm) + (vmem,) * 15,
        scratch_shapes=[
            pltpu.VMEM((D, D), BF16), pltpu.VMEM((D, D), BF16), pltpu.VMEM((D, D), BF16), pltpu.VMEM((D, D), BF16),
            pltpu.VMEM((D, FF), BF16), pltpu.VMEM(slabs, BF16),
            pltpu.VMEM((440, D), BF16), pltpu.VMEM((ROWS, D), BF16), pltpu.VMEM((D, ROWS), BF16),
            pltpu.VMEM((ROWS, D), BF16), pltpu.VMEM((ROWS, D), BF16), pltpu.VMEM((ROWS, D), BF16),
            pltpu.VMEM((2, 12, WIN, WIN), BF16), pltpu.VMEM((32, 384), BF16),
            pltpu.VMEM((ROWS, D), BF16), pltpu.VMEM((D, ROWS), BF16),
            pltpu.VMEM((ROWS, D), F32), pltpu.VMEM((ROWS, D), F32), pltpu.VMEM((ROWS, 1), F32), pltpu.VMEM((ROWS, 1), F32),
            pltpu.VMEM((ROWS, D), BF16), pltpu.VMEM((D, ROWS), BF16),
            pltpu.VMEM((ROWS, D), BF16), pltpu.VMEM((FF, ROWS), BF16), pltpu.VMEM((ROWS, D), F32),
            pltpu.VMEM((ROWS, FF), BF16),
            pltpu.VMEM((32, D), BF16), pltpu.VMEM((440, D), BF16), pltpu.VMEM((32, D), BF16), pltpu.VMEM((440, D), BF16),
            pltpu.VMEM((768, 128), F32), pltpu.VMEM((8, D), F32),
            pltpu.VMEM((16, D), F32), pltpu.VMEM((3, 16, D), F32), pltpu.VMEM((3, 16, D), F32),
            pltpu.VMEM((4, 2, 4, 2, 2, 48, D), BF16),
            pltpu.VMEM((2, 4, 2, 2, 48, D), BF16), pltpu.VMEM((6, 4, 2, 48, D), BF16), pltpu.VMEM((6, 4, 48, D), BF16),
            pltpu.VMEM((6, 3, 48, D), BF16),
            pltpu.SemaphoreType.DMA((10,)), pltpu.SemaphoreType.DMA((4,)),
            pltpu.SemaphoreType.DMA((16,)), pltpu.SemaphoreType.DMA((16,)),
            pltpu.SemaphoreType.DMA((6,)), pltpu.SemaphoreType.DMA((6,)),
            pltpu.SemaphoreType.DMA((6,)), pltpu.SemaphoreType.DMA((6,)),
            pltpu.SemaphoreType.DMA((6,)), pltpu.SemaphoreType.DMA((6,)),
            pltpu.SemaphoreType.DMA((6, 3)), pltpu.SemaphoreType.DMA((6, 3)),
            pltpu.SemaphoreType.DMA((6,)), pltpu.SemaphoreType.DMA((6,)),
            pltpu.SemaphoreType.REGULAR,
        ],
        compiler_params=pltpu.CompilerParams(
            collective_id=0, has_side_effects=True, vmem_limit_bytes=64 * 1024 * 1024 - 65536,
        ),
        name="encoder_layer",
    )(
        query_tokens, passage_tokens, query_lengths, passage_lengths, passage_valid, positives, negatives,
        teacher_margins, query_grad, passage_grad, weight_query, bias_query, weight_key, weight_value, bias_value,
        weight_out, bias_out, gain_attn, shift_attn, weight_in, bias_in, weight_back.reshape(slabs), bias_back,
        gain_ffn, shift_ffn,
    )
    flat = lambda array: array.reshape(-1)
    return tuple(flat(out) if out.shape[0] == 1 else out for out in outs)


def solution(mesh):
    return jax.shard_map(
        on_device_small if mesh.shape["dp"] == 32 else on_device,
        mesh=mesh,
        in_specs=(
            P("dp", None),
            P("dp", None),
            P("dp"),
            P("dp"),
            P("dp"),
            P("dp"),
            P("dp"),
            P("dp"),
            P("dp", None),
            P("dp", None),
            P(),
            P(),
            P(),
            P(),
            P(),
            P(),
            P(),
            P(),
            P(),
            P(),
            P(),
            P(),
            P(),
            P(),
            P(),
        ),
        out_specs=(
            P("dp", None),
            P("dp", None),
            P("dp"),
            P("dp", None),
            P("dp", None),
            P("dp", None),
            P("dp"),
            P("dp", None),
            P("dp", None),
            P("dp"),
            P("dp", None),
            P("dp"),
            P("dp"),
            P("dp"),
            P("dp", None),
            P("dp"),
            P("dp", None),
            P("dp"),
            P("dp"),
            P("dp"),
        ),
        check_vma=False,
    )
```

```python
import jax
import jax.numpy as jnp
from jax import lax
from jax.experimental import pallas as pl
from jax.experimental.pallas import tpu as pltpu
from jax.sharding import PartitionSpec as P

D = 768
HEADS = 12
HEAD_DIM = 64


ln_eps = 1e-12
score_scale = 0.0625
margin_weight = 0.5
root_half = 0.7071067811865476
inv_root_tau = 0.3989422804014327


def matmul(left, right):
    return jnp.dot(left, right, preferred_element_type=jnp.float32)


def left_across(left, right):
    return lax.dot_general(
        left, right, (((0,), (0,)), ((), ())), preferred_element_type=jnp.float32
    )


def right_across(left, right):
    return lax.dot_general(
        left, right, (((1,), (1,)), ((), ())), preferred_element_type=jnp.float32
    )


def normalize(hidden, gain, shift):
    centered = hidden - jnp.mean(hidden, axis=-1, keepdims=True)
    inv_std = lax.rsqrt(jnp.mean(centered * centered, axis=-1, keepdims=True) + ln_eps)
    unit_rows = centered * inv_std
    return (unit_rows * gain.astype(jnp.float32) + shift.astype(jnp.float32), unit_rows, inv_std)


def normalize_back(upstream, unit_rows, inv_std, gain):
    scaled = upstream * gain.astype(jnp.float32)
    hidden_grad = inv_std * (
        scaled
        - jnp.mean(scaled, axis=-1, keepdims=True)
        - unit_rows * jnp.mean(scaled * unit_rows, axis=-1, keepdims=True)
    )
    return (hidden_grad, jnp.sum(upstream * unit_rows, axis=0), jnp.sum(upstream, axis=0))


def gelu_exact(inputs):
    return 0.5 * inputs * (1.0 + lax.erf(inputs * root_half))


def gelu_slope(inputs):
    return 0.5 * (1.0 + lax.erf(inputs * root_half)) + inputs * inv_root_tau * jnp.exp(
        -0.5 * inputs * inputs
    )


def head_scores(query_heads, key_heads, lengths):
    slot_length = query_heads.shape[1]
    allowed = (lax.iota(jnp.int32, slot_length)[None, :] < lengths[:, None])[:, None, None, :]
    raw_scores = 0.125 * jnp.einsum(
        "bqhd,bkhd->bhqk", query_heads, key_heads, preferred_element_type=jnp.float32
    )
    return jnp.where(allowed, raw_scores, -1000000000.0)


def encode_forward(tokens, lengths, params):
    (
        weight_query,
        bias_query,
        weight_key,
        weight_value,
        bias_value,
        weight_out,
        bias_out,
        gain_attn,
        shift_attn,
        weight_in,
        bias_in,
        weight_back,
        bias_back,
        gain_ffn,
        shift_ffn,
    ) = params
    slot_count = lengths.shape[0]
    row_count = tokens.shape[0]
    split_heads = (slot_count, row_count // slot_count, HEADS, HEAD_DIM)
    queries = (matmul(tokens, weight_query) + bias_query.astype(jnp.float32)).astype(jnp.bfloat16)
    keys_all = matmul(tokens, weight_key).astype(jnp.bfloat16)
    values_all = (matmul(tokens, weight_value) + bias_value.astype(jnp.float32)).astype(
        jnp.bfloat16
    )
    scores = head_scores(queries.reshape(split_heads), keys_all.reshape(split_heads), lengths)
    peak_score = jnp.max(scores, axis=-1, keepdims=True)
    exp_scores = jnp.exp(scores - peak_score)
    row_total = jnp.sum(exp_scores, axis=-1, keepdims=True)
    soft_low = (exp_scores / row_total).astype(jnp.bfloat16)
    log_total = peak_score + jnp.log(row_total)
    context = jnp.einsum(
        "bhqk,bkhd->bqhd",
        soft_low,
        values_all.reshape(split_heads),
        preferred_element_type=jnp.float32,
    )
    context = context.reshape(row_count, D).astype(jnp.bfloat16)
    attn_sum = (
        tokens.astype(jnp.float32) + matmul(context, weight_out) + bias_out.astype(jnp.float32)
    )
    middle, unit_attn, inv_attn = normalize(attn_sum, gain_attn, shift_attn)
    middle_low = middle.astype(jnp.bfloat16)
    inner_act = matmul(middle_low, weight_in) + bias_in.astype(jnp.float32)
    gelu_low = gelu_exact(inner_act).astype(jnp.bfloat16)
    ffn_sum = middle + matmul(gelu_low, weight_back) + bias_back.astype(jnp.float32)
    output, unit_ffn, inv_ffn = normalize(ffn_sum, gain_ffn, shift_ffn)
    kept = (
        queries,
        keys_all,
        values_all,
        log_total,
        context,
        unit_attn,
        inv_attn,
        middle_low,
        inner_act,
        gelu_low,
        unit_ffn,
        inv_ffn,
    )
    return (output.astype(jnp.bfloat16), kept)


def ffn_backward(upstream, kept, params):
    (
        queries,
        keys_all,
        values_all,
        log_total,
        context,
        unit_attn,
        inv_attn,
        middle_low,
        inner_act,
        gelu_low,
        unit_ffn,
        inv_ffn,
    ) = kept
    weight_in, weight_back, gain_ffn = (params[9], params[11], params[13])
    ffn_grad, gain_grad, shift_grad = normalize_back(upstream, unit_ffn, inv_ffn, gain_ffn)
    branch_low = ffn_grad.astype(jnp.bfloat16)
    back_weight_grad = left_across(gelu_low, branch_low)
    back_bias_grad = jnp.sum(branch_low, axis=0, dtype=jnp.float32)
    inner_low = (right_across(branch_low, weight_back) * gelu_slope(inner_act)).astype(jnp.bfloat16)
    in_weight_grad = left_across(middle_low, inner_low)
    in_bias_grad = jnp.sum(inner_low, axis=0, dtype=jnp.float32)
    middle_grad = ffn_grad + right_across(inner_low, weight_in)
    return (
        middle_grad,
        (in_weight_grad, in_bias_grad, back_weight_grad, back_bias_grad, gain_grad, shift_grad),
    )


def attention_backward(middle_grad, tokens, lengths, kept, params):
    (
        queries,
        keys_all,
        values_all,
        log_total,
        context,
        unit_attn,
        inv_attn,
        middle_low,
        inner_act,
        gelu_low,
        unit_ffn,
        inv_ffn,
    ) = kept
    weight_query, weight_key, weight_value, weight_out, gain_attn = (
        params[0],
        params[2],
        params[3],
        params[5],
        params[7],
    )
    slot_count = lengths.shape[0]
    row_count = tokens.shape[0]
    split_heads = (slot_count, row_count // slot_count, HEADS, HEAD_DIM)
    attn_grad, gain_grad, shift_grad = normalize_back(middle_grad, unit_attn, inv_attn, gain_attn)
    attn_low = attn_grad.astype(jnp.bfloat16)
    out_weight_grad = left_across(context, attn_low)
    out_bias_grad = jnp.sum(attn_low, axis=0, dtype=jnp.float32)
    context_grad = right_across(attn_low, weight_out).astype(jnp.bfloat16).reshape(split_heads)
    query_heads = queries.reshape(split_heads)
    key_heads = keys_all.reshape(split_heads)
    value_heads = values_all.reshape(split_heads)
    soft_full = jnp.exp(head_scores(query_heads, key_heads, lengths) - log_total)
    soft_grad = jnp.einsum(
        "bqhd,bkhd->bhqk", context_grad, value_heads, preferred_element_type=jnp.float32
    )
    value_grad = jnp.einsum(
        "bhqk,bqhd->bkhd",
        soft_full.astype(jnp.bfloat16),
        context_grad,
        preferred_element_type=jnp.float32,
    )
    value_grad = value_grad.reshape(row_count, D).astype(jnp.bfloat16)
    score_low = (
        soft_full * (soft_grad - jnp.sum(soft_full * soft_grad, axis=-1, keepdims=True))
    ).astype(jnp.bfloat16)
    query_grad_low = 0.125 * jnp.einsum(
        "bhqk,bkhd->bqhd", score_low, key_heads, preferred_element_type=jnp.float32
    )
    query_grad_low = query_grad_low.reshape(row_count, D).astype(jnp.bfloat16)
    key_grad_low = 0.125 * jnp.einsum(
        "bhqk,bqhd->bkhd", score_low, query_heads, preferred_element_type=jnp.float32
    )
    key_grad_low = key_grad_low.reshape(row_count, D).astype(jnp.bfloat16)
    token_grad = (
        attn_grad
        + right_across(query_grad_low, weight_query)
        + right_across(key_grad_low, weight_key)
        + right_across(value_grad, weight_value)
    )
    grads = (
        left_across(tokens, query_grad_low),
        jnp.sum(query_grad_low, axis=0, dtype=jnp.float32),
        left_across(tokens, key_grad_low),
        left_across(tokens, value_grad),
        jnp.sum(value_grad, axis=0, dtype=jnp.float32),
        out_weight_grad,
        out_bias_grad,
        gain_grad,
        shift_grad,
    )
    return (token_grad, grads)


def on_device(
    query_tokens,
    passage_tokens,
    query_lengths,
    passage_lengths,
    passage_valid,
    positives,
    negatives,
    teacher_margins,
    query_grad,
    passage_grad,
    weight_query,
    bias_query,
    weight_key,
    weight_value,
    bias_value,
    weight_out,
    bias_out,
    gain_attn,
    shift_attn,
    weight_in,
    bias_in,
    weight_back,
    bias_back,
    gain_ffn,
    shift_ffn,
):
    params = (
        weight_query,
        bias_query,
        weight_key,
        weight_value,
        bias_value,
        weight_out,
        bias_out,
        gain_attn,
        shift_attn,
        weight_in,
        bias_in,
        weight_back,
        bias_back,
        gain_ffn,
        shift_ffn,
    )
    query_out, query_kept = encode_forward(query_tokens, query_lengths, params)
    passage_out, passage_kept = encode_forward(passage_tokens, passage_lengths, params)
    query_slots = query_lengths.shape[0]
    passage_slots = passage_lengths.shape[0]
    cls_query = query_out.reshape(query_slots, -1, D)[:, 0]
    cls_passage = passage_out.reshape(passage_slots, -1, D)[:, 0]
    valid_low = passage_valid.astype(jnp.bfloat16)

    def score_piece(cls_piece, valid_piece):
        scores = score_scale * right_across(cls_query, cls_piece)
        position = lax.iota(jnp.int32, cls_piece.shape[0])
        is_positive = position[None, :] == positives[:, None]
        is_negative = position[None, :] == negatives[:, None]
        allowed = (valid_piece[None, :] > 0.5) | is_positive
        return (scores, allowed, is_positive, is_negative)

    peak_score = jnp.full((query_slots,), -1e30, jnp.float32)
    scores, allowed, is_positive, is_negative = score_piece(
        lax.all_gather(cls_passage, "dp", axis=0, tiled=True),
        lax.all_gather(valid_low, "dp", axis=0, tiled=True),
    )
    masked = jnp.where(allowed, scores, -1e30)
    new_peak = jnp.maximum(peak_score, jnp.max(masked, axis=1))
    row_total = jnp.sum(jnp.where(allowed, jnp.exp(masked - new_peak[:, None]), 0.0), axis=1)
    positive_score = jnp.sum(jnp.where(is_positive, scores, 0.0), axis=1)
    negative_score = jnp.sum(jnp.where(is_negative, scores, 0.0), axis=1)
    peak_score, row_total, positive_score, negative_score = (
        new_peak,
        row_total,
        positive_score,
        negative_score,
    )
    all_cls, all_valid = (
        lax.all_gather(cls_passage, "dp", axis=0, tiled=True),
        lax.all_gather(valid_low, "dp", axis=0, tiled=True),
    )
    log_total = peak_score + jnp.log(row_total)
    shortfall = positive_score - negative_score - teacher_margins
    query_loss = log_total - positive_score + margin_weight * shortfall * shortfall
    scores, allowed, is_positive, is_negative = score_piece(all_cls, all_valid)
    soft_scores = jnp.where(allowed, jnp.exp(scores - log_total[:, None]), 0.0)
    positive_hit = is_positive.astype(jnp.float32)
    negative_hit = is_negative.astype(jnp.float32)
    score_grad = (
        soft_scores
        - positive_hit
        + 2.0 * margin_weight * shortfall[:, None] * (positive_hit - negative_hit)
    ).astype(jnp.bfloat16)
    cls_query_grad = score_scale * matmul(score_grad, all_cls)
    cls_passage_grad = lax.psum_scatter(
        score_scale * left_across(score_grad, cls_query), "dp", scatter_dimension=0, tiled=True
    )
    query_upstream = (
        query_grad.astype(jnp.float32)
        .reshape(query_slots, -1, D)
        .at[:, 0]
        .add(cls_query_grad)
        .reshape(-1, D)
    )
    passage_upstream = (
        passage_grad.astype(jnp.float32)
        .reshape(passage_slots, -1, D)
        .at[:, 0]
        .add(cls_passage_grad)
        .reshape(-1, D)
    )
    query_middle_grad, query_ffn = ffn_backward(query_upstream, query_kept, params)
    passage_middle_grad, passage_ffn = ffn_backward(passage_upstream, passage_kept, params)
    (
        in_weight_grad,
        in_bias_grad,
        back_weight_grad,
        back_bias_grad,
        ffn_gain_grad,
        ffn_shift_grad,
    ) = tuple((first + second for first, second in zip(query_ffn, passage_ffn)))
    query_tokens_grad, query_attn = attention_backward(
        query_middle_grad, query_tokens, query_lengths, query_kept, params
    )
    passage_tokens_grad, passage_attn = attention_backward(
        passage_middle_grad, passage_tokens, passage_lengths, passage_kept, params
    )
    (
        query_weight_grad,
        query_bias_grad,
        key_weight_grad,
        value_weight_grad,
        value_bias_grad,
        out_weight_grad,
        out_bias_grad,
        attn_gain_grad,
        attn_shift_grad,
    ) = tuple((first + second for first, second in zip(query_attn, passage_attn)))
    (
        query_weight_grad,
        query_bias_grad,
        key_weight_grad,
        value_weight_grad,
        value_bias_grad,
        out_weight_grad,
        out_bias_grad,
        attn_gain_grad,
        attn_shift_grad,
        in_weight_grad,
        in_bias_grad,
        back_weight_grad,
        back_bias_grad,
        ffn_gain_grad,
        ffn_shift_grad,
    ) = (
        lax.psum_scatter(query_weight_grad, "dp", scatter_dimension=0, tiled=True),
        lax.psum_scatter(query_bias_grad, "dp", scatter_dimension=0, tiled=True),
        lax.psum_scatter(key_weight_grad, "dp", scatter_dimension=0, tiled=True),
        lax.psum_scatter(value_weight_grad, "dp", scatter_dimension=0, tiled=True),
        lax.psum_scatter(value_bias_grad, "dp", scatter_dimension=0, tiled=True),
        lax.psum_scatter(out_weight_grad, "dp", scatter_dimension=0, tiled=True),
        lax.psum_scatter(out_bias_grad, "dp", scatter_dimension=0, tiled=True),
        lax.psum_scatter(attn_gain_grad, "dp", scatter_dimension=0, tiled=True),
        lax.psum_scatter(attn_shift_grad, "dp", scatter_dimension=0, tiled=True),
        lax.psum_scatter(in_weight_grad, "dp", scatter_dimension=0, tiled=True),
        lax.psum_scatter(in_bias_grad, "dp", scatter_dimension=0, tiled=True),
        lax.psum_scatter(back_weight_grad, "dp", scatter_dimension=0, tiled=True),
        lax.psum_scatter(back_bias_grad, "dp", scatter_dimension=0, tiled=True),
        lax.psum_scatter(ffn_gain_grad, "dp", scatter_dimension=0, tiled=True),
        lax.psum_scatter(ffn_shift_grad, "dp", scatter_dimension=0, tiled=True),
    )
    return (
        query_out,
        passage_out,
        query_loss,
        query_tokens_grad,
        passage_tokens_grad,
        query_weight_grad,
        query_bias_grad,
        key_weight_grad,
        value_weight_grad,
        value_bias_grad,
        out_weight_grad,
        out_bias_grad,
        attn_gain_grad,
        attn_shift_grad,
        in_weight_grad,
        in_bias_grad,
        back_weight_grad,
        back_bias_grad,
        ffn_gain_grad,
        ffn_shift_grad,
    )


F32 = jnp.float32
BF16 = jnp.bfloat16
MESH = pl.DeviceIdType.MESH
FF = 3072
ROWS = 480
WIN = 240
SLOT = 220
NEG = -1000000000.0


def dot_nn(left, right):
    return jnp.dot(left, right, preferred_element_type=F32)


def dot_nt(left, right):
    return lax.dot_general(left, right, (((1,), (1,)), ((), ())), preferred_element_type=F32)


def dot_tn(left, right):
    return lax.dot_general(left, right, (((0,), (0,)), ((), ())), preferred_element_type=F32)


def row_of(ref, start=0, size=D):
    return ref[pl.ds(start, size)].astype(F32).reshape(1, size)


def iota(shape, dim):
    return lax.broadcasted_iota(jnp.int32, shape, dim)


def fold8(block):
    return jnp.sum(block.reshape(-1, 8, block.shape[-1]), axis=0)


def layer_kernel(
    qtok, ptok, qlen, plen, pvalid, pos, neg, margin, qgrad, pgrad,
    wq_h, bq, wk_h, wv_h, bv, wo_h, bo, ga, sa, wi_h, bi, wb_h, bb, gf, sf,
    qout_h, pout_h, qtg_h, ptg_h, wqg, wkg, wvg, wog, wig, wbg, small_o,
    wq, wk, wv, wo, wi, wb, pstage, x_s, xT, q_s, k_s, v_s, p_s, pq_s, c_s, cT, n1, n2, r1, r2,
    ml, mlT, act_s, actT, tmp, gp, qg_s, pg_s, qo_s, po_s, ex, dcls, vec, vecr, vecz,
    g_s, rc, ra, rb, rz,
    load_sem, out_sem, ex_send, ex_recv, c_send, c_recv, a_send, a_recv, b_send, b_recv,
    z_send, z_recv, v_send, v_recv, credit,
):
    me = lax.axis_index("dp")
    core = lax.rem(me, 2)
    xx = lax.rem(lax.div(me, 2), 2)
    yy = lax.rem(lax.div(me, 4), 2)
    zz = lax.div(me, 8)
    chip = lax.div(me, 2)
    partner = me + 1 - 2 * core
    x_peer = me + 2 - 4 * xx
    y_peer = me + 4 - 8 * yy
    plane = lax.rem(me, 8)

    loads = {}

    def load(name, source, target):
        loads[name] = pltpu.make_async_copy(source, target, load_sem.at[len(loads)])
        loads[name].start()

    load("ptok", ptok, pstage)
    load("qtok", qtok, qo_s)
    load("wq", wq_h, wq)
    load("wk", wk_h, wk)
    load("wv", wv_h, wv)

    barrier = pltpu.get_barrier_semaphore()
    for hop in range(1, 16):
        other = 2 * lax.rem(chip + hop, 16) + core
        pl.semaphore_signal(barrier, inc=1, device_id=(other,), device_id_type=MESH)
    pl.semaphore_signal(barrier, inc=1, device_id=(partner,), device_id_type=MESH)

    loads["ptok"].wait()
    loads["qtok"].wait()
    x_s[0:32, :] = qo_s[...]

    def copy_tokens(i, carry):
        x_s[pl.ds(pl.multiple_of(32 + i * 16, 16), 16), :] = pstage[pl.ds(pl.multiple_of(i * 16, 16), 16), :]
        return carry

    lax.fori_loop(0, 27, copy_tokens, 0)
    x_s[464:480, :] = jnp.concatenate(
        [pstage[432:440, :].astype(F32), jnp.zeros((8, D), F32)], axis=0
    ).astype(BF16)

    loads["wq"].wait()
    load("wo", wo_h, wo)
    load("wi", wi_h, wi)
    q_s[...] = ((dot_nn(x_s[...], wq[...]) + row_of(bq)).astype(BF16) * 0.125).astype(BF16)
    loads["wk"].wait()
    k_s[...] = dot_nn(x_s[...], wk[...]).astype(BF16)
    loads["wv"].wait()
    for h in range(2):
        load("wb" + str(h), wb_h.at[:, :, :, :, :, :, pl.ds(384 * h, 384)], wb.at[h])
    load("qg", qgrad, qg_s)
    load("pg", pgrad, pg_s)
    v_s[...] = (dot_nn(x_s[...], wv[...]) + row_of(bv)).astype(BF16)

    head_of = iota((12, 1, D), 2) // 64
    head_mask = (head_of == iota((12, 1, D), 0)).astype(F32)

    def spread(rows):
        return (rows.astype(F32)[None] * head_mask).astype(BF16).reshape(384, D)

    def gather_heads(stacked):
        return jnp.sum(stacked.reshape(12, 32, D) * head_mask, axis=0)

    raw = dot_nt(k_s[0:32, :], spread(q_s[0:32, :]))
    raw = jnp.where(iota((32, 384), 0) < qlen[0], raw, NEG)
    soft = jnp.exp(raw - jnp.max(raw, axis=0, keepdims=True))
    soft = (soft * (1.0 / jnp.sum(soft, axis=0, keepdims=True))).astype(BF16)
    pq_s[...] = soft
    c_s[0:32, :] = gather_heads(dot_tn(soft, v_s[0:32, :])).astype(BF16)

    lane = iota((1, 128), 1)
    half = ((lane < 64).astype(BF16), (lane >= 64).astype(BF16))
    key_at = iota((WIN, 1), 0)

    def attend(pair, carry):
        lanes = pl.ds(pl.multiple_of(pair * 128, 128), 128)
        for slot in range(2):
            low_at = 12 * slot
            rows = pl.ds(32 + 208 * slot, WIN)
            keys, queries = k_s[rows, lanes], q_s[rows, lanes]
            values_t = v_s[rows, lanes].T
            allowed = (key_at >= low_at) & (key_at < low_at + plen[slot])
            parts = []
            for h in range(2):
                scores = jnp.where(allowed, dot_nt(keys, queries * half[h]), NEG)
                e = jnp.exp(scores - jnp.max(scores, axis=0, keepdims=True))
                p = (e * (1.0 / jnp.sum(e, axis=0, keepdims=True))).astype(BF16)
                p_s[slot, 2 * pair + h] = p
                parts.append(dot_nn(values_t, p)[64 * h:64 * h + 64, :])
            context = jnp.concatenate(parts, axis=0).T
            if slot == 0:
                c_s[rows, lanes] = context.astype(BF16)
            else:
                old = c_s[240:256, lanes].astype(F32)
                c_s[240:256, lanes] = jnp.where(iota((16, 128), 0) >= 12, context[0:16], old).astype(BF16)
                c_s[256:480, lanes] = context[16:240].astype(BF16)
        return carry

    lax.fori_loop(0, 6, attend, 0)

    loads["wo"].wait()
    tmp[...] = dot_nn(c_s[...], wo[...])
    gain1, shift1, bias1 = row_of(ga), row_of(sa), row_of(bo)

    def norm_attn(i, carry):
        rows = pl.ds(pl.multiple_of(i * 48, 16), 48)
        hidden = tmp[rows, :] + x_s[rows, :].astype(F32) + bias1
        centered = hidden - jnp.mean(hidden, axis=-1, keepdims=True)
        inv = lax.rsqrt(jnp.mean(centered * centered, axis=-1, keepdims=True) + ln_eps)
        unit = centered * inv
        n1[rows, :] = unit
        r1[rows, :] = inv
        ml[rows, :] = (unit * gain1 + shift1).astype(BF16)
        return carry

    lax.fori_loop(0, 10, norm_attn, 0)

    loads["wi"].wait()
    loads["wb0"].wait()
    loads["wb1"].wait()

    def wb_tile(t):
        return jnp.concatenate([wb[h, t // 2, t % 2].reshape(D, 384) for h in range(2)], axis=1)

    for t in range(4):
        cols = pl.ds(t * D, D)
        tmp[...] = dot_nn(ml[...], wi[:, cols])
        bias_t = row_of(bi, t * D)

        def activate(i, carry):
            rows = pl.ds(pl.multiple_of(i * 16, 16), 16)
            u = tmp[rows, :] + bias_t
            cdf = 0.5 * (1.0 + lax.erf(u * root_half))
            act_s[rows, :] = (u * cdf).astype(BF16)
            gp[rows, cols] = (cdf + u * inv_root_tau * jnp.exp(-0.5 * u * u)).astype(BF16)
            return carry

        lax.fori_loop(0, 30, activate, 0)
        if t == 0:
            n2[...] = dot_nn(act_s[...], wb_tile(t))
        else:
            n2[...] += dot_nn(act_s[...], wb_tile(t))
        actT[cols, :] = act_s[...].T

    gain2, shift2, bias2 = row_of(gf), row_of(sf), row_of(bb)

    def norm_ffn_at(r0, size):
        rows = pl.ds(r0, size)
        hidden = n2[rows, :] + (n1[rows, :] * gain1 + shift1) + bias2
        centered = hidden - jnp.mean(hidden, axis=-1, keepdims=True)
        inv = lax.rsqrt(jnp.mean(centered * centered, axis=-1, keepdims=True) + ln_eps)
        unit = centered * inv
        n2[rows, :] = unit
        r2[rows, :] = inv
        return (unit * gain2 + shift2).astype(BF16)

    qo_s[...] = norm_ffn_at(0, 32)

    def norm_ffn(i, carry):
        po_s[pl.ds(pl.multiple_of(i * 48, 16), 48), :] = norm_ffn_at(pl.multiple_of(32 + i * 48, 16), 48)
        return carry

    lax.fori_loop(0, 9, norm_ffn, 0)
    po_s[432:440, :] = norm_ffn_at(464, 16)[0:8]

    slot_me = core * 16 + chip
    base = pl.multiple_of(slot_me * 24, 8)
    first_rows = (
        qo_s[0:16, :].astype(F32)[0:1],
        po_s[0:16, :].astype(F32)[0:1],
        po_s[208:224, :].astype(F32)[12:13],
    )
    lane_row = iota((1, 128), 1)
    meta = jnp.zeros((1, 128), F32)
    for at, value in enumerate((
        pvalid[0].astype(F32), pvalid[1].astype(F32), pos[0].astype(F32), neg[0].astype(F32), margin[0],
    )):
        meta = jnp.where(lane_row == at, value, meta)
    pieces = [row[:, 128 * i:128 * i + 128] for row in first_rows for i in range(6)]
    ex[pl.ds(base, 24), :] = jnp.concatenate(pieces + [meta, jnp.zeros((5, 128), F32)], axis=0)

    pl.semaphore_wait(barrier, 16)
    sends = []
    for hop in range(1, 16):
        block = ex.at[pl.ds(base, 24), :]
        sends.append(pltpu.make_async_remote_copy(
            src_ref=block, dst_ref=block, send_sem=ex_send.at[hop], recv_sem=ex_recv.at[hop],
            device_id=(2 * lax.rem(chip + hop, 16) + core,), device_id_type=MESH,
        ))
        sends[-1].start()

    out_q = pltpu.make_async_copy(qo_s, qout_h, out_sem.at[0])
    out_p = pltpu.make_async_copy(po_s, pout_h, out_sem.at[1])
    out_q.start()
    out_p.start()

    mlT[...] = ml[...].T
    xT[...] = x_s[...].T
    cT[...] = c_s[...].T
    loads["qg"].wait()
    loads["pg"].wait()

    def ffn_norm_back(r0, upstream, sums):
        rows = pl.ds(r0, upstream.shape[0])
        unit = n2[rows, :]
        scaled = upstream * gain2
        hidden_grad = r2[rows, :] * (
            scaled
            - jnp.mean(scaled, axis=-1, keepdims=True)
            - unit * jnp.mean(scaled * unit, axis=-1, keepdims=True)
        )
        n2[rows, :] = hidden_grad
        rounded = hidden_grad.astype(BF16)
        ml[rows, :] = rounded
        return (
            sums[0] + fold8(upstream * unit), sums[1] + fold8(upstream), sums[2] + fold8(rounded.astype(F32)),
        )

    def middle_block(i, sums):
        upstream = pg_s[pl.ds(pl.multiple_of(i * 32, 16), 32), :].astype(F32)
        return ffn_norm_back(pl.multiple_of(32 + i * 32, 16), upstream, sums)

    zero8 = jnp.zeros((8, D), F32)
    sums = (zero8, zero8, zero8)
    sums = lax.fori_loop(1, 6, middle_block, sums)
    sums = lax.fori_loop(7, 13, middle_block, sums)
    last = jnp.concatenate([pg_s[416:440, :].astype(F32), jnp.zeros((8, D), F32)], axis=0)
    sums = ffn_norm_back(448, last, sums)

    for send in sends:
        send.wait()
    same_core = ex.at[pl.ds(pl.multiple_of(core * 384, 8), 384), :]
    across = pltpu.make_async_remote_copy(
        src_ref=same_core, dst_ref=same_core, send_sem=ex_send.at[0], recv_sem=ex_recv.at[0],
        device_id=(partner,), device_id_type=MESH,
    )
    across.start()
    across.wait()

    def first(r):
        return ex[pl.ds(r, 32, stride=24), :]

    cls_q = jnp.concatenate([first(i) for i in range(6)], axis=1)
    cls_0 = jnp.concatenate([first(6 + i) for i in range(6)], axis=1).astype(BF16)
    cls_1 = jnp.concatenate([first(12 + i) for i in range(6)], axis=1).astype(BF16)
    metas = first(18)
    metas_t = metas.T
    s0 = score_scale * dot_nt(cls_q.astype(BF16), cls_0)
    s1 = score_scale * dot_nt(cls_q.astype(BF16), cls_1)
    col = iota((1, 32), 1)
    passage = (4 * lax.rem(col, 16) + 2 * lax.div(col, 16)).astype(F32)
    at_pos, at_neg, wanted = metas[:, 2:3], metas[:, 3:4], metas[:, 4:5]
    pos0, pos1 = at_pos == passage, at_pos == passage + 1.0
    neg0, neg1 = at_neg == passage, at_neg == passage + 1.0
    m0 = jnp.where((metas_t[0:1, :] > 0.5) | pos0, s0, -1e30)
    m1 = jnp.where((metas_t[1:2, :] > 0.5) | pos1, s1, -1e30)
    peak = jnp.maximum(jnp.max(m0, axis=1, keepdims=True), jnp.max(m1, axis=1, keepdims=True))
    total = jnp.sum(jnp.exp(m0 - peak), axis=1, keepdims=True) + jnp.sum(jnp.exp(m1 - peak), axis=1, keepdims=True)
    lse = peak + jnp.log(total)

    def picked(where0, where1):
        return jnp.sum(jnp.where(where0, s0, 0.0), axis=1, keepdims=True) + jnp.sum(
            jnp.where(where1, s1, 0.0), axis=1, keepdims=True
        )

    at_positive = picked(pos0, pos1)
    miss = at_positive - picked(neg0, neg1) - wanted
    losses = lse - at_positive + margin_weight * miss * miss
    pos0, pos1, neg0, neg1 = (hit.astype(F32) for hit in (pos0, pos1, neg0, neg1))
    ds0 = (jnp.exp(m0 - lse) - pos0 + 2.0 * margin_weight * miss * (pos0 - neg0)).astype(BF16)
    ds1 = (jnp.exp(m1 - lse) - pos1 + 2.0 * margin_weight * miss * (pos1 - neg1)).astype(BF16)
    mine = iota((32, 1), 0) == slot_me
    mine_col = iota((1, 32), 1) == slot_me
    small_o[9:10, :] = jnp.sum(jnp.where(mine, losses, 0.0), axis=0, keepdims=True) + jnp.zeros((1, 128), F32)
    dq_all = score_scale * (dot_nn(ds0, cls_0) + dot_nn(ds1, cls_1))
    d_query = jnp.sum(jnp.where(mine, dq_all, 0.0), axis=0, keepdims=True)

    def passage_grad_row(ds):
        column = jnp.sum(jnp.where(mine_col, ds.astype(F32), 0.0), axis=1, keepdims=True)
        return score_scale * jnp.sum(column * cls_q, axis=0, keepdims=True)

    d_first = (d_query, passage_grad_row(ds0), passage_grad_row(ds1))

    row32 = iota((32, 1), 0)
    for r0, at, source, add in (
        (0, 0, qg_s[...], d_first[0]), (32, 0, pg_s[0:32, :], d_first[1]), (224, 28, pg_s[192:224, :], d_first[2]),
    ):
        upstream = source.astype(F32) + jnp.where(row32 == at, add, 0.0)
        sums = ffn_norm_back(r0, upstream, sums)
    vec[...] = jnp.zeros_like(vec)
    vec[5:6, :] = jnp.sum(sums[2], axis=0, keepdims=True)
    vec[6:7, :] = jnp.sum(sums[0], axis=0, keepdims=True)
    vec[7:8, :] = jnp.sum(sums[1], axis=0, keepdims=True)

    def chunk(p, h):
        return g_s.at[p, h] if p < 4 else wb.at[h, p - 4]

    def remote(source, target, send, recv, device):
        return pltpu.make_async_remote_copy(
            src_ref=source, dst_ref=target, send_sem=send, recv_sem=recv, device_id=(device,), device_id_type=MESH,
        )

    def step_c(p, h):
        return remote(chunk(p, h).at[1 - core], rc.at[p % 2, h], c_send.at[p, h], c_recv.at[p, h], partner)

    def step_a(p, h):
        away = chunk(p, h).at[core, :, 1 - yy] if h else chunk(p, h).at[core, :, :, 1 - xx]
        return remote(away, ra.at[p, h], a_send.at[p, h], a_recv.at[p, h], y_peer if h else x_peer)

    def step_b(p, h):
        away = chunk(p, h).at[core, :, yy, 1 - xx] if h else chunk(p, h).at[core, :, 1 - yy, xx]
        return remote(away, rb.at[p, h], b_send.at[p, h], b_recv.at[p, h], x_peer if h else y_peer)

    def step_z(p, h, hop):
        to = lax.rem(zz + hop, 4)
        return remote(
            chunk(p, h).at[core, to, yy, xx], rz.at[p, h, hop - 1], z_send.at[p, h, hop - 1], z_recv.at[p, h, hop - 1],
            to * 8 + plane,
        )

    def start_c(p):
        for h in range(2):
            if p >= 2:
                pl.semaphore_wait(credit, 1)
            step_c(p, h).start()

    def end_c(p):
        for h in range(2):
            step_c(p, h).wait()

            def add(z, carry):
                for y in range(2):
                    for x in range(2):
                        chunk(p, h)[core, z, y, x] += rc[p % 2, h, z, y, x]
                return carry

            lax.fori_loop(0, 4, add, 0)
            step_a(p, h).start()
            if p < 4:
                pl.semaphore_signal(credit, inc=1, device_id=(partner,), device_id_type=MESH)

    def end_a(p):
        for h in range(2):
            step_a(p, h).wait()

            def add(z, carry):
                for i in range(2):
                    if h:
                        chunk(p, h)[core, z, yy, i] += ra[p, h, z, i]
                    else:
                        chunk(p, h)[core, z, i, xx] += ra[p, h, z, i]
                return carry

            lax.fori_loop(0, 4, add, 0)
            step_b(p, h).start()

    def end_b(p):
        for h in range(2):
            step_b(p, h).wait()

            def add(z, carry):
                chunk(p, h)[core, z, yy, xx] += rb[p, h, z]
                return carry

            lax.fori_loop(0, 4, add, 0)
            for hop in range(1, 4):
                step_z(p, h, hop).start()

    def end_z(p):
        for h in range(2):
            for hop in range(1, 4):
                step_z(p, h, hop).wait()
            total = chunk(p, h)[core, zz, yy, xx].astype(F32)
            for hop in range(3):
                total += rz[p, h, hop].astype(F32)
            at = 384 * h
            if p < 2:
                wbg[48 * p:48 * p + 48, at:at + 384] = total
                continue
            if p < 4:
                low_ref, high_ref, at, up = wig, wig, (p - 2) * 1536 + at, D
            elif p == 4:
                low_ref, high_ref, up = wvg, wog, 0
            else:
                low_ref, high_ref, up = wqg, wkg, 0
            low_ref[:, at:at + 384] = total[0:24]
            high_ref[:, at + up:at + up + 384] = total[24:48]

    def store_grad(p, t, i, grad):
        for h in range(2):
            chunk(p, h)[i % 2, t, i // 4, (i // 2) % 2] = grad[:, 384 * h:384 * h + 384]

    for h in range(2):
        def back_grad(t, carry):
            left = jnp.concatenate(
                [actT[pl.ds(pl.multiple_of(t * D + 96 * i + 48 * h, 16), 48), :] for i in range(8)], axis=0
            )
            grad = dot_nn(left, ml[...]).astype(BF16)
            for i in range(8):
                store_grad(h, t, i, grad[48 * i:48 * i + 48])
            return carry

        lax.fori_loop(0, 4, back_grad, 0)
        start_c(h)
        if h == 1:
            end_c(0)

    for t in range(4):
        cols = pl.ds(t * D, D)
        tmp[...] = dot_nt(ml[...], wb_tile(t))

        def inner_back(i, total):
            rows = pl.ds(pl.multiple_of(i * 16, 16), 16)
            rounded = (tmp[rows, :] * gp[rows, cols].astype(F32)).astype(BF16)
            gp[rows, cols] = rounded
            return total + fold8(rounded.astype(F32))

        total = lax.fori_loop(0, 30, inner_back, zero8)
        vec[8 + t:9 + t, :] = jnp.sum(total, axis=0, keepdims=True)
        n2[...] += dot_nt(gp[:, cols], wi[:, cols])
        if t == 0:
            end_c(1)
        if t == 2:
            end_a(0)

    def pair_grad(k, left_0, right_0, left_1, right_1):
        def group(t, carry):
            rows = pl.ds(pl.multiple_of(t * 192, 16), 192)
            grad_0 = dot_nn(left_0[rows, :], right_0[...]).reshape(8, 24, D)
            grad_1 = dot_nn(left_1[rows, :], right_1[...]).reshape(8, 24, D)
            both = jnp.concatenate([grad_0, grad_1], axis=1).astype(BF16)
            for i in range(8):
                store_grad(k, t, i, both[i])
            return carry

        lax.fori_loop(0, 4, group, 0)
        start_c(k)

    for j in range(2):
        if j == 1:
            end_c(2)
        pair_grad(2 + j, mlT, gp.at[:, pl.ds(2 * j * D, D)], mlT, gp.at[:, pl.ds((2 * j + 1) * D, D)])

    end_a(1)
    def attn_norm_back(i, sums):
        rows = pl.ds(pl.multiple_of(i * 32, 16), 32)
        upstream, unit = n2[rows, :], n1[rows, :]
        scaled = upstream * gain1
        hidden_grad = r1[rows, :] * (
            scaled
            - jnp.mean(scaled, axis=-1, keepdims=True)
            - unit * jnp.mean(scaled * unit, axis=-1, keepdims=True)
        )
        n1[rows, :] = hidden_grad
        rounded = hidden_grad.astype(BF16)
        ml[rows, :] = rounded
        return (
            sums[0] + fold8(upstream * unit), sums[1] + fold8(upstream), sums[2] + fold8(rounded.astype(F32)),
        )

    sums = lax.fori_loop(0, 15, attn_norm_back, (zero8, zero8, zero8))
    vec[2:3, :] = jnp.sum(sums[2], axis=0, keepdims=True)
    vec[3:4, :] = jnp.sum(sums[0], axis=0, keepdims=True)
    vec[4:5, :] = jnp.sum(sums[1], axis=0, keepdims=True)
    end_c(3)
    c_s[...] = dot_nt(ml[...], wo[...]).astype(BF16)

    q_rows, k_rows, v_rows = spread(q_s[0:32, :]), k_s[0:32, :], v_s[0:32, :]
    dc_rows = spread(c_s[0:32, :])
    soft = pq_s[...]
    dp = dot_nt(v_rows, dc_rows)
    soft_f = soft.astype(F32)
    ds = (soft_f * (dp - jnp.sum(soft_f * dp, axis=0, keepdims=True))).astype(BF16)
    v_s[0:32, :] = dot_nn(soft, dc_rows).astype(BF16)
    k_s[0:32, :] = dot_nn(ds, q_rows).astype(BF16)
    q_s[0:32, :] = (0.125 * gather_heads(dot_tn(ds, k_rows))).astype(BF16)

    def attend_back(pair, carry):
        lanes = pl.ds(pl.multiple_of(pair * 128, 128), 128)
        for slot in range(2):
            low_at = 12 * slot
            rows = pl.ds(32 + 208 * slot, WIN)
            keys, queries, values = k_s[rows, lanes], q_s[rows, lanes], v_s[rows, lanes]
            inside = ((key_at >= low_at) & (key_at < low_at + SLOT)).astype(BF16)
            upstream = c_s[rows, lanes] * inside
            keys_t = keys.T
            parts, dv, dk = [], 0.0, 0.0
            for h in range(2):
                p = p_s[slot, 2 * pair + h]
                dc = upstream * half[h]
                dp = dot_nt(values, dc)
                pf = p.astype(F32)
                ds = (pf * (dp - jnp.sum(pf * dp, axis=0, keepdims=True))).astype(BF16)
                dv += dot_nn(p, dc)
                dk += dot_nn(ds, queries * half[h])
                parts.append(dot_nn(keys_t, ds)[64 * h:64 * h + 64, :])
            dq = 0.125 * jnp.concatenate(parts, axis=0).T
            for ref, new in ((q_s, dq), (k_s, dk), (v_s, dv)):
                if slot == 0:
                    ref[32:240, lanes] = new[0:208].astype(BF16)
                    old = ref[240:272, lanes].astype(F32)
                    ref[240:272, lanes] = jnp.where(iota((32, 128), 0) < 12, new[208:240], old).astype(BF16)
                else:
                    old = ref[240:256, lanes].astype(F32)
                    ref[240:256, lanes] = jnp.where(iota((16, 128), 0) >= 12, new[0:16], old).astype(BF16)
                    ref[256:480, lanes] = new[16:240].astype(BF16)
        return carry

    lax.fori_loop(0, 2, attend_back, 0)
    end_b(0)
    lax.fori_loop(2, 4, attend_back, 0)
    end_a(2)
    lax.fori_loop(4, 6, attend_back, 0)
    end_b(1)

    def column_sum(ref):
        def step(i, total):
            return total + fold8(ref[pl.ds(pl.multiple_of(i * 16, 16), 16), :].astype(F32))

        return jnp.sum(lax.fori_loop(0, 30, step, zero8), axis=0, keepdims=True)

    vec[0:1, :] = column_sum(q_s)
    vec[1:2, :] = column_sum(v_s)
    def vec_step(i, device):
        return remote(vec, vecr.at[i], v_send.at[i], v_recv.at[i], device)

    def vec_z(hop):
        return remote(
            vec, vecz.at[hop - 1], v_send.at[2 + hop], v_recv.at[2 + hop], lax.rem(zz + hop, 4) * 8 + plane
        )

    vec_step(0, partner).start()
    pair_grad(4, xT, v_s, cT, ml)
    pair_grad(5, xT, q_s, xT, k_s)
    vec_step(0, partner).wait()
    vec[...] += vecr[0]
    vec_step(1, x_peer).start()
    end_a(3)
    end_c(4)
    n1[...] += dot_nt(q_s[...], wq[...])
    end_c(5)
    end_b(2)
    vec_step(1, x_peer).wait()
    vec[...] += vecr[1]
    vec_step(2, y_peer).start()
    n1[...] += dot_nt(k_s[...], wk[...])
    n1[...] += dot_nt(v_s[...], wv[...])
    out_qg = pltpu.make_async_copy(n1.at[0:32, :], qtg_h, out_sem.at[2])
    out_pg = pltpu.make_async_copy(n1.at[32:472, :], ptg_h, out_sem.at[3])
    out_qg.start()
    out_pg.start()
    end_z(0)
    end_z(1)
    vec_step(2, y_peer).wait()
    vec[...] += vecr[2]
    for hop in range(1, 4):
        vec_z(hop).start()
    end_a(4)
    end_b(3)
    end_z(2)
    for hop in range(1, 4):
        vec_z(hop).wait()
    whole = vec[...] + vecz[0] + vecz[1] + vecz[2]
    small_o[0:8, :] = pltpu.roll(whole[0:8], D - 24 * me, 1)[:, 0:128]
    wide = pltpu.roll(whole[8:16], D - 96 * plane, 1)
    small_o[8:9, :] = jnp.sum(jnp.where(iota((8, D), 0) == zz, wide, 0.0), axis=0, keepdims=True)[:, 0:128]
    end_a(5)
    end_b(4)
    end_z(3)
    end_b(5)
    end_z(4)
    end_z(5)
    out_q.wait()
    out_p.wait()
    out_qg.wait()
    out_pg.wait()


def hand_on_kernel(*refs):
    count = 10
    sources, small = refs[:count], refs[count]
    targets, vectors = refs[count + 1:2 * count + 1], refs[2 * count + 1:2 * count + 11]
    held, in_sem, out_sem = refs[2 * count + 11:3 * count + 11], refs[-2], refs[-1]
    into = [pltpu.make_async_copy(sources[i], held[i], in_sem.at[i]) for i in range(count)]
    out = [pltpu.make_async_copy(held[i], targets[i], out_sem.at[i]) for i in range(count)]
    for copy in into:
        copy.start()
    for at, ref in enumerate(vectors[:8]):
        ref[...] = small[at:at + 1, 0:24].reshape(24)
    vectors[8][...] = small[8:9, 0:96].reshape(96)
    vectors[9][...] = small[9:10, 0:1].reshape(1)
    for first, second in zip(into, out):
        first.wait()
        second.start()
    for copy in out:
        copy.wait()


def on_device_small(*operands):
    (
        query_tokens, passage_tokens, query_lengths, passage_lengths, passage_valid, positives, negatives,
        teacher_margins, query_grad, passage_grad, weight_query, bias_query, weight_key, weight_value, bias_value,
        weight_out, bias_out, gain_attn, shift_attn, weight_in, bias_in, weight_back, bias_back, gain_ffn, shift_ffn,
    ) = operands
    hbm, vmem, smem = (pl.BlockSpec(memory_space=space) for space in (pl.ANY, pltpu.VMEM, pltpu.SMEM))
    shape = jax.ShapeDtypeStruct
    slabs = (2, 2, 4, 2, 2, 48, D)
    large = (
        shape((32, D), BF16), shape((440, D), BF16), shape((32, D), F32), shape((440, D), F32), shape((24, D), F32),
        shape((24, D), F32), shape((24, D), F32), shape((24, D), F32), shape((24, FF), F32), shape((96, D), F32),
    )
    outs = pl.pallas_call(
        layer_kernel,
        out_shape=(
            *large, shape((16, 128), F32),
        ),
        in_specs=[
            hbm, hbm, smem, smem, smem, smem, smem, smem, hbm, hbm,
            hbm, vmem, hbm, hbm, vmem, hbm, vmem, vmem, vmem, hbm, vmem, hbm, vmem, vmem, vmem,
        ],
        out_specs=(hbm,) * 4 + (vmem,) * 7,
        scratch_shapes=[
            pltpu.VMEM((D, D), BF16), pltpu.VMEM((D, D), BF16), pltpu.VMEM((D, D), BF16), pltpu.VMEM((D, D), BF16),
            pltpu.VMEM((D, FF), BF16), pltpu.VMEM((2, 2, 2, 4, 2, 2, 48, 384), BF16),
            pltpu.VMEM((440, D), BF16), pltpu.VMEM((ROWS, D), BF16), pltpu.VMEM((D, ROWS), BF16),
            pltpu.VMEM((ROWS, D), BF16), pltpu.VMEM((ROWS, D), BF16), pltpu.VMEM((ROWS, D), BF16),
            pltpu.VMEM((2, 12, WIN, WIN), BF16), pltpu.VMEM((32, 384), BF16),
            pltpu.VMEM((ROWS, D), BF16), pltpu.VMEM((D, ROWS), BF16),
            pltpu.VMEM((ROWS, D), F32), pltpu.VMEM((ROWS, D), F32), pltpu.VMEM((ROWS, 1), F32), pltpu.VMEM((ROWS, 1), F32),
            pltpu.VMEM((ROWS, D), BF16), pltpu.VMEM((D, ROWS), BF16),
            pltpu.VMEM((ROWS, D), BF16), pltpu.VMEM((FF, ROWS), BF16), pltpu.VMEM((ROWS, D), F32),
            pltpu.VMEM((ROWS, FF), BF16),
            pltpu.VMEM((32, D), BF16), pltpu.VMEM((440, D), BF16), pltpu.VMEM((32, D), BF16), pltpu.VMEM((440, D), BF16),
            pltpu.VMEM((768, 128), F32), pltpu.VMEM((8, D), F32),
            pltpu.VMEM((16, D), F32), pltpu.VMEM((3, 16, D), F32), pltpu.VMEM((3, 16, D), F32),
            pltpu.VMEM((4, 2, 2, 4, 2, 2, 48, 384), BF16),
            pltpu.VMEM((2, 2, 4, 2, 2, 48, 384), BF16), pltpu.VMEM((6, 2, 4, 2, 48, 384), BF16),
            pltpu.VMEM((6, 2, 4, 48, 384), BF16), pltpu.VMEM((6, 2, 3, 48, 384), BF16),
            pltpu.SemaphoreType.DMA((12,)), pltpu.SemaphoreType.DMA((4,)),
            pltpu.SemaphoreType.DMA((16,)), pltpu.SemaphoreType.DMA((16,)),
            pltpu.SemaphoreType.DMA((6, 2)), pltpu.SemaphoreType.DMA((6, 2)),
            pltpu.SemaphoreType.DMA((6, 2)), pltpu.SemaphoreType.DMA((6, 2)),
            pltpu.SemaphoreType.DMA((6, 2)), pltpu.SemaphoreType.DMA((6, 2)),
            pltpu.SemaphoreType.DMA((6, 2, 3)), pltpu.SemaphoreType.DMA((6, 2, 3)),
            pltpu.SemaphoreType.DMA((6,)), pltpu.SemaphoreType.DMA((6,)),
            pltpu.SemaphoreType.REGULAR,
        ],
        compiler_params=pltpu.CompilerParams(
            collective_id=0, has_side_effects=True, vmem_limit_bytes=64 * 1024 * 1024 - 65536,
        ),
        name="encoder_layer",
    )(
        query_tokens, passage_tokens, query_lengths, passage_lengths, passage_valid, positives, negatives,
        teacher_margins, query_grad, passage_grad, weight_query, bias_query, weight_key, weight_value, bias_value,
        weight_out, bias_out, gain_attn, shift_attn, weight_in, bias_in, weight_back.reshape(slabs), bias_back,
        gain_ffn, shift_ffn,
    )
    done = pl.pallas_call(
        hand_on_kernel,
        out_shape=large + (shape((24,), F32),) * 8 + (shape((96,), F32), shape((1,), F32)),
        in_specs=[hbm] * 10 + [vmem],
        out_specs=(hbm,) * 10 + (vmem,) * 10,
        scratch_shapes=[pltpu.VMEM(out.shape, out.dtype) for out in large]
        + [pltpu.SemaphoreType.DMA((10,)), pltpu.SemaphoreType.DMA((10,))],
        name="hand_on",
    )(*outs)
    qout, pout, qtg, ptg, wqg, wkg, wvg, wog, wig, wbg, bqg, bvg, bog, gag, sag, bbg, gfg, sfg, big, loss = done
    return (
        qout, pout, loss, qtg, ptg, wqg, bqg, wkg, wvg, bvg, wog, bog, gag, sag, wig, big, wbg, bbg, gfg, sfg,
    )


def solution(mesh):
    return jax.shard_map(
        on_device_small if mesh.shape["dp"] == 32 else on_device,
        mesh=mesh,
        in_specs=(
            P("dp", None),
            P("dp", None),
            P("dp"),
            P("dp"),
            P("dp"),
            P("dp"),
            P("dp"),
            P("dp"),
            P("dp", None),
            P("dp", None),
            P(),
            P(),
            P(),
            P(),
            P(),
            P(),
            P(),
            P(),
            P(),
            P(),
            P(),
            P(),
            P(),
            P(),
            P(),
        ),
        out_specs=(
            P("dp", None),
            P("dp", None),
            P("dp"),
            P("dp", None),
            P("dp", None),
            P("dp", None),
            P("dp"),
            P("dp", None),
            P("dp", None),
            P("dp"),
            P("dp", None),
            P("dp"),
            P("dp"),
            P("dp"),
            P("dp", None),
            P("dp"),
            P("dp", None),
            P("dp"),
            P("dp"),
            P("dp"),
        ),
        check_vma=False,
    )
```

```python
import jax
import jax.numpy as jnp
from jax import lax
from jax.experimental import pallas as pl
from jax.experimental.pallas import tpu as pltpu
from jax.sharding import PartitionSpec as P

D = 768
HEADS = 12
HEAD_DIM = 64


ln_eps = 1e-12
score_scale = 0.0625
margin_weight = 0.5
root_half = 0.7071067811865476
inv_root_tau = 0.3989422804014327


def matmul(left, right):
    return jnp.dot(left, right, preferred_element_type=jnp.float32)


def left_across(left, right):
    return lax.dot_general(
        left, right, (((0,), (0,)), ((), ())), preferred_element_type=jnp.float32
    )


def right_across(left, right):
    return lax.dot_general(
        left, right, (((1,), (1,)), ((), ())), preferred_element_type=jnp.float32
    )


def normalize(hidden, gain, shift):
    centered = hidden - jnp.mean(hidden, axis=-1, keepdims=True)
    inv_std = lax.rsqrt(jnp.mean(centered * centered, axis=-1, keepdims=True) + ln_eps)
    unit_rows = centered * inv_std
    return (unit_rows * gain.astype(jnp.float32) + shift.astype(jnp.float32), unit_rows, inv_std)


def normalize_back(upstream, unit_rows, inv_std, gain):
    scaled = upstream * gain.astype(jnp.float32)
    hidden_grad = inv_std * (
        scaled
        - jnp.mean(scaled, axis=-1, keepdims=True)
        - unit_rows * jnp.mean(scaled * unit_rows, axis=-1, keepdims=True)
    )
    return (hidden_grad, jnp.sum(upstream * unit_rows, axis=0), jnp.sum(upstream, axis=0))


def gelu_exact(inputs):
    return 0.5 * inputs * (1.0 + lax.erf(inputs * root_half))


def gelu_slope(inputs):
    return 0.5 * (1.0 + lax.erf(inputs * root_half)) + inputs * inv_root_tau * jnp.exp(
        -0.5 * inputs * inputs
    )


def head_scores(query_heads, key_heads, lengths):
    slot_length = query_heads.shape[1]
    allowed = (lax.iota(jnp.int32, slot_length)[None, :] < lengths[:, None])[:, None, None, :]
    raw_scores = 0.125 * jnp.einsum(
        "bqhd,bkhd->bhqk", query_heads, key_heads, preferred_element_type=jnp.float32
    )
    return jnp.where(allowed, raw_scores, -1000000000.0)


def encode_forward(tokens, lengths, params):
    (
        weight_query,
        bias_query,
        weight_key,
        weight_value,
        bias_value,
        weight_out,
        bias_out,
        gain_attn,
        shift_attn,
        weight_in,
        bias_in,
        weight_back,
        bias_back,
        gain_ffn,
        shift_ffn,
    ) = params
    slot_count = lengths.shape[0]
    row_count = tokens.shape[0]
    split_heads = (slot_count, row_count // slot_count, HEADS, HEAD_DIM)
    queries = (matmul(tokens, weight_query) + bias_query.astype(jnp.float32)).astype(jnp.bfloat16)
    keys_all = matmul(tokens, weight_key).astype(jnp.bfloat16)
    values_all = (matmul(tokens, weight_value) + bias_value.astype(jnp.float32)).astype(
        jnp.bfloat16
    )
    scores = head_scores(queries.reshape(split_heads), keys_all.reshape(split_heads), lengths)
    peak_score = jnp.max(scores, axis=-1, keepdims=True)
    exp_scores = jnp.exp(scores - peak_score)
    row_total = jnp.sum(exp_scores, axis=-1, keepdims=True)
    soft_low = (exp_scores / row_total).astype(jnp.bfloat16)
    log_total = peak_score + jnp.log(row_total)
    context = jnp.einsum(
        "bhqk,bkhd->bqhd",
        soft_low,
        values_all.reshape(split_heads),
        preferred_element_type=jnp.float32,
    )
    context = context.reshape(row_count, D).astype(jnp.bfloat16)
    attn_sum = (
        tokens.astype(jnp.float32) + matmul(context, weight_out) + bias_out.astype(jnp.float32)
    )
    middle, unit_attn, inv_attn = normalize(attn_sum, gain_attn, shift_attn)
    middle_low = middle.astype(jnp.bfloat16)
    inner_act = matmul(middle_low, weight_in) + bias_in.astype(jnp.float32)
    gelu_low = gelu_exact(inner_act).astype(jnp.bfloat16)
    ffn_sum = middle + matmul(gelu_low, weight_back) + bias_back.astype(jnp.float32)
    output, unit_ffn, inv_ffn = normalize(ffn_sum, gain_ffn, shift_ffn)
    kept = (
        queries,
        keys_all,
        values_all,
        log_total,
        context,
        unit_attn,
        inv_attn,
        middle_low,
        inner_act,
        gelu_low,
        unit_ffn,
        inv_ffn,
    )
    return (output.astype(jnp.bfloat16), kept)


def ffn_backward(upstream, kept, params):
    (
        queries,
        keys_all,
        values_all,
        log_total,
        context,
        unit_attn,
        inv_attn,
        middle_low,
        inner_act,
        gelu_low,
        unit_ffn,
        inv_ffn,
    ) = kept
    weight_in, weight_back, gain_ffn = (params[9], params[11], params[13])
    ffn_grad, gain_grad, shift_grad = normalize_back(upstream, unit_ffn, inv_ffn, gain_ffn)
    branch_low = ffn_grad.astype(jnp.bfloat16)
    back_weight_grad = left_across(gelu_low, branch_low)
    back_bias_grad = jnp.sum(branch_low, axis=0, dtype=jnp.float32)
    inner_low = (right_across(branch_low, weight_back) * gelu_slope(inner_act)).astype(jnp.bfloat16)
    in_weight_grad = left_across(middle_low, inner_low)
    in_bias_grad = jnp.sum(inner_low, axis=0, dtype=jnp.float32)
    middle_grad = ffn_grad + right_across(inner_low, weight_in)
    return (
        middle_grad,
        (in_weight_grad, in_bias_grad, back_weight_grad, back_bias_grad, gain_grad, shift_grad),
    )


def attention_backward(middle_grad, tokens, lengths, kept, params):
    (
        queries,
        keys_all,
        values_all,
        log_total,
        context,
        unit_attn,
        inv_attn,
        middle_low,
        inner_act,
        gelu_low,
        unit_ffn,
        inv_ffn,
    ) = kept
    weight_query, weight_key, weight_value, weight_out, gain_attn = (
        params[0],
        params[2],
        params[3],
        params[5],
        params[7],
    )
    slot_count = lengths.shape[0]
    row_count = tokens.shape[0]
    split_heads = (slot_count, row_count // slot_count, HEADS, HEAD_DIM)
    attn_grad, gain_grad, shift_grad = normalize_back(middle_grad, unit_attn, inv_attn, gain_attn)
    attn_low = attn_grad.astype(jnp.bfloat16)
    out_weight_grad = left_across(context, attn_low)
    out_bias_grad = jnp.sum(attn_low, axis=0, dtype=jnp.float32)
    context_grad = right_across(attn_low, weight_out).astype(jnp.bfloat16).reshape(split_heads)
    query_heads = queries.reshape(split_heads)
    key_heads = keys_all.reshape(split_heads)
    value_heads = values_all.reshape(split_heads)
    soft_full = jnp.exp(head_scores(query_heads, key_heads, lengths) - log_total)
    soft_grad = jnp.einsum(
        "bqhd,bkhd->bhqk", context_grad, value_heads, preferred_element_type=jnp.float32
    )
    value_grad = jnp.einsum(
        "bhqk,bqhd->bkhd",
        soft_full.astype(jnp.bfloat16),
        context_grad,
        preferred_element_type=jnp.float32,
    )
    value_grad = value_grad.reshape(row_count, D).astype(jnp.bfloat16)
    score_low = (
        soft_full * (soft_grad - jnp.sum(soft_full * soft_grad, axis=-1, keepdims=True))
    ).astype(jnp.bfloat16)
    query_grad_low = 0.125 * jnp.einsum(
        "bhqk,bkhd->bqhd", score_low, key_heads, preferred_element_type=jnp.float32
    )
    query_grad_low = query_grad_low.reshape(row_count, D).astype(jnp.bfloat16)
    key_grad_low = 0.125 * jnp.einsum(
        "bhqk,bqhd->bkhd", score_low, query_heads, preferred_element_type=jnp.float32
    )
    key_grad_low = key_grad_low.reshape(row_count, D).astype(jnp.bfloat16)
    token_grad = (
        attn_grad
        + right_across(query_grad_low, weight_query)
        + right_across(key_grad_low, weight_key)
        + right_across(value_grad, weight_value)
    )
    grads = (
        left_across(tokens, query_grad_low),
        jnp.sum(query_grad_low, axis=0, dtype=jnp.float32),
        left_across(tokens, key_grad_low),
        left_across(tokens, value_grad),
        jnp.sum(value_grad, axis=0, dtype=jnp.float32),
        out_weight_grad,
        out_bias_grad,
        gain_grad,
        shift_grad,
    )
    return (token_grad, grads)


def on_device(
    query_tokens,
    passage_tokens,
    query_lengths,
    passage_lengths,
    passage_valid,
    positives,
    negatives,
    teacher_margins,
    query_grad,
    passage_grad,
    weight_query,
    bias_query,
    weight_key,
    weight_value,
    bias_value,
    weight_out,
    bias_out,
    gain_attn,
    shift_attn,
    weight_in,
    bias_in,
    weight_back,
    bias_back,
    gain_ffn,
    shift_ffn,
):
    params = (
        weight_query,
        bias_query,
        weight_key,
        weight_value,
        bias_value,
        weight_out,
        bias_out,
        gain_attn,
        shift_attn,
        weight_in,
        bias_in,
        weight_back,
        bias_back,
        gain_ffn,
        shift_ffn,
    )
    query_out, query_kept = encode_forward(query_tokens, query_lengths, params)
    passage_out, passage_kept = encode_forward(passage_tokens, passage_lengths, params)
    query_slots = query_lengths.shape[0]
    passage_slots = passage_lengths.shape[0]
    cls_query = query_out.reshape(query_slots, -1, D)[:, 0]
    cls_passage = passage_out.reshape(passage_slots, -1, D)[:, 0]
    valid_low = passage_valid.astype(jnp.bfloat16)

    def score_piece(cls_piece, valid_piece):
        scores = score_scale * right_across(cls_query, cls_piece)
        position = lax.iota(jnp.int32, cls_piece.shape[0])
        is_positive = position[None, :] == positives[:, None]
        is_negative = position[None, :] == negatives[:, None]
        allowed = (valid_piece[None, :] > 0.5) | is_positive
        return (scores, allowed, is_positive, is_negative)

    peak_score = jnp.full((query_slots,), -1e30, jnp.float32)
    scores, allowed, is_positive, is_negative = score_piece(
        lax.all_gather(cls_passage, "dp", axis=0, tiled=True),
        lax.all_gather(valid_low, "dp", axis=0, tiled=True),
    )
    masked = jnp.where(allowed, scores, -1e30)
    new_peak = jnp.maximum(peak_score, jnp.max(masked, axis=1))
    row_total = jnp.sum(jnp.where(allowed, jnp.exp(masked - new_peak[:, None]), 0.0), axis=1)
    positive_score = jnp.sum(jnp.where(is_positive, scores, 0.0), axis=1)
    negative_score = jnp.sum(jnp.where(is_negative, scores, 0.0), axis=1)
    peak_score, row_total, positive_score, negative_score = (
        new_peak,
        row_total,
        positive_score,
        negative_score,
    )
    all_cls, all_valid = (
        lax.all_gather(cls_passage, "dp", axis=0, tiled=True),
        lax.all_gather(valid_low, "dp", axis=0, tiled=True),
    )
    log_total = peak_score + jnp.log(row_total)
    shortfall = positive_score - negative_score - teacher_margins
    query_loss = log_total - positive_score + margin_weight * shortfall * shortfall
    scores, allowed, is_positive, is_negative = score_piece(all_cls, all_valid)
    soft_scores = jnp.where(allowed, jnp.exp(scores - log_total[:, None]), 0.0)
    positive_hit = is_positive.astype(jnp.float32)
    negative_hit = is_negative.astype(jnp.float32)
    score_grad = (
        soft_scores
        - positive_hit
        + 2.0 * margin_weight * shortfall[:, None] * (positive_hit - negative_hit)
    ).astype(jnp.bfloat16)
    cls_query_grad = score_scale * matmul(score_grad, all_cls)
    cls_passage_grad = lax.psum_scatter(
        score_scale * left_across(score_grad, cls_query), "dp", scatter_dimension=0, tiled=True
    )
    query_upstream = (
        query_grad.astype(jnp.float32)
        .reshape(query_slots, -1, D)
        .at[:, 0]
        .add(cls_query_grad)
        .reshape(-1, D)
    )
    passage_upstream = (
        passage_grad.astype(jnp.float32)
        .reshape(passage_slots, -1, D)
        .at[:, 0]
        .add(cls_passage_grad)
        .reshape(-1, D)
    )
    query_middle_grad, query_ffn = ffn_backward(query_upstream, query_kept, params)
    passage_middle_grad, passage_ffn = ffn_backward(passage_upstream, passage_kept, params)
    (
        in_weight_grad,
        in_bias_grad,
        back_weight_grad,
        back_bias_grad,
        ffn_gain_grad,
        ffn_shift_grad,
    ) = tuple((first + second for first, second in zip(query_ffn, passage_ffn)))
    query_tokens_grad, query_attn = attention_backward(
        query_middle_grad, query_tokens, query_lengths, query_kept, params
    )
    passage_tokens_grad, passage_attn = attention_backward(
        passage_middle_grad, passage_tokens, passage_lengths, passage_kept, params
    )
    (
        query_weight_grad,
        query_bias_grad,
        key_weight_grad,
        value_weight_grad,
        value_bias_grad,
        out_weight_grad,
        out_bias_grad,
        attn_gain_grad,
        attn_shift_grad,
    ) = tuple((first + second for first, second in zip(query_attn, passage_attn)))
    (
        query_weight_grad,
        query_bias_grad,
        key_weight_grad,
        value_weight_grad,
        value_bias_grad,
        out_weight_grad,
        out_bias_grad,
        attn_gain_grad,
        attn_shift_grad,
        in_weight_grad,
        in_bias_grad,
        back_weight_grad,
        back_bias_grad,
        ffn_gain_grad,
        ffn_shift_grad,
    ) = (
        lax.psum_scatter(query_weight_grad, "dp", scatter_dimension=0, tiled=True),
        lax.psum_scatter(query_bias_grad, "dp", scatter_dimension=0, tiled=True),
        lax.psum_scatter(key_weight_grad, "dp", scatter_dimension=0, tiled=True),
        lax.psum_scatter(value_weight_grad, "dp", scatter_dimension=0, tiled=True),
        lax.psum_scatter(value_bias_grad, "dp", scatter_dimension=0, tiled=True),
        lax.psum_scatter(out_weight_grad, "dp", scatter_dimension=0, tiled=True),
        lax.psum_scatter(out_bias_grad, "dp", scatter_dimension=0, tiled=True),
        lax.psum_scatter(attn_gain_grad, "dp", scatter_dimension=0, tiled=True),
        lax.psum_scatter(attn_shift_grad, "dp", scatter_dimension=0, tiled=True),
        lax.psum_scatter(in_weight_grad, "dp", scatter_dimension=0, tiled=True),
        lax.psum_scatter(in_bias_grad, "dp", scatter_dimension=0, tiled=True),
        lax.psum_scatter(back_weight_grad, "dp", scatter_dimension=0, tiled=True),
        lax.psum_scatter(back_bias_grad, "dp", scatter_dimension=0, tiled=True),
        lax.psum_scatter(ffn_gain_grad, "dp", scatter_dimension=0, tiled=True),
        lax.psum_scatter(ffn_shift_grad, "dp", scatter_dimension=0, tiled=True),
    )
    return (
        query_out,
        passage_out,
        query_loss,
        query_tokens_grad,
        passage_tokens_grad,
        query_weight_grad,
        query_bias_grad,
        key_weight_grad,
        value_weight_grad,
        value_bias_grad,
        out_weight_grad,
        out_bias_grad,
        attn_gain_grad,
        attn_shift_grad,
        in_weight_grad,
        in_bias_grad,
        back_weight_grad,
        back_bias_grad,
        ffn_gain_grad,
        ffn_shift_grad,
    )


F32 = jnp.float32
BF16 = jnp.bfloat16
MESH = pl.DeviceIdType.MESH
FF = 3072
ROWS = 480
WIN = 240
SLOT = 220
NEG = -1000000000.0


def dot_nn(left, right):
    return jnp.dot(left, right, preferred_element_type=F32)


def dot_nt(left, right):
    return lax.dot_general(left, right, (((1,), (1,)), ((), ())), preferred_element_type=F32)


def dot_tn(left, right):
    return lax.dot_general(left, right, (((0,), (0,)), ((), ())), preferred_element_type=F32)


def row_of(ref, start=0, size=D):
    return ref[pl.ds(start, size)].astype(F32).reshape(1, size)


def blocks(start, stop, size):
    return [(at, min(size, stop - at)) for at in range(start, stop, size)]


def iota(shape, dim):
    return lax.broadcasted_iota(jnp.int32, shape, dim)


def fold8(block):
    return jnp.sum(block.reshape(-1, 8, block.shape[-1]), axis=0)


Z_FIRST = (1, 1)
ORDER = (
    ("wback", 0), ("c", 0, 0), ("c", 0, 1), ("wback", 1), ("c", 1, 0), ("ec", 0, 0), ("c", 1, 1), ("dinner", 0),
    ("ec", 0, 1), ("dinner", 1), ("win", 2, (0, 1)), ("win", 2, (2, 3)), ("c", 2, 0), ("ec", 1, 0), ("c", 2, 1),
    ("dinner", 2), ("dinner", 3), ("ec", 1, 1), ("win", 3, (0, 1)), ("e1", 0, 0), ("ec", 2, 1), ("win", 3, (2, 3)),
    ("c", 3, 0), ("ec", 2, 0), ("c", 3, 1), ("dmid", 0), ("dmid", 1), ("dmid", 2), ("dmid", 3), ("ec", 3, 1),
    ("lnback",), ("ec", 3, 0), ("dctx",), ("e1", 0, 1), ("e2", 0, 0), ("qslot",), ("attn", 0), ("attn", 1),
    ("attn", 2), ("e1", 1, 0), ("attn", 3), ("attn", 4), ("attn", 5), ("e1", 3, 0), ("sums",), ("vec", 0),
    ("wvo", (0, 1)), ("e1", 3, 1), ("wvo", (2, 3)), ("c", 4, 0), ("e2", 1, 0), ("vec", 1), ("e1", 2, 0), ("c", 4, 1),
    ("wqk", (0, 1)), ("e3", 0, 0), ("e2", 0, 1), ("vec", 2), ("e1", 2, 1), ("wqk", (2, 3)), ("ec", 4, 1),
    ("e2", 3, 0), ("vec", 3), ("c", 5, 0), ("ec", 4, 0), ("e2", 3, 1), ("c", 5, 1), ("tq",), ("ec", 5, 1),
    ("e2", 2, 1), ("vecend",), ("e3", 1, 0), ("e1", 4, 1), ("ec", 5, 0), ("e1", 4, 0), ("tk",), ("e2", 4, 1),
    ("e2", 2, 0), ("e3", 0, 1), ("e3", 2, 1), ("e3", 4, 1), ("e1", 5, 1), ("e2", 4, 0), ("tv",), ("tout",),
    ("e1", 1, 1), ("e1", 5, 0), ("e2", 1, 1), ("e2", 5, 1), ("e3", 3, 0), ("e2", 5, 0), ("e3", 1, 1), ("e3", 5, 1),
    ("e3", 3, 1), ("e3", 2, 0), ("e3", 4, 0), ("e3", 5, 0),
)


def layer_kernel(
    qtok, ptok, qlen, plen, pvalid, pos, neg, margin, qgrad, pgrad,
    wq_h, bq_h, wk_h, wv_h, bv_h, wo_h, bo_h, ga_h, sa_h, wi_h, bi_h, wb_h, bb_h, gf_h, sf_h,
    qout_h, pout_h, qtg_h, ptg_h, wqg, wkg, wvg, wog, wig, wbg, small_o,
    bq, bv, bo, ga, sa, bi, bb, gf, sf, wq, wk, wv, wo, wi, wb, pstage, x_s, xT, q_s, k_s, v_s, p_s, pq_s, c_s, cT, n1, n2, r1, r2,
    ml, mlT, act_a, act_b, actT, tmp_a, tmp_b, gp, qg_s, pg_s, qo_s, po_s, ex, dcls, vec, vecr, vecz,
    g_s, rc, ra, rb, rz, rw,
    load_sem, out_sem, ex_send, ex_recv, c_send, c_recv, a_send, a_recv, b_send, b_recv,
    z_send, z_recv, v_send, v_recv, credit,
):
    me = lax.axis_index("dp")
    core = lax.rem(me, 2)
    xx = lax.rem(lax.div(me, 2), 2)
    yy = lax.rem(lax.div(me, 4), 2)
    zz = lax.div(me, 8)
    chip = lax.div(me, 2)
    partner = me + 1 - 2 * core
    x_peer = me + 2 - 4 * xx
    y_peer = me + 4 - 8 * yy
    plane = lax.rem(me, 8)

    loads = {}

    def load(name, source, target):
        loads[name] = pltpu.make_async_copy(source, target, load_sem.at[len(loads)])
        loads[name].start()

    load("ptok", ptok, pstage)
    load("qtok", qtok, qo_s)
    load("wq", wq_h, wq)
    load("wk", wk_h, wk)
    load("wv", wv_h, wv)
    vectors = ((bq_h, bq), (bv_h, bv), (bo_h, bo), (ga_h, ga), (sa_h, sa), (bi_h, bi), (bb_h, bb), (gf_h, gf), (sf_h, sf))
    for at, (source, target) in enumerate(vectors):
        load("vec" + str(at), source, target)

    barrier = pltpu.get_barrier_semaphore()
    for hop in range(1, 16):
        other = 2 * lax.rem(chip + hop, 16) + core
        pl.semaphore_signal(barrier, inc=1, device_id=(other,), device_id_type=MESH)
    pl.semaphore_signal(barrier, inc=1, device_id=(partner,), device_id_type=MESH)

    loads["ptok"].wait()
    loads["qtok"].wait()
    x_s[0:32, :] = qo_s[...]

    def copy_tokens(i, carry):
        x_s[pl.ds(pl.multiple_of(32 + i * 16, 16), 16), :] = pstage[pl.ds(pl.multiple_of(i * 16, 16), 16), :]
        return carry

    lax.fori_loop(0, 27, copy_tokens, 0)
    x_s[464:480, :] = jnp.concatenate(
        [pstage[432:440, :].astype(F32), jnp.zeros((8, D), F32)], axis=0
    ).astype(BF16)

    loads["wq"].wait()
    for at in range(len(vectors)):
        loads["vec" + str(at)].wait()
    load("wo", wo_h, wo)
    load("wi", wi_h, wi)
    q_s[...] = ((dot_nn(x_s[...], wq[...]) + row_of(bq)).astype(BF16) * 0.125).astype(BF16)
    loads["wk"].wait()
    k_s[...] = dot_nn(x_s[...], wk[...]).astype(BF16)
    loads["wv"].wait()
    for h in range(2):
        load("wb" + str(h), wb_h.at[:, :, :, :, :, :, pl.ds(384 * h, 384)], wb.at[h])
    load("qg", qgrad, qg_s)
    load("pg", pgrad, pg_s)
    v_s[...] = (dot_nn(x_s[...], wv[...]) + row_of(bv)).astype(BF16)

    head_of = iota((12, 1, D), 2) // 64
    head_mask = (head_of == iota((12, 1, D), 0)).astype(F32)

    def spread(rows):
        return (rows.astype(F32)[None] * head_mask).astype(BF16).reshape(384, D)

    def gather_heads(stacked):
        return jnp.sum(stacked.reshape(12, 32, D) * head_mask, axis=0)

    raw = dot_nt(k_s[0:32, :], spread(q_s[0:32, :]))
    raw = jnp.where(iota((32, 384), 0) < qlen[0], raw, NEG)
    soft = jnp.exp(raw - jnp.max(raw, axis=0, keepdims=True))
    soft = (soft * (1.0 / jnp.sum(soft, axis=0, keepdims=True))).astype(BF16)
    pq_s[...] = soft
    c_s[0:32, :] = gather_heads(dot_tn(soft, v_s[0:32, :])).astype(BF16)

    lane = iota((1, 128), 1)
    half = ((lane < 64).astype(BF16), (lane >= 64).astype(BF16))
    key_at = iota((WIN, 1), 0)

    def attend(pair, carry):
        lanes = pl.ds(pl.multiple_of(pair * 128, 128), 128)
        for slot in range(2):
            low_at = 12 * slot
            rows = pl.ds(32 + 208 * slot, WIN)
            keys, queries = k_s[rows, lanes], q_s[rows, lanes]
            values_t = v_s[rows, lanes].T
            allowed = (key_at >= low_at) & (key_at < low_at + plen[slot])
            parts = []
            for h in range(2):
                scores = jnp.where(allowed, dot_nt(keys, queries * half[h]), NEG)
                e = jnp.exp(scores - jnp.max(scores, axis=0, keepdims=True))
                p = (e * (1.0 / jnp.sum(e, axis=0, keepdims=True))).astype(BF16)
                p_s[slot, 2 * pair + h] = p
                parts.append(dot_nn(values_t, p)[64 * h:64 * h + 64, :])
            context = jnp.concatenate(parts, axis=0).T
            if slot == 0:
                c_s[rows, lanes] = context.astype(BF16)
            else:
                old = c_s[240:256, lanes].astype(F32)
                c_s[240:256, lanes] = jnp.where(iota((16, 128), 0) >= 12, context[0:16], old).astype(BF16)
                c_s[256:480, lanes] = context[16:240].astype(BF16)
        return carry

    lax.fori_loop(0, 6, attend, 0)

    loads["wo"].wait()
    gain1, shift1, bias1 = row_of(ga), row_of(sa), row_of(bo)
    gain2, shift2, bias2 = row_of(gf), row_of(sf), row_of(bb)

    def wb_tile(t):
        return jnp.concatenate([wb[h, t // 2, t % 2].reshape(D, 384) for h in range(2)], axis=1)

    def normalized(hidden):
        centered = hidden - jnp.mean(hidden, axis=-1, keepdims=True)
        inv = lax.rsqrt(jnp.mean(centered * centered, axis=-1, keepdims=True) + ln_eps)
        return centered * inv, inv

    def forward_rows(start, stop):
        size = stop - start
        every, own = pl.ds(start, size), pl.ds(0, size)
        tmp_a[own, :] = dot_nn(c_s[every, :], wo[...])
        for at, count in blocks(0, size, 32):
            rows, here = pl.ds(start + at, count), pl.ds(at, count)
            unit, inv = normalized(tmp_a[here, :] + x_s[rows, :].astype(F32) + bias1)
            n1[rows, :] = unit
            r1[rows, :] = inv
            ml[rows, :] = (unit * gain1 + shift1).astype(BF16)
        if start == 0:
            loads["wi"].wait()
            loads["wb0"].wait()
            loads["wb1"].wait()
        inner, acts = (tmp_a, tmp_b), (act_a, act_b)
        tmp_a[own, :] = dot_nn(ml[every, :], wi[:, 0:D])

        def finish(t):
            act = acts[t % 2][own, :]
            if t == 0:
                n2[every, :] = dot_nn(act, wb_tile(t))
            else:
                n2[every, :] += dot_nn(act, wb_tile(t))
            actT[t * D:t * D + D, every] = act.T

        for t in range(4):
            if t < 3:
                inner[(t + 1) % 2][own, :] = dot_nn(ml[every, :], wi[:, t * D + D:t * D + 2 * D])
            bias_t = row_of(bi, t * D)
            for at, count in blocks(0, size, 16):
                here = pl.ds(at, count)
                u = inner[t % 2][here, :] + bias_t
                cdf = 0.5 * (1.0 + lax.erf(u * root_half))
                acts[t % 2][here, :] = (u * cdf).astype(BF16)
                gp[start + at:start + at + count, t * D:t * D + D] = (
                    cdf + u * inv_root_tau * jnp.exp(-0.5 * u * u)
                ).astype(BF16)
            if t > 0:
                finish(t - 1)
        finish(3)
        for at, count in blocks(start, stop, 32):
            rows = pl.ds(at, count)
            unit, inv = normalized(n2[rows, :] + (n1[rows, :] * gain1 + shift1) + bias2)
            n2[rows, :] = unit
            r2[rows, :] = inv
            out = (unit * gain2 + shift2).astype(BF16)
            if at == 0:
                qo_s[...] = out
            else:
                po_s[at - 32:min(at, 440), :] = out[0:min(count, 472 - at)]

    forward_rows(0, 256)

    slot_me = core * 16 + chip
    base = pl.multiple_of(slot_me * 24, 8)
    first_rows = (
        qo_s[0:16, :].astype(F32)[0:1],
        po_s[0:16, :].astype(F32)[0:1],
        po_s[208:224, :].astype(F32)[12:13],
    )
    lane_row = iota((1, 128), 1)
    meta = jnp.zeros((1, 128), F32)
    for at, value in enumerate((
        pvalid[0].astype(F32), pvalid[1].astype(F32), pos[0].astype(F32), neg[0].astype(F32), margin[0],
    )):
        meta = jnp.where(lane_row == at, value, meta)
    pieces = [row[:, 128 * i:128 * i + 128] for row in first_rows for i in range(6)]
    ex[pl.ds(base, 24), :] = jnp.concatenate(pieces + [meta, jnp.zeros((5, 128), F32)], axis=0)

    pl.semaphore_wait(barrier, 16)
    sends = []
    for hop in range(1, 16):
        block = ex.at[pl.ds(base, 24), :]
        sends.append(pltpu.make_async_remote_copy(
            src_ref=block, dst_ref=block, send_sem=ex_send.at[hop], recv_sem=ex_recv.at[hop],
            device_id=(2 * lax.rem(chip + hop, 16) + core,), device_id_type=MESH,
        ))
        sends[-1].start()

    forward_rows(256, 480)
    out_q = pltpu.make_async_copy(qo_s, qout_h, out_sem.at[0])
    out_p = pltpu.make_async_copy(po_s, pout_h, out_sem.at[1])
    out_q.start()
    out_p.start()
    mlT[...] = ml[...].T
    loads["qg"].wait()
    loads["pg"].wait()

    def ffn_norm_back(r0, upstream, sums):
        rows = pl.ds(r0, upstream.shape[0])
        unit = n2[rows, :]
        scaled = upstream * gain2
        hidden_grad = r2[rows, :] * (
            scaled
            - jnp.mean(scaled, axis=-1, keepdims=True)
            - unit * jnp.mean(scaled * unit, axis=-1, keepdims=True)
        )
        n2[rows, :] = hidden_grad
        rounded = hidden_grad.astype(BF16)
        ml[rows, :] = rounded
        return (
            sums[0] + fold8(upstream * unit), sums[1] + fold8(upstream), sums[2] + fold8(rounded.astype(F32)),
        )

    zero8 = jnp.zeros((8, D), F32)
    sums = (zero8, zero8, zero8)
    for i in (1, 2, 3, 4, 5, 7, 8, 9, 10, 11, 12):
        sums = ffn_norm_back(32 + 32 * i, pg_s[32 * i:32 * i + 32, :].astype(F32), sums)
    last = jnp.concatenate([pg_s[416:440, :].astype(F32), jnp.zeros((8, D), F32)], axis=0)
    sums = ffn_norm_back(448, last, sums)

    for send in sends:
        send.wait()
    same_core = ex.at[pl.ds(pl.multiple_of(core * 384, 8), 384), :]
    across = pltpu.make_async_remote_copy(
        src_ref=same_core, dst_ref=same_core, send_sem=ex_send.at[0], recv_sem=ex_recv.at[0],
        device_id=(partner,), device_id_type=MESH,
    )
    across.start()
    xT[...] = x_s[...].T
    cT[...] = c_s[...].T
    across.wait()

    def first(r):
        return ex[pl.ds(r, 32, stride=24), :]

    cls_q = jnp.concatenate([first(i) for i in range(6)], axis=1)
    cls_0 = jnp.concatenate([first(6 + i) for i in range(6)], axis=1).astype(BF16)
    cls_1 = jnp.concatenate([first(12 + i) for i in range(6)], axis=1).astype(BF16)
    metas = first(18)
    metas_t = metas.T
    s0 = score_scale * dot_nt(cls_q.astype(BF16), cls_0)
    s1 = score_scale * dot_nt(cls_q.astype(BF16), cls_1)
    col = iota((1, 32), 1)
    passage = (4 * lax.rem(col, 16) + 2 * lax.div(col, 16)).astype(F32)
    at_pos, at_neg, wanted = metas[:, 2:3], metas[:, 3:4], metas[:, 4:5]
    pos0, pos1 = at_pos == passage, at_pos == passage + 1.0
    neg0, neg1 = at_neg == passage, at_neg == passage + 1.0
    m0 = jnp.where((metas_t[0:1, :] > 0.5) | pos0, s0, -1e30)
    m1 = jnp.where((metas_t[1:2, :] > 0.5) | pos1, s1, -1e30)
    peak = jnp.maximum(jnp.max(m0, axis=1, keepdims=True), jnp.max(m1, axis=1, keepdims=True))
    total = jnp.sum(jnp.exp(m0 - peak), axis=1, keepdims=True) + jnp.sum(jnp.exp(m1 - peak), axis=1, keepdims=True)
    lse = peak + jnp.log(total)

    def picked(where0, where1):
        return jnp.sum(jnp.where(where0, s0, 0.0), axis=1, keepdims=True) + jnp.sum(
            jnp.where(where1, s1, 0.0), axis=1, keepdims=True
        )

    at_positive = picked(pos0, pos1)
    miss = at_positive - picked(neg0, neg1) - wanted
    losses = lse - at_positive + margin_weight * miss * miss
    pos0, pos1, neg0, neg1 = (hit.astype(F32) for hit in (pos0, pos1, neg0, neg1))
    ds0 = (jnp.exp(m0 - lse) - pos0 + 2.0 * margin_weight * miss * (pos0 - neg0)).astype(BF16)
    ds1 = (jnp.exp(m1 - lse) - pos1 + 2.0 * margin_weight * miss * (pos1 - neg1)).astype(BF16)
    mine = iota((32, 1), 0) == slot_me
    mine_col = iota((1, 32), 1) == slot_me
    small_o[9:10, :] = jnp.sum(jnp.where(mine, losses, 0.0), axis=0, keepdims=True) + jnp.zeros((1, 128), F32)
    dq_all = score_scale * (dot_nn(ds0, cls_0) + dot_nn(ds1, cls_1))
    d_query = jnp.sum(jnp.where(mine, dq_all, 0.0), axis=0, keepdims=True)

    def passage_grad_row(ds):
        column = jnp.sum(jnp.where(mine_col, ds.astype(F32), 0.0), axis=1, keepdims=True)
        return score_scale * jnp.sum(column * cls_q, axis=0, keepdims=True)

    d_first = (d_query, passage_grad_row(ds0), passage_grad_row(ds1))

    row32 = iota((32, 1), 0)
    for r0, at, source, add in (
        (0, 0, qg_s[...], d_first[0]), (32, 0, pg_s[0:32, :], d_first[1]), (224, 28, pg_s[192:224, :], d_first[2]),
    ):
        upstream = source.astype(F32) + jnp.where(row32 == at, add, 0.0)
        sums = ffn_norm_back(r0, upstream, sums)
    vec[...] = jnp.zeros_like(vec)
    vec[5:6, :] = jnp.sum(sums[2], axis=0, keepdims=True)
    vec[6:7, :] = jnp.sum(sums[0], axis=0, keepdims=True)
    vec[7:8, :] = jnp.sum(sums[1], axis=0, keepdims=True)

    def chunk(p, h):
        return g_s.at[p, h] if p < 4 else wb.at[h, p - 4]

    def route(p, h):
        return "zyx" if (p, h) == Z_FIRST else ("xyz", "yxz")[h]

    def remote(source, target, send, recv, device):
        return pltpu.make_async_remote_copy(
            src_ref=source, dst_ref=target, send_sem=send, recv_sem=recv, device_id=(device,), device_id_type=MESH,
        )

    def step_c(p, h):
        return [remote(chunk(p, h).at[1 - core], rc.at[p % 2, h], c_send.at[p, h], c_recv.at[p, h], partner)]

    def along_z(p, h, pick, target):
        steps = []
        for hop in range(1, 4):
            to = lax.rem(zz + hop, 4)
            steps.append(remote(
                pick(to), target(hop - 1), z_send.at[p, h, hop - 1], z_recv.at[p, h, hop - 1], to * 8 + plane,
            ))
        return steps

    def step_1(p, h):
        mine, way = chunk(p, h), route(p, h)
        if way == "zyx":
            return along_z(p, h, lambda to: mine.at[core, to], lambda i: rw.at[i])
        away = mine.at[core, :, :, 1 - xx] if way == "xyz" else mine.at[core, :, 1 - yy]
        return [remote(away, ra.at[p, h], a_send.at[p, h], a_recv.at[p, h], x_peer if way == "xyz" else y_peer)]

    def step_2(p, h):
        mine, way = chunk(p, h), route(p, h)
        if way == "zyx":
            away, target = mine.at[core, zz, 1 - yy], rb.at[p, h, 0:2]
        elif way == "xyz":
            away, target = mine.at[core, :, 1 - yy, xx], rb.at[p, h]
        else:
            away, target = mine.at[core, :, yy, 1 - xx], rb.at[p, h]
        return [remote(away, target, b_send.at[p, h], b_recv.at[p, h], x_peer if way == "yxz" else y_peer)]

    def step_3(p, h):
        mine = chunk(p, h)
        if route(p, h) == "zyx":
            return [remote(
                mine.at[core, zz, yy, 1 - xx], rz.at[p, h, 0], a_send.at[p, h], a_recv.at[p, h], x_peer,
            )]
        return along_z(p, h, lambda to: mine.at[core, to, yy, xx], lambda i: rz.at[p, h, i])

    def begin(steps):
        for step in steps:
            step.start()

    def finish_steps(steps):
        for step in steps:
            step.wait()

    def start_c(p, h):
        if p >= 2:
            pl.semaphore_wait(credit.at[p % 2, h], 1)
        begin(step_c(p, h))

    def end_c(p, h):
        finish_steps(step_c(p, h))

        def add(z, carry):
            for y in range(2):
                for x in range(2):
                    chunk(p, h)[core, z, y, x] += rc[p % 2, h, z, y, x]
            return carry

        lax.fori_loop(0, 4, add, 0)
        begin(step_1(p, h))
        if p < 4:
            pl.semaphore_signal(credit.at[p % 2, h], inc=1, device_id=(partner,), device_id_type=MESH)

    def end_1(p, h):
        finish_steps(step_1(p, h))
        mine, way = chunk(p, h), route(p, h)
        if way == "zyx":
            def add(y, carry):
                for x in range(2):
                    total = mine[core, zz, y, x].astype(F32)
                    for i in range(3):
                        total += rw[i, y, x].astype(F32)
                    mine[core, zz, y, x] = total.astype(BF16)
                return carry

            lax.fori_loop(0, 2, add, 0)
        else:
            def add(z, carry):
                for i in range(2):
                    if way == "yxz":
                        mine[core, z, yy, i] += ra[p, h, z, i]
                    else:
                        mine[core, z, i, xx] += ra[p, h, z, i]
                return carry

            lax.fori_loop(0, 4, add, 0)
        begin(step_2(p, h))

    def end_2(p, h):
        finish_steps(step_2(p, h))
        mine = chunk(p, h)
        if route(p, h) == "zyx":
            for x in range(2):
                mine[core, zz, yy, x] += rb[p, h, x]
        else:
            def add(z, carry):
                mine[core, z, yy, xx] += rb[p, h, z]
                return carry

            lax.fori_loop(0, 4, add, 0)
        begin(step_3(p, h))

    def end_3(p, h):
        finish_steps(step_3(p, h))
        total = chunk(p, h)[core, zz, yy, xx].astype(F32)
        for i in range(1 if route(p, h) == "zyx" else 3):
            total += rz[p, h, i].astype(F32)
        at = 384 * h
        if p < 2:
            wbg[48 * p:48 * p + 48, at:at + 384] = total
            return
        if p < 4:
            low_ref, high_ref, at, up = wig, wig, (p - 2) * 1536 + at, D
        elif p == 4:
            low_ref, high_ref, up = wvg, wog, 0
        else:
            low_ref, high_ref, up = wqg, wkg, 0
        low_ref[:, at:at + 384] = total[0:24]
        high_ref[:, at + up:at + up + 384] = total[24:48]

    def store_grad(p, t, i, grad):
        for h in range(2):
            chunk(p, h)[i % 2, t, i // 4, (i // 2) % 2] = grad[:, 384 * h:384 * h + 384]

    def back_grad(p):
        for t in range(4):
            left = jnp.concatenate(
                [actT[t * D + 96 * i + 48 * p:t * D + 96 * i + 48 * p + 48, :] for i in range(8)], axis=0
            )
            grad = dot_nn(left, ml[...]).astype(BF16)
            for i in range(8):
                store_grad(p, t, i, grad[48 * i:48 * i + 48])

    def pair_grad(p, groups, left_0, right_0, left_1, right_1):
        for t in groups:
            rows = pl.ds(t * 192, 192)
            grad_0 = dot_nn(left_0[rows, :], right_0[...]).reshape(8, 24, D)
            grad_1 = dot_nn(left_1[rows, :], right_1[...]).reshape(8, 24, D)
            both = jnp.concatenate([grad_0, grad_1], axis=1).astype(BF16)
            for i in range(8):
                store_grad(p, t, i, both[i])

    def in_grad(p, groups):
        at = (p - 2) * 2 * D
        pair_grad(p, groups, mlT, gp.at[:, pl.ds(at, D)], mlT, gp.at[:, pl.ds(at + D, D)])

    def inner_grad(t):
        cols = pl.ds(t * D, D)
        weight = wb_tile(t)
        tmp_a[...] = dot_nt(ml[0:256, :], weight)
        tmp_b[0:224, :] = dot_nt(ml[256:480, :], weight)
        total = zero8
        for ref, start, size in ((tmp_a, 0, 256), (tmp_b, 256, 224)):
            for at, count in blocks(0, size, 16):
                rows = pl.ds(start + at, count)
                rounded = (ref[at:at + count, :] * gp[rows, cols].astype(F32)).astype(BF16)
                gp[rows, cols] = rounded
                total = total + fold8(rounded.astype(F32))
        vec[8 + t:9 + t, :] = jnp.sum(total, axis=0, keepdims=True)

    def middle_grad(t):
        cols = pl.ds(t * D, D)
        n2[...] += dot_nt(gp[:, cols], wi[:, cols])

    def attn_norm_back():
        sums = (zero8, zero8, zero8)
        for at, count in blocks(0, 480, 32):
            rows = pl.ds(at, count)
            upstream, unit = n2[rows, :], n1[rows, :]
            scaled = upstream * gain1
            hidden_grad = r1[rows, :] * (
                scaled
                - jnp.mean(scaled, axis=-1, keepdims=True)
                - unit * jnp.mean(scaled * unit, axis=-1, keepdims=True)
            )
            n1[rows, :] = hidden_grad
            rounded = hidden_grad.astype(BF16)
            ml[rows, :] = rounded
            sums = (
                sums[0] + fold8(upstream * unit), sums[1] + fold8(upstream), sums[2] + fold8(rounded.astype(F32)),
            )
        vec[2:3, :] = jnp.sum(sums[2], axis=0, keepdims=True)
        vec[3:4, :] = jnp.sum(sums[0], axis=0, keepdims=True)
        vec[4:5, :] = jnp.sum(sums[1], axis=0, keepdims=True)

    def context_grad():
        c_s[...] = dot_nt(ml[...], wo[...]).astype(BF16)

    def query_slot_back():
        q_rows, k_rows, v_rows = spread(q_s[0:32, :]), k_s[0:32, :], v_s[0:32, :]
        dc_rows = spread(c_s[0:32, :])
        soft = pq_s[...]
        dp = dot_nt(v_rows, dc_rows)
        soft_f = soft.astype(F32)
        ds = (soft_f * (dp - jnp.sum(soft_f * dp, axis=0, keepdims=True))).astype(BF16)
        v_s[0:32, :] = dot_nn(soft, dc_rows).astype(BF16)
        k_s[0:32, :] = dot_nn(ds, q_rows).astype(BF16)
        q_s[0:32, :] = (0.125 * gather_heads(dot_tn(ds, k_rows))).astype(BF16)

    def attend_back(pair):
        lanes = pl.ds(pair * 128, 128)
        for slot in range(2):
            low_at = 12 * slot
            rows = pl.ds(32 + 208 * slot, WIN)
            keys, queries, values = k_s[rows, lanes], q_s[rows, lanes], v_s[rows, lanes]
            inside = ((key_at >= low_at) & (key_at < low_at + SLOT)).astype(BF16)
            upstream = c_s[rows, lanes] * inside
            keys_t = keys.T
            parts, dv, dk = [], 0.0, 0.0
            for h in range(2):
                p = p_s[slot, 2 * pair + h]
                dc = upstream * half[h]
                dp = dot_nt(values, dc)
                pf = p.astype(F32)
                ds = (pf * (dp - jnp.sum(pf * dp, axis=0, keepdims=True))).astype(BF16)
                dv += dot_nn(p, dc)
                dk += dot_nn(ds, queries * half[h])
                parts.append(dot_nn(keys_t, ds)[64 * h:64 * h + 64, :])
            dq = 0.125 * jnp.concatenate(parts, axis=0).T
            for ref, new in ((q_s, dq), (k_s, dk), (v_s, dv)):
                if slot == 0:
                    ref[32:240, lanes] = new[0:208].astype(BF16)
                    old = ref[240:272, lanes].astype(F32)
                    ref[240:272, lanes] = jnp.where(iota((32, 128), 0) < 12, new[208:240], old).astype(BF16)
                else:
                    old = ref[240:256, lanes].astype(F32)
                    ref[240:256, lanes] = jnp.where(iota((16, 128), 0) >= 12, new[0:16], old).astype(BF16)
                    ref[256:480, lanes] = new[16:240].astype(BF16)

    def column_sum(ref):
        total = zero8
        for at, count in blocks(0, 480, 32):
            total = total + fold8(ref[at:at + count, :].astype(F32))
        return jnp.sum(total, axis=0, keepdims=True)

    def column_sums():
        vec[0:1, :] = column_sum(q_s)
        vec[1:2, :] = column_sum(v_s)

    def token_grad(grads, weight):
        n1[...] += dot_nt(grads[...], weight[...])

    out_qg = pltpu.make_async_copy(n1.at[0:32, :], qtg_h, out_sem.at[2])
    out_pg = pltpu.make_async_copy(n1.at[32:472, :], ptg_h, out_sem.at[3])

    def send_tokens():
        out_qg.start()
        out_pg.start()

    def vec_step(i):
        return remote(vec, vecr.at[i], v_send.at[i], v_recv.at[i], (partner, x_peer, y_peer)[i])

    def vec_z():
        return [
            remote(vec, vecz.at[hop - 1], v_send.at[2 + hop], v_recv.at[2 + hop], lax.rem(zz + hop, 4) * 8 + plane)
            for hop in range(1, 4)
        ]

    def vec_on(i):
        if i > 0:
            vec_step(i - 1).wait()
            vec[...] += vecr[i - 1]
        begin([vec_step(i)] if i < 3 else vec_z())

    def vec_end():
        finish_steps(vec_z())
        whole = vec[...] + vecz[0] + vecz[1] + vecz[2]
        small_o[0:8, :] = pltpu.roll(whole[0:8], D - 24 * me, 1)[:, 0:128]
        wide = pltpu.roll(whole[8:16], D - 96 * plane, 1)
        small_o[8:9, :] = jnp.sum(jnp.where(iota((8, D), 0) == zz, wide, 0.0), axis=0, keepdims=True)[:, 0:128]

    pieces_of = {
        "wback": back_grad, "dinner": inner_grad, "win": in_grad, "dmid": middle_grad, "lnback": attn_norm_back,
        "dctx": context_grad, "qslot": query_slot_back, "attn": attend_back, "sums": column_sums,
        "wvo": lambda groups: pair_grad(4, groups, xT, v_s, cT, ml),
        "wqk": lambda groups: pair_grad(5, groups, xT, q_s, xT, k_s),
        "tq": lambda: token_grad(q_s, wq), "tk": lambda: token_grad(k_s, wk), "tv": lambda: token_grad(v_s, wv),
        "tout": send_tokens, "vec": vec_on, "vecend": vec_end,
        "c": start_c, "ec": end_c, "e1": end_1, "e2": end_2, "e3": end_3,
    }
    for name, *operands in ORDER:
        pieces_of[name](*operands)

    out_q.wait()
    out_p.wait()
    out_qg.wait()
    out_pg.wait()


def hand_on_kernel(*refs):
    count = 10
    sources, small = refs[:count], refs[count]
    targets, vectors = refs[count + 1:2 * count + 1], refs[2 * count + 1:2 * count + 11]
    held, in_sem, out_sem = refs[2 * count + 11:3 * count + 11], refs[-2], refs[-1]
    into = [pltpu.make_async_copy(sources[i], held[i], in_sem.at[i]) for i in range(count)]
    out = [pltpu.make_async_copy(held[i], targets[i], out_sem.at[i]) for i in range(count)]
    for copy in into:
        copy.start()
    for at, ref in enumerate(vectors[:8]):
        ref[...] = small[at:at + 1, 0:24].reshape(24)
    vectors[8][...] = small[8:9, 0:96].reshape(96)
    vectors[9][...] = small[9:10, 0:1].reshape(1)
    for first, second in zip(into, out):
        first.wait()
        second.start()
    for copy in out:
        copy.wait()


def on_device_small(*operands):
    (
        query_tokens, passage_tokens, query_lengths, passage_lengths, passage_valid, positives, negatives,
        teacher_margins, query_grad, passage_grad, weight_query, bias_query, weight_key, weight_value, bias_value,
        weight_out, bias_out, gain_attn, shift_attn, weight_in, bias_in, weight_back, bias_back, gain_ffn, shift_ffn,
    ) = operands
    hbm, vmem, smem = (pl.BlockSpec(memory_space=space) for space in (pl.ANY, pltpu.VMEM, pltpu.SMEM))
    shape = jax.ShapeDtypeStruct
    slabs = (2, 2, 4, 2, 2, 48, D)
    large = (
        shape((32, D), BF16), shape((440, D), BF16), shape((32, D), F32), shape((440, D), F32), shape((24, D), F32),
        shape((24, D), F32), shape((24, D), F32), shape((24, D), F32), shape((24, FF), F32), shape((96, D), F32),
    )
    outs = pl.pallas_call(
        layer_kernel,
        out_shape=(
            *large, shape((16, 128), F32),
        ),
        in_specs=[
            hbm, hbm, smem, smem, smem, smem, smem, smem, hbm, hbm,
            *(hbm,) * 15,
        ],
        out_specs=(hbm,) * 4 + (vmem,) * 7,
        scratch_shapes=[
            *(pltpu.VMEM((size,), BF16) for size in (D, D, D, D, D, FF, D, D, D)),
            pltpu.VMEM((D, D), BF16), pltpu.VMEM((D, D), BF16), pltpu.VMEM((D, D), BF16), pltpu.VMEM((D, D), BF16),
            pltpu.VMEM((D, FF), BF16), pltpu.VMEM((2, 2, 2, 4, 2, 2, 48, 384), BF16),
            pltpu.VMEM((440, D), BF16), pltpu.VMEM((ROWS, D), BF16), pltpu.VMEM((D, ROWS), BF16),
            pltpu.VMEM((ROWS, D), BF16), pltpu.VMEM((ROWS, D), BF16), pltpu.VMEM((ROWS, D), BF16),
            pltpu.VMEM((2, 12, WIN, WIN), BF16), pltpu.VMEM((32, 384), BF16),
            pltpu.VMEM((ROWS, D), BF16), pltpu.VMEM((D, ROWS), BF16),
            pltpu.VMEM((ROWS, D), F32), pltpu.VMEM((ROWS, D), F32), pltpu.VMEM((ROWS, 1), F32), pltpu.VMEM((ROWS, 1), F32),
            pltpu.VMEM((ROWS, D), BF16), pltpu.VMEM((D, ROWS), BF16),
            pltpu.VMEM((256, D), BF16), pltpu.VMEM((256, D), BF16), pltpu.VMEM((FF, ROWS), BF16),
            pltpu.VMEM((256, D), F32), pltpu.VMEM((256, D), F32),
            pltpu.VMEM((ROWS, FF), BF16),
            pltpu.VMEM((32, D), BF16), pltpu.VMEM((440, D), BF16), pltpu.VMEM((32, D), BF16), pltpu.VMEM((440, D), BF16),
            pltpu.VMEM((768, 128), F32), pltpu.VMEM((8, D), F32),
            pltpu.VMEM((16, D), F32), pltpu.VMEM((3, 16, D), F32), pltpu.VMEM((3, 16, D), F32),
            pltpu.VMEM((4, 2, 2, 4, 2, 2, 48, 384), BF16),
            pltpu.VMEM((2, 2, 4, 2, 2, 48, 384), BF16), pltpu.VMEM((6, 2, 4, 2, 48, 384), BF16),
            pltpu.VMEM((6, 2, 4, 48, 384), BF16), pltpu.VMEM((6, 2, 3, 48, 384), BF16),
            pltpu.VMEM((3, 2, 2, 48, 384), BF16),
            pltpu.SemaphoreType.DMA((24,)), pltpu.SemaphoreType.DMA((4,)),
            pltpu.SemaphoreType.DMA((16,)), pltpu.SemaphoreType.DMA((16,)),
            pltpu.SemaphoreType.DMA((6, 2)), pltpu.SemaphoreType.DMA((6, 2)),
            pltpu.SemaphoreType.DMA((6, 2)), pltpu.SemaphoreType.DMA((6, 2)),
            pltpu.SemaphoreType.DMA((6, 2)), pltpu.SemaphoreType.DMA((6, 2)),
            pltpu.SemaphoreType.DMA((6, 2, 3)), pltpu.SemaphoreType.DMA((6, 2, 3)),
            pltpu.SemaphoreType.DMA((6,)), pltpu.SemaphoreType.DMA((6,)),
            pltpu.SemaphoreType.REGULAR((2, 2)),
        ],
        compiler_params=pltpu.CompilerParams(
            collective_id=0, has_side_effects=True, vmem_limit_bytes=64 * 1024 * 1024 - 65536,
        ),
        name="encoder_layer",
    )(
        query_tokens, passage_tokens, query_lengths, passage_lengths, passage_valid, positives, negatives,
        teacher_margins, query_grad, passage_grad, weight_query, bias_query, weight_key, weight_value, bias_value,
        weight_out, bias_out, gain_attn, shift_attn, weight_in, bias_in, weight_back.reshape(slabs), bias_back,
        gain_ffn, shift_ffn,
    )
    done = pl.pallas_call(
        hand_on_kernel,
        out_shape=large + (shape((24,), F32),) * 8 + (shape((96,), F32), shape((1,), F32)),
        in_specs=[hbm] * 10 + [vmem],
        out_specs=(hbm,) * 10 + (vmem,) * 10,
        scratch_shapes=[pltpu.VMEM(out.shape, out.dtype) for out in large]
        + [pltpu.SemaphoreType.DMA((10,)), pltpu.SemaphoreType.DMA((10,))],
        name="hand_on",
    )(*outs)
    qout, pout, qtg, ptg, wqg, wkg, wvg, wog, wig, wbg, bqg, bvg, bog, gag, sag, bbg, gfg, sfg, big, loss = done
    return (
        qout, pout, loss, qtg, ptg, wqg, bqg, wkg, wvg, bvg, wog, bog, gag, sag, wig, big, wbg, bbg, gfg, sfg,
    )


def solution(mesh):
    return jax.shard_map(
        on_device_small if mesh.shape["dp"] == 32 else on_device,
        mesh=mesh,
        in_specs=(
            P("dp", None),
            P("dp", None),
            P("dp"),
            P("dp"),
            P("dp"),
            P("dp"),
            P("dp"),
            P("dp"),
            P("dp", None),
            P("dp", None),
            P(),
            P(),
            P(),
            P(),
            P(),
            P(),
            P(),
            P(),
            P(),
            P(),
            P(),
            P(),
            P(),
            P(),
            P(),
        ),
        out_specs=(
            P("dp", None),
            P("dp", None),
            P("dp"),
            P("dp", None),
            P("dp", None),
            P("dp", None),
            P("dp"),
            P("dp", None),
            P("dp", None),
            P("dp"),
            P("dp", None),
            P("dp"),
            P("dp"),
            P("dp"),
            P("dp", None),
            P("dp"),
            P("dp", None),
            P("dp"),
            P("dp"),
            P("dp"),
        ),
        check_vma=False,
    )
```

```python
import jax
import jax.numpy as jnp
from jax import lax
from jax.experimental import pallas as pl
from jax.experimental.pallas import tpu as pltpu
from jax.sharding import PartitionSpec as P

D = 768
HEADS = 12
HEAD_DIM = 64


ln_eps = 1e-12
score_scale = 0.0625
margin_weight = 0.5
root_half = 0.7071067811865476
inv_root_tau = 0.3989422804014327


def matmul(left, right):
    return jnp.dot(left, right, preferred_element_type=jnp.float32)


def left_across(left, right):
    return lax.dot_general(
        left, right, (((0,), (0,)), ((), ())), preferred_element_type=jnp.float32
    )


def right_across(left, right):
    return lax.dot_general(
        left, right, (((1,), (1,)), ((), ())), preferred_element_type=jnp.float32
    )


def normalize(hidden, gain, shift):
    centered = hidden - jnp.mean(hidden, axis=-1, keepdims=True)
    inv_std = lax.rsqrt(jnp.mean(centered * centered, axis=-1, keepdims=True) + ln_eps)
    unit_rows = centered * inv_std
    return (unit_rows * gain.astype(jnp.float32) + shift.astype(jnp.float32), unit_rows, inv_std)


def normalize_back(upstream, unit_rows, inv_std, gain):
    scaled = upstream * gain.astype(jnp.float32)
    hidden_grad = inv_std * (
        scaled
        - jnp.mean(scaled, axis=-1, keepdims=True)
        - unit_rows * jnp.mean(scaled * unit_rows, axis=-1, keepdims=True)
    )
    return (hidden_grad, jnp.sum(upstream * unit_rows, axis=0), jnp.sum(upstream, axis=0))


def gelu_exact(inputs):
    return 0.5 * inputs * (1.0 + lax.erf(inputs * root_half))


def gelu_slope(inputs):
    return 0.5 * (1.0 + lax.erf(inputs * root_half)) + inputs * inv_root_tau * jnp.exp(
        -0.5 * inputs * inputs
    )


def head_scores(query_heads, key_heads, lengths):
    slot_length = query_heads.shape[1]
    allowed = (lax.iota(jnp.int32, slot_length)[None, :] < lengths[:, None])[:, None, None, :]
    raw_scores = 0.125 * jnp.einsum(
        "bqhd,bkhd->bhqk", query_heads, key_heads, preferred_element_type=jnp.float32
    )
    return jnp.where(allowed, raw_scores, -1000000000.0)


def encode_forward(tokens, lengths, params):
    (
        weight_query,
        bias_query,
        weight_key,
        weight_value,
        bias_value,
        weight_out,
        bias_out,
        gain_attn,
        shift_attn,
        weight_in,
        bias_in,
        weight_back,
        bias_back,
        gain_ffn,
        shift_ffn,
    ) = params
    slot_count = lengths.shape[0]
    row_count = tokens.shape[0]
    split_heads = (slot_count, row_count // slot_count, HEADS, HEAD_DIM)
    queries = (matmul(tokens, weight_query) + bias_query.astype(jnp.float32)).astype(jnp.bfloat16)
    keys_all = matmul(tokens, weight_key).astype(jnp.bfloat16)
    values_all = (matmul(tokens, weight_value) + bias_value.astype(jnp.float32)).astype(
        jnp.bfloat16
    )
    scores = head_scores(queries.reshape(split_heads), keys_all.reshape(split_heads), lengths)
    peak_score = jnp.max(scores, axis=-1, keepdims=True)
    exp_scores = jnp.exp(scores - peak_score)
    row_total = jnp.sum(exp_scores, axis=-1, keepdims=True)
    soft_low = (exp_scores / row_total).astype(jnp.bfloat16)
    log_total = peak_score + jnp.log(row_total)
    context = jnp.einsum(
        "bhqk,bkhd->bqhd",
        soft_low,
        values_all.reshape(split_heads),
        preferred_element_type=jnp.float32,
    )
    context = context.reshape(row_count, D).astype(jnp.bfloat16)
    attn_sum = (
        tokens.astype(jnp.float32) + matmul(context, weight_out) + bias_out.astype(jnp.float32)
    )
    middle, unit_attn, inv_attn = normalize(attn_sum, gain_attn, shift_attn)
    middle_low = middle.astype(jnp.bfloat16)
    inner_act = matmul(middle_low, weight_in) + bias_in.astype(jnp.float32)
    gelu_low = gelu_exact(inner_act).astype(jnp.bfloat16)
    ffn_sum = middle + matmul(gelu_low, weight_back) + bias_back.astype(jnp.float32)
    output, unit_ffn, inv_ffn = normalize(ffn_sum, gain_ffn, shift_ffn)
    kept = (
        queries,
        keys_all,
        values_all,
        log_total,
        context,
        unit_attn,
        inv_attn,
        middle_low,
        inner_act,
        gelu_low,
        unit_ffn,
        inv_ffn,
    )
    return (output.astype(jnp.bfloat16), kept)


def ffn_backward(upstream, kept, params):
    (
        queries,
        keys_all,
        values_all,
        log_total,
        context,
        unit_attn,
        inv_attn,
        middle_low,
        inner_act,
        gelu_low,
        unit_ffn,
        inv_ffn,
    ) = kept
    weight_in, weight_back, gain_ffn = (params[9], params[11], params[13])
    ffn_grad, gain_grad, shift_grad = normalize_back(upstream, unit_ffn, inv_ffn, gain_ffn)
    branch_low = ffn_grad.astype(jnp.bfloat16)
    back_weight_grad = left_across(gelu_low, branch_low)
    back_bias_grad = jnp.sum(branch_low, axis=0, dtype=jnp.float32)
    inner_low = (right_across(branch_low, weight_back) * gelu_slope(inner_act)).astype(jnp.bfloat16)
    in_weight_grad = left_across(middle_low, inner_low)
    in_bias_grad = jnp.sum(inner_low, axis=0, dtype=jnp.float32)
    middle_grad = ffn_grad + right_across(inner_low, weight_in)
    return (
        middle_grad,
        (in_weight_grad, in_bias_grad, back_weight_grad, back_bias_grad, gain_grad, shift_grad),
    )


def attention_backward(middle_grad, tokens, lengths, kept, params):
    (
        queries,
        keys_all,
        values_all,
        log_total,
        context,
        unit_attn,
        inv_attn,
        middle_low,
        inner_act,
        gelu_low,
        unit_ffn,
        inv_ffn,
    ) = kept
    weight_query, weight_key, weight_value, weight_out, gain_attn = (
        params[0],
        params[2],
        params[3],
        params[5],
        params[7],
    )
    slot_count = lengths.shape[0]
    row_count = tokens.shape[0]
    split_heads = (slot_count, row_count // slot_count, HEADS, HEAD_DIM)
    attn_grad, gain_grad, shift_grad = normalize_back(middle_grad, unit_attn, inv_attn, gain_attn)
    attn_low = attn_grad.astype(jnp.bfloat16)
    out_weight_grad = left_across(context, attn_low)
    out_bias_grad = jnp.sum(attn_low, axis=0, dtype=jnp.float32)
    context_grad = right_across(attn_low, weight_out).astype(jnp.bfloat16).reshape(split_heads)
    query_heads = queries.reshape(split_heads)
    key_heads = keys_all.reshape(split_heads)
    value_heads = values_all.reshape(split_heads)
    soft_full = jnp.exp(head_scores(query_heads, key_heads, lengths) - log_total)
    soft_grad = jnp.einsum(
        "bqhd,bkhd->bhqk", context_grad, value_heads, preferred_element_type=jnp.float32
    )
    value_grad = jnp.einsum(
        "bhqk,bqhd->bkhd",
        soft_full.astype(jnp.bfloat16),
        context_grad,
        preferred_element_type=jnp.float32,
    )
    value_grad = value_grad.reshape(row_count, D).astype(jnp.bfloat16)
    score_low = (
        soft_full * (soft_grad - jnp.sum(soft_full * soft_grad, axis=-1, keepdims=True))
    ).astype(jnp.bfloat16)
    query_grad_low = 0.125 * jnp.einsum(
        "bhqk,bkhd->bqhd", score_low, key_heads, preferred_element_type=jnp.float32
    )
    query_grad_low = query_grad_low.reshape(row_count, D).astype(jnp.bfloat16)
    key_grad_low = 0.125 * jnp.einsum(
        "bhqk,bqhd->bkhd", score_low, query_heads, preferred_element_type=jnp.float32
    )
    key_grad_low = key_grad_low.reshape(row_count, D).astype(jnp.bfloat16)
    token_grad = (
        attn_grad
        + right_across(query_grad_low, weight_query)
        + right_across(key_grad_low, weight_key)
        + right_across(value_grad, weight_value)
    )
    grads = (
        left_across(tokens, query_grad_low),
        jnp.sum(query_grad_low, axis=0, dtype=jnp.float32),
        left_across(tokens, key_grad_low),
        left_across(tokens, value_grad),
        jnp.sum(value_grad, axis=0, dtype=jnp.float32),
        out_weight_grad,
        out_bias_grad,
        gain_grad,
        shift_grad,
    )
    return (token_grad, grads)


def on_device(
    query_tokens,
    passage_tokens,
    query_lengths,
    passage_lengths,
    passage_valid,
    positives,
    negatives,
    teacher_margins,
    query_grad,
    passage_grad,
    weight_query,
    bias_query,
    weight_key,
    weight_value,
    bias_value,
    weight_out,
    bias_out,
    gain_attn,
    shift_attn,
    weight_in,
    bias_in,
    weight_back,
    bias_back,
    gain_ffn,
    shift_ffn,
):
    params = (
        weight_query,
        bias_query,
        weight_key,
        weight_value,
        bias_value,
        weight_out,
        bias_out,
        gain_attn,
        shift_attn,
        weight_in,
        bias_in,
        weight_back,
        bias_back,
        gain_ffn,
        shift_ffn,
    )
    query_out, query_kept = encode_forward(query_tokens, query_lengths, params)
    passage_out, passage_kept = encode_forward(passage_tokens, passage_lengths, params)
    query_slots = query_lengths.shape[0]
    passage_slots = passage_lengths.shape[0]
    cls_query = query_out.reshape(query_slots, -1, D)[:, 0]
    cls_passage = passage_out.reshape(passage_slots, -1, D)[:, 0]
    valid_low = passage_valid.astype(jnp.bfloat16)

    def score_piece(cls_piece, valid_piece):
        scores = score_scale * right_across(cls_query, cls_piece)
        position = lax.iota(jnp.int32, cls_piece.shape[0])
        is_positive = position[None, :] == positives[:, None]
        is_negative = position[None, :] == negatives[:, None]
        allowed = (valid_piece[None, :] > 0.5) | is_positive
        return (scores, allowed, is_positive, is_negative)

    peak_score = jnp.full((query_slots,), -1e30, jnp.float32)
    scores, allowed, is_positive, is_negative = score_piece(
        lax.all_gather(cls_passage, "dp", axis=0, tiled=True),
        lax.all_gather(valid_low, "dp", axis=0, tiled=True),
    )
    masked = jnp.where(allowed, scores, -1e30)
    new_peak = jnp.maximum(peak_score, jnp.max(masked, axis=1))
    row_total = jnp.sum(jnp.where(allowed, jnp.exp(masked - new_peak[:, None]), 0.0), axis=1)
    positive_score = jnp.sum(jnp.where(is_positive, scores, 0.0), axis=1)
    negative_score = jnp.sum(jnp.where(is_negative, scores, 0.0), axis=1)
    peak_score, row_total, positive_score, negative_score = (
        new_peak,
        row_total,
        positive_score,
        negative_score,
    )
    all_cls, all_valid = (
        lax.all_gather(cls_passage, "dp", axis=0, tiled=True),
        lax.all_gather(valid_low, "dp", axis=0, tiled=True),
    )
    log_total = peak_score + jnp.log(row_total)
    shortfall = positive_score - negative_score - teacher_margins
    query_loss = log_total - positive_score + margin_weight * shortfall * shortfall
    scores, allowed, is_positive, is_negative = score_piece(all_cls, all_valid)
    soft_scores = jnp.where(allowed, jnp.exp(scores - log_total[:, None]), 0.0)
    positive_hit = is_positive.astype(jnp.float32)
    negative_hit = is_negative.astype(jnp.float32)
    score_grad = (
        soft_scores
        - positive_hit
        + 2.0 * margin_weight * shortfall[:, None] * (positive_hit - negative_hit)
    ).astype(jnp.bfloat16)
    cls_query_grad = score_scale * matmul(score_grad, all_cls)
    cls_passage_grad = lax.psum_scatter(
        score_scale * left_across(score_grad, cls_query), "dp", scatter_dimension=0, tiled=True
    )
    query_upstream = (
        query_grad.astype(jnp.float32)
        .reshape(query_slots, -1, D)
        .at[:, 0]
        .add(cls_query_grad)
        .reshape(-1, D)
    )
    passage_upstream = (
        passage_grad.astype(jnp.float32)
        .reshape(passage_slots, -1, D)
        .at[:, 0]
        .add(cls_passage_grad)
        .reshape(-1, D)
    )
    query_middle_grad, query_ffn = ffn_backward(query_upstream, query_kept, params)
    passage_middle_grad, passage_ffn = ffn_backward(passage_upstream, passage_kept, params)
    (
        in_weight_grad,
        in_bias_grad,
        back_weight_grad,
        back_bias_grad,
        ffn_gain_grad,
        ffn_shift_grad,
    ) = tuple((first + second for first, second in zip(query_ffn, passage_ffn)))
    query_tokens_grad, query_attn = attention_backward(
        query_middle_grad, query_tokens, query_lengths, query_kept, params
    )
    passage_tokens_grad, passage_attn = attention_backward(
        passage_middle_grad, passage_tokens, passage_lengths, passage_kept, params
    )
    (
        query_weight_grad,
        query_bias_grad,
        key_weight_grad,
        value_weight_grad,
        value_bias_grad,
        out_weight_grad,
        out_bias_grad,
        attn_gain_grad,
        attn_shift_grad,
    ) = tuple((first + second for first, second in zip(query_attn, passage_attn)))
    (
        query_weight_grad,
        query_bias_grad,
        key_weight_grad,
        value_weight_grad,
        value_bias_grad,
        out_weight_grad,
        out_bias_grad,
        attn_gain_grad,
        attn_shift_grad,
        in_weight_grad,
        in_bias_grad,
        back_weight_grad,
        back_bias_grad,
        ffn_gain_grad,
        ffn_shift_grad,
    ) = (
        lax.psum_scatter(query_weight_grad, "dp", scatter_dimension=0, tiled=True),
        lax.psum_scatter(query_bias_grad, "dp", scatter_dimension=0, tiled=True),
        lax.psum_scatter(key_weight_grad, "dp", scatter_dimension=0, tiled=True),
        lax.psum_scatter(value_weight_grad, "dp", scatter_dimension=0, tiled=True),
        lax.psum_scatter(value_bias_grad, "dp", scatter_dimension=0, tiled=True),
        lax.psum_scatter(out_weight_grad, "dp", scatter_dimension=0, tiled=True),
        lax.psum_scatter(out_bias_grad, "dp", scatter_dimension=0, tiled=True),
        lax.psum_scatter(attn_gain_grad, "dp", scatter_dimension=0, tiled=True),
        lax.psum_scatter(attn_shift_grad, "dp", scatter_dimension=0, tiled=True),
        lax.psum_scatter(in_weight_grad, "dp", scatter_dimension=0, tiled=True),
        lax.psum_scatter(in_bias_grad, "dp", scatter_dimension=0, tiled=True),
        lax.psum_scatter(back_weight_grad, "dp", scatter_dimension=0, tiled=True),
        lax.psum_scatter(back_bias_grad, "dp", scatter_dimension=0, tiled=True),
        lax.psum_scatter(ffn_gain_grad, "dp", scatter_dimension=0, tiled=True),
        lax.psum_scatter(ffn_shift_grad, "dp", scatter_dimension=0, tiled=True),
    )
    return (
        query_out,
        passage_out,
        query_loss,
        query_tokens_grad,
        passage_tokens_grad,
        query_weight_grad,
        query_bias_grad,
        key_weight_grad,
        value_weight_grad,
        value_bias_grad,
        out_weight_grad,
        out_bias_grad,
        attn_gain_grad,
        attn_shift_grad,
        in_weight_grad,
        in_bias_grad,
        back_weight_grad,
        back_bias_grad,
        ffn_gain_grad,
        ffn_shift_grad,
    )


F32 = jnp.float32
BF16 = jnp.bfloat16
MESH = pl.DeviceIdType.MESH
FF = 3072
ROWS = 480
WIN = 240
SLOT = 220
NEG = -1000000000.0


def dot_nn(left, right):
    return jnp.dot(left, right, preferred_element_type=F32)


def dot_nt(left, right):
    return lax.dot_general(left, right, (((1,), (1,)), ((), ())), preferred_element_type=F32)


def dot_tn(left, right):
    return lax.dot_general(left, right, (((0,), (0,)), ((), ())), preferred_element_type=F32)


def row_of(ref, start=0, size=D):
    return ref[pl.ds(start, size)].astype(F32).reshape(1, size)


def blocks(start, stop, size):
    return [(at, min(size, stop - at)) for at in range(start, stop, size)]


def iota(shape, dim):
    return lax.broadcasted_iota(jnp.int32, shape, dim)


def fold8(block):
    return jnp.sum(block.reshape(-1, 8, block.shape[-1]), axis=0)


WIDE = 256
ROUTE = (
    "xyz", "yxz", "zyx", "xyz", "zxy", "zyx", "yxz", "xyz", "yxz", "xyz", "yxz", "xyz", "yxz", "xyz", "yxz", "xyz",
    "yxz", "xyz",
)
ORDER = (
    ("wback", 0, 0), ("c", 0, 0), ("wback", 0, 1), ("c", 0, 1), ("wback", 0, 2), ("c", 0, 2), ("wback", 1, 0),
    ("c", 1, 0), ("wback", 1, 1), ("c", 1, 1), ("wback", 1, 2), ("c", 1, 2), ("dinner", 0), ("ec", 0, 0),
    ("dinner", 1), ("ec", 0, 2), ("win", 2, 0), ("ec", 0, 1), ("c", 2, 0), ("win", 2, 1), ("ec", 1, 0), ("c", 2, 1),
    ("win", 2, 2), ("ec", 1, 2), ("ec", 1, 1), ("c", 2, 2), ("dinner", 2), ("dinner", 3), ("win", 3, 0), ("c", 3, 0),
    ("ec", 2, 0), ("win", 3, 1), ("ec", 2, 1), ("c", 3, 1), ("win", 3, 2), ("c", 3, 2), ("dmid", 0), ("dmid", 1),
    ("ec", 2, 2), ("dmid", 2), ("dmid", 3), ("lnback",), ("dctx",), ("ec", 3, 1), ("ec", 3, 0), ("qslot",),
    ("e1", 1, 0), ("attn", 0), ("ec", 3, 2), ("attn", 1), ("attn", 2), ("attn", 3), ("attn", 4), ("e1", 0, 2),
    ("e1", 2, 2), ("attn", 5), ("sums",), ("wvo", 0), ("c", 4, 0), ("e1", 0, 1), ("e1", 2, 0), ("e1", 0, 0),
    ("wvo", 1), ("c", 4, 1), ("wvo", 2), ("e1", 3, 1), ("c", 4, 2), ("vec", 0), ("e1", 2, 1), ("ec", 4, 0),
    ("wqk", 0), ("c", 5, 0), ("ec", 4, 1), ("e2", 2, 2), ("e1", 3, 0), ("ec", 4, 2), ("e2", 0, 0), ("wqk", 1),
    ("e1", 3, 2), ("e2", 0, 1), ("c", 5, 1), ("e2", 1, 0), ("vec", 1), ("wqk", 2), ("c", 5, 2), ("e2", 3, 1),
    ("e1", 4, 0), ("e2", 2, 1), ("ec", 5, 2), ("e1", 4, 1), ("ec", 5, 1), ("e2", 2, 0), ("e3", 2, 2), ("e1", 4, 2),
    ("e2", 3, 0), ("ec", 5, 0), ("e3", 0, 1), ("e2", 4, 0), ("e1", 5, 2), ("tq",), ("e3", 2, 1), ("e2", 3, 2),
    ("e3", 2, 0), ("e2", 4, 2), ("e3", 3, 1), ("e1", 1, 2), ("e1", 1, 1), ("e2", 4, 1), ("e1", 5, 1), ("vec", 2),
    ("e1", 5, 0), ("e2", 5, 2), ("e3", 3, 2), ("e3", 1, 0), ("vec", 3), ("e2", 5, 1), ("e3", 0, 0), ("tk",),
    ("e3", 4, 0), ("e2", 0, 2), ("e2", 5, 0), ("e3", 4, 1), ("e2", 1, 1), ("e3", 4, 2), ("e2", 1, 2), ("e3", 1, 2),
    ("e3", 5, 1), ("e3", 3, 0), ("vecend",), ("tv",), ("tout",), ("e3", 5, 2), ("e3", 1, 1), ("e3", 0, 2),
    ("e3", 5, 0),
)


def layer_kernel(
    qtok, ptok, qlen, plen, pvalid, pos, neg, margin, qgrad, pgrad,
    wq_h, bq_h, wk_h, wv_h, bv_h, wo_h, bo_h, ga_h, sa_h, wi_h, bi_h, wb_h, bb_h, gf_h, sf_h,
    qout_h, pout_h, qtg_h, ptg_h, wqg, wkg, wvg, wog, wig, wbg, small_h,
    bq, bv, bo, ga, sa, bi, bb, gf, sf, wq, wk, wv, wo, wi, wb, pstage, x_s, xT, q_s, k_s, v_s, p_s, pq_s, c_s, cT, n1, n2, r1, r2,
    ml, mlT, act_a, act_b, actT, tmp_a, tmp_b, gp, qg_s, pg_s, qo_s, po_s, ex, ex_f, vec, vecr, vecs, vecz, small_o, parts,
    g_s, rc, ra, rb, rz, rw,
    load_sem, out_sem, part_sem, ex_send, ex_recv, c_send, c_recv, a_send, a_recv, b_send, b_recv,
    z_send, z_recv, v_send, v_recv, credit,
):
    me = lax.axis_index("dp")
    core = lax.rem(me, 2)
    xx = lax.rem(lax.div(me, 2), 2)
    yy = lax.rem(lax.div(me, 4), 2)
    zz = lax.div(me, 8)
    chip = lax.div(me, 2)
    partner = me + 1 - 2 * core
    x_peer = me + 2 - 4 * xx
    y_peer = me + 4 - 8 * yy
    plane = lax.rem(me, 8)

    loads = {}

    def load(name, source, target):
        loads[name] = pltpu.make_async_copy(source, target, load_sem.at[len(loads)])
        loads[name].start()

    load("ptok", ptok, pstage)
    load("qtok", qtok, qo_s)
    load("wq", wq_h, wq)
    load("wk", wk_h, wk)
    load("wv", wv_h, wv)
    vectors = ((bq_h, bq), (bv_h, bv), (bo_h, bo), (ga_h, ga), (sa_h, sa), (bi_h, bi), (bb_h, bb), (gf_h, gf), (sf_h, sf))
    for at, (source, target) in enumerate(vectors):
        load("vec" + str(at), source, target)

    barrier = pltpu.get_barrier_semaphore()
    for hop in range(1, 16):
        other = 2 * lax.rem(chip + hop, 16) + core
        pl.semaphore_signal(barrier, inc=1, device_id=(other,), device_id_type=MESH)
    pl.semaphore_signal(barrier, inc=1, device_id=(partner,), device_id_type=MESH)

    loads["ptok"].wait()
    loads["qtok"].wait()
    x_s[0:32, :] = qo_s[...]

    def copy_tokens(i, carry):
        x_s[pl.ds(pl.multiple_of(32 + i * 16, 16), 16), :] = pstage[pl.ds(pl.multiple_of(i * 16, 16), 16), :]
        return carry

    lax.fori_loop(0, 27, copy_tokens, 0)
    x_s[464:480, :] = jnp.concatenate(
        [pstage[432:440, :].astype(F32), jnp.zeros((8, D), F32)], axis=0
    ).astype(BF16)

    loads["wq"].wait()
    for at in range(len(vectors)):
        loads["vec" + str(at)].wait()
    load("wo", wo_h, wo)
    load("wi", wi_h, wi)

    def project_queries(start, stop):
        rows = pl.ds(start, stop - start)
        q_s[rows, :] = ((dot_nn(x_s[rows, :], wq[...]) + row_of(bq)).astype(BF16) * 0.125).astype(BF16)

    project_queries(0, 256)
    loads["wk"].wait()
    k_s[...] = dot_nn(x_s[...], wk[...]).astype(BF16)
    loads["wv"].wait()
    for h in range(3):
        load("wb" + str(h), wb_h.at[:, :, :, :, :, :, pl.ds(WIDE * h, WIDE)], wb.at[h])
    load("qg", qgrad, qg_s)
    load("pg", pgrad, pg_s)
    v_s[...] = (dot_nn(x_s[...], wv[...]) + row_of(bv)).astype(BF16)

    head_of = iota((12, 1, D), 2) // 64
    head_mask = (head_of == iota((12, 1, D), 0)).astype(F32)

    def spread(rows):
        return (rows.astype(F32)[None] * head_mask).astype(BF16).reshape(384, D)

    def gather_heads(stacked):
        return jnp.sum(stacked.reshape(12, 32, D) * head_mask, axis=0)

    raw = dot_nt(k_s[0:32, :], spread(q_s[0:32, :]))
    raw = jnp.where(iota((32, 384), 0) < qlen[0], raw, NEG)
    soft = jnp.exp(raw - jnp.max(raw, axis=0, keepdims=True))
    soft = (soft * (1.0 / jnp.sum(soft, axis=0, keepdims=True))).astype(BF16)
    pq_s[...] = soft
    c_s[0:32, :] = gather_heads(dot_tn(soft, v_s[0:32, :])).astype(BF16)

    lane = iota((1, 128), 1)
    half = ((lane < 64).astype(BF16), (lane >= 64).astype(BF16))
    key_at = iota((WIN, 1), 0)

    def attend(pair, slot):
        lanes = pl.ds(pl.multiple_of(pair * 128, 128), 128)
        low_at = 12 * slot
        first_row = 32 + 208 * slot
        rows = pl.ds(first_row, WIN)
        keys, queries = k_s[rows, lanes], q_s[rows, lanes]
        values_t = v_s[rows, lanes].T
        allowed = (key_at >= low_at) & (key_at < low_at + plen[slot])
        parts = []
        for h in range(2):
            scores = jnp.where(allowed, dot_nt(keys, queries * half[h]), NEG)
            e = jnp.exp(scores - jnp.max(scores, axis=0, keepdims=True))
            p = (e * (1.0 / jnp.sum(e, axis=0, keepdims=True))).astype(BF16)
            p_s[slot, 2 * pair + h] = p
            parts.append(dot_nn(values_t, p)[64 * h:64 * h + 64, :])
        context = jnp.concatenate(parts, axis=0).T
        if slot == 0:
            c_s[rows, lanes] = context.astype(BF16)
            return
        old = c_s[240:256, lanes].astype(F32)
        c_s[240:256, lanes] = jnp.where(iota((16, 128), 0) >= 12, context[0:16], old).astype(BF16)
        c_s[256:480, lanes] = context[16:240].astype(BF16)

    def attend_slot(slot):
        def two_pairs(i, carry):
            attend(2 * i, slot)
            attend(2 * i + 1, slot)
            return carry

        lax.fori_loop(0, 3, two_pairs, 0)

    attend_slot(0)

    by_head = (q_s[240:256, :].astype(F32)[None] * head_mask).astype(BF16).reshape(192, D)
    raw = dot_nt(by_head, k_s[240:480, :])
    key_lane = iota((1, WIN), 1)
    raw = jnp.where((key_lane >= 12) & (key_lane < 12 + plen[1]), raw, NEG)
    soft = jnp.exp(raw - jnp.max(raw, axis=1, keepdims=True))
    soft = (soft * (1.0 / jnp.sum(soft, axis=1, keepdims=True))).astype(BF16)
    block = jnp.sum(dot_nn(soft, v_s[240:480, :]).reshape(12, 16, D) * head_mask, axis=0)
    old = c_s[240:256, :].astype(F32)
    c_s[240:256, :] = jnp.where(iota((16, 1), 0) >= 12, block, old).astype(BF16)

    loads["wo"].wait()
    gain1, shift1, bias1 = row_of(ga), row_of(sa), row_of(bo)
    gain2, shift2, bias2 = row_of(gf), row_of(sf), row_of(bb)

    def wb_tile(t):
        return jnp.concatenate([wb[h, t // 2, t % 2].reshape(D, WIDE) for h in range(3)], axis=1)

    def normalized(hidden):
        centered = hidden - jnp.mean(hidden, axis=-1, keepdims=True)
        inv = lax.rsqrt(jnp.mean(centered * centered, axis=-1, keepdims=True) + ln_eps)
        return centered * inv, inv

    def forward_rows(start, stop):
        size = stop - start
        every, own = pl.ds(start, size), pl.ds(0, size)
        tmp_a[own, :] = dot_nn(c_s[every, :], wo[...])
        for at, count in blocks(0, size, 32):
            rows, here = pl.ds(start + at, count), pl.ds(at, count)
            unit, inv = normalized(tmp_a[here, :] + x_s[rows, :].astype(F32) + bias1)
            n1[rows, :] = unit
            r1[rows, :] = inv
            ml[rows, :] = (unit * gain1 + shift1).astype(BF16)
        if start == 0:
            loads["wi"].wait()
            for h in range(3):
                loads["wb" + str(h)].wait()
        inner, acts = (tmp_a, tmp_b), (act_a, act_b)
        tmp_a[own, :] = dot_nn(ml[every, :], wi[:, 0:D])

        def finish(t):
            act = acts[t % 2][own, :]
            if t == 0:
                n2[every, :] = dot_nn(act, wb_tile(t))
            else:
                n2[every, :] += dot_nn(act, wb_tile(t))
            actT[t * D:t * D + D, every] = act.T

        for t in range(4):
            if t < 3:
                inner[(t + 1) % 2][own, :] = dot_nn(ml[every, :], wi[:, t * D + D:t * D + 2 * D])
            bias_t = row_of(bi, t * D)
            for at, count in blocks(0, size, 16):
                here = pl.ds(at, count)
                u = inner[t % 2][here, :] + bias_t
                cdf = 0.5 * (1.0 + lax.erf(u * root_half))
                acts[t % 2][here, :] = (u * cdf).astype(BF16)
                gp[start + at:start + at + count, t * D:t * D + D] = (
                    cdf + u * inv_root_tau * jnp.exp(-0.5 * u * u)
                ).astype(BF16)
            if t > 0:
                finish(t - 1)
        finish(3)
        for at, count in blocks(start, stop, 32):
            rows = pl.ds(at, count)
            unit, inv = normalized(n2[rows, :] + (n1[rows, :] * gain1 + shift1) + bias2)
            n2[rows, :] = unit
            r2[rows, :] = inv
            out = (unit * gain2 + shift2).astype(BF16)
            if at == 0:
                qo_s[...] = out
            else:
                po_s[at - 32:min(at, 440), :] = out[0:min(count, 472 - at)]

    forward_rows(0, 256)

    slot_me = core * 16 + chip
    base = pl.multiple_of(slot_me * 32, 32)
    first_rows = (
        qo_s[0:16, :].astype(F32)[0:1],
        po_s[0:16, :].astype(F32)[0:1],
        po_s[208:224, :].astype(F32)[12:13],
    )
    lane_row = iota((1, 128), 1)
    meta = jnp.zeros((1, 128), F32)
    margin_1 = (jnp.zeros((1, 128), F32) + margin[0]).astype(BF16).astype(F32)
    margin_2 = (margin[0] - margin_1).astype(BF16).astype(F32)
    for at, value in enumerate((
        pvalid[0].astype(F32), pvalid[1].astype(F32), pos[0].astype(F32), neg[0].astype(F32),
        margin_1, margin_2, margin[0] - margin_1 - margin_2,
    )):
        meta = jnp.where(lane_row == at, value, meta)
    pieces = [row[:, 128 * i:128 * i + 128] for row in first_rows for i in range(6)]
    ex[pl.ds(base, 32), :] = jnp.concatenate(pieces + [meta, jnp.zeros((13, 128), F32)], axis=0).astype(BF16)

    pl.semaphore_wait(barrier, 16)
    sends = []
    for hop in range(1, 16):
        block = ex.at[pl.ds(base, 32), :]
        sends.append(pltpu.make_async_remote_copy(
            src_ref=block, dst_ref=block, send_sem=ex_send.at[hop], recv_sem=ex_recv.at[hop],
            device_id=(2 * lax.rem(chip + hop, 16) + core,), device_id_type=MESH,
        ))
        sends[-1].start()

    project_queries(256, 480)
    attend_slot(1)
    forward_rows(256, 480)
    out_q = pltpu.make_async_copy(qo_s, qout_h, out_sem.at[0])
    out_p = pltpu.make_async_copy(po_s, pout_h, out_sem.at[1])
    out_q.start()
    out_p.start()
    mlT[...] = ml[...].T
    loads["qg"].wait()
    loads["pg"].wait()

    def ffn_norm_back(r0, upstream, sums):
        rows = pl.ds(r0, upstream.shape[0])
        unit = n2[rows, :]
        scaled = upstream * gain2
        hidden_grad = r2[rows, :] * (
            scaled
            - jnp.mean(scaled, axis=-1, keepdims=True)
            - unit * jnp.mean(scaled * unit, axis=-1, keepdims=True)
        )
        n2[rows, :] = hidden_grad
        rounded = hidden_grad.astype(BF16)
        ml[rows, :] = rounded
        return (
            sums[0] + fold8(upstream * unit), sums[1] + fold8(upstream), sums[2] + fold8(rounded.astype(F32)),
        )

    zero8 = jnp.zeros((8, D), F32)
    sums = (zero8, zero8, zero8)
    for i in (1, 2, 3, 4, 5, 7, 8, 9, 10, 11, 12):
        sums = ffn_norm_back(32 + 32 * i, pg_s[32 * i:32 * i + 32, :].astype(F32), sums)
    last = jnp.concatenate([pg_s[416:440, :].astype(F32), jnp.zeros((8, D), F32)], axis=0)
    sums = ffn_norm_back(448, last, sums)

    for send in sends:
        send.wait()
    same_core = ex.at[pl.ds(pl.multiple_of(core * 512, 512), 512), :]
    across = pltpu.make_async_remote_copy(
        src_ref=same_core, dst_ref=same_core, send_sem=ex_send.at[0], recv_sem=ex_recv.at[0],
        device_id=(partner,), device_id_type=MESH,
    )
    across.start()
    xT[...] = x_s[...].T
    cT[...] = c_s[...].T
    across.wait()

    ex_f[...] = ex[...].astype(F32)

    def first(r):
        return ex_f[pl.ds(r, 32, stride=32), :]

    cls_q = jnp.concatenate([first(i) for i in range(6)], axis=1)
    cls_0 = jnp.concatenate([first(6 + i) for i in range(6)], axis=1).astype(BF16)
    cls_1 = jnp.concatenate([first(12 + i) for i in range(6)], axis=1).astype(BF16)
    metas = first(18)
    metas_t = metas.T
    s0 = score_scale * dot_nt(cls_q.astype(BF16), cls_0)
    s1 = score_scale * dot_nt(cls_q.astype(BF16), cls_1)
    col = iota((1, 32), 1)
    passage = (4 * lax.rem(col, 16) + 2 * lax.div(col, 16)).astype(F32)
    at_pos, at_neg, wanted = metas[:, 2:3], metas[:, 3:4], metas[:, 4:5] + metas[:, 5:6] + metas[:, 6:7]
    pos0, pos1 = at_pos == passage, at_pos == passage + 1.0
    neg0, neg1 = at_neg == passage, at_neg == passage + 1.0
    m0 = jnp.where((metas_t[0:1, :] > 0.5) | pos0, s0, -1e30)
    m1 = jnp.where((metas_t[1:2, :] > 0.5) | pos1, s1, -1e30)
    peak = jnp.maximum(jnp.max(m0, axis=1, keepdims=True), jnp.max(m1, axis=1, keepdims=True))
    total = jnp.sum(jnp.exp(m0 - peak), axis=1, keepdims=True) + jnp.sum(jnp.exp(m1 - peak), axis=1, keepdims=True)
    lse = peak + jnp.log(total)

    def picked(where0, where1):
        return jnp.sum(jnp.where(where0, s0, 0.0), axis=1, keepdims=True) + jnp.sum(
            jnp.where(where1, s1, 0.0), axis=1, keepdims=True
        )

    at_positive = picked(pos0, pos1)
    miss = at_positive - picked(neg0, neg1) - wanted
    losses = lse - at_positive + margin_weight * miss * miss
    pos0, pos1, neg0, neg1 = (hit.astype(F32) for hit in (pos0, pos1, neg0, neg1))
    ds0 = (jnp.exp(m0 - lse) - pos0 + 2.0 * margin_weight * miss * (pos0 - neg0)).astype(BF16)
    ds1 = (jnp.exp(m1 - lse) - pos1 + 2.0 * margin_weight * miss * (pos1 - neg1)).astype(BF16)
    mine = iota((32, 1), 0) == slot_me
    mine_col = iota((1, 32), 1) == slot_me
    small_o[9:10, :] = jnp.sum(jnp.where(mine, losses, 0.0), axis=0, keepdims=True) + jnp.zeros((1, 128), F32)
    dq_all = score_scale * (dot_nn(ds0, cls_0) + dot_nn(ds1, cls_1))
    d_query = jnp.sum(jnp.where(mine, dq_all, 0.0), axis=0, keepdims=True)

    def passage_grad_row(ds):
        column = jnp.sum(jnp.where(mine_col, ds.astype(F32), 0.0), axis=1, keepdims=True)
        return score_scale * jnp.sum(column * cls_q, axis=0, keepdims=True)

    d_first = (d_query, passage_grad_row(ds0), passage_grad_row(ds1))

    row32 = iota((32, 1), 0)
    for r0, at, source, add in (
        (0, 0, qg_s[...], d_first[0]), (32, 0, pg_s[0:32, :], d_first[1]), (224, 28, pg_s[192:224, :], d_first[2]),
    ):
        upstream = source.astype(F32) + jnp.where(row32 == at, add, 0.0)
        sums = ffn_norm_back(r0, upstream, sums)
    vec[...] = jnp.zeros_like(vec)
    vec[5:6, :] = jnp.sum(sums[2], axis=0, keepdims=True)
    vec[6:7, :] = jnp.sum(sums[0], axis=0, keepdims=True)
    vec[7:8, :] = jnp.sum(sums[1], axis=0, keepdims=True)

    def chunk(p, h):
        return g_s.at[p, h] if p < 4 else wb.at[h, p - 4]

    z_slot = {}
    for at, way in enumerate(ROUTE):
        if way[0] == "z":
            z_slot[(at // 3, at % 3)] = len(z_slot)

    def route(p, h):
        return ROUTE[3 * p + h]

    def remote(source, target, send, recv, device):
        return pltpu.make_async_remote_copy(
            src_ref=source, dst_ref=target, send_sem=send, recv_sem=recv, device_id=(device,), device_id_type=MESH,
        )

    def step_c(p, h):
        return [remote(chunk(p, h).at[1 - core], rc.at[p % 2, h], c_send.at[p, h], c_recv.at[p, h], partner)]

    def along_z(p, h, pick, target):
        steps = []
        for hop in range(1, 4):
            to = lax.rem(zz + hop, 4)
            steps.append(remote(
                pick(to), target(hop - 1), z_send.at[p, h, hop - 1], z_recv.at[p, h, hop - 1], to * 8 + plane,
            ))
        return steps

    def step_1(p, h):
        mine, way = chunk(p, h), route(p, h)
        if way[0] == "z":
            return along_z(p, h, lambda to: mine.at[core, to], lambda i: rw.at[z_slot[(p, h)], i])
        away = mine.at[core, :, :, 1 - xx] if way == "xyz" else mine.at[core, :, 1 - yy]
        return [remote(away, ra.at[p, h], a_send.at[p, h], a_recv.at[p, h], x_peer if way == "xyz" else y_peer)]

    def step_2(p, h):
        mine, way = chunk(p, h), route(p, h)
        if way == "zyx":
            away, target = mine.at[core, zz, 1 - yy], rb.at[p, h, 0:2]
        elif way == "zxy":
            away, target = mine.at[core, zz, :, 1 - xx], rb.at[p, h, 0:2]
        elif way == "xyz":
            away, target = mine.at[core, :, 1 - yy, xx], rb.at[p, h]
        else:
            away, target = mine.at[core, :, yy, 1 - xx], rb.at[p, h]
        return [remote(away, target, b_send.at[p, h], b_recv.at[p, h], x_peer if way[1] == "x" else y_peer)]

    def step_3(p, h):
        mine = chunk(p, h)
        way = route(p, h)
        if way[0] == "z":
            away = mine.at[core, zz, yy, 1 - xx] if way == "zyx" else mine.at[core, zz, 1 - yy, xx]
            return [remote(
                away, rz.at[p, h, 0], a_send.at[p, h], a_recv.at[p, h], x_peer if way == "zyx" else y_peer,
            )]
        return along_z(p, h, lambda to: mine.at[core, to, yy, xx], lambda i: rz.at[p, h, i])

    def begin(steps):
        for step in steps:
            step.start()

    def finish_steps(steps):
        for step in steps:
            step.wait()

    def start_c(p, h):
        if p >= 2:
            pl.semaphore_wait(credit.at[p % 2, h], 1)
        begin(step_c(p, h))

    def end_c(p, h):
        finish_steps(step_c(p, h))

        def add(z, carry):
            for y in range(2):
                for x in range(2):
                    chunk(p, h)[core, z, y, x] += rc[p % 2, h, z, y, x]
            return carry

        lax.fori_loop(0, 4, add, 0)
        begin(step_1(p, h))
        if p < 4:
            pl.semaphore_signal(credit.at[p % 2, h], inc=1, device_id=(partner,), device_id_type=MESH)

    def end_1(p, h):
        finish_steps(step_1(p, h))
        mine, way = chunk(p, h), route(p, h)
        if way[0] == "z":
            def add(y, carry):
                for x in range(2):
                    total = mine[core, zz, y, x].astype(F32)
                    for i in range(3):
                        total += rw[z_slot[(p, h)], i, y, x].astype(F32)
                    mine[core, zz, y, x] = total.astype(BF16)
                return carry

            lax.fori_loop(0, 2, add, 0)
        else:
            def add(z, carry):
                for i in range(2):
                    if way == "yxz":
                        mine[core, z, yy, i] += ra[p, h, z, i]
                    else:
                        mine[core, z, i, xx] += ra[p, h, z, i]
                return carry

            lax.fori_loop(0, 4, add, 0)
        begin(step_2(p, h))

    def end_2(p, h):
        finish_steps(step_2(p, h))
        mine = chunk(p, h)
        way = route(p, h)
        if way[0] == "z":
            for i in range(2):
                if way == "zyx":
                    mine[core, zz, yy, i] += rb[p, h, i]
                else:
                    mine[core, zz, i, xx] += rb[p, h, i]
        else:
            def add(z, carry):
                mine[core, z, yy, xx] += rb[p, h, z]
                return carry

            lax.fori_loop(0, 4, add, 0)
        begin(step_3(p, h))

    outs = []

    def end_3(p, h):
        finish_steps(step_3(p, h))
        total = chunk(p, h)[core, zz, yy, xx].astype(F32)
        for i in range(1 if route(p, h)[0] == "z" else 3):
            total += rz[p, h, i].astype(F32)
        parts[p, h] = total
        at = WIDE * h
        if p < 2:
            targets = [wbg.at[pl.ds(48 * p, 48), pl.ds(at, WIDE)]]
        elif p < 4:
            at += (p - 2) * 2 * D
            targets = [wig.at[:, pl.ds(at, WIDE)], wig.at[:, pl.ds(at + D, WIDE)]]
        else:
            targets = [ref.at[:, pl.ds(at, WIDE)] for ref in ((wvg, wog) if p == 4 else (wqg, wkg))]
        rows = 48 // len(targets)
        for i, target in enumerate(targets):
            outs.append(pltpu.make_async_copy(parts.at[p, h, pl.ds(rows * i, rows)], target, part_sem.at[p, h, i]))
            outs[-1].start()

    def store_grad(p, h, grad):
        for i in range(32):
            chunk(p, h)[i % 2, i // 8, (i // 4) % 2, (i // 2) % 2] = grad[i]

    def back_grad(p, h):
        left = jnp.concatenate([actT[96 * i + 48 * p:96 * i + 48 * p + 48, :] for i in range(32)], axis=0)
        grad = dot_nn(left, ml[:, WIDE * h:WIDE * h + WIDE]).astype(BF16)
        store_grad(p, h, grad.reshape(32, 48, WIDE))

    def pair_grad(p, h, left_0, right_0, left_1, right_1):
        cols = pl.ds(WIDE * h, WIDE)
        grad_0 = dot_nn(left_0[...], right_0[:, cols]).reshape(32, 24, WIDE)
        grad_1 = dot_nn(left_1[...], right_1[:, cols]).reshape(32, 24, WIDE)
        store_grad(p, h, jnp.concatenate([grad_0, grad_1], axis=1).astype(BF16))

    def in_grad(p, h):
        at = (p - 2) * 2 * D
        pair_grad(p, h, mlT, gp.at[:, pl.ds(at, D)], mlT, gp.at[:, pl.ds(at + D, D)])

    def inner_grad(t):
        cols = pl.ds(t * D, D)
        weight = wb_tile(t)
        tmp_a[...] = dot_nt(ml[0:256, :], weight)
        tmp_b[0:224, :] = dot_nt(ml[256:480, :], weight)
        total = zero8
        for ref, start, size in ((tmp_a, 0, 256), (tmp_b, 256, 224)):
            for at, count in blocks(0, size, 16):
                rows = pl.ds(start + at, count)
                rounded = (ref[at:at + count, :] * gp[rows, cols].astype(F32)).astype(BF16)
                gp[rows, cols] = rounded
                total = total + fold8(rounded.astype(F32))
        vec[8 + t:9 + t, :] = jnp.sum(total, axis=0, keepdims=True)

    def middle_grad(t):
        cols = pl.ds(t * D, D)
        n2[...] += dot_nt(gp[:, cols], wi[:, cols])

    def attn_norm_back():
        sums = (zero8, zero8, zero8)
        for at, count in blocks(0, 480, 32):
            rows = pl.ds(at, count)
            upstream, unit = n2[rows, :], n1[rows, :]
            scaled = upstream * gain1
            hidden_grad = r1[rows, :] * (
                scaled
                - jnp.mean(scaled, axis=-1, keepdims=True)
                - unit * jnp.mean(scaled * unit, axis=-1, keepdims=True)
            )
            n1[rows, :] = hidden_grad
            rounded = hidden_grad.astype(BF16)
            ml[rows, :] = rounded
            sums = (
                sums[0] + fold8(upstream * unit), sums[1] + fold8(upstream), sums[2] + fold8(rounded.astype(F32)),
            )
        vec[2:3, :] = jnp.sum(sums[2], axis=0, keepdims=True)
        vec[3:4, :] = jnp.sum(sums[0], axis=0, keepdims=True)
        vec[4:5, :] = jnp.sum(sums[1], axis=0, keepdims=True)

    def context_grad():
        c_s[...] = dot_nt(ml[...], wo[...]).astype(BF16)

    def query_slot_back():
        q_rows, k_rows, v_rows = spread(q_s[0:32, :]), k_s[0:32, :], v_s[0:32, :]
        dc_rows = spread(c_s[0:32, :])
        soft = pq_s[...]
        dp = dot_nt(v_rows, dc_rows)
        soft_f = soft.astype(F32)
        ds = (soft_f * (dp - jnp.sum(soft_f * dp, axis=0, keepdims=True))).astype(BF16)
        v_s[0:32, :] = dot_nn(soft, dc_rows).astype(BF16)
        k_s[0:32, :] = dot_nn(ds, q_rows).astype(BF16)
        q_s[0:32, :] = (0.125 * gather_heads(dot_tn(ds, k_rows))).astype(BF16)

    def attend_back(pair):
        lanes = pl.ds(pair * 128, 128)
        for slot in range(2):
            low_at = 12 * slot
            rows = pl.ds(32 + 208 * slot, WIN)
            keys, queries, values = k_s[rows, lanes], q_s[rows, lanes], v_s[rows, lanes]
            inside = ((key_at >= low_at) & (key_at < low_at + SLOT)).astype(BF16)
            upstream = c_s[rows, lanes] * inside
            keys_t = keys.T
            parts, dv, dk = [], 0.0, 0.0
            for h in range(2):
                p = p_s[slot, 2 * pair + h]
                dc = upstream * half[h]
                dp = dot_nt(values, dc)
                pf = p.astype(F32)
                ds = (pf * (dp - jnp.sum(pf * dp, axis=0, keepdims=True))).astype(BF16)
                dv += dot_nn(p, dc)
                dk += dot_nn(ds, queries * half[h])
                parts.append(dot_nn(keys_t, ds)[64 * h:64 * h + 64, :])
            dq = 0.125 * jnp.concatenate(parts, axis=0).T
            for ref, new in ((q_s, dq), (k_s, dk), (v_s, dv)):
                if slot == 0:
                    ref[32:240, lanes] = new[0:208].astype(BF16)
                    old = ref[240:272, lanes].astype(F32)
                    ref[240:272, lanes] = jnp.where(iota((32, 128), 0) < 12, new[208:240], old).astype(BF16)
                else:
                    old = ref[240:256, lanes].astype(F32)
                    ref[240:256, lanes] = jnp.where(iota((16, 128), 0) >= 12, new[0:16], old).astype(BF16)
                    ref[256:480, lanes] = new[16:240].astype(BF16)

    def column_sum(ref):
        total = zero8
        for at, count in blocks(0, 480, 32):
            total = total + fold8(ref[at:at + count, :].astype(F32))
        return jnp.sum(total, axis=0, keepdims=True)

    def column_sums():
        vec[0:1, :] = column_sum(q_s)
        vec[1:2, :] = column_sum(v_s)

    def token_grad(grads, weight):
        n1[...] += dot_nt(grads[...], weight[...])

    out_qg = pltpu.make_async_copy(n1.at[0:32, :], qtg_h, out_sem.at[2])
    out_pg = pltpu.make_async_copy(n1.at[32:472, :], ptg_h, out_sem.at[3])

    def send_tokens():
        out_qg.start()
        out_pg.start()

    def vec_step(i):
        return remote(vec, vecr.at[i], v_send.at[i], v_recv.at[i], (partner, x_peer, y_peer)[i])

    def vec_part(whole, to):
        device = to * 8 + plane
        narrow = pltpu.roll(whole[0:8], D - 24 * device, 1)[:, 0:128]
        wide = pltpu.roll(whole[8:16], D - 96 * plane, 1)[:, 0:128]
        wide = jnp.sum(jnp.where(iota((8, 128), 0) == to, wide, 0.0), axis=0, keepdims=True)
        return jnp.concatenate([narrow, wide, jnp.zeros((7, 128), F32)], axis=0)

    def vec_z():
        return [
            remote(
                vecs.at[hop - 1], vecz.at[hop - 1], v_send.at[2 + hop], v_recv.at[2 + hop],
                lax.rem(zz + hop, 4) * 8 + plane,
            )
            for hop in range(1, 4)
        ]

    def vec_on(i):
        if i > 0:
            vec_step(i - 1).wait()
            vec[...] += vecr[i - 1]
        if i < 3:
            vec_step(i).start()
        else:
            whole = vec[...]
            for hop in range(1, 4):
                vecs[hop - 1] = vec_part(whole, lax.rem(zz + hop, 4))
            begin(vec_z())

    def vec_end():
        finish_steps(vec_z())
        part = vec_part(vec[...], zz) + vecz[0] + vecz[1] + vecz[2]
        small_o[0:9, :] = part[0:9]
        outs.append(pltpu.make_async_copy(small_o, small_h, out_sem.at[4]))
        outs[-1].start()

    pieces_of = {
        "wback": back_grad, "dinner": inner_grad, "win": in_grad, "dmid": middle_grad, "lnback": attn_norm_back,
        "dctx": context_grad, "qslot": query_slot_back, "attn": attend_back, "sums": column_sums,
        "wvo": lambda h: pair_grad(4, h, xT, v_s, cT, ml), "wqk": lambda h: pair_grad(5, h, xT, q_s, xT, k_s),
        "tq": lambda: token_grad(q_s, wq), "tk": lambda: token_grad(k_s, wk), "tv": lambda: token_grad(v_s, wv),
        "tout": send_tokens, "vec": vec_on, "vecend": vec_end,
        "c": start_c, "ec": end_c, "e1": end_1, "e2": end_2, "e3": end_3,
    }
    for name, *operands in ORDER:
        pieces_of[name](*operands)

    out_q.wait()
    out_p.wait()
    out_qg.wait()
    out_pg.wait()
    for out in outs:
        out.wait()


def hand_on_kernel(*refs):
    count = 10
    sources, small = refs[:count], refs[count]
    targets, vectors = refs[count + 1:2 * count + 1], refs[2 * count + 1:2 * count + 11]
    held, rest = refs[2 * count + 11:3 * count + 11], refs[3 * count + 11:]
    small_v, lines, in_sem, out_sem = rest[0], rest[1:11], rest[11], rest[12]
    whole = [(i, None) for i in range(count) if i != 3]
    pieces = [(3, pl.ds(at, size)) for at, size in blocks(0, 440, 112)] + whole
    into, out = [], []
    for at, (i, rows) in enumerate(pieces):
        source, kept, target = (ref if rows is None else ref.at[rows, :] for ref in (sources[i], held[i], targets[i]))
        into.append(pltpu.make_async_copy(source, kept, in_sem.at[at]))
        out.append(pltpu.make_async_copy(kept, target, out_sem.at[at]))
    last = pltpu.make_async_copy(small, small_v, in_sem.at[len(pieces)])
    last.start()
    for copy in into:
        copy.start()
    last.wait()
    for at, ref in enumerate(lines[:8]):
        ref[...] = small_v[at:at + 1, 0:24].reshape(24)
    lines[8][...] = small_v[8:9, 0:96].reshape(96)
    lines[9][...] = small_v[9:10, 0:1].reshape(1)
    for at, (line, vector) in enumerate(zip(lines, vectors)):
        out.append(pltpu.make_async_copy(line, vector, out_sem.at[len(pieces) + at]))
        out[-1].start()
    for first, second in zip(into, out):
        first.wait()
        second.start()
    for copy in out:
        copy.wait()


def on_device_small(*operands):
    (
        query_tokens, passage_tokens, query_lengths, passage_lengths, passage_valid, positives, negatives,
        teacher_margins, query_grad, passage_grad, weight_query, bias_query, weight_key, weight_value, bias_value,
        weight_out, bias_out, gain_attn, shift_attn, weight_in, bias_in, weight_back, bias_back, gain_ffn, shift_ffn,
    ) = operands
    hbm, vmem, smem = (pl.BlockSpec(memory_space=space) for space in (pl.ANY, pltpu.VMEM, pltpu.SMEM))
    shape = jax.ShapeDtypeStruct
    slabs = (2, 2, 4, 2, 2, 48, D)
    large = (
        shape((32, D), BF16), shape((440, D), BF16), shape((32, D), F32), shape((440, D), F32), shape((24, D), F32),
        shape((24, D), F32), shape((24, D), F32), shape((24, D), F32), shape((24, FF), F32), shape((96, D), F32),
    )
    outs = pl.pallas_call(
        layer_kernel,
        out_shape=(
            *large, shape((16, 128), F32),
        ),
        in_specs=[
            hbm, hbm, smem, smem, smem, smem, smem, smem, hbm, hbm,
            *(hbm,) * 15,
        ],
        out_specs=(hbm,) * 11,
        scratch_shapes=[
            *(pltpu.VMEM((size,), BF16) for size in (D, D, D, D, D, FF, D, D, D)),
            pltpu.VMEM((D, D), BF16), pltpu.VMEM((D, D), BF16), pltpu.VMEM((D, D), BF16), pltpu.VMEM((D, D), BF16),
            pltpu.VMEM((D, FF), BF16), pltpu.VMEM((3, 2, 2, 4, 2, 2, 48, WIDE), BF16),
            pltpu.VMEM((440, D), BF16), pltpu.VMEM((ROWS, D), BF16), pltpu.VMEM((D, ROWS), BF16),
            pltpu.VMEM((ROWS, D), BF16), pltpu.VMEM((ROWS, D), BF16), pltpu.VMEM((ROWS, D), BF16),
            pltpu.VMEM((2, 12, WIN, WIN), BF16), pltpu.VMEM((32, 384), BF16),
            pltpu.VMEM((ROWS, D), BF16), pltpu.VMEM((D, ROWS), BF16),
            pltpu.VMEM((ROWS, D), F32), pltpu.VMEM((ROWS, D), F32), pltpu.VMEM((ROWS, 1), F32), pltpu.VMEM((ROWS, 1), F32),
            pltpu.VMEM((ROWS, D), BF16), pltpu.VMEM((D, ROWS), BF16),
            pltpu.VMEM((256, D), BF16), pltpu.VMEM((256, D), BF16), pltpu.VMEM((FF, ROWS), BF16),
            pltpu.VMEM((256, D), F32), pltpu.VMEM((256, D), F32),
            pltpu.VMEM((ROWS, FF), BF16),
            pltpu.VMEM((32, D), BF16), pltpu.VMEM((440, D), BF16), pltpu.VMEM((32, D), BF16), pltpu.VMEM((440, D), BF16),
            pltpu.VMEM((1024, 128), BF16), pltpu.VMEM((1024, 128), F32),
            pltpu.VMEM((16, D), F32), pltpu.VMEM((3, 16, D), F32), pltpu.VMEM((3, 16, 128), F32), pltpu.VMEM((3, 16, 128), F32),
            pltpu.VMEM((16, 128), F32), pltpu.VMEM((6, 3, 48, WIDE), F32),
            pltpu.VMEM((4, 3, 2, 4, 2, 2, 48, WIDE), BF16),
            pltpu.VMEM((2, 3, 4, 2, 2, 48, WIDE), BF16), pltpu.VMEM((6, 3, 4, 2, 48, WIDE), BF16),
            pltpu.VMEM((6, 3, 4, 48, WIDE), BF16), pltpu.VMEM((6, 3, 3, 48, WIDE), BF16),
            pltpu.VMEM((sum(way[0] == "z" for way in ROUTE), 3, 2, 2, 48, WIDE), BF16),
            pltpu.SemaphoreType.DMA((24,)), pltpu.SemaphoreType.DMA((5,)), pltpu.SemaphoreType.DMA((6, 3, 2)),
            pltpu.SemaphoreType.DMA((16,)), pltpu.SemaphoreType.DMA((16,)),
            pltpu.SemaphoreType.DMA((6, 3)), pltpu.SemaphoreType.DMA((6, 3)),
            pltpu.SemaphoreType.DMA((6, 3)), pltpu.SemaphoreType.DMA((6, 3)),
            pltpu.SemaphoreType.DMA((6, 3)), pltpu.SemaphoreType.DMA((6, 3)),
            pltpu.SemaphoreType.DMA((6, 3, 3)), pltpu.SemaphoreType.DMA((6, 3, 3)),
            pltpu.SemaphoreType.DMA((6,)), pltpu.SemaphoreType.DMA((6,)),
            pltpu.SemaphoreType.REGULAR((2, 3)),
        ],
        compiler_params=pltpu.CompilerParams(
            collective_id=0, has_side_effects=True, vmem_limit_bytes=64 * 1024 * 1024 - 65536,
        ),
        name="encoder_layer",
    )(
        query_tokens, passage_tokens, query_lengths, passage_lengths, passage_valid, positives, negatives,
        teacher_margins, query_grad, passage_grad, weight_query, bias_query, weight_key, weight_value, bias_value,
        weight_out, bias_out, gain_attn, shift_attn, weight_in, bias_in, weight_back.reshape(slabs), bias_back,
        gain_ffn, shift_ffn,
    )
    done = pl.pallas_call(
        hand_on_kernel,
        out_shape=large + (shape((24,), F32),) * 8 + (shape((96,), F32), shape((1,), F32)),
        in_specs=[hbm] * 11,
        out_specs=(hbm,) * 20,
        scratch_shapes=[pltpu.VMEM(out.shape, out.dtype) for out in large]
        + [pltpu.VMEM((16, 128), F32)] + [pltpu.VMEM((size,), F32) for size in (24,) * 8 + (96, 1)]
        + [pltpu.SemaphoreType.DMA((24,)), pltpu.SemaphoreType.DMA((24,))],
        name="hand_on",
    )(*outs)
    qout, pout, qtg, ptg, wqg, wkg, wvg, wog, wig, wbg, bqg, bvg, bog, gag, sag, bbg, gfg, sfg, big, loss = done
    return (
        qout, pout, loss, qtg, ptg, wqg, bqg, wkg, wvg, bvg, wog, bog, gag, sag, wig, big, wbg, bbg, gfg, sfg,
    )


def solution(mesh):
    return jax.shard_map(
        on_device_small if mesh.shape["dp"] == 32 else on_device,
        mesh=mesh,
        in_specs=(
            P("dp", None),
            P("dp", None),
            P("dp"),
            P("dp"),
            P("dp"),
            P("dp"),
            P("dp"),
            P("dp"),
            P("dp", None),
            P("dp", None),
            P(),
            P(),
            P(),
            P(),
            P(),
            P(),
            P(),
            P(),
            P(),
            P(),
            P(),
            P(),
            P(),
            P(),
            P(),
        ),
        out_specs=(
            P("dp", None),
            P("dp", None),
            P("dp"),
            P("dp", None),
            P("dp", None),
            P("dp", None),
            P("dp"),
            P("dp", None),
            P("dp", None),
            P("dp"),
            P("dp", None),
            P("dp"),
            P("dp"),
            P("dp"),
            P("dp", None),
            P("dp"),
            P("dp", None),
            P("dp"),
            P("dp"),
            P("dp"),
        ),
        check_vma=False,
    )
```

```python
import jax
import jax.numpy as jnp
from jax import lax
from jax.experimental import pallas as pl
from jax.experimental.pallas import tpu as pltpu
from jax.sharding import PartitionSpec as P

D = 768
HEADS = 12
HEAD_DIM = 64


ln_eps = 1e-12
score_scale = 0.0625
margin_weight = 0.5
root_half = 0.7071067811865476
inv_root_tau = 0.3989422804014327


def matmul(left, right):
    return jnp.dot(left, right, preferred_element_type=jnp.float32)


def left_across(left, right):
    return lax.dot_general(
        left, right, (((0,), (0,)), ((), ())), preferred_element_type=jnp.float32
    )


def right_across(left, right):
    return lax.dot_general(
        left, right, (((1,), (1,)), ((), ())), preferred_element_type=jnp.float32
    )


def normalize(hidden, gain, shift):
    centered = hidden - jnp.mean(hidden, axis=-1, keepdims=True)
    inv_std = lax.rsqrt(jnp.mean(centered * centered, axis=-1, keepdims=True) + ln_eps)
    unit_rows = centered * inv_std
    return (unit_rows * gain.astype(jnp.float32) + shift.astype(jnp.float32), unit_rows, inv_std)


def normalize_back(upstream, unit_rows, inv_std, gain):
    scaled = upstream * gain.astype(jnp.float32)
    hidden_grad = inv_std * (
        scaled
        - jnp.mean(scaled, axis=-1, keepdims=True)
        - unit_rows * jnp.mean(scaled * unit_rows, axis=-1, keepdims=True)
    )
    return (hidden_grad, jnp.sum(upstream * unit_rows, axis=0), jnp.sum(upstream, axis=0))


def gelu_exact(inputs):
    return 0.5 * inputs * (1.0 + lax.erf(inputs * root_half))


def gelu_slope(inputs):
    return 0.5 * (1.0 + lax.erf(inputs * root_half)) + inputs * inv_root_tau * jnp.exp(
        -0.5 * inputs * inputs
    )


def head_scores(query_heads, key_heads, lengths):
    slot_length = query_heads.shape[1]
    allowed = (lax.iota(jnp.int32, slot_length)[None, :] < lengths[:, None])[:, None, None, :]
    raw_scores = 0.125 * jnp.einsum(
        "bqhd,bkhd->bhqk", query_heads, key_heads, preferred_element_type=jnp.float32
    )
    return jnp.where(allowed, raw_scores, -1000000000.0)


def encode_forward(tokens, lengths, params):
    (
        weight_query,
        bias_query,
        weight_key,
        weight_value,
        bias_value,
        weight_out,
        bias_out,
        gain_attn,
        shift_attn,
        weight_in,
        bias_in,
        weight_back,
        bias_back,
        gain_ffn,
        shift_ffn,
    ) = params
    slot_count = lengths.shape[0]
    row_count = tokens.shape[0]
    split_heads = (slot_count, row_count // slot_count, HEADS, HEAD_DIM)
    queries = (matmul(tokens, weight_query) + bias_query.astype(jnp.float32)).astype(jnp.bfloat16)
    keys_all = matmul(tokens, weight_key).astype(jnp.bfloat16)
    values_all = (matmul(tokens, weight_value) + bias_value.astype(jnp.float32)).astype(
        jnp.bfloat16
    )
    scores = head_scores(queries.reshape(split_heads), keys_all.reshape(split_heads), lengths)
    peak_score = jnp.max(scores, axis=-1, keepdims=True)
    exp_scores = jnp.exp(scores - peak_score)
    row_total = jnp.sum(exp_scores, axis=-1, keepdims=True)
    soft_low = (exp_scores / row_total).astype(jnp.bfloat16)
    log_total = peak_score + jnp.log(row_total)
    context = jnp.einsum(
        "bhqk,bkhd->bqhd",
        soft_low,
        values_all.reshape(split_heads),
        preferred_element_type=jnp.float32,
    )
    context = context.reshape(row_count, D).astype(jnp.bfloat16)
    attn_sum = (
        tokens.astype(jnp.float32) + matmul(context, weight_out) + bias_out.astype(jnp.float32)
    )
    middle, unit_attn, inv_attn = normalize(attn_sum, gain_attn, shift_attn)
    middle_low = middle.astype(jnp.bfloat16)
    inner_act = matmul(middle_low, weight_in) + bias_in.astype(jnp.float32)
    gelu_low = gelu_exact(inner_act).astype(jnp.bfloat16)
    ffn_sum = middle + matmul(gelu_low, weight_back) + bias_back.astype(jnp.float32)
    output, unit_ffn, inv_ffn = normalize(ffn_sum, gain_ffn, shift_ffn)
    kept = (
        queries,
        keys_all,
        values_all,
        log_total,
        context,
        unit_attn,
        inv_attn,
        middle_low,
        inner_act,
        gelu_low,
        unit_ffn,
        inv_ffn,
    )
    return (output.astype(jnp.bfloat16), kept)


def ffn_backward(upstream, kept, params):
    (
        queries,
        keys_all,
        values_all,
        log_total,
        context,
        unit_attn,
        inv_attn,
        middle_low,
        inner_act,
        gelu_low,
        unit_ffn,
        inv_ffn,
    ) = kept
    weight_in, weight_back, gain_ffn = (params[9], params[11], params[13])
    ffn_grad, gain_grad, shift_grad = normalize_back(upstream, unit_ffn, inv_ffn, gain_ffn)
    branch_low = ffn_grad.astype(jnp.bfloat16)
    back_weight_grad = left_across(gelu_low, branch_low)
    back_bias_grad = jnp.sum(branch_low, axis=0, dtype=jnp.float32)
    inner_low = (right_across(branch_low, weight_back) * gelu_slope(inner_act)).astype(jnp.bfloat16)
    in_weight_grad = left_across(middle_low, inner_low)
    in_bias_grad = jnp.sum(inner_low, axis=0, dtype=jnp.float32)
    middle_grad = ffn_grad + right_across(inner_low, weight_in)
    return (
        middle_grad,
        (in_weight_grad, in_bias_grad, back_weight_grad, back_bias_grad, gain_grad, shift_grad),
    )


def attention_backward(middle_grad, tokens, lengths, kept, params):
    (
        queries,
        keys_all,
        values_all,
        log_total,
        context,
        unit_attn,
        inv_attn,
        middle_low,
        inner_act,
        gelu_low,
        unit_ffn,
        inv_ffn,
    ) = kept
    weight_query, weight_key, weight_value, weight_out, gain_attn = (
        params[0],
        params[2],
        params[3],
        params[5],
        params[7],
    )
    slot_count = lengths.shape[0]
    row_count = tokens.shape[0]
    split_heads = (slot_count, row_count // slot_count, HEADS, HEAD_DIM)
    attn_grad, gain_grad, shift_grad = normalize_back(middle_grad, unit_attn, inv_attn, gain_attn)
    attn_low = attn_grad.astype(jnp.bfloat16)
    out_weight_grad = left_across(context, attn_low)
    out_bias_grad = jnp.sum(attn_low, axis=0, dtype=jnp.float32)
    context_grad = right_across(attn_low, weight_out).astype(jnp.bfloat16).reshape(split_heads)
    query_heads = queries.reshape(split_heads)
    key_heads = keys_all.reshape(split_heads)
    value_heads = values_all.reshape(split_heads)
    soft_full = jnp.exp(head_scores(query_heads, key_heads, lengths) - log_total)
    soft_grad = jnp.einsum(
        "bqhd,bkhd->bhqk", context_grad, value_heads, preferred_element_type=jnp.float32
    )
    value_grad = jnp.einsum(
        "bhqk,bqhd->bkhd",
        soft_full.astype(jnp.bfloat16),
        context_grad,
        preferred_element_type=jnp.float32,
    )
    value_grad = value_grad.reshape(row_count, D).astype(jnp.bfloat16)
    score_low = (
        soft_full * (soft_grad - jnp.sum(soft_full * soft_grad, axis=-1, keepdims=True))
    ).astype(jnp.bfloat16)
    query_grad_low = 0.125 * jnp.einsum(
        "bhqk,bkhd->bqhd", score_low, key_heads, preferred_element_type=jnp.float32
    )
    query_grad_low = query_grad_low.reshape(row_count, D).astype(jnp.bfloat16)
    key_grad_low = 0.125 * jnp.einsum(
        "bhqk,bqhd->bkhd", score_low, query_heads, preferred_element_type=jnp.float32
    )
    key_grad_low = key_grad_low.reshape(row_count, D).astype(jnp.bfloat16)
    token_grad = (
        attn_grad
        + right_across(query_grad_low, weight_query)
        + right_across(key_grad_low, weight_key)
        + right_across(value_grad, weight_value)
    )
    grads = (
        left_across(tokens, query_grad_low),
        jnp.sum(query_grad_low, axis=0, dtype=jnp.float32),
        left_across(tokens, key_grad_low),
        left_across(tokens, value_grad),
        jnp.sum(value_grad, axis=0, dtype=jnp.float32),
        out_weight_grad,
        out_bias_grad,
        gain_grad,
        shift_grad,
    )
    return (token_grad, grads)


def on_device(
    query_tokens,
    passage_tokens,
    query_lengths,
    passage_lengths,
    passage_valid,
    positives,
    negatives,
    teacher_margins,
    query_grad,
    passage_grad,
    weight_query,
    bias_query,
    weight_key,
    weight_value,
    bias_value,
    weight_out,
    bias_out,
    gain_attn,
    shift_attn,
    weight_in,
    bias_in,
    weight_back,
    bias_back,
    gain_ffn,
    shift_ffn,
):
    params = (
        weight_query,
        bias_query,
        weight_key,
        weight_value,
        bias_value,
        weight_out,
        bias_out,
        gain_attn,
        shift_attn,
        weight_in,
        bias_in,
        weight_back,
        bias_back,
        gain_ffn,
        shift_ffn,
    )
    query_out, query_kept = encode_forward(query_tokens, query_lengths, params)
    passage_out, passage_kept = encode_forward(passage_tokens, passage_lengths, params)
    query_slots = query_lengths.shape[0]
    passage_slots = passage_lengths.shape[0]
    cls_query = query_out.reshape(query_slots, -1, D)[:, 0]
    cls_passage = passage_out.reshape(passage_slots, -1, D)[:, 0]
    valid_low = passage_valid.astype(jnp.bfloat16)

    def score_piece(cls_piece, valid_piece):
        scores = score_scale * right_across(cls_query, cls_piece)
        position = lax.iota(jnp.int32, cls_piece.shape[0])
        is_positive = position[None, :] == positives[:, None]
        is_negative = position[None, :] == negatives[:, None]
        allowed = (valid_piece[None, :] > 0.5) | is_positive
        return (scores, allowed, is_positive, is_negative)

    peak_score = jnp.full((query_slots,), -1e30, jnp.float32)
    scores, allowed, is_positive, is_negative = score_piece(
        lax.all_gather(cls_passage, "dp", axis=0, tiled=True),
        lax.all_gather(valid_low, "dp", axis=0, tiled=True),
    )
    masked = jnp.where(allowed, scores, -1e30)
    new_peak = jnp.maximum(peak_score, jnp.max(masked, axis=1))
    row_total = jnp.sum(jnp.where(allowed, jnp.exp(masked - new_peak[:, None]), 0.0), axis=1)
    positive_score = jnp.sum(jnp.where(is_positive, scores, 0.0), axis=1)
    negative_score = jnp.sum(jnp.where(is_negative, scores, 0.0), axis=1)
    peak_score, row_total, positive_score, negative_score = (
        new_peak,
        row_total,
        positive_score,
        negative_score,
    )
    all_cls, all_valid = (
        lax.all_gather(cls_passage, "dp", axis=0, tiled=True),
        lax.all_gather(valid_low, "dp", axis=0, tiled=True),
    )
    log_total = peak_score + jnp.log(row_total)
    shortfall = positive_score - negative_score - teacher_margins
    query_loss = log_total - positive_score + margin_weight * shortfall * shortfall
    scores, allowed, is_positive, is_negative = score_piece(all_cls, all_valid)
    soft_scores = jnp.where(allowed, jnp.exp(scores - log_total[:, None]), 0.0)
    positive_hit = is_positive.astype(jnp.float32)
    negative_hit = is_negative.astype(jnp.float32)
    score_grad = (
        soft_scores
        - positive_hit
        + 2.0 * margin_weight * shortfall[:, None] * (positive_hit - negative_hit)
    ).astype(jnp.bfloat16)
    cls_query_grad = score_scale * matmul(score_grad, all_cls)
    cls_passage_grad = lax.psum_scatter(
        score_scale * left_across(score_grad, cls_query), "dp", scatter_dimension=0, tiled=True
    )
    query_upstream = (
        query_grad.astype(jnp.float32)
        .reshape(query_slots, -1, D)
        .at[:, 0]
        .add(cls_query_grad)
        .reshape(-1, D)
    )
    passage_upstream = (
        passage_grad.astype(jnp.float32)
        .reshape(passage_slots, -1, D)
        .at[:, 0]
        .add(cls_passage_grad)
        .reshape(-1, D)
    )
    query_middle_grad, query_ffn = ffn_backward(query_upstream, query_kept, params)
    passage_middle_grad, passage_ffn = ffn_backward(passage_upstream, passage_kept, params)
    (
        in_weight_grad,
        in_bias_grad,
        back_weight_grad,
        back_bias_grad,
        ffn_gain_grad,
        ffn_shift_grad,
    ) = tuple((first + second for first, second in zip(query_ffn, passage_ffn)))
    query_tokens_grad, query_attn = attention_backward(
        query_middle_grad, query_tokens, query_lengths, query_kept, params
    )
    passage_tokens_grad, passage_attn = attention_backward(
        passage_middle_grad, passage_tokens, passage_lengths, passage_kept, params
    )
    (
        query_weight_grad,
        query_bias_grad,
        key_weight_grad,
        value_weight_grad,
        value_bias_grad,
        out_weight_grad,
        out_bias_grad,
        attn_gain_grad,
        attn_shift_grad,
    ) = tuple((first + second for first, second in zip(query_attn, passage_attn)))
    (
        query_weight_grad,
        query_bias_grad,
        key_weight_grad,
        value_weight_grad,
        value_bias_grad,
        out_weight_grad,
        out_bias_grad,
        attn_gain_grad,
        attn_shift_grad,
        in_weight_grad,
        in_bias_grad,
        back_weight_grad,
        back_bias_grad,
        ffn_gain_grad,
        ffn_shift_grad,
    ) = (
        lax.psum_scatter(query_weight_grad, "dp", scatter_dimension=0, tiled=True),
        lax.psum_scatter(query_bias_grad, "dp", scatter_dimension=0, tiled=True),
        lax.psum_scatter(key_weight_grad, "dp", scatter_dimension=0, tiled=True),
        lax.psum_scatter(value_weight_grad, "dp", scatter_dimension=0, tiled=True),
        lax.psum_scatter(value_bias_grad, "dp", scatter_dimension=0, tiled=True),
        lax.psum_scatter(out_weight_grad, "dp", scatter_dimension=0, tiled=True),
        lax.psum_scatter(out_bias_grad, "dp", scatter_dimension=0, tiled=True),
        lax.psum_scatter(attn_gain_grad, "dp", scatter_dimension=0, tiled=True),
        lax.psum_scatter(attn_shift_grad, "dp", scatter_dimension=0, tiled=True),
        lax.psum_scatter(in_weight_grad, "dp", scatter_dimension=0, tiled=True),
        lax.psum_scatter(in_bias_grad, "dp", scatter_dimension=0, tiled=True),
        lax.psum_scatter(back_weight_grad, "dp", scatter_dimension=0, tiled=True),
        lax.psum_scatter(back_bias_grad, "dp", scatter_dimension=0, tiled=True),
        lax.psum_scatter(ffn_gain_grad, "dp", scatter_dimension=0, tiled=True),
        lax.psum_scatter(ffn_shift_grad, "dp", scatter_dimension=0, tiled=True),
    )
    return (
        query_out,
        passage_out,
        query_loss,
        query_tokens_grad,
        passage_tokens_grad,
        query_weight_grad,
        query_bias_grad,
        key_weight_grad,
        value_weight_grad,
        value_bias_grad,
        out_weight_grad,
        out_bias_grad,
        attn_gain_grad,
        attn_shift_grad,
        in_weight_grad,
        in_bias_grad,
        back_weight_grad,
        back_bias_grad,
        ffn_gain_grad,
        ffn_shift_grad,
    )


F32 = jnp.float32
BF16 = jnp.bfloat16
MESH = pl.DeviceIdType.MESH
FF = 3072
ROWS = 480
WIN = 240
SLOT = 220
NEG = -1000000000.0


def dot_nn(left, right):
    return jnp.dot(left, right, preferred_element_type=F32)


def dot_nt(left, right):
    return lax.dot_general(left, right, (((1,), (1,)), ((), ())), preferred_element_type=F32)


def dot_tn(left, right):
    return lax.dot_general(left, right, (((0,), (0,)), ((), ())), preferred_element_type=F32)


def row_of(ref, start=0, size=D):
    return ref[pl.ds(start, size)].astype(F32).reshape(1, size)


def one(ref):
    return ref[...].reshape(1, 1)


def blocks(start, stop, size):
    return [(at, min(size, stop - at)) for at in range(start, stop, size)]


def iota(shape, dim):
    return lax.broadcasted_iota(jnp.int32, shape, dim)


def fold8(block):
    return jnp.sum(block.reshape(-1, 8, block.shape[-1]), axis=0)


WIDE = 256
ROUTE = (
    "xyz", "yxz", "zyx", "xyz", "zxy", "zyx", "yxz", "xyz", "yxz", "xyz", "yxz", "xyz", "yxz", "xyz", "yxz", "xyz",
    "yxz", "xyz",
)
ORDER = (
    ("wback", 0, 0), ("c", 0, 0), ("wback", 0, 1), ("c", 0, 1), ("wback", 0, 2), ("c", 0, 2), ("wback", 1, 0),
    ("c", 1, 0), ("wback", 1, 1), ("c", 1, 1), ("wback", 1, 2), ("c", 1, 2), ("dinner", 0), ("ec", 0, 0),
    ("dinner", 1), ("ec", 0, 2), ("win", 2, 0), ("ec", 0, 1), ("c", 2, 0), ("win", 2, 1), ("ec", 1, 0), ("c", 2, 1),
    ("win", 2, 2), ("ec", 1, 2), ("ec", 1, 1), ("c", 2, 2), ("dinner", 2), ("dinner", 3), ("win", 3, 0), ("c", 3, 0),
    ("ec", 2, 0), ("win", 3, 1), ("ec", 2, 1), ("c", 3, 1), ("win", 3, 2), ("c", 3, 2), ("dmid", 0), ("dmid", 1),
    ("ec", 2, 2), ("dmid", 2), ("dmid", 3), ("lnback",), ("dctx",), ("ec", 3, 1), ("ec", 3, 0), ("qslot",),
    ("e1", 1, 0), ("attn", 0, 1), ("ec", 3, 2), ("attn", 1, 4), ("e1", 0, 2), ("e1", 2, 2), ("attn", 5, 1),
    ("sums",), ("wvo", 0), ("c", 4, 0), ("e1", 0, 1), ("e1", 2, 0), ("e1", 0, 0), ("wvo", 1), ("c", 4, 1),
    ("wvo", 2), ("e1", 3, 1), ("c", 4, 2), ("vec", 0), ("e1", 2, 1), ("ec", 4, 0), ("wqk", 0), ("c", 5, 0),
    ("ec", 4, 1), ("e2", 2, 2), ("e1", 3, 0), ("ec", 4, 2), ("e2", 0, 0), ("wqk", 1), ("e1", 3, 2), ("e2", 0, 1),
    ("c", 5, 1), ("e2", 1, 0), ("vec", 1), ("wqk", 2), ("c", 5, 2), ("e2", 3, 1), ("e1", 4, 0), ("e2", 2, 1),
    ("ec", 5, 2), ("e1", 4, 1), ("ec", 5, 1), ("e2", 2, 0), ("e3", 2, 2), ("e1", 4, 2), ("e2", 3, 0), ("ec", 5, 0),
    ("e3", 0, 1), ("e2", 4, 0), ("e1", 5, 2), ("tq",), ("e3", 2, 1), ("e2", 3, 2), ("e3", 2, 0), ("e2", 4, 2),
    ("e3", 3, 1), ("e1", 1, 2), ("e1", 1, 1), ("e2", 4, 1), ("e1", 5, 1), ("vec", 2), ("e1", 5, 0), ("e2", 5, 2),
    ("e3", 3, 2), ("e3", 1, 0), ("vec", 3), ("e2", 5, 1), ("e3", 0, 0), ("tk",), ("e3", 4, 0), ("e2", 0, 2),
    ("e2", 5, 0), ("e3", 4, 1), ("e2", 1, 1), ("e3", 4, 2), ("e2", 1, 2), ("e3", 1, 2), ("e3", 5, 1), ("e3", 3, 0),
    ("vecend",), ("tv",), ("tout",), ("e3", 5, 2), ("e3", 1, 1), ("e3", 0, 2), ("e3", 5, 0),
)


def layer_kernel(
    qtok, ptok, qlen_h, plen, pvalid, pos_h, neg_h, margin_h, qgrad, pgrad,
    wq_h, bq_h, wk_h, wv_h, bv_h, wo_h, bo_h, ga_h, sa_h, wi_h, bi_h, wb_h, bb_h, gf_h, sf_h,
    qout_h, pout_h, qtg_h, ptg_h, wqg, wkg, wvg, wog, wig, wbg, small_h,
    qlen, pos, neg, margin, bq, bv, bo, ga, sa, bi, bb, gf, sf, wq, wk, wv, wo, wi, wb, pstage, x_s, xT, q_s, k_s, v_s, p_s, pq_s, c_s, cT, n1, n2, r1, r2,
    ml, mlT, act_a, act_b, actT, tmp_a, tmp_b, gp, qg_s, pg_s, qo_s, po_s, ex, ex_f, vec, vecr, vecs, vecz, small_o, parts,
    g_s, rc, ra, rb, rz, rw,
    load_sem, out_sem, part_sem, ex_send, ex_recv, c_send, c_recv, a_send, a_recv, b_send, b_recv,
    z_send, z_recv, v_send, v_recv, credit,
):
    me = lax.axis_index("dp")
    core = lax.rem(me, 2)
    xx = lax.rem(lax.div(me, 2), 2)
    yy = lax.rem(lax.div(me, 4), 2)
    zz = lax.div(me, 8)
    chip = lax.div(me, 2)
    partner = me + 1 - 2 * core
    x_peer = me + 2 - 4 * xx
    y_peer = me + 4 - 8 * yy
    plane = lax.rem(me, 8)

    loads = {}

    def load(name, source, target):
        loads[name] = pltpu.make_async_copy(source, target, load_sem.at[len(loads)])
        loads[name].start()

    load("ptok", ptok, pstage)
    load("qtok", qtok, qo_s)
    load("wq", wq_h, wq)
    load("wk", wk_h, wk)
    load("wv", wv_h, wv)
    vectors = ((qlen_h, qlen), (pos_h, pos), (neg_h, neg), (margin_h, margin), (bq_h, bq), (bv_h, bv), (bo_h, bo), (ga_h, ga), (sa_h, sa), (bi_h, bi), (bb_h, bb), (gf_h, gf), (sf_h, sf))
    for at, (source, target) in enumerate(vectors):
        load("vec" + str(at), source, target)

    barrier = pltpu.get_barrier_semaphore()
    for hop in range(1, 16):
        other = 2 * lax.rem(chip + hop, 16) + core
        pl.semaphore_signal(barrier, inc=1, device_id=(other,), device_id_type=MESH)
    pl.semaphore_signal(barrier, inc=1, device_id=(partner,), device_id_type=MESH)

    loads["ptok"].wait()
    loads["qtok"].wait()
    x_s[0:32, :] = qo_s[...]

    def copy_tokens(i, carry):
        x_s[pl.ds(pl.multiple_of(32 + i * 16, 16), 16), :] = pstage[pl.ds(pl.multiple_of(i * 16, 16), 16), :]
        return carry

    lax.fori_loop(0, 27, copy_tokens, 0)
    x_s[464:480, :] = jnp.concatenate(
        [pstage[432:440, :].astype(F32), jnp.zeros((8, D), F32)], axis=0
    ).astype(BF16)

    loads["wq"].wait()
    for at in range(len(vectors)):
        loads["vec" + str(at)].wait()
    load("wo", wo_h, wo)
    load("wi", wi_h, wi)
    q_s[...] = ((dot_nn(x_s[...], wq[...]) + row_of(bq)).astype(BF16) * 0.125).astype(BF16)
    loads["wk"].wait()
    k_s[...] = dot_nn(x_s[...], wk[...]).astype(BF16)
    loads["wv"].wait()
    for h in range(3):
        load("wb" + str(h), wb_h.at[:, :, :, :, :, :, pl.ds(WIDE * h, WIDE)], wb.at[h])
    load("qg", qgrad, qg_s)
    load("pg", pgrad, pg_s)
    v_s[...] = (dot_nn(x_s[...], wv[...]) + row_of(bv)).astype(BF16)

    head_of = iota((12, 1, D), 2) // 64
    head_mask = (head_of == iota((12, 1, D), 0)).astype(F32)

    def spread(rows):
        return (rows.astype(F32)[None] * head_mask).astype(BF16).reshape(384, D)

    def gather_heads(stacked):
        return jnp.sum(stacked.reshape(12, 32, D) * head_mask, axis=0)

    raw = dot_nt(k_s[0:32, :], spread(q_s[0:32, :]))
    raw = jnp.where(iota((32, 384), 0) < one(qlen), raw, NEG)
    soft = jnp.exp(raw - jnp.max(raw, axis=0, keepdims=True))
    soft = (soft * (1.0 / jnp.sum(soft, axis=0, keepdims=True))).astype(BF16)
    pq_s[...] = soft
    c_s[0:32, :] = gather_heads(dot_tn(soft, v_s[0:32, :])).astype(BF16)

    lane = iota((1, 128), 1)
    half = ((lane < 64).astype(BF16), (lane >= 64).astype(BF16))
    key_at = iota((WIN, 1), 0)

    def attend(pair, slot):
        lanes = pl.ds(pl.multiple_of(pair * 128, 128), 128)
        low_at = 12 * slot
        first_row = 32 + 208 * slot
        rows = pl.ds(first_row, WIN)
        keys, queries = k_s[rows, lanes], q_s[rows, lanes]
        values_t = v_s[rows, lanes].T
        allowed = (key_at >= low_at) & (key_at < low_at + plen[slot])
        parts = []
        for h in range(2):
            scores = jnp.where(allowed, dot_nt(keys, queries * half[h]), NEG)
            e = jnp.exp(scores - jnp.max(scores, axis=0, keepdims=True))
            p = (e * (1.0 / jnp.sum(e, axis=0, keepdims=True))).astype(BF16)
            p_s[slot, 2 * pair + h] = p
            parts.append(dot_nn(values_t, p)[64 * h:64 * h + 64, :])
        context = jnp.concatenate(parts, axis=0).T
        if slot == 0:
            c_s[rows, lanes] = context.astype(BF16)
            return
        old = c_s[240:256, lanes].astype(F32)
        c_s[240:256, lanes] = jnp.where(iota((16, 128), 0) >= 12, context[0:16], old).astype(BF16)
        c_s[256:480, lanes] = context[16:240].astype(BF16)

    def both_slots(pair, carry):
        attend(pair, 0)
        attend(pair, 1)
        return carry

    lax.fori_loop(0, 6, both_slots, 0)

    loads["wo"].wait()
    gain1, shift1, bias1 = row_of(ga), row_of(sa), row_of(bo)
    gain2, shift2, bias2 = row_of(gf), row_of(sf), row_of(bb)

    def wb_tile(t):
        return jnp.concatenate([wb[h, t // 2, t % 2].reshape(D, WIDE) for h in range(3)], axis=1)

    def normalized(hidden):
        centered = hidden - jnp.mean(hidden, axis=-1, keepdims=True)
        inv = lax.rsqrt(jnp.mean(centered * centered, axis=-1, keepdims=True) + ln_eps)
        return centered * inv, inv

    def forward_rows(start, stop):
        size = stop - start
        every, own = pl.ds(start, size), pl.ds(0, size)
        tmp_a[own, :] = dot_nn(c_s[every, :], wo[...])
        for at, count in blocks(0, size, 32):
            rows, here = pl.ds(start + at, count), pl.ds(at, count)
            unit, inv = normalized(tmp_a[here, :] + x_s[rows, :].astype(F32) + bias1)
            n1[rows, :] = unit
            r1[rows, :] = inv
            ml[rows, :] = (unit * gain1 + shift1).astype(BF16)
        if start == 0:
            loads["wi"].wait()
            for h in range(3):
                loads["wb" + str(h)].wait()
        inner, acts = (tmp_a, tmp_b), (act_a, act_b)
        tmp_a[own, :] = dot_nn(ml[every, :], wi[:, 0:D])
        mlT[:, every] = ml[every, :].T
        xT[:, every] = x_s[every, :].T
        cT[:, every] = c_s[every, :].T

        def finish(t):
            act = acts[t % 2][own, :]
            if t == 0:
                n2[every, :] = dot_nn(act, wb_tile(t))
            else:
                n2[every, :] += dot_nn(act, wb_tile(t))
            actT[t * D:t * D + D, every] = act.T

        for t in range(4):
            if t < 3:
                inner[(t + 1) % 2][own, :] = dot_nn(ml[every, :], wi[:, t * D + D:t * D + 2 * D])
            bias_t = row_of(bi, t * D)
            for at, count in blocks(0, size, 16):
                here = pl.ds(at, count)
                u = inner[t % 2][here, :] + bias_t
                cdf = 0.5 * (1.0 + lax.erf(u * root_half))
                acts[t % 2][here, :] = (u * cdf).astype(BF16)
                gp[start + at:start + at + count, t * D:t * D + D] = (
                    cdf + u * inv_root_tau * jnp.exp(-0.5 * u * u)
                ).astype(BF16)
            if t > 0:
                finish(t - 1)
        finish(3)
        for at, count in blocks(start, stop, 32):
            rows = pl.ds(at, count)
            unit, inv = normalized(n2[rows, :] + (n1[rows, :] * gain1 + shift1) + bias2)
            n2[rows, :] = unit
            r2[rows, :] = inv
            out = (unit * gain2 + shift2).astype(BF16)
            if at == 0:
                qo_s[...] = out
            else:
                po_s[at - 32:min(at, 440), :] = out[0:min(count, 472 - at)]

    forward_rows(0, 256)

    slot_me = core * 16 + chip
    base = pl.multiple_of(slot_me * 32, 32)
    first_rows = (
        qo_s[0:16, :].astype(F32)[0:1],
        po_s[0:16, :].astype(F32)[0:1],
        po_s[208:224, :].astype(F32)[12:13],
    )
    lane_row = iota((1, 128), 1)
    meta = jnp.zeros((1, 128), F32)
    margin_0 = jnp.zeros((1, 128), F32) + one(margin)
    margin_1 = margin_0.astype(BF16).astype(F32)
    margin_2 = (margin_0 - margin_1).astype(BF16).astype(F32)
    for at, value in enumerate((
        pvalid[0].astype(F32), pvalid[1].astype(F32), one(pos).astype(F32), one(neg).astype(F32),
        margin_1, margin_2, margin_0 - margin_1 - margin_2,
    )):
        meta = jnp.where(lane_row == at, value, meta)
    pieces = [row[:, 128 * i:128 * i + 128] for row in first_rows for i in range(6)]
    ex[pl.ds(base, 32), :] = jnp.concatenate(pieces + [meta, jnp.zeros((13, 128), F32)], axis=0).astype(BF16)

    pl.semaphore_wait(barrier, 16)
    sends = []
    for hop in range(1, 16):
        block = ex.at[pl.ds(base, 32), :]
        sends.append(pltpu.make_async_remote_copy(
            src_ref=block, dst_ref=block, send_sem=ex_send.at[hop], recv_sem=ex_recv.at[hop],
            device_id=(2 * lax.rem(chip + hop, 16) + core,), device_id_type=MESH,
        ))
        sends[-1].start()

    forward_rows(256, 480)
    out_q = pltpu.make_async_copy(qo_s, qout_h, out_sem.at[0])
    out_p = pltpu.make_async_copy(po_s, pout_h, out_sem.at[1])
    out_q.start()
    out_p.start()
    loads["qg"].wait()
    loads["pg"].wait()

    def ffn_norm_back(r0, upstream, sums):
        rows = pl.ds(r0, upstream.shape[0])
        unit = n2[rows, :]
        scaled = upstream * gain2
        hidden_grad = r2[rows, :] * (
            scaled
            - jnp.mean(scaled, axis=-1, keepdims=True)
            - unit * jnp.mean(scaled * unit, axis=-1, keepdims=True)
        )
        n2[rows, :] = hidden_grad
        rounded = hidden_grad.astype(BF16)
        ml[rows, :] = rounded
        return (
            sums[0] + fold8(upstream * unit), sums[1] + fold8(upstream), sums[2] + fold8(rounded.astype(F32)),
        )

    zero8 = jnp.zeros((8, D), F32)
    sums = (zero8, zero8, zero8)

    def middle_block(i, sums):
        upstream = pg_s[pl.ds(pl.multiple_of(i * 32, 32), 32), :].astype(F32)
        return ffn_norm_back(pl.multiple_of(32 + i * 32, 32), upstream, sums)

    sums = lax.fori_loop(1, 6, middle_block, sums)
    sums = lax.fori_loop(7, 13, middle_block, sums)
    last = jnp.concatenate([pg_s[416:440, :].astype(F32), jnp.zeros((8, D), F32)], axis=0)
    sums = ffn_norm_back(448, last, sums)

    for send in sends:
        send.wait()
    same_core = ex.at[pl.ds(pl.multiple_of(core * 512, 512), 512), :]
    across = pltpu.make_async_remote_copy(
        src_ref=same_core, dst_ref=same_core, send_sem=ex_send.at[0], recv_sem=ex_recv.at[0],
        device_id=(partner,), device_id_type=MESH,
    )
    across.start()
    across.wait()

    ex_f[...] = ex[...].astype(F32)

    def first(r):
        return ex_f[pl.ds(r, 32, stride=32), :]

    cls_q = jnp.concatenate([first(i) for i in range(6)], axis=1)
    cls_0 = jnp.concatenate([first(6 + i) for i in range(6)], axis=1).astype(BF16)
    cls_1 = jnp.concatenate([first(12 + i) for i in range(6)], axis=1).astype(BF16)
    metas = first(18)
    metas_t = metas.T
    s0 = score_scale * dot_nt(cls_q.astype(BF16), cls_0)
    s1 = score_scale * dot_nt(cls_q.astype(BF16), cls_1)
    col = iota((1, 32), 1)
    passage = (4 * lax.rem(col, 16) + 2 * lax.div(col, 16)).astype(F32)
    at_pos, at_neg, wanted = metas[:, 2:3], metas[:, 3:4], metas[:, 4:5] + metas[:, 5:6] + metas[:, 6:7]
    pos0, pos1 = at_pos == passage, at_pos == passage + 1.0
    neg0, neg1 = at_neg == passage, at_neg == passage + 1.0
    m0 = jnp.where((metas_t[0:1, :] > 0.5) | pos0, s0, -1e30)
    m1 = jnp.where((metas_t[1:2, :] > 0.5) | pos1, s1, -1e30)
    peak = jnp.maximum(jnp.max(m0, axis=1, keepdims=True), jnp.max(m1, axis=1, keepdims=True))
    total = jnp.sum(jnp.exp(m0 - peak), axis=1, keepdims=True) + jnp.sum(jnp.exp(m1 - peak), axis=1, keepdims=True)
    lse = peak + jnp.log(total)

    def picked(where0, where1):
        return jnp.sum(jnp.where(where0, s0, 0.0), axis=1, keepdims=True) + jnp.sum(
            jnp.where(where1, s1, 0.0), axis=1, keepdims=True
        )

    at_positive = picked(pos0, pos1)
    miss = at_positive - picked(neg0, neg1) - wanted
    losses = lse - at_positive + margin_weight * miss * miss
    pos0, pos1, neg0, neg1 = (hit.astype(F32) for hit in (pos0, pos1, neg0, neg1))
    ds0 = (jnp.exp(m0 - lse) - pos0 + 2.0 * margin_weight * miss * (pos0 - neg0)).astype(BF16)
    ds1 = (jnp.exp(m1 - lse) - pos1 + 2.0 * margin_weight * miss * (pos1 - neg1)).astype(BF16)
    mine = iota((32, 1), 0) == slot_me
    mine_col = iota((1, 32), 1) == slot_me
    small_o[9:10, :] = jnp.sum(jnp.where(mine, losses, 0.0), axis=0, keepdims=True) + jnp.zeros((1, 128), F32)
    dq_all = score_scale * (dot_nn(ds0, cls_0) + dot_nn(ds1, cls_1))
    d_query = jnp.sum(jnp.where(mine, dq_all, 0.0), axis=0, keepdims=True)

    def passage_grad_row(ds):
        column = jnp.sum(jnp.where(mine_col, ds.astype(F32), 0.0), axis=1, keepdims=True)
        return score_scale * jnp.sum(column * cls_q, axis=0, keepdims=True)

    d_first = (d_query, passage_grad_row(ds0), passage_grad_row(ds1))

    row32 = iota((32, 1), 0)
    for r0, at, source, add in (
        (0, 0, qg_s[...], d_first[0]), (32, 0, pg_s[0:32, :], d_first[1]), (224, 28, pg_s[192:224, :], d_first[2]),
    ):
        upstream = source.astype(F32) + jnp.where(row32 == at, add, 0.0)
        sums = ffn_norm_back(r0, upstream, sums)
    vec[...] = jnp.zeros_like(vec)
    vec[5:6, :] = jnp.sum(sums[2], axis=0, keepdims=True)
    vec[6:7, :] = jnp.sum(sums[0], axis=0, keepdims=True)
    vec[7:8, :] = jnp.sum(sums[1], axis=0, keepdims=True)

    def chunk(p, h):
        return g_s.at[p, h] if p < 4 else wb.at[h, p - 4]

    z_slot = {}
    for at, way in enumerate(ROUTE):
        if way[0] == "z":
            z_slot[(at // 3, at % 3)] = len(z_slot)

    def route(p, h):
        return ROUTE[3 * p + h]

    def remote(source, target, send, recv, device):
        return pltpu.make_async_remote_copy(
            src_ref=source, dst_ref=target, send_sem=send, recv_sem=recv, device_id=(device,), device_id_type=MESH,
        )

    def step_c(p, h):
        return [remote(chunk(p, h).at[1 - core], rc.at[p % 2, h], c_send.at[p, h], c_recv.at[p, h], partner)]

    def along_z(p, h, pick, target):
        steps = []
        for hop in range(1, 4):
            to = lax.rem(zz + hop, 4)
            steps.append(remote(
                pick(to), target(hop - 1), z_send.at[p, h, hop - 1], z_recv.at[p, h, hop - 1], to * 8 + plane,
            ))
        return steps

    def step_1(p, h):
        mine, way = chunk(p, h), route(p, h)
        if way[0] == "z":
            return along_z(p, h, lambda to: mine.at[core, to], lambda i: rw.at[z_slot[(p, h)], i])
        away = mine.at[core, :, :, 1 - xx] if way == "xyz" else mine.at[core, :, 1 - yy]
        return [remote(away, ra.at[p, h], a_send.at[p, h], a_recv.at[p, h], x_peer if way == "xyz" else y_peer)]

    def step_2(p, h):
        mine, way = chunk(p, h), route(p, h)
        if way == "zyx":
            away, target = mine.at[core, zz, 1 - yy], rb.at[p, h, 0:2]
        elif way == "zxy":
            away, target = mine.at[core, zz, :, 1 - xx], rb.at[p, h, 0:2]
        elif way == "xyz":
            away, target = mine.at[core, :, 1 - yy, xx], rb.at[p, h]
        else:
            away, target = mine.at[core, :, yy, 1 - xx], rb.at[p, h]
        return [remote(away, target, b_send.at[p, h], b_recv.at[p, h], x_peer if way[1] == "x" else y_peer)]

    def step_3(p, h):
        mine = chunk(p, h)
        way = route(p, h)
        if way[0] == "z":
            away = mine.at[core, zz, yy, 1 - xx] if way == "zyx" else mine.at[core, zz, 1 - yy, xx]
            return [remote(
                away, rz.at[p, h, 0], a_send.at[p, h], a_recv.at[p, h], x_peer if way == "zyx" else y_peer,
            )]
        return along_z(p, h, lambda to: mine.at[core, to, yy, xx], lambda i: rz.at[p, h, i])

    def begin(steps):
        for step in steps:
            step.start()

    def finish_steps(steps):
        for step in steps:
            step.wait()

    def start_c(p, h):
        if p >= 2:
            pl.semaphore_wait(credit.at[p % 2, h], 1)
        begin(step_c(p, h))

    def end_c(p, h):
        finish_steps(step_c(p, h))

        def add(z, carry):
            for y in range(2):
                for x in range(2):
                    chunk(p, h)[core, z, y, x] += rc[p % 2, h, z, y, x]
            return carry

        lax.fori_loop(0, 4, add, 0)
        begin(step_1(p, h))
        if p < 4:
            pl.semaphore_signal(credit.at[p % 2, h], inc=1, device_id=(partner,), device_id_type=MESH)

    def end_1(p, h):
        finish_steps(step_1(p, h))
        mine, way = chunk(p, h), route(p, h)
        if way[0] == "z":
            def add(y, carry):
                for x in range(2):
                    total = mine[core, zz, y, x].astype(F32)
                    for i in range(3):
                        total += rw[z_slot[(p, h)], i, y, x].astype(F32)
                    mine[core, zz, y, x] = total.astype(BF16)
                return carry

            lax.fori_loop(0, 2, add, 0)
        else:
            def add(z, carry):
                for i in range(2):
                    if way == "yxz":
                        mine[core, z, yy, i] += ra[p, h, z, i]
                    else:
                        mine[core, z, i, xx] += ra[p, h, z, i]
                return carry

            lax.fori_loop(0, 4, add, 0)
        begin(step_2(p, h))

    def end_2(p, h):
        finish_steps(step_2(p, h))
        mine = chunk(p, h)
        way = route(p, h)
        if way[0] == "z":
            for i in range(2):
                if way == "zyx":
                    mine[core, zz, yy, i] += rb[p, h, i]
                else:
                    mine[core, zz, i, xx] += rb[p, h, i]
        else:
            def add(z, carry):
                mine[core, z, yy, xx] += rb[p, h, z]
                return carry

            lax.fori_loop(0, 4, add, 0)
        begin(step_3(p, h))

    outs = []

    def end_3(p, h):
        finish_steps(step_3(p, h))
        total = chunk(p, h)[core, zz, yy, xx].astype(F32)
        for i in range(1 if route(p, h)[0] == "z" else 3):
            total += rz[p, h, i].astype(F32)
        parts[p, h] = total
        at = WIDE * h
        if p < 2:
            targets = [wbg.at[pl.ds(48 * p, 48), pl.ds(at, WIDE)]]
        elif p < 4:
            at += (p - 2) * 2 * D
            targets = [wig.at[:, pl.ds(at, WIDE)], wig.at[:, pl.ds(at + D, WIDE)]]
        else:
            targets = [ref.at[:, pl.ds(at, WIDE)] for ref in ((wvg, wog) if p == 4 else (wqg, wkg))]
        rows = 48 // len(targets)
        for i, target in enumerate(targets):
            outs.append(pltpu.make_async_copy(parts.at[p, h, pl.ds(rows * i, rows)], target, part_sem.at[p, h, i]))
            outs[-1].start()

    def store_grad(p, h, grad):
        for i in range(32):
            chunk(p, h)[i % 2, i // 8, (i // 4) % 2, (i // 2) % 2] = grad[i]

    def back_grad(p, h):
        left = jnp.concatenate([actT[96 * i + 48 * p:96 * i + 48 * p + 48, :] for i in range(32)], axis=0)
        grad = dot_nn(left, ml[:, WIDE * h:WIDE * h + WIDE]).astype(BF16)
        store_grad(p, h, grad.reshape(32, 48, WIDE))

    def pair_grad(p, h, left_0, right_0, left_1, right_1):
        cols = pl.ds(WIDE * h, WIDE)
        grad_0 = dot_nn(left_0[...], right_0[:, cols]).reshape(32, 24, WIDE)
        grad_1 = dot_nn(left_1[...], right_1[:, cols]).reshape(32, 24, WIDE)
        store_grad(p, h, jnp.concatenate([grad_0, grad_1], axis=1).astype(BF16))

    def in_grad(p, h):
        at = (p - 2) * 2 * D
        pair_grad(p, h, mlT, gp.at[:, pl.ds(at, D)], mlT, gp.at[:, pl.ds(at + D, D)])

    def inner_grad(t):
        cols = pl.ds(t * D, D)
        weight = wb_tile(t)
        tmp_a[...] = dot_nt(ml[0:256, :], weight)
        tmp_b[0:224, :] = dot_nt(ml[256:480, :], weight)
        total = zero8
        for ref, start, size in ((tmp_a, 0, 256), (tmp_b, 256, 224)):
            for at, count in blocks(0, size, 16):
                rows = pl.ds(start + at, count)
                rounded = (ref[at:at + count, :] * gp[rows, cols].astype(F32)).astype(BF16)
                gp[rows, cols] = rounded
                total = total + fold8(rounded.astype(F32))
        vec[8 + t:9 + t, :] = jnp.sum(total, axis=0, keepdims=True)

    def middle_grad(t):
        cols = pl.ds(t * D, D)
        n2[...] += dot_nt(gp[:, cols], wi[:, cols])

    def attn_norm_back():
        def block(i, sums):
            rows = pl.ds(pl.multiple_of(i * 32, 32), 32)
            upstream, unit = n2[rows, :], n1[rows, :]
            scaled = upstream * gain1
            hidden_grad = r1[rows, :] * (
                scaled
                - jnp.mean(scaled, axis=-1, keepdims=True)
                - unit * jnp.mean(scaled * unit, axis=-1, keepdims=True)
            )
            n1[rows, :] = hidden_grad
            rounded = hidden_grad.astype(BF16)
            ml[rows, :] = rounded
            return (
                sums[0] + fold8(upstream * unit), sums[1] + fold8(upstream), sums[2] + fold8(rounded.astype(F32)),
            )

        sums = lax.fori_loop(0, 15, block, (zero8, zero8, zero8))
        vec[2:3, :] = jnp.sum(sums[2], axis=0, keepdims=True)
        vec[3:4, :] = jnp.sum(sums[0], axis=0, keepdims=True)
        vec[4:5, :] = jnp.sum(sums[1], axis=0, keepdims=True)

    def context_grad():
        c_s[...] = dot_nt(ml[...], wo[...]).astype(BF16)

    def query_slot_back():
        q_rows, k_rows, v_rows = spread(q_s[0:32, :]), k_s[0:32, :], v_s[0:32, :]
        dc_rows = spread(c_s[0:32, :])
        soft = pq_s[...]
        dp = dot_nt(v_rows, dc_rows)
        soft_f = soft.astype(F32)
        ds = (soft_f * (dp - jnp.sum(soft_f * dp, axis=0, keepdims=True))).astype(BF16)
        v_s[0:32, :] = dot_nn(soft, dc_rows).astype(BF16)
        k_s[0:32, :] = dot_nn(ds, q_rows).astype(BF16)
        q_s[0:32, :] = (0.125 * gather_heads(dot_tn(ds, k_rows))).astype(BF16)

    def attend_back_pair(pair):
        lanes = pl.ds(pl.multiple_of(pair * 128, 128), 128)
        for slot in range(2):
            low_at = 12 * slot
            rows = pl.ds(32 + 208 * slot, WIN)
            keys, queries, values = k_s[rows, lanes], q_s[rows, lanes], v_s[rows, lanes]
            inside = ((key_at >= low_at) & (key_at < low_at + SLOT)).astype(BF16)
            upstream = c_s[rows, lanes] * inside
            keys_t = keys.T
            parts, dv, dk = [], 0.0, 0.0
            for h in range(2):
                p = p_s[slot, 2 * pair + h]
                dc = upstream * half[h]
                dp = dot_nt(values, dc)
                pf = p.astype(F32)
                ds = (pf * (dp - jnp.sum(pf * dp, axis=0, keepdims=True))).astype(BF16)
                dv += dot_nn(p, dc)
                dk += dot_nn(ds, queries * half[h])
                parts.append(dot_nn(keys_t, ds)[64 * h:64 * h + 64, :])
            dq = 0.125 * jnp.concatenate(parts, axis=0).T
            for ref, new in ((q_s, dq), (k_s, dk), (v_s, dv)):
                if slot == 0:
                    ref[32:240, lanes] = new[0:208].astype(BF16)
                    old = ref[240:272, lanes].astype(F32)
                    ref[240:272, lanes] = jnp.where(iota((32, 128), 0) < 12, new[208:240], old).astype(BF16)
                else:
                    old = ref[240:256, lanes].astype(F32)
                    ref[240:256, lanes] = jnp.where(iota((16, 128), 0) >= 12, new[0:16], old).astype(BF16)
                    ref[256:480, lanes] = new[16:240].astype(BF16)

    def attend_back(first, count):
        def step(i, carry):
            attend_back_pair(first + i)
            return carry

        lax.fori_loop(0, count, step, 0)

    def column_sum(ref):
        def step(i, total):
            return total + fold8(ref[pl.ds(pl.multiple_of(i * 32, 32), 32), :].astype(F32))

        return jnp.sum(lax.fori_loop(0, 15, step, zero8), axis=0, keepdims=True)

    def column_sums():
        vec[0:1, :] = column_sum(q_s)
        vec[1:2, :] = column_sum(v_s)

    def token_grad(grads, weight):
        n1[...] += dot_nt(grads[...], weight[...])

    out_qg = pltpu.make_async_copy(n1.at[0:32, :], qtg_h, out_sem.at[2])
    out_pg = pltpu.make_async_copy(n1.at[32:472, :], ptg_h, out_sem.at[3])

    def send_tokens():
        out_qg.start()
        out_pg.start()

    def vec_step(i):
        return remote(vec, vecr.at[i], v_send.at[i], v_recv.at[i], (partner, x_peer, y_peer)[i])

    def vec_part(whole, to):
        device = to * 8 + plane
        narrow = pltpu.roll(whole[0:8], D - 24 * device, 1)[:, 0:128]
        wide = pltpu.roll(whole[8:16], D - 96 * plane, 1)[:, 0:128]
        wide = jnp.sum(jnp.where(iota((8, 128), 0) == to, wide, 0.0), axis=0, keepdims=True)
        return jnp.concatenate([narrow, wide, jnp.zeros((7, 128), F32)], axis=0)

    def vec_z():
        return [
            remote(
                vecs.at[hop - 1], vecz.at[hop - 1], v_send.at[2 + hop], v_recv.at[2 + hop],
                lax.rem(zz + hop, 4) * 8 + plane,
            )
            for hop in range(1, 4)
        ]

    def vec_on(i):
        if i > 0:
            vec_step(i - 1).wait()
            vec[...] += vecr[i - 1]
        if i < 3:
            vec_step(i).start()
        else:
            whole = vec[...]
            for hop in range(1, 4):
                vecs[hop - 1] = vec_part(whole, lax.rem(zz + hop, 4))
            begin(vec_z())

    def vec_end():
        finish_steps(vec_z())
        part = vec_part(vec[...], zz) + vecz[0] + vecz[1] + vecz[2]
        small_o[0:9, :] = part[0:9]
        outs.append(pltpu.make_async_copy(small_o, small_h, out_sem.at[4]))
        outs[-1].start()

    pieces_of = {
        "wback": back_grad, "dinner": inner_grad, "win": in_grad, "dmid": middle_grad, "lnback": attn_norm_back,
        "dctx": context_grad, "qslot": query_slot_back, "attn": attend_back, "sums": column_sums,
        "wvo": lambda h: pair_grad(4, h, xT, v_s, cT, ml), "wqk": lambda h: pair_grad(5, h, xT, q_s, xT, k_s),
        "tq": lambda: token_grad(q_s, wq), "tk": lambda: token_grad(k_s, wk), "tv": lambda: token_grad(v_s, wv),
        "tout": send_tokens, "vec": vec_on, "vecend": vec_end,
        "c": start_c, "ec": end_c, "e1": end_1, "e2": end_2, "e3": end_3,
    }
    for name, *operands in ORDER:
        pieces_of[name](*operands)

    out_q.wait()
    out_p.wait()
    out_qg.wait()
    out_pg.wait()
    for out in outs:
        out.wait()


def hand_on_kernel(*refs):
    count = 10
    sources, small = refs[:count], refs[count]
    targets, vectors = refs[count + 1:2 * count + 1], refs[2 * count + 1:2 * count + 11]
    held, rest = refs[2 * count + 11:3 * count + 11], refs[3 * count + 11:]
    small_v, lines, in_sem, out_sem = rest[0], rest[1:11], rest[11], rest[12]
    whole = [(i, None) for i in range(count) if i != 3]
    pieces = [(3, pl.ds(at, size)) for at, size in blocks(0, 440, 112)] + whole
    into, out = [], []
    for at, (i, rows) in enumerate(pieces):
        source, kept, target = (ref if rows is None else ref.at[rows, :] for ref in (sources[i], held[i], targets[i]))
        into.append(pltpu.make_async_copy(source, kept, in_sem.at[at]))
        out.append(pltpu.make_async_copy(kept, target, out_sem.at[at]))
    last = pltpu.make_async_copy(small, small_v, in_sem.at[len(pieces)])
    last.start()
    for copy in into:
        copy.start()
    last.wait()
    for at, ref in enumerate(lines[:8]):
        ref[...] = small_v[at:at + 1, 0:24].reshape(24)
    lines[8][...] = small_v[8:9, 0:96].reshape(96)
    lines[9][...] = small_v[9:10, 0:1].reshape(1)
    for at, (line, vector) in enumerate(zip(lines, vectors)):
        out.append(pltpu.make_async_copy(line, vector, out_sem.at[len(pieces) + at]))
        out[-1].start()
    for first, second in zip(into, out):
        first.wait()
        second.start()
    for copy in out:
        copy.wait()


def on_device_small(*operands):
    (
        query_tokens, passage_tokens, query_lengths, passage_lengths, passage_valid, positives, negatives,
        teacher_margins, query_grad, passage_grad, weight_query, bias_query, weight_key, weight_value, bias_value,
        weight_out, bias_out, gain_attn, shift_attn, weight_in, bias_in, weight_back, bias_back, gain_ffn, shift_ffn,
    ) = operands
    hbm, far, smem = (pl.BlockSpec(memory_space=space) for space in (pl.ANY, pltpu.HBM, pltpu.SMEM))
    shape = jax.ShapeDtypeStruct
    slabs = (2, 2, 4, 2, 2, 48, D)
    large = (
        shape((32, D), BF16), shape((440, D), BF16), shape((32, D), F32), shape((440, D), F32), shape((24, D), F32),
        shape((24, D), F32), shape((24, D), F32), shape((24, D), F32), shape((24, FF), F32), shape((96, D), F32),
    )
    outs = pl.pallas_call(
        layer_kernel,
        out_shape=(
            *large, shape((16, 128), F32),
        ),
        in_specs=[
            hbm, hbm, far, smem, smem, far, far, far, hbm, hbm,
            *(hbm,) * 15,
        ],
        out_specs=(hbm,) * 11,
        scratch_shapes=[
            *(pltpu.VMEM((1,), kind) for kind in (jnp.int32, jnp.int32, jnp.int32, F32)),
            *(pltpu.VMEM((size,), BF16) for size in (D, D, D, D, D, FF, D, D, D)),
            pltpu.VMEM((D, D), BF16), pltpu.VMEM((D, D), BF16), pltpu.VMEM((D, D), BF16), pltpu.VMEM((D, D), BF16),
            pltpu.VMEM((D, FF), BF16), pltpu.VMEM((3, 2, 2, 4, 2, 2, 48, WIDE), BF16),
            pltpu.VMEM((440, D), BF16), pltpu.VMEM((ROWS, D), BF16), pltpu.VMEM((D, ROWS), BF16),
            pltpu.VMEM((ROWS, D), BF16), pltpu.VMEM((ROWS, D), BF16), pltpu.VMEM((ROWS, D), BF16),
            pltpu.VMEM((2, 12, WIN, WIN), BF16), pltpu.VMEM((32, 384), BF16),
            pltpu.VMEM((ROWS, D), BF16), pltpu.VMEM((D, ROWS), BF16),
            pltpu.VMEM((ROWS, D), F32), pltpu.VMEM((ROWS, D), F32), pltpu.VMEM((ROWS, 1), F32), pltpu.VMEM((ROWS, 1), F32),
            pltpu.VMEM((ROWS, D), BF16), pltpu.VMEM((D, ROWS), BF16),
            pltpu.VMEM((256, D), BF16), pltpu.VMEM((256, D), BF16), pltpu.VMEM((FF, ROWS), BF16),
            pltpu.VMEM((256, D), F32), pltpu.VMEM((256, D), F32),
            pltpu.VMEM((ROWS, FF), BF16),
            pltpu.VMEM((32, D), BF16), pltpu.VMEM((440, D), BF16), pltpu.VMEM((32, D), BF16), pltpu.VMEM((440, D), BF16),
            pltpu.VMEM((1024, 128), BF16), pltpu.VMEM((1024, 128), F32),
            pltpu.VMEM((16, D), F32), pltpu.VMEM((3, 16, D), F32), pltpu.VMEM((3, 16, 128), F32), pltpu.VMEM((3, 16, 128), F32),
            pltpu.VMEM((16, 128), F32), pltpu.VMEM((6, 3, 48, WIDE), F32),
            pltpu.VMEM((4, 3, 2, 4, 2, 2, 48, WIDE), BF16),
            pltpu.VMEM((2, 3, 4, 2, 2, 48, WIDE), BF16), pltpu.VMEM((6, 3, 4, 2, 48, WIDE), BF16),
            pltpu.VMEM((6, 3, 4, 48, WIDE), BF16), pltpu.VMEM((6, 3, 3, 48, WIDE), BF16),
            pltpu.VMEM((sum(way[0] == "z" for way in ROUTE), 3, 2, 2, 48, WIDE), BF16),
            pltpu.SemaphoreType.DMA((32,)), pltpu.SemaphoreType.DMA((5,)), pltpu.SemaphoreType.DMA((6, 3, 2)),
            pltpu.SemaphoreType.DMA((16,)), pltpu.SemaphoreType.DMA((16,)),
            pltpu.SemaphoreType.DMA((6, 3)), pltpu.SemaphoreType.DMA((6, 3)),
            pltpu.SemaphoreType.DMA((6, 3)), pltpu.SemaphoreType.DMA((6, 3)),
            pltpu.SemaphoreType.DMA((6, 3)), pltpu.SemaphoreType.DMA((6, 3)),
            pltpu.SemaphoreType.DMA((6, 3, 3)), pltpu.SemaphoreType.DMA((6, 3, 3)),
            pltpu.SemaphoreType.DMA((6,)), pltpu.SemaphoreType.DMA((6,)),
            pltpu.SemaphoreType.REGULAR((2, 3)),
        ],
        compiler_params=pltpu.CompilerParams(
            collective_id=0, has_side_effects=True, vmem_limit_bytes=64 * 1024 * 1024 - 65536,
        ),
        name="encoder_layer",
    )(
        query_tokens, passage_tokens, query_lengths, passage_lengths, passage_valid, positives, negatives,
        teacher_margins, query_grad, passage_grad, weight_query, bias_query, weight_key, weight_value, bias_value,
        weight_out, bias_out, gain_attn, shift_attn, weight_in, bias_in, weight_back.reshape(slabs), bias_back,
        gain_ffn, shift_ffn,
    )
    done = pl.pallas_call(
        hand_on_kernel,
        out_shape=large + (shape((24,), F32),) * 8 + (shape((96,), F32), shape((1,), F32)),
        in_specs=[hbm] * 11,
        out_specs=(hbm,) * 20,
        scratch_shapes=[pltpu.VMEM(out.shape, out.dtype) for out in large]
        + [pltpu.VMEM((16, 128), F32)] + [pltpu.VMEM((size,), F32) for size in (24,) * 8 + (96, 1)]
        + [pltpu.SemaphoreType.DMA((24,)), pltpu.SemaphoreType.DMA((24,))],
        name="hand_on",
    )(*outs)
    qout, pout, qtg, ptg, wqg, wkg, wvg, wog, wig, wbg, bqg, bvg, bog, gag, sag, bbg, gfg, sfg, big, loss = done
    return (
        qout, pout, loss, qtg, ptg, wqg, bqg, wkg, wvg, bvg, wog, bog, gag, sag, wig, big, wbg, bbg, gfg, sfg,
    )


def solution(mesh):
    return jax.shard_map(
        on_device_small if mesh.shape["dp"] == 32 else on_device,
        mesh=mesh,
        in_specs=(
            P("dp", None),
            P("dp", None),
            P("dp"),
            P("dp"),
            P("dp"),
            P("dp"),
            P("dp"),
            P("dp"),
            P("dp", None),
            P("dp", None),
            P(),
            P(),
            P(),
            P(),
            P(),
            P(),
            P(),
            P(),
            P(),
            P(),
            P(),
            P(),
            P(),
            P(),
            P(),
        ),
        out_specs=(
            P("dp", None),
            P("dp", None),
            P("dp"),
            P("dp", None),
            P("dp", None),
            P("dp", None),
            P("dp"),
            P("dp", None),
            P("dp", None),
            P("dp"),
            P("dp", None),
            P("dp"),
            P("dp"),
            P("dp"),
            P("dp", None),
            P("dp"),
            P("dp", None),
            P("dp"),
            P("dp"),
            P("dp"),
        ),
        check_vma=False,
    )
```

```python
import jax
import jax.numpy as jnp
from jax import lax
from jax.experimental import pallas as pl
from jax.experimental.pallas import tpu as pltpu
from jax.sharding import PartitionSpec as P

D = 768
HEADS = 12
HEAD_DIM = 64


ln_eps = 1e-12
score_scale = 0.0625
margin_weight = 0.5
root_half = 0.7071067811865476
inv_root_tau = 0.3989422804014327


def matmul(left, right):
    return jnp.dot(left, right, preferred_element_type=jnp.float32)


def left_across(left, right):
    return lax.dot_general(
        left, right, (((0,), (0,)), ((), ())), preferred_element_type=jnp.float32
    )


def right_across(left, right):
    return lax.dot_general(
        left, right, (((1,), (1,)), ((), ())), preferred_element_type=jnp.float32
    )


def normalize(hidden, gain, shift):
    centered = hidden - jnp.mean(hidden, axis=-1, keepdims=True)
    inv_std = lax.rsqrt(jnp.mean(centered * centered, axis=-1, keepdims=True) + ln_eps)
    unit_rows = centered * inv_std
    return (unit_rows * gain.astype(jnp.float32) + shift.astype(jnp.float32), unit_rows, inv_std)


def normalize_back(upstream, unit_rows, inv_std, gain):
    scaled = upstream * gain.astype(jnp.float32)
    hidden_grad = inv_std * (
        scaled
        - jnp.mean(scaled, axis=-1, keepdims=True)
        - unit_rows * jnp.mean(scaled * unit_rows, axis=-1, keepdims=True)
    )
    return (hidden_grad, jnp.sum(upstream * unit_rows, axis=0), jnp.sum(upstream, axis=0))


def gelu_exact(inputs):
    return 0.5 * inputs * (1.0 + lax.erf(inputs * root_half))


def gelu_slope(inputs):
    return 0.5 * (1.0 + lax.erf(inputs * root_half)) + inputs * inv_root_tau * jnp.exp(
        -0.5 * inputs * inputs
    )


def head_scores(query_heads, key_heads, lengths):
    slot_length = query_heads.shape[1]
    allowed = (lax.iota(jnp.int32, slot_length)[None, :] < lengths[:, None])[:, None, None, :]
    raw_scores = 0.125 * jnp.einsum(
        "bqhd,bkhd->bhqk", query_heads, key_heads, preferred_element_type=jnp.float32
    )
    return jnp.where(allowed, raw_scores, -1000000000.0)


def encode_forward(tokens, lengths, params):
    (
        weight_query,
        bias_query,
        weight_key,
        weight_value,
        bias_value,
        weight_out,
        bias_out,
        gain_attn,
        shift_attn,
        weight_in,
        bias_in,
        weight_back,
        bias_back,
        gain_ffn,
        shift_ffn,
    ) = params
    slot_count = lengths.shape[0]
    row_count = tokens.shape[0]
    split_heads = (slot_count, row_count // slot_count, HEADS, HEAD_DIM)
    queries = (matmul(tokens, weight_query) + bias_query.astype(jnp.float32)).astype(jnp.bfloat16)
    keys_all = matmul(tokens, weight_key).astype(jnp.bfloat16)
    values_all = (matmul(tokens, weight_value) + bias_value.astype(jnp.float32)).astype(
        jnp.bfloat16
    )
    scores = head_scores(queries.reshape(split_heads), keys_all.reshape(split_heads), lengths)
    peak_score = jnp.max(scores, axis=-1, keepdims=True)
    exp_scores = jnp.exp(scores - peak_score)
    row_total = jnp.sum(exp_scores, axis=-1, keepdims=True)
    soft_low = (exp_scores / row_total).astype(jnp.bfloat16)
    log_total = peak_score + jnp.log(row_total)
    context = jnp.einsum(
        "bhqk,bkhd->bqhd",
        soft_low,
        values_all.reshape(split_heads),
        preferred_element_type=jnp.float32,
    )
    context = context.reshape(row_count, D).astype(jnp.bfloat16)
    attn_sum = (
        tokens.astype(jnp.float32) + matmul(context, weight_out) + bias_out.astype(jnp.float32)
    )
    middle, unit_attn, inv_attn = normalize(attn_sum, gain_attn, shift_attn)
    middle_low = middle.astype(jnp.bfloat16)
    inner_act = matmul(middle_low, weight_in) + bias_in.astype(jnp.float32)
    gelu_low = gelu_exact(inner_act).astype(jnp.bfloat16)
    ffn_sum = middle + matmul(gelu_low, weight_back) + bias_back.astype(jnp.float32)
    output, unit_ffn, inv_ffn = normalize(ffn_sum, gain_ffn, shift_ffn)
    kept = (
        queries,
        keys_all,
        values_all,
        log_total,
        context,
        unit_attn,
        inv_attn,
        middle_low,
        inner_act,
        gelu_low,
        unit_ffn,
        inv_ffn,
    )
    return (output.astype(jnp.bfloat16), kept)


def ffn_backward(upstream, kept, params):
    (
        queries,
        keys_all,
        values_all,
        log_total,
        context,
        unit_attn,
        inv_attn,
        middle_low,
        inner_act,
        gelu_low,
        unit_ffn,
        inv_ffn,
    ) = kept
    weight_in, weight_back, gain_ffn = (params[9], params[11], params[13])
    ffn_grad, gain_grad, shift_grad = normalize_back(upstream, unit_ffn, inv_ffn, gain_ffn)
    branch_low = ffn_grad.astype(jnp.bfloat16)
    back_weight_grad = left_across(gelu_low, branch_low)
    back_bias_grad = jnp.sum(branch_low, axis=0, dtype=jnp.float32)
    inner_low = (right_across(branch_low, weight_back) * gelu_slope(inner_act)).astype(jnp.bfloat16)
    in_weight_grad = left_across(middle_low, inner_low)
    in_bias_grad = jnp.sum(inner_low, axis=0, dtype=jnp.float32)
    middle_grad = ffn_grad + right_across(inner_low, weight_in)
    return (
        middle_grad,
        (in_weight_grad, in_bias_grad, back_weight_grad, back_bias_grad, gain_grad, shift_grad),
    )


def attention_backward(middle_grad, tokens, lengths, kept, params):
    (
        queries,
        keys_all,
        values_all,
        log_total,
        context,
        unit_attn,
        inv_attn,
        middle_low,
        inner_act,
        gelu_low,
        unit_ffn,
        inv_ffn,
    ) = kept
    weight_query, weight_key, weight_value, weight_out, gain_attn = (
        params[0],
        params[2],
        params[3],
        params[5],
        params[7],
    )
    slot_count = lengths.shape[0]
    row_count = tokens.shape[0]
    split_heads = (slot_count, row_count // slot_count, HEADS, HEAD_DIM)
    attn_grad, gain_grad, shift_grad = normalize_back(middle_grad, unit_attn, inv_attn, gain_attn)
    attn_low = attn_grad.astype(jnp.bfloat16)
    out_weight_grad = left_across(context, attn_low)
    out_bias_grad = jnp.sum(attn_low, axis=0, dtype=jnp.float32)
    context_grad = right_across(attn_low, weight_out).astype(jnp.bfloat16).reshape(split_heads)
    query_heads = queries.reshape(split_heads)
    key_heads = keys_all.reshape(split_heads)
    value_heads = values_all.reshape(split_heads)
    soft_full = jnp.exp(head_scores(query_heads, key_heads, lengths) - log_total)
    soft_grad = jnp.einsum(
        "bqhd,bkhd->bhqk", context_grad, value_heads, preferred_element_type=jnp.float32
    )
    value_grad = jnp.einsum(
        "bhqk,bqhd->bkhd",
        soft_full.astype(jnp.bfloat16),
        context_grad,
        preferred_element_type=jnp.float32,
    )
    value_grad = value_grad.reshape(row_count, D).astype(jnp.bfloat16)
    score_low = (
        soft_full * (soft_grad - jnp.sum(soft_full * soft_grad, axis=-1, keepdims=True))
    ).astype(jnp.bfloat16)
    query_grad_low = 0.125 * jnp.einsum(
        "bhqk,bkhd->bqhd", score_low, key_heads, preferred_element_type=jnp.float32
    )
    query_grad_low = query_grad_low.reshape(row_count, D).astype(jnp.bfloat16)
    key_grad_low = 0.125 * jnp.einsum(
        "bhqk,bqhd->bkhd", score_low, query_heads, preferred_element_type=jnp.float32
    )
    key_grad_low = key_grad_low.reshape(row_count, D).astype(jnp.bfloat16)
    token_grad = (
        attn_grad
        + right_across(query_grad_low, weight_query)
        + right_across(key_grad_low, weight_key)
        + right_across(value_grad, weight_value)
    )
    grads = (
        left_across(tokens, query_grad_low),
        jnp.sum(query_grad_low, axis=0, dtype=jnp.float32),
        left_across(tokens, key_grad_low),
        left_across(tokens, value_grad),
        jnp.sum(value_grad, axis=0, dtype=jnp.float32),
        out_weight_grad,
        out_bias_grad,
        gain_grad,
        shift_grad,
    )
    return (token_grad, grads)


def on_device(
    query_tokens,
    passage_tokens,
    query_lengths,
    passage_lengths,
    passage_valid,
    positives,
    negatives,
    teacher_margins,
    query_grad,
    passage_grad,
    weight_query,
    bias_query,
    weight_key,
    weight_value,
    bias_value,
    weight_out,
    bias_out,
    gain_attn,
    shift_attn,
    weight_in,
    bias_in,
    weight_back,
    bias_back,
    gain_ffn,
    shift_ffn,
):
    params = (
        weight_query,
        bias_query,
        weight_key,
        weight_value,
        bias_value,
        weight_out,
        bias_out,
        gain_attn,
        shift_attn,
        weight_in,
        bias_in,
        weight_back,
        bias_back,
        gain_ffn,
        shift_ffn,
    )
    query_out, query_kept = encode_forward(query_tokens, query_lengths, params)
    passage_out, passage_kept = encode_forward(passage_tokens, passage_lengths, params)
    query_slots = query_lengths.shape[0]
    passage_slots = passage_lengths.shape[0]
    cls_query = query_out.reshape(query_slots, -1, D)[:, 0]
    cls_passage = passage_out.reshape(passage_slots, -1, D)[:, 0]
    valid_low = passage_valid.astype(jnp.bfloat16)

    def score_piece(cls_piece, valid_piece):
        scores = score_scale * right_across(cls_query, cls_piece)
        position = lax.iota(jnp.int32, cls_piece.shape[0])
        is_positive = position[None, :] == positives[:, None]
        is_negative = position[None, :] == negatives[:, None]
        allowed = (valid_piece[None, :] > 0.5) | is_positive
        return (scores, allowed, is_positive, is_negative)

    peak_score = jnp.full((query_slots,), -1e30, jnp.float32)
    scores, allowed, is_positive, is_negative = score_piece(
        lax.all_gather(cls_passage, "dp", axis=0, tiled=True),
        lax.all_gather(valid_low, "dp", axis=0, tiled=True),
    )
    masked = jnp.where(allowed, scores, -1e30)
    new_peak = jnp.maximum(peak_score, jnp.max(masked, axis=1))
    row_total = jnp.sum(jnp.where(allowed, jnp.exp(masked - new_peak[:, None]), 0.0), axis=1)
    positive_score = jnp.sum(jnp.where(is_positive, scores, 0.0), axis=1)
    negative_score = jnp.sum(jnp.where(is_negative, scores, 0.0), axis=1)
    peak_score, row_total, positive_score, negative_score = (
        new_peak,
        row_total,
        positive_score,
        negative_score,
    )
    all_cls, all_valid = (
        lax.all_gather(cls_passage, "dp", axis=0, tiled=True),
        lax.all_gather(valid_low, "dp", axis=0, tiled=True),
    )
    log_total = peak_score + jnp.log(row_total)
    shortfall = positive_score - negative_score - teacher_margins
    query_loss = log_total - positive_score + margin_weight * shortfall * shortfall
    scores, allowed, is_positive, is_negative = score_piece(all_cls, all_valid)
    soft_scores = jnp.where(allowed, jnp.exp(scores - log_total[:, None]), 0.0)
    positive_hit = is_positive.astype(jnp.float32)
    negative_hit = is_negative.astype(jnp.float32)
    score_grad = (
        soft_scores
        - positive_hit
        + 2.0 * margin_weight * shortfall[:, None] * (positive_hit - negative_hit)
    ).astype(jnp.bfloat16)
    cls_query_grad = score_scale * matmul(score_grad, all_cls)
    cls_passage_grad = lax.psum_scatter(
        score_scale * left_across(score_grad, cls_query), "dp", scatter_dimension=0, tiled=True
    )
    query_upstream = (
        query_grad.astype(jnp.float32)
        .reshape(query_slots, -1, D)
        .at[:, 0]
        .add(cls_query_grad)
        .reshape(-1, D)
    )
    passage_upstream = (
        passage_grad.astype(jnp.float32)
        .reshape(passage_slots, -1, D)
        .at[:, 0]
        .add(cls_passage_grad)
        .reshape(-1, D)
    )
    query_middle_grad, query_ffn = ffn_backward(query_upstream, query_kept, params)
    passage_middle_grad, passage_ffn = ffn_backward(passage_upstream, passage_kept, params)
    (
        in_weight_grad,
        in_bias_grad,
        back_weight_grad,
        back_bias_grad,
        ffn_gain_grad,
        ffn_shift_grad,
    ) = tuple((first + second for first, second in zip(query_ffn, passage_ffn)))
    query_tokens_grad, query_attn = attention_backward(
        query_middle_grad, query_tokens, query_lengths, query_kept, params
    )
    passage_tokens_grad, passage_attn = attention_backward(
        passage_middle_grad, passage_tokens, passage_lengths, passage_kept, params
    )
    (
        query_weight_grad,
        query_bias_grad,
        key_weight_grad,
        value_weight_grad,
        value_bias_grad,
        out_weight_grad,
        out_bias_grad,
        attn_gain_grad,
        attn_shift_grad,
    ) = tuple((first + second for first, second in zip(query_attn, passage_attn)))
    (
        query_weight_grad,
        query_bias_grad,
        key_weight_grad,
        value_weight_grad,
        value_bias_grad,
        out_weight_grad,
        out_bias_grad,
        attn_gain_grad,
        attn_shift_grad,
        in_weight_grad,
        in_bias_grad,
        back_weight_grad,
        back_bias_grad,
        ffn_gain_grad,
        ffn_shift_grad,
    ) = (
        lax.psum_scatter(query_weight_grad, "dp", scatter_dimension=0, tiled=True),
        lax.psum_scatter(query_bias_grad, "dp", scatter_dimension=0, tiled=True),
        lax.psum_scatter(key_weight_grad, "dp", scatter_dimension=0, tiled=True),
        lax.psum_scatter(value_weight_grad, "dp", scatter_dimension=0, tiled=True),
        lax.psum_scatter(value_bias_grad, "dp", scatter_dimension=0, tiled=True),
        lax.psum_scatter(out_weight_grad, "dp", scatter_dimension=0, tiled=True),
        lax.psum_scatter(out_bias_grad, "dp", scatter_dimension=0, tiled=True),
        lax.psum_scatter(attn_gain_grad, "dp", scatter_dimension=0, tiled=True),
        lax.psum_scatter(attn_shift_grad, "dp", scatter_dimension=0, tiled=True),
        lax.psum_scatter(in_weight_grad, "dp", scatter_dimension=0, tiled=True),
        lax.psum_scatter(in_bias_grad, "dp", scatter_dimension=0, tiled=True),
        lax.psum_scatter(back_weight_grad, "dp", scatter_dimension=0, tiled=True),
        lax.psum_scatter(back_bias_grad, "dp", scatter_dimension=0, tiled=True),
        lax.psum_scatter(ffn_gain_grad, "dp", scatter_dimension=0, tiled=True),
        lax.psum_scatter(ffn_shift_grad, "dp", scatter_dimension=0, tiled=True),
    )
    return (
        query_out,
        passage_out,
        query_loss,
        query_tokens_grad,
        passage_tokens_grad,
        query_weight_grad,
        query_bias_grad,
        key_weight_grad,
        value_weight_grad,
        value_bias_grad,
        out_weight_grad,
        out_bias_grad,
        attn_gain_grad,
        attn_shift_grad,
        in_weight_grad,
        in_bias_grad,
        back_weight_grad,
        back_bias_grad,
        ffn_gain_grad,
        ffn_shift_grad,
    )


F32 = jnp.float32
BF16 = jnp.bfloat16
MESH = pl.DeviceIdType.MESH
FF = 3072
ROWS = 480
WIN = 240
SLOT = 220
NEG = -1000000000.0


def dot_nn(left, right):
    return jnp.dot(left, right, preferred_element_type=F32)


def dot_nt(left, right):
    return lax.dot_general(left, right, (((1,), (1,)), ((), ())), preferred_element_type=F32)


def dot_tn(left, right):
    return lax.dot_general(left, right, (((0,), (0,)), ((), ())), preferred_element_type=F32)


def row_of(ref, start=0, size=D):
    return ref[pl.ds(start, size)].astype(F32).reshape(1, size)


def item(ref, at):
    return ref[...].reshape(1, 2)[:, at:at + 1]


def blocks(start, stop, size):
    return [(at, min(size, stop - at)) for at in range(start, stop, size)]


def iota(shape, dim):
    return lax.broadcasted_iota(jnp.int32, shape, dim)


def fold8(block):
    return jnp.sum(block.reshape(-1, 8, block.shape[-1]), axis=0)


WIDE = 256
ROUTE = (
    "xyz", "zyx", "zxy", "yxz", "xyz", "zyx", "yxz", "xyz", "yxz", "xyz", "yxz", "xyz", "yxz", "xyz", "yxz", "xyz",
    "yxz", "xyz",
)
ORDER = (
    ("wback", 0, 0), ("c", 0, 0), ("wback", 0, 1), ("c", 0, 1), ("wback", 0, 2), ("c", 0, 2), ("wback", 1, 0),
    ("c", 1, 0), ("wback", 1, 1), ("ec", 0, 0), ("c", 1, 1), ("wback", 1, 2), ("ec", 0, 1), ("c", 1, 2),
    ("dinner", 0), ("ec", 1, 0), ("dinner", 1), ("win", 2, 0), ("c", 2, 0), ("ec", 1, 2), ("win", 2, 1),
    ("ec", 0, 2), ("ec", 1, 1), ("c", 2, 1), ("win", 2, 2), ("ec", 2, 0), ("c", 2, 2), ("dinner", 2), ("dinner", 3),
    ("ec", 2, 1), ("win", 3, 0), ("c", 3, 0), ("ec", 2, 2), ("win", 3, 1), ("c", 3, 1), ("win", 3, 2), ("e1", 0, 0),
    ("c", 3, 2), ("dmid", 0), ("ec", 3, 0), ("e1", 1, 0), ("dmid", 1), ("dmid", 2), ("dmid", 3), ("lnback",),
    ("dctx",), ("e1", 2, 0), ("qslot",), ("attn", 0, 1), ("e1", 2, 1), ("ec", 3, 1), ("attn", 1, 1), ("e1", 2, 2),
    ("attn", 2, 4), ("e2", 2, 1), ("e1", 1, 1), ("ec", 3, 2), ("sums",), ("wvo", 0), ("c", 4, 0), ("wvo", 1),
    ("c", 4, 1), ("wvo", 2), ("e1", 3, 0), ("e1", 3, 1), ("c", 4, 2), ("wqk", 0), ("ec", 4, 0), ("e2", 1, 1),
    ("ec", 4, 2), ("e2", 0, 0), ("e2", 2, 2), ("c", 5, 0), ("ec", 4, 1), ("wqk", 1), ("e1", 3, 2), ("vec", 0),
    ("e2", 2, 0), ("c", 5, 1), ("e2", 3, 0), ("wqk", 2), ("c", 5, 2), ("e1", 0, 1), ("ec", 5, 2), ("e1", 4, 1),
    ("e3", 1, 1), ("e1", 4, 0), ("e2", 3, 1), ("e1", 4, 2), ("ec", 5, 1), ("e1", 1, 2), ("vec", 1), ("e3", 0, 0),
    ("e2", 1, 0), ("e2", 3, 2), ("ec", 5, 0), ("e1", 5, 2), ("e2", 4, 0), ("tq",), ("e2", 4, 1), ("e1", 5, 1),
    ("e2", 4, 2), ("e2", 0, 1), ("vec", 2), ("e3", 2, 1), ("tk",), ("e1", 5, 0), ("e2", 5, 2), ("e3", 3, 0),
    ("e3", 3, 2), ("e1", 0, 2), ("vec", 3), ("e3", 1, 0), ("e2", 5, 1), ("e3", 2, 2), ("e2", 5, 0), ("e2", 0, 2),
    ("e2", 1, 2), ("e3", 4, 1), ("e3", 0, 2), ("e3", 5, 2), ("tv",), ("tout",), ("e3", 0, 1), ("vecend",),
    ("e3", 4, 0), ("e3", 2, 0), ("e3", 1, 2), ("e3", 3, 1), ("e3", 5, 1), ("e3", 4, 2), ("e3", 5, 0),
)


def layer_kernel(
    qtok, ptok, qlen, plen_h, pvalid_h, pos, neg, margin, qgrad, pgrad,
    wq_h, bq_h, wk_h, wv_h, bv_h, wo_h, bo_h, ga_h, sa_h, wi_h, bi_h, wb_h, bb_h, gf_h, sf_h,
    qout_h, pout_h, qtg_h, ptg_h, wqg, wkg, wvg, wog, wig, wbg, small_h,
    plen, pvalid, bq, bv, bo, ga, sa, bi, bb, gf, sf, wq, wk, wv, wo, wi, wb, pstage, x_s, xT, q_s, k_s, v_s, p_s, pq_s, c_s, cT, n1, n2, r1, r2,
    ml, mlT, act_a, act_b, actT, tmp_a, tmp_b, gp, qg_s, pg_s, qo_s, po_s, ex, ex_f, vec, vecr, vecs, vecz, small_o, parts,
    g_s, rc, ra, rb, rz, rw,
    load_sem, out_sem, part_sem, ex_send, ex_recv, c_send, c_recv, a_send, a_recv, b_send, b_recv,
    z_send, z_recv, v_send, v_recv, credit,
):
    me = lax.axis_index("dp")
    core = lax.rem(me, 2)
    xx = lax.rem(lax.div(me, 2), 2)
    yy = lax.rem(lax.div(me, 4), 2)
    zz = lax.div(me, 8)
    chip = lax.div(me, 2)
    partner = me + 1 - 2 * core
    x_peer = me + 2 - 4 * xx
    y_peer = me + 4 - 8 * yy
    plane = lax.rem(me, 8)

    loads = {}

    def load(name, source, target):
        loads[name] = pltpu.make_async_copy(source, target, load_sem.at[len(loads)])
        loads[name].start()

    load("ptok", ptok, pstage)
    load("qtok", qtok, qo_s)
    load("wq", wq_h, wq)
    vectors = (
        (plen_h, plen), (pvalid_h, pvalid), (bq_h, bq), (bv_h, bv), (bo_h, bo), (ga_h, ga), (sa_h, sa), (bi_h, bi),
        (bb_h, bb), (gf_h, gf), (sf_h, sf),
    )
    for at, (source, target) in enumerate(vectors):
        load("vec" + str(at), source, target)
    load("wk", wk_h, wk)
    load("wv", wv_h, wv)

    barrier = pltpu.get_barrier_semaphore()
    for hop in range(1, 16):
        other = 2 * lax.rem(chip + hop, 16) + core
        pl.semaphore_signal(barrier, inc=1, device_id=(other,), device_id_type=MESH)
    pl.semaphore_signal(barrier, inc=1, device_id=(partner,), device_id_type=MESH)

    loads["ptok"].wait()
    loads["qtok"].wait()
    x_s[0:32, :] = qo_s[...]

    def copy_tokens(i, carry):
        x_s[pl.ds(pl.multiple_of(32 + i * 16, 16), 16), :] = pstage[pl.ds(pl.multiple_of(i * 16, 16), 16), :]
        return carry

    lax.fori_loop(0, 27, copy_tokens, 0)
    x_s[464:480, :] = jnp.concatenate(
        [pstage[432:440, :].astype(F32), jnp.zeros((8, D), F32)], axis=0
    ).astype(BF16)

    loads["wq"].wait()
    for at in range(len(vectors)):
        loads["vec" + str(at)].wait()
    load("wo", wo_h, wo)
    load("wi", wi_h, wi)

    def project_queries(start, stop):
        rows = pl.ds(start, stop - start)
        q_s[rows, :] = ((dot_nn(x_s[rows, :], wq[...]) + row_of(bq)).astype(BF16) * 0.125).astype(BF16)

    project_queries(0, 256)
    loads["wk"].wait()
    k_s[...] = dot_nn(x_s[...], wk[...]).astype(BF16)
    loads["wv"].wait()
    for h in range(3):
        load("wb" + str(h), wb_h.at[:, :, :, :, :, :, pl.ds(WIDE * h, WIDE)], wb.at[h])
    load("qg", qgrad, qg_s)
    load("pg", pgrad, pg_s)
    v_s[...] = (dot_nn(x_s[...], wv[...]) + row_of(bv)).astype(BF16)

    head_of = iota((12, 1, D), 2) // 64
    head_mask = (head_of == iota((12, 1, D), 0)).astype(F32)

    def spread(rows):
        return (rows.astype(F32)[None] * head_mask).astype(BF16).reshape(384, D)

    def gather_heads(stacked):
        return jnp.sum(stacked.reshape(12, 32, D) * head_mask, axis=0)

    raw = dot_nt(k_s[0:32, :], spread(q_s[0:32, :]))
    raw = jnp.where(iota((32, 384), 0) < qlen[0], raw, NEG)
    soft = jnp.exp(raw - jnp.max(raw, axis=0, keepdims=True))
    soft = (soft * (1.0 / jnp.sum(soft, axis=0, keepdims=True))).astype(BF16)
    pq_s[...] = soft
    c_s[0:32, :] = gather_heads(dot_tn(soft, v_s[0:32, :])).astype(BF16)

    by_head = (q_s[240:256, :].astype(F32)[None] * head_mask).astype(BF16).reshape(192, D)
    raw = dot_nt(by_head, k_s[240:480, :])
    key_lane = iota((1, WIN), 1)
    raw = jnp.where((key_lane >= 12) & (key_lane < 12 + item(plen, 1)), raw, NEG)
    soft = jnp.exp(raw - jnp.max(raw, axis=1, keepdims=True))
    soft = (soft * (1.0 / jnp.sum(soft, axis=1, keepdims=True))).astype(BF16)
    block = jnp.sum(dot_nn(soft, v_s[240:480, :]).reshape(12, 16, D) * head_mask, axis=0)

    lane = iota((1, 128), 1)
    half = ((lane < 64).astype(BF16), (lane >= 64).astype(BF16))
    key_at = iota((WIN, 1), 0)

    def attend(pair, slot):
        lanes = pl.ds(pl.multiple_of(pair * 128, 128), 128)
        low_at = 12 * slot
        first_row = 32 + 208 * slot
        rows = pl.ds(first_row, WIN)
        keys, queries = k_s[rows, lanes], q_s[rows, lanes]
        values_t = v_s[rows, lanes].T
        allowed = (key_at >= low_at) & (key_at < low_at + item(plen, slot))
        parts = []
        for h in range(2):
            scores = jnp.where(allowed, dot_nt(keys, queries * half[h]), NEG)
            e = jnp.exp(scores - jnp.max(scores, axis=0, keepdims=True))
            p = (e * (1.0 / jnp.sum(e, axis=0, keepdims=True))).astype(BF16)
            p_s[slot, 2 * pair + h] = p
            parts.append(dot_nn(values_t, p)[64 * h:64 * h + 64, :])
        context = jnp.concatenate(parts, axis=0).T
        if slot == 0:
            c_s[rows, lanes] = context.astype(BF16)
            return
        old = c_s[240:256, lanes].astype(F32)
        c_s[240:256, lanes] = jnp.where(iota((16, 128), 0) >= 12, context[0:16], old).astype(BF16)
        c_s[256:480, lanes] = context[16:240].astype(BF16)

    def attend_slot(slot):
        def two_pairs(i, carry):
            attend(2 * i, slot)
            attend(2 * i + 1, slot)
            return carry

        lax.fori_loop(0, 3, two_pairs, 0)

    attend_slot(0)
    old = c_s[240:256, :].astype(F32)
    c_s[240:256, :] = jnp.where(iota((16, 1), 0) >= 12, block, old).astype(BF16)

    loads["wo"].wait()
    gain1, shift1, bias1 = row_of(ga), row_of(sa), row_of(bo)
    gain2, shift2, bias2 = row_of(gf), row_of(sf), row_of(bb)

    def wb_tile(t):
        return jnp.concatenate([wb[h, t // 2, t % 2].reshape(D, WIDE) for h in range(3)], axis=1)

    def normalized(hidden):
        centered = hidden - jnp.mean(hidden, axis=-1, keepdims=True)
        inv = lax.rsqrt(jnp.mean(centered * centered, axis=-1, keepdims=True) + ln_eps)
        return centered * inv, inv

    def forward_rows(start, stop):
        size = stop - start
        every, own = pl.ds(start, size), pl.ds(0, size)
        tmp_a[own, :] = dot_nn(c_s[every, :], wo[...])
        for at, count in blocks(0, size, 32):
            rows, here = pl.ds(start + at, count), pl.ds(at, count)
            unit, inv = normalized(tmp_a[here, :] + x_s[rows, :].astype(F32) + bias1)
            n1[rows, :] = unit
            r1[rows, :] = inv
            ml[rows, :] = (unit * gain1 + shift1).astype(BF16)
        if start == 0:
            loads["wi"].wait()
            for h in range(3):
                loads["wb" + str(h)].wait()
        inner, acts = (tmp_a, tmp_b), (act_a, act_b)
        tmp_a[own, :] = dot_nn(ml[every, :], wi[:, 0:D])
        mlT[:, every] = ml[every, :].T
        xT[:, every] = x_s[every, :].T
        cT[:, every] = c_s[every, :].T

        def finish(t):
            act = acts[t % 2][own, :]
            if t == 0:
                n2[every, :] = dot_nn(act, wb_tile(t))
            else:
                n2[every, :] += dot_nn(act, wb_tile(t))
            actT[t * D:t * D + D, every] = act.T

        for t in range(4):
            if t < 3:
                inner[(t + 1) % 2][own, :] = dot_nn(ml[every, :], wi[:, t * D + D:t * D + 2 * D])
            bias_t = row_of(bi, t * D)
            for at, count in blocks(0, size, 16):
                here = pl.ds(at, count)
                u = inner[t % 2][here, :] + bias_t
                cdf = 0.5 * (1.0 + lax.erf(u * root_half))
                acts[t % 2][here, :] = (u * cdf).astype(BF16)
                gp[start + at:start + at + count, t * D:t * D + D] = (
                    cdf + u * inv_root_tau * jnp.exp(-0.5 * u * u)
                ).astype(BF16)
            if t > 0:
                finish(t - 1)
        finish(3)
        for at, count in blocks(start, stop, 32):
            rows = pl.ds(at, count)
            unit, inv = normalized(n2[rows, :] + (n1[rows, :] * gain1 + shift1) + bias2)
            n2[rows, :] = unit
            r2[rows, :] = inv
            out = (unit * gain2 + shift2).astype(BF16)
            if at == 0:
                qo_s[...] = out
            else:
                po_s[at - 32:min(at, 440), :] = out[0:min(count, 472 - at)]

    forward_rows(0, 256)

    slot_me = core * 16 + chip
    base = pl.multiple_of(slot_me * 32, 32)
    first_rows = (
        qo_s[0:16, :].astype(F32)[0:1],
        po_s[0:16, :].astype(F32)[0:1],
        po_s[208:224, :].astype(F32)[12:13],
    )
    lane_row = iota((1, 128), 1)
    meta = jnp.zeros((1, 128), F32)
    margin_0 = jnp.zeros((1, 128), F32) + margin[0]
    margin_1 = margin_0.astype(BF16).astype(F32)
    margin_2 = (margin_0 - margin_1).astype(BF16).astype(F32)
    for at, value in enumerate((
        item(pvalid, 0).astype(F32), item(pvalid, 1).astype(F32), pos[0].astype(F32), neg[0].astype(F32),
        margin_1, margin_2, margin_0 - margin_1 - margin_2,
    )):
        meta = jnp.where(lane_row == at, value, meta)
    pieces = [row[:, 128 * i:128 * i + 128] for row in first_rows for i in range(6)]
    ex[pl.ds(base, 32), :] = jnp.concatenate(pieces + [meta, jnp.zeros((13, 128), F32)], axis=0).astype(BF16)

    pl.semaphore_wait(barrier, 16)
    sends = []
    for hop in range(1, 16):
        block = ex.at[pl.ds(base, 32), :]
        sends.append(pltpu.make_async_remote_copy(
            src_ref=block, dst_ref=block, send_sem=ex_send.at[hop], recv_sem=ex_recv.at[hop],
            device_id=(2 * lax.rem(chip + hop, 16) + core,), device_id_type=MESH,
        ))
        sends[-1].start()

    project_queries(256, 480)
    attend_slot(1)
    forward_rows(256, 480)
    out_q = pltpu.make_async_copy(qo_s, qout_h, out_sem.at[0])
    out_p = pltpu.make_async_copy(po_s, pout_h, out_sem.at[1])
    out_q.start()
    out_p.start()
    loads["qg"].wait()
    loads["pg"].wait()

    def ffn_norm_back(r0, upstream, sums):
        rows = pl.ds(r0, upstream.shape[0])
        unit = n2[rows, :]
        scaled = upstream * gain2
        hidden_grad = r2[rows, :] * (
            scaled
            - jnp.mean(scaled, axis=-1, keepdims=True)
            - unit * jnp.mean(scaled * unit, axis=-1, keepdims=True)
        )
        n2[rows, :] = hidden_grad
        rounded = hidden_grad.astype(BF16)
        ml[rows, :] = rounded
        return (
            sums[0] + fold8(upstream * unit), sums[1] + fold8(upstream), sums[2] + fold8(rounded.astype(F32)),
        )

    zero8 = jnp.zeros((8, D), F32)
    sums = (zero8, zero8, zero8)

    def middle_block(i, sums):
        upstream = pg_s[pl.ds(pl.multiple_of(i * 32, 32), 32), :].astype(F32)
        return ffn_norm_back(pl.multiple_of(32 + i * 32, 32), upstream, sums)

    sums = lax.fori_loop(1, 6, middle_block, sums)
    sums = lax.fori_loop(7, 13, middle_block, sums)
    last = jnp.concatenate([pg_s[416:440, :].astype(F32), jnp.zeros((8, D), F32)], axis=0)
    sums = ffn_norm_back(448, last, sums)

    for send in sends:
        send.wait()
    same_core = ex.at[pl.ds(pl.multiple_of(core * 512, 512), 512), :]
    across = pltpu.make_async_remote_copy(
        src_ref=same_core, dst_ref=same_core, send_sem=ex_send.at[0], recv_sem=ex_recv.at[0],
        device_id=(partner,), device_id_type=MESH,
    )
    across.start()
    across.wait()

    ex_f[...] = ex[...].astype(F32)

    def first(r):
        return ex_f[pl.ds(r, 32, stride=32), :]

    cls_q = jnp.concatenate([first(i) for i in range(6)], axis=1)
    cls_0 = jnp.concatenate([first(6 + i) for i in range(6)], axis=1).astype(BF16)
    cls_1 = jnp.concatenate([first(12 + i) for i in range(6)], axis=1).astype(BF16)
    metas = first(18)
    metas_t = metas.T
    s0 = score_scale * dot_nt(cls_q.astype(BF16), cls_0)
    s1 = score_scale * dot_nt(cls_q.astype(BF16), cls_1)
    col = iota((1, 32), 1)
    passage = (4 * lax.rem(col, 16) + 2 * lax.div(col, 16)).astype(F32)
    at_pos, at_neg, wanted = metas[:, 2:3], metas[:, 3:4], metas[:, 4:5] + metas[:, 5:6] + metas[:, 6:7]
    pos0, pos1 = at_pos == passage, at_pos == passage + 1.0
    neg0, neg1 = at_neg == passage, at_neg == passage + 1.0
    m0 = jnp.where((metas_t[0:1, :] > 0.5) | pos0, s0, -1e30)
    m1 = jnp.where((metas_t[1:2, :] > 0.5) | pos1, s1, -1e30)
    peak = jnp.maximum(jnp.max(m0, axis=1, keepdims=True), jnp.max(m1, axis=1, keepdims=True))
    total = jnp.sum(jnp.exp(m0 - peak), axis=1, keepdims=True) + jnp.sum(jnp.exp(m1 - peak), axis=1, keepdims=True)
    lse = peak + jnp.log(total)

    def picked(where0, where1):
        return jnp.sum(jnp.where(where0, s0, 0.0), axis=1, keepdims=True) + jnp.sum(
            jnp.where(where1, s1, 0.0), axis=1, keepdims=True
        )

    at_positive = picked(pos0, pos1)
    miss = at_positive - picked(neg0, neg1) - wanted
    losses = lse - at_positive + margin_weight * miss * miss
    pos0, pos1, neg0, neg1 = (hit.astype(F32) for hit in (pos0, pos1, neg0, neg1))
    ds0 = (jnp.exp(m0 - lse) - pos0 + 2.0 * margin_weight * miss * (pos0 - neg0)).astype(BF16)
    ds1 = (jnp.exp(m1 - lse) - pos1 + 2.0 * margin_weight * miss * (pos1 - neg1)).astype(BF16)
    mine = iota((32, 1), 0) == slot_me
    mine_col = iota((1, 32), 1) == slot_me
    small_o[9:10, :] = jnp.sum(jnp.where(mine, losses, 0.0), axis=0, keepdims=True) + jnp.zeros((1, 128), F32)
    dq_all = score_scale * (dot_nn(ds0, cls_0) + dot_nn(ds1, cls_1))
    d_query = jnp.sum(jnp.where(mine, dq_all, 0.0), axis=0, keepdims=True)

    def passage_grad_row(ds):
        column = jnp.sum(jnp.where(mine_col, ds.astype(F32), 0.0), axis=1, keepdims=True)
        return score_scale * jnp.sum(column * cls_q, axis=0, keepdims=True)

    d_first = (d_query, passage_grad_row(ds0), passage_grad_row(ds1))

    row32 = iota((32, 1), 0)
    for r0, at, source, add in (
        (0, 0, qg_s[...], d_first[0]), (32, 0, pg_s[0:32, :], d_first[1]), (224, 28, pg_s[192:224, :], d_first[2]),
    ):
        upstream = source.astype(F32) + jnp.where(row32 == at, add, 0.0)
        sums = ffn_norm_back(r0, upstream, sums)
    vec[...] = jnp.zeros_like(vec)
    vec[5:6, :] = jnp.sum(sums[2], axis=0, keepdims=True)
    vec[6:7, :] = jnp.sum(sums[0], axis=0, keepdims=True)
    vec[7:8, :] = jnp.sum(sums[1], axis=0, keepdims=True)

    def chunk(p, h):
        return g_s.at[p, h] if p < 4 else wb.at[h, p - 4]

    z_slot = {}
    for at, way in enumerate(ROUTE):
        if way[0] == "z":
            z_slot[(at // 3, at % 3)] = len(z_slot)

    def route(p, h):
        return ROUTE[3 * p + h]

    def remote(source, target, send, recv, device):
        return pltpu.make_async_remote_copy(
            src_ref=source, dst_ref=target, send_sem=send, recv_sem=recv, device_id=(device,), device_id_type=MESH,
        )

    def step_c(p, h):
        return [remote(chunk(p, h).at[1 - core], rc.at[p % 2, h], c_send.at[p, h], c_recv.at[p, h], partner)]

    def along_z(p, h, pick, target):
        steps = []
        for hop in range(1, 4):
            to = lax.rem(zz + hop, 4)
            steps.append(remote(
                pick(to), target(hop - 1), z_send.at[p, h, hop - 1], z_recv.at[p, h, hop - 1], to * 8 + plane,
            ))
        return steps

    def step_1(p, h):
        mine, way = chunk(p, h), route(p, h)
        if way[0] == "z":
            return along_z(p, h, lambda to: mine.at[core, to], lambda i: rw.at[z_slot[(p, h)], i])
        away = mine.at[core, :, :, 1 - xx] if way == "xyz" else mine.at[core, :, 1 - yy]
        return [remote(away, ra.at[p, h], a_send.at[p, h], a_recv.at[p, h], x_peer if way == "xyz" else y_peer)]

    def step_2(p, h):
        mine, way = chunk(p, h), route(p, h)
        if way == "zyx":
            away, target = mine.at[core, zz, 1 - yy], rb.at[p, h, 0:2]
        elif way == "zxy":
            away, target = mine.at[core, zz, :, 1 - xx], rb.at[p, h, 0:2]
        elif way == "xyz":
            away, target = mine.at[core, :, 1 - yy, xx], rb.at[p, h]
        else:
            away, target = mine.at[core, :, yy, 1 - xx], rb.at[p, h]
        return [remote(away, target, b_send.at[p, h], b_recv.at[p, h], x_peer if way[1] == "x" else y_peer)]

    def step_3(p, h):
        mine = chunk(p, h)
        way = route(p, h)
        if way[0] == "z":
            away = mine.at[core, zz, yy, 1 - xx] if way == "zyx" else mine.at[core, zz, 1 - yy, xx]
            return [remote(
                away, rz.at[p, h, 0], a_send.at[p, h], a_recv.at[p, h], x_peer if way == "zyx" else y_peer,
            )]
        return along_z(p, h, lambda to: mine.at[core, to, yy, xx], lambda i: rz.at[p, h, i])

    def begin(steps):
        for step in steps:
            step.start()

    def finish_steps(steps):
        for step in steps:
            step.wait()

    def start_c(p, h):
        if p >= 2:
            pl.semaphore_wait(credit.at[p % 2, h], 1)
        begin(step_c(p, h))

    def end_c(p, h):
        finish_steps(step_c(p, h))

        def add(z, carry):
            for y in range(2):
                for x in range(2):
                    chunk(p, h)[core, z, y, x] += rc[p % 2, h, z, y, x]
            return carry

        lax.fori_loop(0, 4, add, 0)
        begin(step_1(p, h))
        if p < 4:
            pl.semaphore_signal(credit.at[p % 2, h], inc=1, device_id=(partner,), device_id_type=MESH)

    def end_1(p, h):
        finish_steps(step_1(p, h))
        mine, way = chunk(p, h), route(p, h)
        if way[0] == "z":
            def add(y, carry):
                for x in range(2):
                    total = mine[core, zz, y, x].astype(F32)
                    for i in range(3):
                        total += rw[z_slot[(p, h)], i, y, x].astype(F32)
                    mine[core, zz, y, x] = total.astype(BF16)
                return carry

            lax.fori_loop(0, 2, add, 0)
        else:
            def add(z, carry):
                for i in range(2):
                    if way == "yxz":
                        mine[core, z, yy, i] += ra[p, h, z, i]
                    else:
                        mine[core, z, i, xx] += ra[p, h, z, i]
                return carry

            lax.fori_loop(0, 4, add, 0)
        begin(step_2(p, h))

    def end_2(p, h):
        finish_steps(step_2(p, h))
        mine = chunk(p, h)
        way = route(p, h)
        if way[0] == "z":
            for i in range(2):
                if way == "zyx":
                    mine[core, zz, yy, i] += rb[p, h, i]
                else:
                    mine[core, zz, i, xx] += rb[p, h, i]
        else:
            def add(z, carry):
                mine[core, z, yy, xx] += rb[p, h, z]
                return carry

            lax.fori_loop(0, 4, add, 0)
        begin(step_3(p, h))

    outs = []

    def end_3(p, h):
        finish_steps(step_3(p, h))
        total = chunk(p, h)[core, zz, yy, xx].astype(F32)
        for i in range(1 if route(p, h)[0] == "z" else 3):
            total += rz[p, h, i].astype(F32)
        parts[p, h] = total
        at = WIDE * h
        if p < 2:
            targets = [wbg.at[pl.ds(48 * p, 48), pl.ds(at, WIDE)]]
        elif p < 4:
            at += (p - 2) * 2 * D
            targets = [wig.at[:, pl.ds(at, WIDE)], wig.at[:, pl.ds(at + D, WIDE)]]
        else:
            targets = [ref.at[:, pl.ds(at, WIDE)] for ref in ((wvg, wog) if p == 4 else (wqg, wkg))]
        rows = 48 // len(targets)
        for i, target in enumerate(targets):
            outs.append(pltpu.make_async_copy(parts.at[p, h, pl.ds(rows * i, rows)], target, part_sem.at[p, h, i]))
            outs[-1].start()

    def store_grad(p, h, grad):
        for i in range(32):
            chunk(p, h)[i % 2, i // 8, (i // 4) % 2, (i // 2) % 2] = grad[i]

    def back_grad(p, h):
        left = jnp.concatenate([actT[96 * i + 48 * p:96 * i + 48 * p + 48, :] for i in range(32)], axis=0)
        grad = dot_nn(left, ml[:, WIDE * h:WIDE * h + WIDE]).astype(BF16)
        store_grad(p, h, grad.reshape(32, 48, WIDE))

    def pair_grad(p, h, left_0, right_0, left_1, right_1):
        cols = pl.ds(WIDE * h, WIDE)
        grad_0 = dot_nn(left_0[...], right_0[:, cols]).reshape(32, 24, WIDE)
        grad_1 = dot_nn(left_1[...], right_1[:, cols]).reshape(32, 24, WIDE)
        store_grad(p, h, jnp.concatenate([grad_0, grad_1], axis=1).astype(BF16))

    def in_grad(p, h):
        at = (p - 2) * 2 * D
        pair_grad(p, h, mlT, gp.at[:, pl.ds(at, D)], mlT, gp.at[:, pl.ds(at + D, D)])

    def inner_grad(t):
        cols = pl.ds(t * D, D)
        weight = wb_tile(t)
        tmp_a[...] = dot_nt(ml[0:256, :], weight)
        tmp_b[0:224, :] = dot_nt(ml[256:480, :], weight)
        total = zero8
        for ref, start, size in ((tmp_a, 0, 256), (tmp_b, 256, 224)):
            for at, count in blocks(0, size, 16):
                rows = pl.ds(start + at, count)
                rounded = (ref[at:at + count, :] * gp[rows, cols].astype(F32)).astype(BF16)
                gp[rows, cols] = rounded
                total = total + fold8(rounded.astype(F32))
        vec[8 + t:9 + t, :] = jnp.sum(total, axis=0, keepdims=True)

    def middle_grad(t):
        cols = pl.ds(t * D, D)
        n2[...] += dot_nt(gp[:, cols], wi[:, cols])

    def attn_norm_back():
        def block(i, sums):
            rows = pl.ds(pl.multiple_of(i * 32, 32), 32)
            upstream, unit = n2[rows, :], n1[rows, :]
            scaled = upstream * gain1
            hidden_grad = r1[rows, :] * (
                scaled
                - jnp.mean(scaled, axis=-1, keepdims=True)
                - unit * jnp.mean(scaled * unit, axis=-1, keepdims=True)
            )
            n1[rows, :] = hidden_grad
            rounded = hidden_grad.astype(BF16)
            ml[rows, :] = rounded
            return (
                sums[0] + fold8(upstream * unit), sums[1] + fold8(upstream), sums[2] + fold8(rounded.astype(F32)),
            )

        sums = lax.fori_loop(0, 15, block, (zero8, zero8, zero8))
        vec[2:3, :] = jnp.sum(sums[2], axis=0, keepdims=True)
        vec[3:4, :] = jnp.sum(sums[0], axis=0, keepdims=True)
        vec[4:5, :] = jnp.sum(sums[1], axis=0, keepdims=True)

    def context_grad():
        c_s[...] = dot_nt(ml[...], wo[...]).astype(BF16)

    def query_slot_back():
        q_rows, k_rows, v_rows = spread(q_s[0:32, :]), k_s[0:32, :], v_s[0:32, :]
        dc_rows = spread(c_s[0:32, :])
        soft = pq_s[...]
        dp = dot_nt(v_rows, dc_rows)
        soft_f = soft.astype(F32)
        ds = (soft_f * (dp - jnp.sum(soft_f * dp, axis=0, keepdims=True))).astype(BF16)
        v_s[0:32, :] = dot_nn(soft, dc_rows).astype(BF16)
        k_s[0:32, :] = dot_nn(ds, q_rows).astype(BF16)
        q_s[0:32, :] = (0.125 * gather_heads(dot_tn(ds, k_rows))).astype(BF16)

    def attend_back_pair(pair):
        lanes = pl.ds(pl.multiple_of(pair * 128, 128), 128)
        for slot in range(2):
            low_at = 12 * slot
            rows = pl.ds(32 + 208 * slot, WIN)
            keys, queries, values = k_s[rows, lanes], q_s[rows, lanes], v_s[rows, lanes]
            inside = ((key_at >= low_at) & (key_at < low_at + SLOT)).astype(BF16)
            upstream = c_s[rows, lanes] * inside
            keys_t = keys.T
            parts, dv, dk = [], 0.0, 0.0
            for h in range(2):
                p = p_s[slot, 2 * pair + h]
                dc = upstream * half[h]
                dp = dot_nt(values, dc)
                pf = p.astype(F32)
                ds = (pf * (dp - jnp.sum(pf * dp, axis=0, keepdims=True))).astype(BF16)
                dv += dot_nn(p, dc)
                dk += dot_nn(ds, queries * half[h])
                parts.append(dot_nn(keys_t, ds)[64 * h:64 * h + 64, :])
            dq = 0.125 * jnp.concatenate(parts, axis=0).T
            for ref, new in ((q_s, dq), (k_s, dk), (v_s, dv)):
                if slot == 0:
                    ref[32:240, lanes] = new[0:208].astype(BF16)
                    old = ref[240:272, lanes].astype(F32)
                    ref[240:272, lanes] = jnp.where(iota((32, 128), 0) < 12, new[208:240], old).astype(BF16)
                else:
                    old = ref[240:256, lanes].astype(F32)
                    ref[240:256, lanes] = jnp.where(iota((16, 128), 0) >= 12, new[0:16], old).astype(BF16)
                    ref[256:480, lanes] = new[16:240].astype(BF16)

    def attend_back(first, count):
        def step(i, carry):
            attend_back_pair(first + i)
            return carry

        lax.fori_loop(0, count, step, 0)

    def column_sum(ref):
        def step(i, total):
            return total + fold8(ref[pl.ds(pl.multiple_of(i * 32, 32), 32), :].astype(F32))

        return jnp.sum(lax.fori_loop(0, 15, step, zero8), axis=0, keepdims=True)

    def column_sums():
        vec[0:1, :] = column_sum(q_s)
        vec[1:2, :] = column_sum(v_s)

    def token_grad(grads, weight):
        n1[...] += dot_nt(grads[...], weight[...])

    out_qg = pltpu.make_async_copy(n1.at[0:32, :], qtg_h, out_sem.at[2])
    out_pg = pltpu.make_async_copy(n1.at[32:472, :], ptg_h, out_sem.at[3])

    def send_tokens():
        out_qg.start()
        out_pg.start()

    def vec_step(i):
        return remote(vec, vecr.at[i], v_send.at[i], v_recv.at[i], (partner, x_peer, y_peer)[i])

    def vec_part(whole, to):
        device = to * 8 + plane
        narrow = pltpu.roll(whole[0:8], D - 24 * device, 1)[:, 0:128]
        wide = pltpu.roll(whole[8:16], D - 96 * plane, 1)[:, 0:128]
        wide = jnp.sum(jnp.where(iota((8, 128), 0) == to, wide, 0.0), axis=0, keepdims=True)
        return jnp.concatenate([narrow, wide, jnp.zeros((7, 128), F32)], axis=0)

    def vec_z():
        return [
            remote(
                vecs.at[hop - 1], vecz.at[hop - 1], v_send.at[2 + hop], v_recv.at[2 + hop],
                lax.rem(zz + hop, 4) * 8 + plane,
            )
            for hop in range(1, 4)
        ]

    def vec_on(i):
        if i > 0:
            vec_step(i - 1).wait()
            vec[...] += vecr[i - 1]
        if i < 3:
            vec_step(i).start()
        else:
            whole = vec[...]
            for hop in range(1, 4):
                vecs[hop - 1] = vec_part(whole, lax.rem(zz + hop, 4))
            begin(vec_z())

    def vec_end():
        finish_steps(vec_z())
        part = vec_part(vec[...], zz) + vecz[0] + vecz[1] + vecz[2]
        small_o[0:9, :] = part[0:9]
        outs.append(pltpu.make_async_copy(small_o, small_h, out_sem.at[4]))
        outs[-1].start()

    pieces_of = {
        "wback": back_grad, "dinner": inner_grad, "win": in_grad, "dmid": middle_grad, "lnback": attn_norm_back,
        "dctx": context_grad, "qslot": query_slot_back, "attn": attend_back, "sums": column_sums,
        "wvo": lambda h: pair_grad(4, h, xT, v_s, cT, ml), "wqk": lambda h: pair_grad(5, h, xT, q_s, xT, k_s),
        "tq": lambda: token_grad(q_s, wq), "tk": lambda: token_grad(k_s, wk), "tv": lambda: token_grad(v_s, wv),
        "tout": send_tokens, "vec": vec_on, "vecend": vec_end,
        "c": start_c, "ec": end_c, "e1": end_1, "e2": end_2, "e3": end_3,
    }
    for name, *operands in ORDER:
        pieces_of[name](*operands)

    out_q.wait()
    out_p.wait()
    out_qg.wait()
    out_pg.wait()
    for out in outs:
        out.wait()


def hand_on_kernel(*refs):
    count = 10
    sources, small = refs[:count], refs[count]
    targets, vectors = refs[count + 1:2 * count + 1], refs[2 * count + 1:2 * count + 11]
    held, rest = refs[2 * count + 11:3 * count + 11], refs[3 * count + 11:]
    small_v, lines, in_sem, out_sem = rest[0], rest[1:11], rest[11], rest[12]
    whole = [(i, None) for i in range(count) if i != 3]
    pieces = [(3, pl.ds(at, size)) for at, size in blocks(0, 440, 112)] + whole
    into, out = [], []
    for at, (i, rows) in enumerate(pieces):
        source, kept, target = (ref if rows is None else ref.at[rows, :] for ref in (sources[i], held[i], targets[i]))
        into.append(pltpu.make_async_copy(source, kept, in_sem.at[at]))
        out.append(pltpu.make_async_copy(kept, target, out_sem.at[at]))
    last = pltpu.make_async_copy(small, small_v, in_sem.at[len(pieces)])
    last.start()
    for copy in into:
        copy.start()
    last.wait()
    for at, ref in enumerate(lines[:8]):
        ref[...] = small_v[at:at + 1, 0:24].reshape(24)
    lines[8][...] = small_v[8:9, 0:96].reshape(96)
    lines[9][...] = small_v[9:10, 0:1].reshape(1)
    for at, (line, vector) in enumerate(zip(lines, vectors)):
        out.append(pltpu.make_async_copy(line, vector, out_sem.at[len(pieces) + at]))
        out[-1].start()
    for first, second in zip(into, out):
        first.wait()
        second.start()
    for copy in out:
        copy.wait()


def on_device_small(*operands):
    (
        query_tokens, passage_tokens, query_lengths, passage_lengths, passage_valid, positives, negatives,
        teacher_margins, query_grad, passage_grad, weight_query, bias_query, weight_key, weight_value, bias_value,
        weight_out, bias_out, gain_attn, shift_attn, weight_in, bias_in, weight_back, bias_back, gain_ffn, shift_ffn,
    ) = operands
    hbm, smem = (pl.BlockSpec(memory_space=space) for space in (pl.ANY, pltpu.SMEM))
    shape = jax.ShapeDtypeStruct
    slabs = (2, 2, 4, 2, 2, 48, D)
    large = (
        shape((32, D), BF16), shape((440, D), BF16), shape((32, D), F32), shape((440, D), F32), shape((24, D), F32),
        shape((24, D), F32), shape((24, D), F32), shape((24, D), F32), shape((24, FF), F32), shape((96, D), F32),
    )
    outs = pl.pallas_call(
        layer_kernel,
        out_shape=(
            *large, shape((16, 128), F32),
        ),
        in_specs=[
            hbm, hbm, smem, hbm, hbm, smem, smem, smem, hbm, hbm,
            *(hbm,) * 15,
        ],
        out_specs=(hbm,) * 11,
        scratch_shapes=[
            pltpu.VMEM((2,), jnp.int32), pltpu.VMEM((2,), jnp.int32),
            *(pltpu.VMEM((size,), BF16) for size in (D, D, D, D, D, FF, D, D, D)),
            pltpu.VMEM((D, D), BF16), pltpu.VMEM((D, D), BF16), pltpu.VMEM((D, D), BF16), pltpu.VMEM((D, D), BF16),
            pltpu.VMEM((D, FF), BF16), pltpu.VMEM((3, 2, 2, 4, 2, 2, 48, WIDE), BF16),
            pltpu.VMEM((440, D), BF16), pltpu.VMEM((ROWS, D), BF16), pltpu.VMEM((D, ROWS), BF16),
            pltpu.VMEM((ROWS, D), BF16), pltpu.VMEM((ROWS, D), BF16), pltpu.VMEM((ROWS, D), BF16),
            pltpu.VMEM((2, 12, WIN, WIN), BF16), pltpu.VMEM((32, 384), BF16),
            pltpu.VMEM((ROWS, D), BF16), pltpu.VMEM((D, ROWS), BF16),
            pltpu.VMEM((ROWS, D), F32), pltpu.VMEM((ROWS, D), F32), pltpu.VMEM((ROWS, 1), F32), pltpu.VMEM((ROWS, 1), F32),
            pltpu.VMEM((ROWS, D), BF16), pltpu.VMEM((D, ROWS), BF16),
            pltpu.VMEM((256, D), BF16), pltpu.VMEM((256, D), BF16), pltpu.VMEM((FF, ROWS), BF16),
            pltpu.VMEM((256, D), F32), pltpu.VMEM((256, D), F32),
            pltpu.VMEM((ROWS, FF), BF16),
            pltpu.VMEM((32, D), BF16), pltpu.VMEM((440, D), BF16), pltpu.VMEM((32, D), BF16), pltpu.VMEM((440, D), BF16),
            pltpu.VMEM((1024, 128), BF16), pltpu.VMEM((1024, 128), F32),
            pltpu.VMEM((16, D), F32), pltpu.VMEM((3, 16, D), F32), pltpu.VMEM((3, 16, 128), F32), pltpu.VMEM((3, 16, 128), F32),
            pltpu.VMEM((16, 128), F32), pltpu.VMEM((6, 3, 48, WIDE), F32),
            pltpu.VMEM((4, 3, 2, 4, 2, 2, 48, WIDE), BF16),
            pltpu.VMEM((2, 3, 4, 2, 2, 48, WIDE), BF16), pltpu.VMEM((6, 3, 4, 2, 48, WIDE), BF16),
            pltpu.VMEM((6, 3, 4, 48, WIDE), BF16), pltpu.VMEM((6, 3, 3, 48, WIDE), BF16),
            pltpu.VMEM((sum(way[0] == "z" for way in ROUTE), 3, 2, 2, 48, WIDE), BF16),
            pltpu.SemaphoreType.DMA((32,)), pltpu.SemaphoreType.DMA((5,)), pltpu.SemaphoreType.DMA((6, 3, 2)),
            pltpu.SemaphoreType.DMA((16,)), pltpu.SemaphoreType.DMA((16,)),
            pltpu.SemaphoreType.DMA((6, 3)), pltpu.SemaphoreType.DMA((6, 3)),
            pltpu.SemaphoreType.DMA((6, 3)), pltpu.SemaphoreType.DMA((6, 3)),
            pltpu.SemaphoreType.DMA((6, 3)), pltpu.SemaphoreType.DMA((6, 3)),
            pltpu.SemaphoreType.DMA((6, 3, 3)), pltpu.SemaphoreType.DMA((6, 3, 3)),
            pltpu.SemaphoreType.DMA((6,)), pltpu.SemaphoreType.DMA((6,)),
            pltpu.SemaphoreType.REGULAR((2, 3)),
        ],
        compiler_params=pltpu.CompilerParams(
            collective_id=0, has_side_effects=True, vmem_limit_bytes=64 * 1024 * 1024 - 65536,
        ),
        name="encoder_layer",
    )(
        query_tokens, passage_tokens, query_lengths, passage_lengths, passage_valid, positives, negatives,
        teacher_margins, query_grad, passage_grad, weight_query, bias_query, weight_key, weight_value, bias_value,
        weight_out, bias_out, gain_attn, shift_attn, weight_in, bias_in, weight_back.reshape(slabs), bias_back,
        gain_ffn, shift_ffn,
    )
    done = pl.pallas_call(
        hand_on_kernel,
        out_shape=large + (shape((24,), F32),) * 8 + (shape((96,), F32), shape((1,), F32)),
        in_specs=[hbm] * 11,
        out_specs=(hbm,) * 20,
        scratch_shapes=[pltpu.VMEM(out.shape, out.dtype) for out in large]
        + [pltpu.VMEM((16, 128), F32)] + [pltpu.VMEM((size,), F32) for size in (24,) * 8 + (96, 1)]
        + [pltpu.SemaphoreType.DMA((24,)), pltpu.SemaphoreType.DMA((24,))],
        name="hand_on",
    )(*outs)
    qout, pout, qtg, ptg, wqg, wkg, wvg, wog, wig, wbg, bqg, bvg, bog, gag, sag, bbg, gfg, sfg, big, loss = done
    return (
        qout, pout, loss, qtg, ptg, wqg, bqg, wkg, wvg, bvg, wog, bog, gag, sag, wig, big, wbg, bbg, gfg, sfg,
    )


def solution(mesh):
    return jax.shard_map(
        on_device_small if mesh.shape["dp"] == 32 else on_device,
        mesh=mesh,
        in_specs=(
            P("dp", None),
            P("dp", None),
            P("dp"),
            P("dp"),
            P("dp"),
            P("dp"),
            P("dp"),
            P("dp"),
            P("dp", None),
            P("dp", None),
            P(),
            P(),
            P(),
            P(),
            P(),
            P(),
            P(),
            P(),
            P(),
            P(),
            P(),
            P(),
            P(),
            P(),
            P(),
        ),
        out_specs=(
            P("dp", None),
            P("dp", None),
            P("dp"),
            P("dp", None),
            P("dp", None),
            P("dp", None),
            P("dp"),
            P("dp", None),
            P("dp", None),
            P("dp"),
            P("dp", None),
            P("dp"),
            P("dp"),
            P("dp"),
            P("dp", None),
            P("dp"),
            P("dp", None),
            P("dp"),
            P("dp"),
            P("dp"),
        ),
        check_vma=False,
    )
```

```python
import jax
import jax.numpy as jnp
from jax import lax
from jax.experimental import pallas as pl
from jax.experimental.pallas import tpu as pltpu
from jax.sharding import PartitionSpec as P

D = 768
HEADS = 12
HEAD_DIM = 64


ln_eps = 1e-12
score_scale = 0.0625
margin_weight = 0.5
root_half = 0.7071067811865476
inv_root_tau = 0.3989422804014327


def matmul(left, right):
    return jnp.dot(left, right, preferred_element_type=jnp.float32)


def left_across(left, right):
    return lax.dot_general(
        left, right, (((0,), (0,)), ((), ())), preferred_element_type=jnp.float32
    )


def right_across(left, right):
    return lax.dot_general(
        left, right, (((1,), (1,)), ((), ())), preferred_element_type=jnp.float32
    )


def normalize(hidden, gain, shift):
    centered = hidden - jnp.mean(hidden, axis=-1, keepdims=True)
    inv_std = lax.rsqrt(jnp.mean(centered * centered, axis=-1, keepdims=True) + ln_eps)
    unit_rows = centered * inv_std
    return (unit_rows * gain.astype(jnp.float32) + shift.astype(jnp.float32), unit_rows, inv_std)


def normalize_back(upstream, unit_rows, inv_std, gain):
    scaled = upstream * gain.astype(jnp.float32)
    hidden_grad = inv_std * (
        scaled
        - jnp.mean(scaled, axis=-1, keepdims=True)
        - unit_rows * jnp.mean(scaled * unit_rows, axis=-1, keepdims=True)
    )
    return (hidden_grad, jnp.sum(upstream * unit_rows, axis=0), jnp.sum(upstream, axis=0))


def gelu_exact(inputs):
    return 0.5 * inputs * (1.0 + lax.erf(inputs * root_half))


def gelu_slope(inputs):
    return 0.5 * (1.0 + lax.erf(inputs * root_half)) + inputs * inv_root_tau * jnp.exp(
        -0.5 * inputs * inputs
    )


def head_scores(query_heads, key_heads, lengths):
    slot_length = query_heads.shape[1]
    allowed = (lax.iota(jnp.int32, slot_length)[None, :] < lengths[:, None])[:, None, None, :]
    raw_scores = 0.125 * jnp.einsum(
        "bqhd,bkhd->bhqk", query_heads, key_heads, preferred_element_type=jnp.float32
    )
    return jnp.where(allowed, raw_scores, -1000000000.0)


def encode_forward(tokens, lengths, params):
    (
        weight_query,
        bias_query,
        weight_key,
        weight_value,
        bias_value,
        weight_out,
        bias_out,
        gain_attn,
        shift_attn,
        weight_in,
        bias_in,
        weight_back,
        bias_back,
        gain_ffn,
        shift_ffn,
    ) = params
    slot_count = lengths.shape[0]
    row_count = tokens.shape[0]
    split_heads = (slot_count, row_count // slot_count, HEADS, HEAD_DIM)
    queries = (matmul(tokens, weight_query) + bias_query.astype(jnp.float32)).astype(jnp.bfloat16)
    keys_all = matmul(tokens, weight_key).astype(jnp.bfloat16)
    values_all = (matmul(tokens, weight_value) + bias_value.astype(jnp.float32)).astype(
        jnp.bfloat16
    )
    scores = head_scores(queries.reshape(split_heads), keys_all.reshape(split_heads), lengths)
    peak_score = jnp.max(scores, axis=-1, keepdims=True)
    exp_scores = jnp.exp(scores - peak_score)
    row_total = jnp.sum(exp_scores, axis=-1, keepdims=True)
    soft_low = (exp_scores / row_total).astype(jnp.bfloat16)
    log_total = peak_score + jnp.log(row_total)
    context = jnp.einsum(
        "bhqk,bkhd->bqhd",
        soft_low,
        values_all.reshape(split_heads),
        preferred_element_type=jnp.float32,
    )
    context = context.reshape(row_count, D).astype(jnp.bfloat16)
    attn_sum = (
        tokens.astype(jnp.float32) + matmul(context, weight_out) + bias_out.astype(jnp.float32)
    )
    middle, unit_attn, inv_attn = normalize(attn_sum, gain_attn, shift_attn)
    middle_low = middle.astype(jnp.bfloat16)
    inner_act = matmul(middle_low, weight_in) + bias_in.astype(jnp.float32)
    gelu_low = gelu_exact(inner_act).astype(jnp.bfloat16)
    ffn_sum = middle + matmul(gelu_low, weight_back) + bias_back.astype(jnp.float32)
    output, unit_ffn, inv_ffn = normalize(ffn_sum, gain_ffn, shift_ffn)
    kept = (
        queries,
        keys_all,
        values_all,
        log_total,
        context,
        unit_attn,
        inv_attn,
        middle_low,
        inner_act,
        gelu_low,
        unit_ffn,
        inv_ffn,
    )
    return (output.astype(jnp.bfloat16), kept)


def ffn_backward(upstream, kept, params):
    (
        queries,
        keys_all,
        values_all,
        log_total,
        context,
        unit_attn,
        inv_attn,
        middle_low,
        inner_act,
        gelu_low,
        unit_ffn,
        inv_ffn,
    ) = kept
    weight_in, weight_back, gain_ffn = (params[9], params[11], params[13])
    ffn_grad, gain_grad, shift_grad = normalize_back(upstream, unit_ffn, inv_ffn, gain_ffn)
    branch_low = ffn_grad.astype(jnp.bfloat16)
    back_weight_grad = left_across(gelu_low, branch_low)
    back_bias_grad = jnp.sum(branch_low, axis=0, dtype=jnp.float32)
    inner_low = (right_across(branch_low, weight_back) * gelu_slope(inner_act)).astype(jnp.bfloat16)
    in_weight_grad = left_across(middle_low, inner_low)
    in_bias_grad = jnp.sum(inner_low, axis=0, dtype=jnp.float32)
    middle_grad = ffn_grad + right_across(inner_low, weight_in)
    return (
        middle_grad,
        (in_weight_grad, in_bias_grad, back_weight_grad, back_bias_grad, gain_grad, shift_grad),
    )


def attention_backward(middle_grad, tokens, lengths, kept, params):
    (
        queries,
        keys_all,
        values_all,
        log_total,
        context,
        unit_attn,
        inv_attn,
        middle_low,
        inner_act,
        gelu_low,
        unit_ffn,
        inv_ffn,
    ) = kept
    weight_query, weight_key, weight_value, weight_out, gain_attn = (
        params[0],
        params[2],
        params[3],
        params[5],
        params[7],
    )
    slot_count = lengths.shape[0]
    row_count = tokens.shape[0]
    split_heads = (slot_count, row_count // slot_count, HEADS, HEAD_DIM)
    attn_grad, gain_grad, shift_grad = normalize_back(middle_grad, unit_attn, inv_attn, gain_attn)
    attn_low = attn_grad.astype(jnp.bfloat16)
    out_weight_grad = left_across(context, attn_low)
    out_bias_grad = jnp.sum(attn_low, axis=0, dtype=jnp.float32)
    context_grad = right_across(attn_low, weight_out).astype(jnp.bfloat16).reshape(split_heads)
    query_heads = queries.reshape(split_heads)
    key_heads = keys_all.reshape(split_heads)
    value_heads = values_all.reshape(split_heads)
    soft_full = jnp.exp(head_scores(query_heads, key_heads, lengths) - log_total)
    soft_grad = jnp.einsum(
        "bqhd,bkhd->bhqk", context_grad, value_heads, preferred_element_type=jnp.float32
    )
    value_grad = jnp.einsum(
        "bhqk,bqhd->bkhd",
        soft_full.astype(jnp.bfloat16),
        context_grad,
        preferred_element_type=jnp.float32,
    )
    value_grad = value_grad.reshape(row_count, D).astype(jnp.bfloat16)
    score_low = (
        soft_full * (soft_grad - jnp.sum(soft_full * soft_grad, axis=-1, keepdims=True))
    ).astype(jnp.bfloat16)
    query_grad_low = 0.125 * jnp.einsum(
        "bhqk,bkhd->bqhd", score_low, key_heads, preferred_element_type=jnp.float32
    )
    query_grad_low = query_grad_low.reshape(row_count, D).astype(jnp.bfloat16)
    key_grad_low = 0.125 * jnp.einsum(
        "bhqk,bqhd->bkhd", score_low, query_heads, preferred_element_type=jnp.float32
    )
    key_grad_low = key_grad_low.reshape(row_count, D).astype(jnp.bfloat16)
    token_grad = (
        attn_grad
        + right_across(query_grad_low, weight_query)
        + right_across(key_grad_low, weight_key)
        + right_across(value_grad, weight_value)
    )
    grads = (
        left_across(tokens, query_grad_low),
        jnp.sum(query_grad_low, axis=0, dtype=jnp.float32),
        left_across(tokens, key_grad_low),
        left_across(tokens, value_grad),
        jnp.sum(value_grad, axis=0, dtype=jnp.float32),
        out_weight_grad,
        out_bias_grad,
        gain_grad,
        shift_grad,
    )
    return (token_grad, grads)


def on_device(
    query_tokens,
    passage_tokens,
    query_lengths,
    passage_lengths,
    passage_valid,
    positives,
    negatives,
    teacher_margins,
    query_grad,
    passage_grad,
    weight_query,
    bias_query,
    weight_key,
    weight_value,
    bias_value,
    weight_out,
    bias_out,
    gain_attn,
    shift_attn,
    weight_in,
    bias_in,
    weight_back,
    bias_back,
    gain_ffn,
    shift_ffn,
):
    params = (
        weight_query,
        bias_query,
        weight_key,
        weight_value,
        bias_value,
        weight_out,
        bias_out,
        gain_attn,
        shift_attn,
        weight_in,
        bias_in,
        weight_back,
        bias_back,
        gain_ffn,
        shift_ffn,
    )
    query_out, query_kept = encode_forward(query_tokens, query_lengths, params)
    passage_out, passage_kept = encode_forward(passage_tokens, passage_lengths, params)
    query_slots = query_lengths.shape[0]
    passage_slots = passage_lengths.shape[0]
    cls_query = query_out.reshape(query_slots, -1, D)[:, 0]
    cls_passage = passage_out.reshape(passage_slots, -1, D)[:, 0]
    valid_low = passage_valid.astype(jnp.bfloat16)

    def score_piece(cls_piece, valid_piece):
        scores = score_scale * right_across(cls_query, cls_piece)
        position = lax.iota(jnp.int32, cls_piece.shape[0])
        is_positive = position[None, :] == positives[:, None]
        is_negative = position[None, :] == negatives[:, None]
        allowed = (valid_piece[None, :] > 0.5) | is_positive
        return (scores, allowed, is_positive, is_negative)

    peak_score = jnp.full((query_slots,), -1e30, jnp.float32)
    scores, allowed, is_positive, is_negative = score_piece(
        lax.all_gather(cls_passage, "dp", axis=0, tiled=True),
        lax.all_gather(valid_low, "dp", axis=0, tiled=True),
    )
    masked = jnp.where(allowed, scores, -1e30)
    new_peak = jnp.maximum(peak_score, jnp.max(masked, axis=1))
    row_total = jnp.sum(jnp.where(allowed, jnp.exp(masked - new_peak[:, None]), 0.0), axis=1)
    positive_score = jnp.sum(jnp.where(is_positive, scores, 0.0), axis=1)
    negative_score = jnp.sum(jnp.where(is_negative, scores, 0.0), axis=1)
    peak_score, row_total, positive_score, negative_score = (
        new_peak,
        row_total,
        positive_score,
        negative_score,
    )
    all_cls, all_valid = (
        lax.all_gather(cls_passage, "dp", axis=0, tiled=True),
        lax.all_gather(valid_low, "dp", axis=0, tiled=True),
    )
    log_total = peak_score + jnp.log(row_total)
    shortfall = positive_score - negative_score - teacher_margins
    query_loss = log_total - positive_score + margin_weight * shortfall * shortfall
    scores, allowed, is_positive, is_negative = score_piece(all_cls, all_valid)
    soft_scores = jnp.where(allowed, jnp.exp(scores - log_total[:, None]), 0.0)
    positive_hit = is_positive.astype(jnp.float32)
    negative_hit = is_negative.astype(jnp.float32)
    score_grad = (
        soft_scores
        - positive_hit
        + 2.0 * margin_weight * shortfall[:, None] * (positive_hit - negative_hit)
    ).astype(jnp.bfloat16)
    cls_query_grad = score_scale * matmul(score_grad, all_cls)
    cls_passage_grad = lax.psum_scatter(
        score_scale * left_across(score_grad, cls_query), "dp", scatter_dimension=0, tiled=True
    )
    query_upstream = (
        query_grad.astype(jnp.float32)
        .reshape(query_slots, -1, D)
        .at[:, 0]
        .add(cls_query_grad)
        .reshape(-1, D)
    )
    passage_upstream = (
        passage_grad.astype(jnp.float32)
        .reshape(passage_slots, -1, D)
        .at[:, 0]
        .add(cls_passage_grad)
        .reshape(-1, D)
    )
    query_middle_grad, query_ffn = ffn_backward(query_upstream, query_kept, params)
    passage_middle_grad, passage_ffn = ffn_backward(passage_upstream, passage_kept, params)
    (
        in_weight_grad,
        in_bias_grad,
        back_weight_grad,
        back_bias_grad,
        ffn_gain_grad,
        ffn_shift_grad,
    ) = tuple((first + second for first, second in zip(query_ffn, passage_ffn)))
    query_tokens_grad, query_attn = attention_backward(
        query_middle_grad, query_tokens, query_lengths, query_kept, params
    )
    passage_tokens_grad, passage_attn = attention_backward(
        passage_middle_grad, passage_tokens, passage_lengths, passage_kept, params
    )
    (
        query_weight_grad,
        query_bias_grad,
        key_weight_grad,
        value_weight_grad,
        value_bias_grad,
        out_weight_grad,
        out_bias_grad,
        attn_gain_grad,
        attn_shift_grad,
    ) = tuple((first + second for first, second in zip(query_attn, passage_attn)))
    (
        query_weight_grad,
        query_bias_grad,
        key_weight_grad,
        value_weight_grad,
        value_bias_grad,
        out_weight_grad,
        out_bias_grad,
        attn_gain_grad,
        attn_shift_grad,
        in_weight_grad,
        in_bias_grad,
        back_weight_grad,
        back_bias_grad,
        ffn_gain_grad,
        ffn_shift_grad,
    ) = (
        lax.psum_scatter(query_weight_grad, "dp", scatter_dimension=0, tiled=True),
        lax.psum_scatter(query_bias_grad, "dp", scatter_dimension=0, tiled=True),
        lax.psum_scatter(key_weight_grad, "dp", scatter_dimension=0, tiled=True),
        lax.psum_scatter(value_weight_grad, "dp", scatter_dimension=0, tiled=True),
        lax.psum_scatter(value_bias_grad, "dp", scatter_dimension=0, tiled=True),
        lax.psum_scatter(out_weight_grad, "dp", scatter_dimension=0, tiled=True),
        lax.psum_scatter(out_bias_grad, "dp", scatter_dimension=0, tiled=True),
        lax.psum_scatter(attn_gain_grad, "dp", scatter_dimension=0, tiled=True),
        lax.psum_scatter(attn_shift_grad, "dp", scatter_dimension=0, tiled=True),
        lax.psum_scatter(in_weight_grad, "dp", scatter_dimension=0, tiled=True),
        lax.psum_scatter(in_bias_grad, "dp", scatter_dimension=0, tiled=True),
        lax.psum_scatter(back_weight_grad, "dp", scatter_dimension=0, tiled=True),
        lax.psum_scatter(back_bias_grad, "dp", scatter_dimension=0, tiled=True),
        lax.psum_scatter(ffn_gain_grad, "dp", scatter_dimension=0, tiled=True),
        lax.psum_scatter(ffn_shift_grad, "dp", scatter_dimension=0, tiled=True),
    )
    return (
        query_out,
        passage_out,
        query_loss,
        query_tokens_grad,
        passage_tokens_grad,
        query_weight_grad,
        query_bias_grad,
        key_weight_grad,
        value_weight_grad,
        value_bias_grad,
        out_weight_grad,
        out_bias_grad,
        attn_gain_grad,
        attn_shift_grad,
        in_weight_grad,
        in_bias_grad,
        back_weight_grad,
        back_bias_grad,
        ffn_gain_grad,
        ffn_shift_grad,
    )


F32 = jnp.float32
BF16 = jnp.bfloat16
MESH = pl.DeviceIdType.MESH
FF = 3072
ROWS = 480
WIN = 240
SLOT = 220
NEG = -1000000000.0


def dot_nn(left, right):
    return jnp.dot(left, right, preferred_element_type=F32)


def dot_nt(left, right):
    return lax.dot_general(left, right, (((1,), (1,)), ((), ())), preferred_element_type=F32)


def dot_tn(left, right):
    return lax.dot_general(left, right, (((0,), (0,)), ((), ())), preferred_element_type=F32)


def row_of(ref, start=0, size=D):
    return ref[pl.ds(start, size)].astype(F32).reshape(1, size)


def item(ref, at):
    return ref[...].reshape(1, 2)[:, at:at + 1]


def blocks(start, stop, size):
    return [(at, min(size, stop - at)) for at in range(start, stop, size)]


def iota(shape, dim):
    return lax.broadcasted_iota(jnp.int32, shape, dim)


def fold8(block):
    return jnp.sum(block.reshape(-1, 8, block.shape[-1]), axis=0)


WIDE = 256
ROUTE = (
    "xyz", "yxz", "ryx", "xyz", "rxy", "ryx", "yxz", "xyz", "yxz", "xyz", "yxz", "xyz", "yxz", "xyz", "yxz", "xyz",
    "yxz", "xyz",
)
ORDER = (
    ("wback", 0, 0), ("c", 0, 0), ("wback", 0, 1), ("c", 0, 1), ("wback", 0, 2), ("c", 0, 2), ("wback", 1, 0),
    ("c", 1, 0), ("ec", 0, 0), ("wback", 1, 1), ("ec", 0, 1), ("c", 1, 1), ("wback", 1, 2), ("ec", 0, 2),
    ("c", 1, 2), ("dinner", 0), ("dinner", 1), ("win", 2, 0), ("c", 2, 0), ("ec", 1, 0), ("win", 2, 1), ("c", 2, 1),
    ("win", 2, 2), ("c", 2, 2), ("ec", 1, 1), ("ec", 2, 0), ("dinner", 2), ("dinner", 3), ("e1", 0, 1),
    ("win", 3, 0), ("c", 3, 0), ("win", 3, 1), ("e1", 0, 0), ("c", 3, 1), ("win", 3, 2), ("ec", 2, 1), ("ec", 1, 2),
    ("c", 3, 2), ("dmid", 0), ("dmid", 1), ("ec", 2, 2), ("ec", 3, 1), ("e1", 0, 2), ("ec", 3, 0), ("dmid", 2),
    ("dmid", 3), ("ec", 3, 2), ("lnback",), ("e2", 0, 1), ("dctx",), ("e1", 1, 0), ("e2", 0, 0), ("qslot",),
    ("attn", 0, 1), ("e1", 2, 0), ("e1", 1, 1), ("attn", 1, 2), ("e1", 2, 1), ("attn", 3, 3), ("sums",),
    ("e1", 3, 0), ("e1", 1, 2), ("wvo", 0), ("e1", 3, 1), ("c", 4, 0), ("vec", 0), ("wvo", 1), ("c", 4, 1),
    ("e1", 2, 2), ("wvo", 2), ("e1", 3, 2), ("c", 4, 2), ("wqk", 0), ("c", 5, 0), ("wqk", 1), ("ec", 4, 1),
    ("c", 5, 1), ("wqk", 2), ("e2", 2, 1), ("ec", 4, 2), ("e3", 0, 1), ("e2", 3, 0), ("e2", 2, 0), ("vec", 1),
    ("e2", 3, 1), ("ec", 5, 1), ("e2", 1, 0), ("e2", 3, 2), ("ec", 5, 0), ("e2", 2, 2), ("e1", 4, 1), ("e1", 4, 2),
    ("vec", 2), ("ec", 4, 0), ("c", 5, 2), ("tq",), ("e3", 3, 0), ("e1", 5, 1), ("ec", 5, 2), ("e2", 4, 1),
    ("e1", 5, 0), ("vec", 3), ("e3", 0, 0), ("e2", 0, 2), ("e2", 5, 1), ("tk",), ("e2", 1, 2), ("e1", 4, 0),
    ("e2", 4, 2), ("e3", 2, 0), ("e1", 5, 2), ("e2", 5, 0), ("e3", 3, 1), ("e2", 1, 1), ("e2", 4, 0), ("e3", 2, 2),
    ("e2", 5, 2), ("e3", 1, 2), ("e3", 1, 1), ("e3", 4, 2), ("e3", 0, 2), ("e3", 4, 1), ("e4", 1, 1), ("e3", 2, 1),
    ("vecend",), ("e3", 5, 1), ("e3", 5, 0), ("e3", 3, 2), ("tv",), ("tout",), ("e3", 4, 0), ("e3", 1, 0),
    ("e4", 0, 2), ("e4", 1, 2), ("e3", 5, 2),
)


RELAYS = max(1, sum(way[0] == "r" for way in ROUTE))


def layer_kernel(
    qtok, ptok, qlen, plen_h, pvalid_h, pos, neg, margin, qgrad, pgrad,
    wq_h, bq_h, wk_h, wv_h, bv_h, wo_h, bo_h, ga_h, sa_h, wi_h, bi_h, wb_h, bb_h, gf_h, sf_h,
    qout_h, pout_h, qtg_h, ptg_h, wqg, wkg, wvg, wog, wig, wbg, small_h,
    plen, pvalid, bq, bv, bo, ga, sa, bi, bb, gf, sf, wq, wk, wv, wo, wi, wb, pstage, x_s, xT, q_s, k_s, v_s, p_s, pq_s, c_s, cT, n1, n2, r1, r2,
    ml, mlT, act_a, act_b, actT, tmp_a, tmp_b, gp, qg_s, pg_s, qo_s, po_s, ex, ex_f, vec, vecr, vecs, vecz, small_o, parts,
    g_s, rc, ra, rb, rz, rw, rw_mate, rw_far, rw_in,
    load_sem, out_sem, part_sem, ex_send, ex_recv, c_send, c_recv, a_send, a_recv, b_send, b_recv,
    z_send, z_recv, r_send, v_send, v_recv, credit,
):
    me = lax.axis_index("dp")
    core = lax.rem(me, 2)
    xx = lax.rem(lax.div(me, 2), 2)
    yy = lax.rem(lax.div(me, 4), 2)
    zz = lax.div(me, 8)
    chip = lax.div(me, 2)
    partner = me + 1 - 2 * core
    x_peer = me + 2 - 4 * xx
    y_peer = me + 4 - 8 * yy
    plane = lax.rem(me, 8)

    loads = {}

    def load(name, source, target):
        loads[name] = pltpu.make_async_copy(source, target, load_sem.at[len(loads)])
        loads[name].start()

    load("ptok", ptok, pstage)
    load("qtok", qtok, qo_s)
    load("wq", wq_h, wq)
    vectors = (
        (plen_h, plen), (pvalid_h, pvalid), (bq_h, bq), (bv_h, bv), (bo_h, bo), (ga_h, ga), (sa_h, sa), (bi_h, bi),
        (bb_h, bb), (gf_h, gf), (sf_h, sf),
    )
    for at, (source, target) in enumerate(vectors):
        load("vec" + str(at), source, target)
    load("wk", wk_h, wk)
    load("wv", wv_h, wv)

    barrier = pltpu.get_barrier_semaphore()
    for hop in range(1, 16):
        other = 2 * lax.rem(chip + hop, 16) + core
        pl.semaphore_signal(barrier, inc=1, device_id=(other,), device_id_type=MESH)
    pl.semaphore_signal(barrier, inc=1, device_id=(partner,), device_id_type=MESH)

    loads["ptok"].wait()
    loads["qtok"].wait()
    x_s[0:32, :] = qo_s[...]

    def copy_tokens(i, carry):
        x_s[pl.ds(pl.multiple_of(32 + i * 16, 16), 16), :] = pstage[pl.ds(pl.multiple_of(i * 16, 16), 16), :]
        return carry

    lax.fori_loop(0, 27, copy_tokens, 0)
    x_s[464:480, :] = jnp.concatenate(
        [pstage[432:440, :].astype(F32), jnp.zeros((8, D), F32)], axis=0
    ).astype(BF16)

    loads["wq"].wait()
    for at in range(len(vectors)):
        loads["vec" + str(at)].wait()
    load("wo", wo_h, wo)
    load("wi", wi_h, wi)

    def project_queries(start, stop):
        rows = pl.ds(start, stop - start)
        q_s[rows, :] = ((dot_nn(x_s[rows, :], wq[...]) + row_of(bq)).astype(BF16) * 0.125).astype(BF16)

    project_queries(0, 256)
    loads["wk"].wait()
    k_s[...] = dot_nn(x_s[...], wk[...]).astype(BF16)
    loads["wv"].wait()
    for h in range(3):
        load("wb" + str(h), wb_h.at[:, :, :, :, :, :, pl.ds(WIDE * h, WIDE)], wb.at[h])
    load("qg", qgrad, qg_s)
    load("pg", pgrad, pg_s)
    v_s[...] = (dot_nn(x_s[...], wv[...]) + row_of(bv)).astype(BF16)

    head_of = iota((12, 1, D), 2) // 64
    head_mask = (head_of == iota((12, 1, D), 0)).astype(F32)

    def spread(rows):
        return (rows.astype(F32)[None] * head_mask).astype(BF16).reshape(384, D)

    def gather_heads(stacked):
        return jnp.sum(stacked.reshape(12, 32, D) * head_mask, axis=0)

    raw = dot_nt(k_s[0:32, :], spread(q_s[0:32, :]))
    raw = jnp.where(iota((32, 384), 0) < qlen[0], raw, NEG)
    soft = jnp.exp(raw - jnp.max(raw, axis=0, keepdims=True))
    soft = (soft * (1.0 / jnp.sum(soft, axis=0, keepdims=True))).astype(BF16)
    pq_s[...] = soft
    c_s[0:32, :] = gather_heads(dot_tn(soft, v_s[0:32, :])).astype(BF16)

    by_head = (q_s[240:256, :].astype(F32)[None] * head_mask).astype(BF16).reshape(192, D)
    raw = dot_nt(by_head, k_s[240:480, :])
    key_lane = iota((1, WIN), 1)
    raw = jnp.where((key_lane >= 12) & (key_lane < 12 + item(plen, 1)), raw, NEG)
    soft = jnp.exp(raw - jnp.max(raw, axis=1, keepdims=True))
    soft = (soft * (1.0 / jnp.sum(soft, axis=1, keepdims=True))).astype(BF16)
    block = jnp.sum(dot_nn(soft, v_s[240:480, :]).reshape(12, 16, D) * head_mask, axis=0)

    lane = iota((1, 128), 1)
    half = ((lane < 64).astype(BF16), (lane >= 64).astype(BF16))
    key_at = iota((WIN, 1), 0)

    def attend(pair, slot):
        lanes = pl.ds(pl.multiple_of(pair * 128, 128), 128)
        low_at = 12 * slot
        first_row = 32 + 208 * slot
        rows = pl.ds(first_row, WIN)
        keys, queries = k_s[rows, lanes], q_s[rows, lanes]
        values_t = v_s[rows, lanes].T
        allowed = (key_at >= low_at) & (key_at < low_at + item(plen, slot))
        parts = []
        for h in range(2):
            scores = jnp.where(allowed, dot_nt(keys, queries * half[h]), NEG)
            e = jnp.exp(scores - jnp.max(scores, axis=0, keepdims=True))
            p = (e * (1.0 / jnp.sum(e, axis=0, keepdims=True))).astype(BF16)
            p_s[slot, 2 * pair + h] = p
            parts.append(dot_nn(values_t, p)[64 * h:64 * h + 64, :])
        context = jnp.concatenate(parts, axis=0).T
        if slot == 0:
            c_s[rows, lanes] = context.astype(BF16)
            return
        old = c_s[240:256, lanes].astype(F32)
        c_s[240:256, lanes] = jnp.where(iota((16, 128), 0) >= 12, context[0:16], old).astype(BF16)
        c_s[256:480, lanes] = context[16:240].astype(BF16)

    def attend_slot(slot):
        def two_pairs(i, carry):
            attend(2 * i, slot)
            attend(2 * i + 1, slot)
            return carry

        lax.fori_loop(0, 3, two_pairs, 0)

    attend_slot(0)
    old = c_s[240:256, :].astype(F32)
    c_s[240:256, :] = jnp.where(iota((16, 1), 0) >= 12, block, old).astype(BF16)

    loads["wo"].wait()
    gain1, shift1, bias1 = row_of(ga), row_of(sa), row_of(bo)
    gain2, shift2, bias2 = row_of(gf), row_of(sf), row_of(bb)

    def wb_tile(t):
        return jnp.concatenate([wb[h, t // 2, t % 2].reshape(D, WIDE) for h in range(3)], axis=1)

    def normalized(hidden):
        centered = hidden - jnp.mean(hidden, axis=-1, keepdims=True)
        inv = lax.rsqrt(jnp.mean(centered * centered, axis=-1, keepdims=True) + ln_eps)
        return centered * inv, inv

    def forward_rows(start, stop):
        size = stop - start
        every, own = pl.ds(start, size), pl.ds(0, size)
        tmp_a[own, :] = dot_nn(c_s[every, :], wo[...])
        for at, count in blocks(0, size, 32):
            rows, here = pl.ds(start + at, count), pl.ds(at, count)
            unit, inv = normalized(tmp_a[here, :] + x_s[rows, :].astype(F32) + bias1)
            n1[rows, :] = unit
            r1[rows, :] = inv
            ml[rows, :] = (unit * gain1 + shift1).astype(BF16)
        if start == 0:
            loads["wi"].wait()
            for h in range(3):
                loads["wb" + str(h)].wait()
        inner, acts = (tmp_a, tmp_b), (act_a, act_b)
        tmp_a[own, :] = dot_nn(ml[every, :], wi[:, 0:D])
        mlT[:, every] = ml[every, :].T
        xT[:, every] = x_s[every, :].T
        cT[:, every] = c_s[every, :].T

        def finish(t):
            act = acts[t % 2][own, :]
            if t == 0:
                n2[every, :] = dot_nn(act, wb_tile(t))
            else:
                n2[every, :] += dot_nn(act, wb_tile(t))
            actT[t * D:t * D + D, every] = act.T

        for t in range(4):
            if t < 3:
                inner[(t + 1) % 2][own, :] = dot_nn(ml[every, :], wi[:, t * D + D:t * D + 2 * D])
            bias_t = row_of(bi, t * D)
            for at, count in blocks(0, size, 16):
                here = pl.ds(at, count)
                u = inner[t % 2][here, :] + bias_t
                cdf = 0.5 * (1.0 + lax.erf(u * root_half))
                acts[t % 2][here, :] = (u * cdf).astype(BF16)
                gp[start + at:start + at + count, t * D:t * D + D] = (
                    cdf + u * inv_root_tau * jnp.exp(-0.5 * u * u)
                ).astype(BF16)
            if t > 0:
                finish(t - 1)
        finish(3)
        for at, count in blocks(start, stop, 32):
            rows = pl.ds(at, count)
            unit, inv = normalized(n2[rows, :] + (n1[rows, :] * gain1 + shift1) + bias2)
            n2[rows, :] = unit
            r2[rows, :] = inv
            out = (unit * gain2 + shift2).astype(BF16)
            if at == 0:
                qo_s[...] = out
            else:
                po_s[at - 32:min(at, 440), :] = out[0:min(count, 472 - at)]

    forward_rows(0, 256)

    slot_me = core * 16 + chip
    base = pl.multiple_of(slot_me * 32, 32)
    first_rows = (
        qo_s[0:16, :].astype(F32)[0:1],
        po_s[0:16, :].astype(F32)[0:1],
        po_s[208:224, :].astype(F32)[12:13],
    )
    lane_row = iota((1, 128), 1)
    meta = jnp.zeros((1, 128), F32)
    margin_0 = jnp.zeros((1, 128), F32) + margin[0]
    margin_1 = margin_0.astype(BF16).astype(F32)
    margin_2 = (margin_0 - margin_1).astype(BF16).astype(F32)
    for at, value in enumerate((
        item(pvalid, 0).astype(F32), item(pvalid, 1).astype(F32), pos[0].astype(F32), neg[0].astype(F32),
        margin_1, margin_2, margin_0 - margin_1 - margin_2,
    )):
        meta = jnp.where(lane_row == at, value, meta)
    pieces = [row[:, 128 * i:128 * i + 128] for row in first_rows for i in range(6)]
    ex[pl.ds(base, 32), :] = jnp.concatenate(pieces + [meta, jnp.zeros((13, 128), F32)], axis=0).astype(BF16)

    pl.semaphore_wait(barrier, 16)
    sends = []
    for hop in range(1, 16):
        block = ex.at[pl.ds(base, 32), :]
        sends.append(pltpu.make_async_remote_copy(
            src_ref=block, dst_ref=block, send_sem=ex_send.at[hop], recv_sem=ex_recv.at[hop],
            device_id=(2 * lax.rem(chip + hop, 16) + core,), device_id_type=MESH,
        ))
        sends[-1].start()

    project_queries(256, 480)
    attend_slot(1)
    forward_rows(256, 480)
    out_q = pltpu.make_async_copy(qo_s, qout_h, out_sem.at[0])
    out_p = pltpu.make_async_copy(po_s, pout_h, out_sem.at[1])
    out_q.start()
    out_p.start()
    loads["qg"].wait()
    loads["pg"].wait()

    def ffn_norm_back(r0, upstream, sums):
        rows = pl.ds(r0, upstream.shape[0])
        unit = n2[rows, :]
        scaled = upstream * gain2
        hidden_grad = r2[rows, :] * (
            scaled
            - jnp.mean(scaled, axis=-1, keepdims=True)
            - unit * jnp.mean(scaled * unit, axis=-1, keepdims=True)
        )
        n2[rows, :] = hidden_grad
        rounded = hidden_grad.astype(BF16)
        ml[rows, :] = rounded
        return (
            sums[0] + fold8(upstream * unit), sums[1] + fold8(upstream), sums[2] + fold8(rounded.astype(F32)),
        )

    zero8 = jnp.zeros((8, D), F32)
    sums = (zero8, zero8, zero8)

    def middle_block(i, sums):
        upstream = pg_s[pl.ds(pl.multiple_of(i * 32, 32), 32), :].astype(F32)
        return ffn_norm_back(pl.multiple_of(32 + i * 32, 32), upstream, sums)

    sums = lax.fori_loop(1, 6, middle_block, sums)
    sums = lax.fori_loop(7, 13, middle_block, sums)
    last = jnp.concatenate([pg_s[416:440, :].astype(F32), jnp.zeros((8, D), F32)], axis=0)
    sums = ffn_norm_back(448, last, sums)

    for send in sends:
        send.wait()
    same_core = ex.at[pl.ds(pl.multiple_of(core * 512, 512), 512), :]
    across = pltpu.make_async_remote_copy(
        src_ref=same_core, dst_ref=same_core, send_sem=ex_send.at[0], recv_sem=ex_recv.at[0],
        device_id=(partner,), device_id_type=MESH,
    )
    across.start()
    across.wait()

    ex_f[...] = ex[...].astype(F32)

    def first(r):
        return ex_f[pl.ds(r, 32, stride=32), :]

    cls_q = jnp.concatenate([first(i) for i in range(6)], axis=1)
    cls_0 = jnp.concatenate([first(6 + i) for i in range(6)], axis=1).astype(BF16)
    cls_1 = jnp.concatenate([first(12 + i) for i in range(6)], axis=1).astype(BF16)
    metas = first(18)
    metas_t = metas.T
    s0 = score_scale * dot_nt(cls_q.astype(BF16), cls_0)
    s1 = score_scale * dot_nt(cls_q.astype(BF16), cls_1)
    col = iota((1, 32), 1)
    passage = (4 * lax.rem(col, 16) + 2 * lax.div(col, 16)).astype(F32)
    at_pos, at_neg, wanted = metas[:, 2:3], metas[:, 3:4], metas[:, 4:5] + metas[:, 5:6] + metas[:, 6:7]
    pos0, pos1 = at_pos == passage, at_pos == passage + 1.0
    neg0, neg1 = at_neg == passage, at_neg == passage + 1.0
    m0 = jnp.where((metas_t[0:1, :] > 0.5) | pos0, s0, -1e30)
    m1 = jnp.where((metas_t[1:2, :] > 0.5) | pos1, s1, -1e30)
    peak = jnp.maximum(jnp.max(m0, axis=1, keepdims=True), jnp.max(m1, axis=1, keepdims=True))
    total = jnp.sum(jnp.exp(m0 - peak), axis=1, keepdims=True) + jnp.sum(jnp.exp(m1 - peak), axis=1, keepdims=True)
    lse = peak + jnp.log(total)

    def picked(where0, where1):
        return jnp.sum(jnp.where(where0, s0, 0.0), axis=1, keepdims=True) + jnp.sum(
            jnp.where(where1, s1, 0.0), axis=1, keepdims=True
        )

    at_positive = picked(pos0, pos1)
    miss = at_positive - picked(neg0, neg1) - wanted
    losses = lse - at_positive + margin_weight * miss * miss
    pos0, pos1, neg0, neg1 = (hit.astype(F32) for hit in (pos0, pos1, neg0, neg1))
    ds0 = (jnp.exp(m0 - lse) - pos0 + 2.0 * margin_weight * miss * (pos0 - neg0)).astype(BF16)
    ds1 = (jnp.exp(m1 - lse) - pos1 + 2.0 * margin_weight * miss * (pos1 - neg1)).astype(BF16)
    mine = iota((32, 1), 0) == slot_me
    mine_col = iota((1, 32), 1) == slot_me
    small_o[9:10, :] = jnp.sum(jnp.where(mine, losses, 0.0), axis=0, keepdims=True) + jnp.zeros((1, 128), F32)
    dq_all = score_scale * (dot_nn(ds0, cls_0) + dot_nn(ds1, cls_1))
    d_query = jnp.sum(jnp.where(mine, dq_all, 0.0), axis=0, keepdims=True)

    def passage_grad_row(ds):
        column = jnp.sum(jnp.where(mine_col, ds.astype(F32), 0.0), axis=1, keepdims=True)
        return score_scale * jnp.sum(column * cls_q, axis=0, keepdims=True)

    d_first = (d_query, passage_grad_row(ds0), passage_grad_row(ds1))

    row32 = iota((32, 1), 0)
    for r0, at, source, add in (
        (0, 0, qg_s[...], d_first[0]), (32, 0, pg_s[0:32, :], d_first[1]), (224, 28, pg_s[192:224, :], d_first[2]),
    ):
        upstream = source.astype(F32) + jnp.where(row32 == at, add, 0.0)
        sums = ffn_norm_back(r0, upstream, sums)
    vec[...] = jnp.zeros_like(vec)
    vec[5:6, :] = jnp.sum(sums[2], axis=0, keepdims=True)
    vec[6:7, :] = jnp.sum(sums[0], axis=0, keepdims=True)
    vec[7:8, :] = jnp.sum(sums[1], axis=0, keepdims=True)

    def chunk(p, h):
        return g_s.at[p, h] if p < 4 else wb.at[h, p - 4]

    z_slot, r_slot = {}, {}
    for at, way in enumerate(ROUTE):
        for kind, slots in (("z", z_slot), ("r", r_slot)):
            if way[0] == kind:
                slots[(at // 3, at % 3)] = len(slots)
    inner = (zz == 1) | (zz == 2)
    mate = zz + 1 - 2 * lax.rem(zz, 2)
    far = 2 - 2 * lax.div(zz, 2)

    def route(p, h):
        return ROUTE[3 * p + h]

    def remote(source, target, send, recv, device):
        return pltpu.make_async_remote_copy(
            src_ref=source, dst_ref=target, send_sem=send, recv_sem=recv, device_id=(device,), device_id_type=MESH,
        )

    def step_c(p, h):
        return [remote(chunk(p, h).at[1 - core], rc.at[p % 2, h], c_send.at[p, h], c_recv.at[p, h], partner)]

    def along_z(p, h, pick, target):
        steps = []
        for hop in range(1, 4):
            to = lax.rem(zz + hop, 4)
            steps.append(remote(
                pick(to), target(hop - 1), z_send.at[p, h, hop - 1], z_recv.at[p, h, hop - 1], to * 8 + plane,
            ))
        return steps

    def step_1(p, h):
        mine, way = chunk(p, h), route(p, h)
        if way[0] == "z":
            return along_z(p, h, lambda to: mine.at[core, to], lambda i: rw.at[z_slot[(p, h)], i])
        away = mine.at[core, :, :, 1 - xx] if way == "xyz" else mine.at[core, :, 1 - yy]
        return [remote(away, ra.at[p, h], a_send.at[p, h], a_recv.at[p, h], x_peer if way == "xyz" else y_peer)]

    def step_2(p, h):
        mine, way = chunk(p, h), route(p, h)
        if way in ("zyx", "ryx"):
            away, target = mine.at[core, zz, 1 - yy], rb.at[p, h, 0:2]
        elif way in ("zxy", "rxy"):
            away, target = mine.at[core, zz, :, 1 - xx], rb.at[p, h, 0:2]
        elif way == "xyz":
            away, target = mine.at[core, :, 1 - yy, xx], rb.at[p, h]
        else:
            away, target = mine.at[core, :, yy, 1 - xx], rb.at[p, h]
        return [remote(away, target, b_send.at[p, h], b_recv.at[p, h], x_peer if way[1] == "x" else y_peer)]

    def step_3(p, h):
        mine = chunk(p, h)
        way = route(p, h)
        if way[0] in "zr":
            away = mine.at[core, zz, yy, 1 - xx] if way[2] == "x" else mine.at[core, zz, 1 - yy, xx]
            return [remote(
                away, rz.at[p, h, 0], a_send.at[p, h], a_recv.at[p, h], x_peer if way[2] == "x" else y_peer,
            )]
        return along_z(p, h, lambda to: mine.at[core, to, yy, xx], lambda i: rz.at[p, h, i])

    def begin(steps):
        for step in steps:
            step.start()

    def finish_steps(steps):
        for step in steps:
            step.wait()

    def mate_step(p, h):
        return remote(
            chunk(p, h).at[core, mate], rw_mate.at[r_slot[(p, h)]], z_send.at[p, h, 0], z_recv.at[p, h, 0],
            mate * 8 + plane,
        )

    def far_step(p, h):
        return remote(
            chunk(p, h).at[core, pl.ds(far, 2)], rw_far.at[r_slot[(p, h)]], z_send.at[p, h, 1], z_recv.at[p, h, 1],
            mate * 8 + plane,
        )

    def relay_step(p, h, i):
        return remote(
            chunk(p, h).at[core, far + i], rw_in.at[r_slot[(p, h)]], r_send.at[r_slot[(p, h)], i], z_recv.at[p, h, 2],
            (far + i) * 8 + plane,
        )

    def start_relay(p, h):
        mate_step(p, h).start()

        @pl.when(jnp.logical_not(inner))
        def _():
            far_step(p, h).start()

    def relay_on(p, h):
        @pl.when(inner)
        def _():
            far_step(p, h).wait_recv()

            def add(i, carry):
                for y in range(2):
                    for x in range(2):
                        chunk(p, h)[core, far + i, y, x] += rw_far[r_slot[(p, h)], i, y, x]
                return carry

            lax.fori_loop(0, 2, add, 0)
            for i in range(2):
                relay_step(p, h, i).start()

        @pl.when(jnp.logical_not(inner))
        def _():
            far_step(p, h).wait_send()

    def end_relay(p, h):
        mate_step(p, h).wait()
        relay_step(p, h, 0).wait_recv()

        @pl.when(inner)
        def _():
            for i in range(2):
                relay_step(p, h, i).wait_send()

        mine, at = chunk(p, h), r_slot[(p, h)]

        def add(y, carry):
            for x in range(2):
                total = mine[core, zz, y, x].astype(F32) + rw_mate[at, y, x].astype(F32) + rw_in[at, y, x].astype(F32)
                mine[core, zz, y, x] = total.astype(BF16)
            return carry

        lax.fori_loop(0, 2, add, 0)
        begin(step_2(p, h))

    def start_c(p, h):
        if p >= 2:
            pl.semaphore_wait(credit.at[p % 2, h], 1)
        begin(step_c(p, h))

    def end_c(p, h):
        finish_steps(step_c(p, h))

        def add(z, carry):
            for y in range(2):
                for x in range(2):
                    chunk(p, h)[core, z, y, x] += rc[p % 2, h, z, y, x]
            return carry

        lax.fori_loop(0, 4, add, 0)
        if route(p, h)[0] == "r":
            start_relay(p, h)
        else:
            begin(step_1(p, h))
        if p < 4:
            pl.semaphore_signal(credit.at[p % 2, h], inc=1, device_id=(partner,), device_id_type=MESH)

    def end_1(p, h):
        finish_steps(step_1(p, h))
        mine, way = chunk(p, h), route(p, h)
        if way[0] == "z":
            def add(y, carry):
                for x in range(2):
                    total = mine[core, zz, y, x].astype(F32)
                    for i in range(3):
                        total += rw[z_slot[(p, h)], i, y, x].astype(F32)
                    mine[core, zz, y, x] = total.astype(BF16)
                return carry

            lax.fori_loop(0, 2, add, 0)
        else:
            def add(z, carry):
                for i in range(2):
                    if way == "yxz":
                        mine[core, z, yy, i] += ra[p, h, z, i]
                    else:
                        mine[core, z, i, xx] += ra[p, h, z, i]
                return carry

            lax.fori_loop(0, 4, add, 0)
        begin(step_2(p, h))

    def end_2(p, h):
        finish_steps(step_2(p, h))
        mine = chunk(p, h)
        way = route(p, h)
        if way[0] in "zr":
            for i in range(2):
                if way[1] == "y":
                    mine[core, zz, yy, i] += rb[p, h, i]
                else:
                    mine[core, zz, i, xx] += rb[p, h, i]
        else:
            def add(z, carry):
                mine[core, z, yy, xx] += rb[p, h, z]
                return carry

            lax.fori_loop(0, 4, add, 0)
        begin(step_3(p, h))

    outs = []

    def end_3(p, h):
        finish_steps(step_3(p, h))
        total = chunk(p, h)[core, zz, yy, xx].astype(F32)
        for i in range(1 if route(p, h)[0] in "zr" else 3):
            total += rz[p, h, i].astype(F32)
        parts[p, h] = total
        at = WIDE * h
        if p < 2:
            targets = [wbg.at[pl.ds(48 * p, 48), pl.ds(at, WIDE)]]
        elif p < 4:
            at += (p - 2) * 2 * D
            targets = [wig.at[:, pl.ds(at, WIDE)], wig.at[:, pl.ds(at + D, WIDE)]]
        else:
            targets = [ref.at[:, pl.ds(at, WIDE)] for ref in ((wvg, wog) if p == 4 else (wqg, wkg))]
        rows = 48 // len(targets)
        for i, target in enumerate(targets):
            outs.append(pltpu.make_async_copy(parts.at[p, h, pl.ds(rows * i, rows)], target, part_sem.at[p, h, i]))
            outs[-1].start()

    def store_grad(p, h, grad):
        for i in range(32):
            chunk(p, h)[i % 2, i // 8, (i // 4) % 2, (i // 2) % 2] = grad[i]

    def back_grad(p, h):
        left = jnp.concatenate([actT[96 * i + 48 * p:96 * i + 48 * p + 48, :] for i in range(32)], axis=0)
        grad = dot_nn(left, ml[:, WIDE * h:WIDE * h + WIDE]).astype(BF16)
        store_grad(p, h, grad.reshape(32, 48, WIDE))

    def pair_grad(p, h, left_0, right_0, left_1, right_1):
        cols = pl.ds(WIDE * h, WIDE)
        grad_0 = dot_nn(left_0[...], right_0[:, cols]).reshape(32, 24, WIDE)
        grad_1 = dot_nn(left_1[...], right_1[:, cols]).reshape(32, 24, WIDE)
        store_grad(p, h, jnp.concatenate([grad_0, grad_1], axis=1).astype(BF16))

    def in_grad(p, h):
        at = (p - 2) * 2 * D
        pair_grad(p, h, mlT, gp.at[:, pl.ds(at, D)], mlT, gp.at[:, pl.ds(at + D, D)])

    def inner_grad(t):
        cols = pl.ds(t * D, D)
        weight = wb_tile(t)
        tmp_a[...] = dot_nt(ml[0:256, :], weight)
        tmp_b[0:224, :] = dot_nt(ml[256:480, :], weight)
        total = zero8
        for ref, start, size in ((tmp_a, 0, 256), (tmp_b, 256, 224)):
            for at, count in blocks(0, size, 16):
                rows = pl.ds(start + at, count)
                rounded = (ref[at:at + count, :] * gp[rows, cols].astype(F32)).astype(BF16)
                gp[rows, cols] = rounded
                total = total + fold8(rounded.astype(F32))
        vec[8 + t:9 + t, :] = jnp.sum(total, axis=0, keepdims=True)

    def middle_grad(t):
        cols = pl.ds(t * D, D)
        n2[...] += dot_nt(gp[:, cols], wi[:, cols])

    def attn_norm_back():
        def block(i, sums):
            rows = pl.ds(pl.multiple_of(i * 32, 32), 32)
            upstream, unit = n2[rows, :], n1[rows, :]
            scaled = upstream * gain1
            hidden_grad = r1[rows, :] * (
                scaled
                - jnp.mean(scaled, axis=-1, keepdims=True)
                - unit * jnp.mean(scaled * unit, axis=-1, keepdims=True)
            )
            n1[rows, :] = hidden_grad
            rounded = hidden_grad.astype(BF16)
            ml[rows, :] = rounded
            return (
                sums[0] + fold8(upstream * unit), sums[1] + fold8(upstream), sums[2] + fold8(rounded.astype(F32)),
            )

        sums = lax.fori_loop(0, 15, block, (zero8, zero8, zero8))
        vec[2:3, :] = jnp.sum(sums[2], axis=0, keepdims=True)
        vec[3:4, :] = jnp.sum(sums[0], axis=0, keepdims=True)
        vec[4:5, :] = jnp.sum(sums[1], axis=0, keepdims=True)

    def context_grad():
        c_s[...] = dot_nt(ml[...], wo[...]).astype(BF16)

    def query_slot_back():
        q_rows, k_rows, v_rows = spread(q_s[0:32, :]), k_s[0:32, :], v_s[0:32, :]
        dc_rows = spread(c_s[0:32, :])
        soft = pq_s[...]
        dp = dot_nt(v_rows, dc_rows)
        soft_f = soft.astype(F32)
        ds = (soft_f * (dp - jnp.sum(soft_f * dp, axis=0, keepdims=True))).astype(BF16)
        v_s[0:32, :] = dot_nn(soft, dc_rows).astype(BF16)
        k_s[0:32, :] = dot_nn(ds, q_rows).astype(BF16)
        q_s[0:32, :] = (0.125 * gather_heads(dot_tn(ds, k_rows))).astype(BF16)

    def attend_back_pair(pair):
        lanes = pl.ds(pl.multiple_of(pair * 128, 128), 128)
        for slot in range(2):
            low_at = 12 * slot
            rows = pl.ds(32 + 208 * slot, WIN)
            keys, queries, values = k_s[rows, lanes], q_s[rows, lanes], v_s[rows, lanes]
            inside = ((key_at >= low_at) & (key_at < low_at + SLOT)).astype(BF16)
            upstream = c_s[rows, lanes] * inside
            keys_t = keys.T
            parts, dv, dk = [], 0.0, 0.0
            for h in range(2):
                p = p_s[slot, 2 * pair + h]
                dc = upstream * half[h]
                dp = dot_nt(values, dc)
                pf = p.astype(F32)
                ds = (pf * (dp - jnp.sum(pf * dp, axis=0, keepdims=True))).astype(BF16)
                dv += dot_nn(p, dc)
                dk += dot_nn(ds, queries * half[h])
                parts.append(dot_nn(keys_t, ds)[64 * h:64 * h + 64, :])
            dq = 0.125 * jnp.concatenate(parts, axis=0).T
            for ref, new in ((q_s, dq), (k_s, dk), (v_s, dv)):
                if slot == 0:
                    ref[32:240, lanes] = new[0:208].astype(BF16)
                    old = ref[240:272, lanes].astype(F32)
                    ref[240:272, lanes] = jnp.where(iota((32, 128), 0) < 12, new[208:240], old).astype(BF16)
                else:
                    old = ref[240:256, lanes].astype(F32)
                    ref[240:256, lanes] = jnp.where(iota((16, 128), 0) >= 12, new[0:16], old).astype(BF16)
                    ref[256:480, lanes] = new[16:240].astype(BF16)

    def attend_back(first, count):
        def step(i, carry):
            attend_back_pair(first + i)
            return carry

        lax.fori_loop(0, count, step, 0)

    def column_sum(ref):
        def step(i, total):
            return total + fold8(ref[pl.ds(pl.multiple_of(i * 32, 32), 32), :].astype(F32))

        return jnp.sum(lax.fori_loop(0, 15, step, zero8), axis=0, keepdims=True)

    def column_sums():
        vec[0:1, :] = column_sum(q_s)
        vec[1:2, :] = column_sum(v_s)

    def token_grad(grads, weight):
        n1[...] += dot_nt(grads[...], weight[...])

    out_qg = pltpu.make_async_copy(n1.at[0:32, :], qtg_h, out_sem.at[2])
    out_pg = pltpu.make_async_copy(n1.at[32:472, :], ptg_h, out_sem.at[3])

    def send_tokens():
        out_qg.start()
        out_pg.start()

    def vec_step(i):
        return remote(vec, vecr.at[i], v_send.at[i], v_recv.at[i], (partner, x_peer, y_peer)[i])

    def vec_part(whole, to):
        device = to * 8 + plane
        narrow = pltpu.roll(whole[0:8], D - 24 * device, 1)[:, 0:128]
        wide = pltpu.roll(whole[8:16], D - 96 * plane, 1)[:, 0:128]
        wide = jnp.sum(jnp.where(iota((8, 128), 0) == to, wide, 0.0), axis=0, keepdims=True)
        return jnp.concatenate([narrow, wide, jnp.zeros((7, 128), F32)], axis=0)

    def vec_z():
        return [
            remote(
                vecs.at[hop - 1], vecz.at[hop - 1], v_send.at[2 + hop], v_recv.at[2 + hop],
                lax.rem(zz + hop, 4) * 8 + plane,
            )
            for hop in range(1, 4)
        ]

    def vec_on(i):
        if i > 0:
            vec_step(i - 1).wait()
            vec[...] += vecr[i - 1]
        if i < 3:
            vec_step(i).start()
        else:
            whole = vec[...]
            for hop in range(1, 4):
                vecs[hop - 1] = vec_part(whole, lax.rem(zz + hop, 4))
            begin(vec_z())

    def vec_end():
        finish_steps(vec_z())
        part = vec_part(vec[...], zz) + vecz[0] + vecz[1] + vecz[2]
        small_o[0:9, :] = part[0:9]
        outs.append(pltpu.make_async_copy(small_o, small_h, out_sem.at[4]))
        outs[-1].start()

    def serve(at, p, h):
        relayed = route(p, h)[0] == "r"
        ((relay_on, end_relay, end_2, end_3) if relayed else (end_1, end_2, end_3))[at](p, h)

    pieces_of = {
        "wback": back_grad, "dinner": inner_grad, "win": in_grad, "dmid": middle_grad, "lnback": attn_norm_back,
        "dctx": context_grad, "qslot": query_slot_back, "attn": attend_back, "sums": column_sums,
        "wvo": lambda h: pair_grad(4, h, xT, v_s, cT, ml), "wqk": lambda h: pair_grad(5, h, xT, q_s, xT, k_s),
        "tq": lambda: token_grad(q_s, wq), "tk": lambda: token_grad(k_s, wk), "tv": lambda: token_grad(v_s, wv),
        "tout": send_tokens, "vec": vec_on, "vecend": vec_end,
        "c": start_c, "ec": end_c, "e1": lambda p, h: serve(0, p, h), "e2": lambda p, h: serve(1, p, h),
        "e3": lambda p, h: serve(2, p, h), "e4": lambda p, h: serve(3, p, h),
    }
    for name, *operands in ORDER:
        pieces_of[name](*operands)

    out_q.wait()
    out_p.wait()
    out_qg.wait()
    out_pg.wait()
    for out in outs:
        out.wait()


def hand_on_kernel(*refs):
    count = 10
    sources, small = refs[:count], refs[count]
    targets, vectors = refs[count + 1:2 * count + 1], refs[2 * count + 1:2 * count + 11]
    held, rest = refs[2 * count + 11:3 * count + 11], refs[3 * count + 11:]
    small_v, lines, in_sem, out_sem = rest[0], rest[1:11], rest[11], rest[12]
    whole = [(i, None) for i in range(count) if i != 3]
    pieces = [(3, pl.ds(at, size)) for at, size in blocks(0, 440, 112)] + whole
    into, out = [], []
    for at, (i, rows) in enumerate(pieces):
        source, kept, target = (ref if rows is None else ref.at[rows, :] for ref in (sources[i], held[i], targets[i]))
        into.append(pltpu.make_async_copy(source, kept, in_sem.at[at]))
        out.append(pltpu.make_async_copy(kept, target, out_sem.at[at]))
    last = pltpu.make_async_copy(small, small_v, in_sem.at[len(pieces)])
    last.start()
    for copy in into:
        copy.start()
    last.wait()
    for at, ref in enumerate(lines[:8]):
        ref[...] = small_v[at:at + 1, 0:24].reshape(24)
    lines[8][...] = small_v[8:9, 0:96].reshape(96)
    lines[9][...] = small_v[9:10, 0:1].reshape(1)
    for at, (line, vector) in enumerate(zip(lines, vectors)):
        out.append(pltpu.make_async_copy(line, vector, out_sem.at[len(pieces) + at]))
        out[-1].start()
    for first, second in zip(into, out):
        first.wait()
        second.start()
    for copy in out:
        copy.wait()


def on_device_small(*operands):
    (
        query_tokens, passage_tokens, query_lengths, passage_lengths, passage_valid, positives, negatives,
        teacher_margins, query_grad, passage_grad, weight_query, bias_query, weight_key, weight_value, bias_value,
        weight_out, bias_out, gain_attn, shift_attn, weight_in, bias_in, weight_back, bias_back, gain_ffn, shift_ffn,
    ) = operands
    hbm, smem = (pl.BlockSpec(memory_space=space) for space in (pl.ANY, pltpu.SMEM))
    shape = jax.ShapeDtypeStruct
    slabs = (2, 2, 4, 2, 2, 48, D)
    large = (
        shape((32, D), BF16), shape((440, D), BF16), shape((32, D), F32), shape((440, D), F32), shape((24, D), F32),
        shape((24, D), F32), shape((24, D), F32), shape((24, D), F32), shape((24, FF), F32), shape((96, D), F32),
    )
    outs = pl.pallas_call(
        layer_kernel,
        out_shape=(
            *large, shape((16, 128), F32),
        ),
        in_specs=[
            hbm, hbm, smem, hbm, hbm, smem, smem, smem, hbm, hbm,
            *(hbm,) * 15,
        ],
        out_specs=(hbm,) * 11,
        scratch_shapes=[
            pltpu.VMEM((2,), jnp.int32), pltpu.VMEM((2,), jnp.int32),
            *(pltpu.VMEM((size,), BF16) for size in (D, D, D, D, D, FF, D, D, D)),
            pltpu.VMEM((D, D), BF16), pltpu.VMEM((D, D), BF16), pltpu.VMEM((D, D), BF16), pltpu.VMEM((D, D), BF16),
            pltpu.VMEM((D, FF), BF16), pltpu.VMEM((3, 2, 2, 4, 2, 2, 48, WIDE), BF16),
            pltpu.VMEM((440, D), BF16), pltpu.VMEM((ROWS, D), BF16), pltpu.VMEM((D, ROWS), BF16),
            pltpu.VMEM((ROWS, D), BF16), pltpu.VMEM((ROWS, D), BF16), pltpu.VMEM((ROWS, D), BF16),
            pltpu.VMEM((2, 12, WIN, WIN), BF16), pltpu.VMEM((32, 384), BF16),
            pltpu.VMEM((ROWS, D), BF16), pltpu.VMEM((D, ROWS), BF16),
            pltpu.VMEM((ROWS, D), F32), pltpu.VMEM((ROWS, D), F32), pltpu.VMEM((ROWS, 1), F32), pltpu.VMEM((ROWS, 1), F32),
            pltpu.VMEM((ROWS, D), BF16), pltpu.VMEM((D, ROWS), BF16),
            pltpu.VMEM((256, D), BF16), pltpu.VMEM((256, D), BF16), pltpu.VMEM((FF, ROWS), BF16),
            pltpu.VMEM((256, D), F32), pltpu.VMEM((256, D), F32),
            pltpu.VMEM((ROWS, FF), BF16),
            pltpu.VMEM((32, D), BF16), pltpu.VMEM((440, D), BF16), pltpu.VMEM((32, D), BF16), pltpu.VMEM((440, D), BF16),
            pltpu.VMEM((1024, 128), BF16), pltpu.VMEM((1024, 128), F32),
            pltpu.VMEM((16, D), F32), pltpu.VMEM((3, 16, D), F32), pltpu.VMEM((3, 16, 128), F32), pltpu.VMEM((3, 16, 128), F32),
            pltpu.VMEM((16, 128), F32), pltpu.VMEM((6, 3, 48, WIDE), F32),
            pltpu.VMEM((4, 3, 2, 4, 2, 2, 48, WIDE), BF16),
            pltpu.VMEM((2, 3, 4, 2, 2, 48, WIDE), BF16), pltpu.VMEM((6, 3, 4, 2, 48, WIDE), BF16),
            pltpu.VMEM((6, 3, 4, 48, WIDE), BF16), pltpu.VMEM((6, 3, 3, 48, WIDE), BF16),
            pltpu.VMEM((max(1, sum(way[0] == "z" for way in ROUTE)), 3, 2, 2, 48, WIDE), BF16),
            pltpu.VMEM((RELAYS, 2, 2, 48, WIDE), BF16), pltpu.VMEM((RELAYS, 2, 2, 2, 48, WIDE), BF16),
            pltpu.VMEM((RELAYS, 2, 2, 48, WIDE), BF16),
            pltpu.SemaphoreType.DMA((32,)), pltpu.SemaphoreType.DMA((5,)), pltpu.SemaphoreType.DMA((6, 3, 2)),
            pltpu.SemaphoreType.DMA((16,)), pltpu.SemaphoreType.DMA((16,)),
            pltpu.SemaphoreType.DMA((6, 3)), pltpu.SemaphoreType.DMA((6, 3)),
            pltpu.SemaphoreType.DMA((6, 3)), pltpu.SemaphoreType.DMA((6, 3)),
            pltpu.SemaphoreType.DMA((6, 3)), pltpu.SemaphoreType.DMA((6, 3)),
            pltpu.SemaphoreType.DMA((6, 3, 3)), pltpu.SemaphoreType.DMA((6, 3, 3)), pltpu.SemaphoreType.DMA((RELAYS, 2)),
            pltpu.SemaphoreType.DMA((6,)), pltpu.SemaphoreType.DMA((6,)),
            pltpu.SemaphoreType.REGULAR((2, 3)),
        ],
        compiler_params=pltpu.CompilerParams(
            collective_id=0, has_side_effects=True, vmem_limit_bytes=64 * 1024 * 1024 - 65536,
        ),
        name="encoder_layer",
    )(
        query_tokens, passage_tokens, query_lengths, passage_lengths, passage_valid, positives, negatives,
        teacher_margins, query_grad, passage_grad, weight_query, bias_query, weight_key, weight_value, bias_value,
        weight_out, bias_out, gain_attn, shift_attn, weight_in, bias_in, weight_back.reshape(slabs), bias_back,
        gain_ffn, shift_ffn,
    )
    done = pl.pallas_call(
        hand_on_kernel,
        out_shape=large + (shape((24,), F32),) * 8 + (shape((96,), F32), shape((1,), F32)),
        in_specs=[hbm] * 11,
        out_specs=(hbm,) * 20,
        scratch_shapes=[pltpu.VMEM(out.shape, out.dtype) for out in large]
        + [pltpu.VMEM((16, 128), F32)] + [pltpu.VMEM((size,), F32) for size in (24,) * 8 + (96, 1)]
        + [pltpu.SemaphoreType.DMA((24,)), pltpu.SemaphoreType.DMA((24,))],
        name="hand_on",
    )(*outs)
    qout, pout, qtg, ptg, wqg, wkg, wvg, wog, wig, wbg, bqg, bvg, bog, gag, sag, bbg, gfg, sfg, big, loss = done
    return (
        qout, pout, loss, qtg, ptg, wqg, bqg, wkg, wvg, bvg, wog, bog, gag, sag, wig, big, wbg, bbg, gfg, sfg,
    )


def solution(mesh):
    return jax.shard_map(
        on_device_small if mesh.shape["dp"] == 32 else on_device,
        mesh=mesh,
        in_specs=(
            P("dp", None),
            P("dp", None),
            P("dp"),
            P("dp"),
            P("dp"),
            P("dp"),
            P("dp"),
            P("dp"),
            P("dp", None),
            P("dp", None),
            P(),
            P(),
            P(),
            P(),
            P(),
            P(),
            P(),
            P(),
            P(),
            P(),
            P(),
            P(),
            P(),
            P(),
            P(),
        ),
        out_specs=(
            P("dp", None),
            P("dp", None),
            P("dp"),
            P("dp", None),
            P("dp", None),
            P("dp", None),
            P("dp"),
            P("dp", None),
            P("dp", None),
            P("dp"),
            P("dp", None),
            P("dp"),
            P("dp"),
            P("dp"),
            P("dp", None),
            P("dp"),
            P("dp", None),
            P("dp"),
            P("dp"),
            P("dp"),
        ),
        check_vma=False,
    )
```

```python
import jax
import jax.numpy as jnp
from jax import lax
from jax.experimental import pallas as pl
from jax.experimental.pallas import tpu as pltpu
from jax.sharding import PartitionSpec as P

D = 768
HEADS = 12
HEAD_DIM = 64


ln_eps = 1e-12
score_scale = 0.0625
margin_weight = 0.5
root_half = 0.7071067811865476
inv_root_tau = 0.3989422804014327


def matmul(left, right):
    return jnp.dot(left, right, preferred_element_type=jnp.float32)


def left_across(left, right):
    return lax.dot_general(
        left, right, (((0,), (0,)), ((), ())), preferred_element_type=jnp.float32
    )


def right_across(left, right):
    return lax.dot_general(
        left, right, (((1,), (1,)), ((), ())), preferred_element_type=jnp.float32
    )


def normalize(hidden, gain, shift):
    centered = hidden - jnp.mean(hidden, axis=-1, keepdims=True)
    inv_std = lax.rsqrt(jnp.mean(centered * centered, axis=-1, keepdims=True) + ln_eps)
    unit_rows = centered * inv_std
    return (unit_rows * gain.astype(jnp.float32) + shift.astype(jnp.float32), unit_rows, inv_std)


def normalize_back(upstream, unit_rows, inv_std, gain):
    scaled = upstream * gain.astype(jnp.float32)
    hidden_grad = inv_std * (
        scaled
        - jnp.mean(scaled, axis=-1, keepdims=True)
        - unit_rows * jnp.mean(scaled * unit_rows, axis=-1, keepdims=True)
    )
    return (hidden_grad, jnp.sum(upstream * unit_rows, axis=0), jnp.sum(upstream, axis=0))


def gelu_exact(inputs):
    return 0.5 * inputs * (1.0 + lax.erf(inputs * root_half))


def gelu_slope(inputs):
    return 0.5 * (1.0 + lax.erf(inputs * root_half)) + inputs * inv_root_tau * jnp.exp(
        -0.5 * inputs * inputs
    )


def head_scores(query_heads, key_heads, lengths):
    slot_length = query_heads.shape[1]
    allowed = (lax.iota(jnp.int32, slot_length)[None, :] < lengths[:, None])[:, None, None, :]
    raw_scores = 0.125 * jnp.einsum(
        "bqhd,bkhd->bhqk", query_heads, key_heads, preferred_element_type=jnp.float32
    )
    return jnp.where(allowed, raw_scores, -1000000000.0)


def encode_forward(tokens, lengths, params):
    (
        weight_query,
        bias_query,
        weight_key,
        weight_value,
        bias_value,
        weight_out,
        bias_out,
        gain_attn,
        shift_attn,
        weight_in,
        bias_in,
        weight_back,
        bias_back,
        gain_ffn,
        shift_ffn,
    ) = params
    slot_count = lengths.shape[0]
    row_count = tokens.shape[0]
    split_heads = (slot_count, row_count // slot_count, HEADS, HEAD_DIM)
    queries = (matmul(tokens, weight_query) + bias_query.astype(jnp.float32)).astype(jnp.bfloat16)
    keys_all = matmul(tokens, weight_key).astype(jnp.bfloat16)
    values_all = (matmul(tokens, weight_value) + bias_value.astype(jnp.float32)).astype(
        jnp.bfloat16
    )
    scores = head_scores(queries.reshape(split_heads), keys_all.reshape(split_heads), lengths)
    peak_score = jnp.max(scores, axis=-1, keepdims=True)
    exp_scores = jnp.exp(scores - peak_score)
    row_total = jnp.sum(exp_scores, axis=-1, keepdims=True)
    soft_low = (exp_scores / row_total).astype(jnp.bfloat16)
    log_total = peak_score + jnp.log(row_total)
    context = jnp.einsum(
        "bhqk,bkhd->bqhd",
        soft_low,
        values_all.reshape(split_heads),
        preferred_element_type=jnp.float32,
    )
    context = context.reshape(row_count, D).astype(jnp.bfloat16)
    attn_sum = (
        tokens.astype(jnp.float32) + matmul(context, weight_out) + bias_out.astype(jnp.float32)
    )
    middle, unit_attn, inv_attn = normalize(attn_sum, gain_attn, shift_attn)
    middle_low = middle.astype(jnp.bfloat16)
    inner_act = matmul(middle_low, weight_in) + bias_in.astype(jnp.float32)
    gelu_low = gelu_exact(inner_act).astype(jnp.bfloat16)
    ffn_sum = middle + matmul(gelu_low, weight_back) + bias_back.astype(jnp.float32)
    output, unit_ffn, inv_ffn = normalize(ffn_sum, gain_ffn, shift_ffn)
    kept = (
        queries,
        keys_all,
        values_all,
        log_total,
        context,
        unit_attn,
        inv_attn,
        middle_low,
        inner_act,
        gelu_low,
        unit_ffn,
        inv_ffn,
    )
    return (output.astype(jnp.bfloat16), kept)


def ffn_backward(upstream, kept, params):
    (
        queries,
        keys_all,
        values_all,
        log_total,
        context,
        unit_attn,
        inv_attn,
        middle_low,
        inner_act,
        gelu_low,
        unit_ffn,
        inv_ffn,
    ) = kept
    weight_in, weight_back, gain_ffn = (params[9], params[11], params[13])
    ffn_grad, gain_grad, shift_grad = normalize_back(upstream, unit_ffn, inv_ffn, gain_ffn)
    branch_low = ffn_grad.astype(jnp.bfloat16)
    back_weight_grad = left_across(gelu_low, branch_low)
    back_bias_grad = jnp.sum(branch_low, axis=0, dtype=jnp.float32)
    inner_low = (right_across(branch_low, weight_back) * gelu_slope(inner_act)).astype(jnp.bfloat16)
    in_weight_grad = left_across(middle_low, inner_low)
    in_bias_grad = jnp.sum(inner_low, axis=0, dtype=jnp.float32)
    middle_grad = ffn_grad + right_across(inner_low, weight_in)
    return (
        middle_grad,
        (in_weight_grad, in_bias_grad, back_weight_grad, back_bias_grad, gain_grad, shift_grad),
    )


def attention_backward(middle_grad, tokens, lengths, kept, params):
    (
        queries,
        keys_all,
        values_all,
        log_total,
        context,
        unit_attn,
        inv_attn,
        middle_low,
        inner_act,
        gelu_low,
        unit_ffn,
        inv_ffn,
    ) = kept
    weight_query, weight_key, weight_value, weight_out, gain_attn = (
        params[0],
        params[2],
        params[3],
        params[5],
        params[7],
    )
    slot_count = lengths.shape[0]
    row_count = tokens.shape[0]
    split_heads = (slot_count, row_count // slot_count, HEADS, HEAD_DIM)
    attn_grad, gain_grad, shift_grad = normalize_back(middle_grad, unit_attn, inv_attn, gain_attn)
    attn_low = attn_grad.astype(jnp.bfloat16)
    out_weight_grad = left_across(context, attn_low)
    out_bias_grad = jnp.sum(attn_low, axis=0, dtype=jnp.float32)
    context_grad = right_across(attn_low, weight_out).astype(jnp.bfloat16).reshape(split_heads)
    query_heads = queries.reshape(split_heads)
    key_heads = keys_all.reshape(split_heads)
    value_heads = values_all.reshape(split_heads)
    soft_full = jnp.exp(head_scores(query_heads, key_heads, lengths) - log_total)
    soft_grad = jnp.einsum(
        "bqhd,bkhd->bhqk", context_grad, value_heads, preferred_element_type=jnp.float32
    )
    value_grad = jnp.einsum(
        "bhqk,bqhd->bkhd",
        soft_full.astype(jnp.bfloat16),
        context_grad,
        preferred_element_type=jnp.float32,
    )
    value_grad = value_grad.reshape(row_count, D).astype(jnp.bfloat16)
    score_low = (
        soft_full * (soft_grad - jnp.sum(soft_full * soft_grad, axis=-1, keepdims=True))
    ).astype(jnp.bfloat16)
    query_grad_low = 0.125 * jnp.einsum(
        "bhqk,bkhd->bqhd", score_low, key_heads, preferred_element_type=jnp.float32
    )
    query_grad_low = query_grad_low.reshape(row_count, D).astype(jnp.bfloat16)
    key_grad_low = 0.125 * jnp.einsum(
        "bhqk,bqhd->bkhd", score_low, query_heads, preferred_element_type=jnp.float32
    )
    key_grad_low = key_grad_low.reshape(row_count, D).astype(jnp.bfloat16)
    token_grad = (
        attn_grad
        + right_across(query_grad_low, weight_query)
        + right_across(key_grad_low, weight_key)
        + right_across(value_grad, weight_value)
    )
    grads = (
        left_across(tokens, query_grad_low),
        jnp.sum(query_grad_low, axis=0, dtype=jnp.float32),
        left_across(tokens, key_grad_low),
        left_across(tokens, value_grad),
        jnp.sum(value_grad, axis=0, dtype=jnp.float32),
        out_weight_grad,
        out_bias_grad,
        gain_grad,
        shift_grad,
    )
    return (token_grad, grads)


def on_device(
    query_tokens,
    passage_tokens,
    query_lengths,
    passage_lengths,
    passage_valid,
    positives,
    negatives,
    teacher_margins,
    query_grad,
    passage_grad,
    weight_query,
    bias_query,
    weight_key,
    weight_value,
    bias_value,
    weight_out,
    bias_out,
    gain_attn,
    shift_attn,
    weight_in,
    bias_in,
    weight_back,
    bias_back,
    gain_ffn,
    shift_ffn,
):
    params = (
        weight_query,
        bias_query,
        weight_key,
        weight_value,
        bias_value,
        weight_out,
        bias_out,
        gain_attn,
        shift_attn,
        weight_in,
        bias_in,
        weight_back,
        bias_back,
        gain_ffn,
        shift_ffn,
    )
    query_out, query_kept = encode_forward(query_tokens, query_lengths, params)
    passage_out, passage_kept = encode_forward(passage_tokens, passage_lengths, params)
    query_slots = query_lengths.shape[0]
    passage_slots = passage_lengths.shape[0]
    cls_query = query_out.reshape(query_slots, -1, D)[:, 0]
    cls_passage = passage_out.reshape(passage_slots, -1, D)[:, 0]
    valid_low = passage_valid.astype(jnp.bfloat16)

    def score_piece(cls_piece, valid_piece):
        scores = score_scale * right_across(cls_query, cls_piece)
        position = lax.iota(jnp.int32, cls_piece.shape[0])
        is_positive = position[None, :] == positives[:, None]
        is_negative = position[None, :] == negatives[:, None]
        allowed = (valid_piece[None, :] > 0.5) | is_positive
        return (scores, allowed, is_positive, is_negative)

    peak_score = jnp.full((query_slots,), -1e30, jnp.float32)
    scores, allowed, is_positive, is_negative = score_piece(
        lax.all_gather(cls_passage, "dp", axis=0, tiled=True),
        lax.all_gather(valid_low, "dp", axis=0, tiled=True),
    )
    masked = jnp.where(allowed, scores, -1e30)
    new_peak = jnp.maximum(peak_score, jnp.max(masked, axis=1))
    row_total = jnp.sum(jnp.where(allowed, jnp.exp(masked - new_peak[:, None]), 0.0), axis=1)
    positive_score = jnp.sum(jnp.where(is_positive, scores, 0.0), axis=1)
    negative_score = jnp.sum(jnp.where(is_negative, scores, 0.0), axis=1)
    peak_score, row_total, positive_score, negative_score = (
        new_peak,
        row_total,
        positive_score,
        negative_score,
    )
    all_cls, all_valid = (
        lax.all_gather(cls_passage, "dp", axis=0, tiled=True),
        lax.all_gather(valid_low, "dp", axis=0, tiled=True),
    )
    log_total = peak_score + jnp.log(row_total)
    shortfall = positive_score - negative_score - teacher_margins
    query_loss = log_total - positive_score + margin_weight * shortfall * shortfall
    scores, allowed, is_positive, is_negative = score_piece(all_cls, all_valid)
    soft_scores = jnp.where(allowed, jnp.exp(scores - log_total[:, None]), 0.0)
    positive_hit = is_positive.astype(jnp.float32)
    negative_hit = is_negative.astype(jnp.float32)
    score_grad = (
        soft_scores
        - positive_hit
        + 2.0 * margin_weight * shortfall[:, None] * (positive_hit - negative_hit)
    ).astype(jnp.bfloat16)
    cls_query_grad = score_scale * matmul(score_grad, all_cls)
    cls_passage_grad = lax.psum_scatter(
        score_scale * left_across(score_grad, cls_query), "dp", scatter_dimension=0, tiled=True
    )
    query_upstream = (
        query_grad.astype(jnp.float32)
        .reshape(query_slots, -1, D)
        .at[:, 0]
        .add(cls_query_grad)
        .reshape(-1, D)
    )
    passage_upstream = (
        passage_grad.astype(jnp.float32)
        .reshape(passage_slots, -1, D)
        .at[:, 0]
        .add(cls_passage_grad)
        .reshape(-1, D)
    )
    query_middle_grad, query_ffn = ffn_backward(query_upstream, query_kept, params)
    passage_middle_grad, passage_ffn = ffn_backward(passage_upstream, passage_kept, params)
    (
        in_weight_grad,
        in_bias_grad,
        back_weight_grad,
        back_bias_grad,
        ffn_gain_grad,
        ffn_shift_grad,
    ) = tuple((first + second for first, second in zip(query_ffn, passage_ffn)))
    query_tokens_grad, query_attn = attention_backward(
        query_middle_grad, query_tokens, query_lengths, query_kept, params
    )
    passage_tokens_grad, passage_attn = attention_backward(
        passage_middle_grad, passage_tokens, passage_lengths, passage_kept, params
    )
    (
        query_weight_grad,
        query_bias_grad,
        key_weight_grad,
        value_weight_grad,
        value_bias_grad,
        out_weight_grad,
        out_bias_grad,
        attn_gain_grad,
        attn_shift_grad,
    ) = tuple((first + second for first, second in zip(query_attn, passage_attn)))
    (
        query_weight_grad,
        query_bias_grad,
        key_weight_grad,
        value_weight_grad,
        value_bias_grad,
        out_weight_grad,
        out_bias_grad,
        attn_gain_grad,
        attn_shift_grad,
        in_weight_grad,
        in_bias_grad,
        back_weight_grad,
        back_bias_grad,
        ffn_gain_grad,
        ffn_shift_grad,
    ) = (
        lax.psum_scatter(query_weight_grad, "dp", scatter_dimension=0, tiled=True),
        lax.psum_scatter(query_bias_grad, "dp", scatter_dimension=0, tiled=True),
        lax.psum_scatter(key_weight_grad, "dp", scatter_dimension=0, tiled=True),
        lax.psum_scatter(value_weight_grad, "dp", scatter_dimension=0, tiled=True),
        lax.psum_scatter(value_bias_grad, "dp", scatter_dimension=0, tiled=True),
        lax.psum_scatter(out_weight_grad, "dp", scatter_dimension=0, tiled=True),
        lax.psum_scatter(out_bias_grad, "dp", scatter_dimension=0, tiled=True),
        lax.psum_scatter(attn_gain_grad, "dp", scatter_dimension=0, tiled=True),
        lax.psum_scatter(attn_shift_grad, "dp", scatter_dimension=0, tiled=True),
        lax.psum_scatter(in_weight_grad, "dp", scatter_dimension=0, tiled=True),
        lax.psum_scatter(in_bias_grad, "dp", scatter_dimension=0, tiled=True),
        lax.psum_scatter(back_weight_grad, "dp", scatter_dimension=0, tiled=True),
        lax.psum_scatter(back_bias_grad, "dp", scatter_dimension=0, tiled=True),
        lax.psum_scatter(ffn_gain_grad, "dp", scatter_dimension=0, tiled=True),
        lax.psum_scatter(ffn_shift_grad, "dp", scatter_dimension=0, tiled=True),
    )
    return (
        query_out,
        passage_out,
        query_loss,
        query_tokens_grad,
        passage_tokens_grad,
        query_weight_grad,
        query_bias_grad,
        key_weight_grad,
        value_weight_grad,
        value_bias_grad,
        out_weight_grad,
        out_bias_grad,
        attn_gain_grad,
        attn_shift_grad,
        in_weight_grad,
        in_bias_grad,
        back_weight_grad,
        back_bias_grad,
        ffn_gain_grad,
        ffn_shift_grad,
    )


F32 = jnp.float32
BF16 = jnp.bfloat16
MESH = pl.DeviceIdType.MESH
FF = 3072
ROWS = 480
WIN = 240
SLOT = 220
NEG = -1000000000.0


def dot_nn(left, right):
    return jnp.dot(left, right, preferred_element_type=F32)


def dot_nt(left, right):
    return lax.dot_general(left, right, (((1,), (1,)), ((), ())), preferred_element_type=F32)


def dot_tn(left, right):
    return lax.dot_general(left, right, (((0,), (0,)), ((), ())), preferred_element_type=F32)


def row_of(ref, start=0, size=D):
    return ref[pl.ds(start, size)].astype(F32).reshape(1, size)


def item(ref, at):
    return ref[...].reshape(1, 2)[:, at:at + 1]


def blocks(start, stop, size):
    return [(at, min(size, stop - at)) for at in range(start, stop, size)]


def iota(shape, dim):
    return lax.broadcasted_iota(jnp.int32, shape, dim)


def fold8(block):
    return jnp.sum(block.reshape(-1, 8, block.shape[-1]), axis=0)


WIDE = 256
ROUTE = (
    "xyz", "yxz", "ryx", "xyz", "rxy", "ryx", "yxz", "xyz", "yxz", "xyz", "yxz", "xyz", "yxz", "xyz", "yxz", "xyz",
    "yxz", "xyz",
)
ORDER = (
    ("wback", 0, 0), ("c", 0, 0), ("wback", 0, 1), ("c", 0, 1), ("wback", 0, 2), ("c", 0, 2), ("wback", 1, 0),
    ("c", 1, 0), ("ec", 0, 0), ("wback", 1, 1), ("ec", 0, 1), ("c", 1, 1), ("wback", 1, 2), ("ec", 0, 2),
    ("c", 1, 2), ("dinner", 0), ("dinner", 1), ("win", 2, 0), ("c", 2, 0), ("ec", 1, 0), ("win", 2, 1), ("c", 2, 1),
    ("win", 2, 2), ("c", 2, 2), ("ec", 1, 1), ("ec", 2, 0), ("dinner", 2), ("dinner", 3), ("e1", 0, 1),
    ("win", 3, 0), ("c", 3, 0), ("win", 3, 1), ("e1", 0, 0), ("c", 3, 1), ("win", 3, 2), ("ec", 2, 1), ("ec", 1, 2),
    ("c", 3, 2), ("dmid", 0), ("dmid", 1), ("ec", 2, 2), ("ec", 3, 1), ("e1", 0, 2), ("ec", 3, 0), ("dmid", 2),
    ("dmid", 3), ("ec", 3, 2), ("lnback",), ("e2", 0, 1), ("dctx",), ("e1", 1, 0), ("e2", 0, 0), ("qslot",),
    ("attn", 0, 1), ("e1", 2, 0), ("e1", 1, 1), ("attn", 1, 2), ("e1", 2, 1), ("attn", 3, 3), ("sums",),
    ("e1", 3, 0), ("e1", 1, 2), ("wvo", 0), ("e1", 3, 1), ("c", 4, 0), ("vec", 0), ("wvo", 1), ("c", 4, 1),
    ("e1", 2, 2), ("wvo", 2), ("e1", 3, 2), ("c", 4, 2), ("wqk", 0), ("c", 5, 0), ("wqk", 1), ("ec", 4, 1),
    ("c", 5, 1), ("wqk", 2), ("e2", 2, 1), ("ec", 4, 2), ("e3", 0, 1), ("e2", 3, 0), ("e2", 2, 0), ("vec", 1),
    ("e2", 3, 1), ("ec", 5, 1), ("e2", 1, 0), ("e2", 3, 2), ("ec", 5, 0), ("e2", 2, 2), ("e1", 4, 1), ("e1", 4, 2),
    ("vec", 2), ("ec", 4, 0), ("c", 5, 2), ("tq",), ("e3", 3, 0), ("e1", 5, 1), ("ec", 5, 2), ("e2", 4, 1),
    ("e1", 5, 0), ("vec", 3), ("e3", 0, 0), ("e2", 0, 2), ("e2", 5, 1), ("tk",), ("e2", 1, 2), ("e1", 4, 0),
    ("e2", 4, 2), ("e3", 2, 0), ("e1", 5, 2), ("e2", 5, 0), ("e3", 3, 1), ("e2", 1, 1), ("e2", 4, 0), ("e3", 2, 2),
    ("e2", 5, 2), ("e3", 1, 2), ("e3", 1, 1), ("e3", 4, 2), ("e3", 0, 2), ("e3", 4, 1), ("e4", 1, 1), ("e3", 2, 1),
    ("vecend",), ("e3", 5, 1), ("e3", 5, 0), ("e3", 3, 2), ("tv",), ("tout",), ("e3", 4, 0), ("e3", 1, 0),
    ("e4", 0, 2), ("e4", 1, 2), ("e3", 5, 2),
)


RELAYS = max(1, sum(way[0] == "r" for way in ROUTE))


def layer_kernel(
    qtok, ptok, qlen, plen_h, pvalid_h, pos, neg, margin, qgrad, pgrad,
    wq_h, bq_h, wk_h, wv_h, bv_h, wo_h, bo_h, ga_h, sa_h, wi_h, bi_h, wb_h, bb_h, gf_h, sf_h,
    qout_h, pout_h, qtg_h, ptg_h, wqg, wkg, wvg, wog, wig, wbg, small_h,
    plen, pvalid, bq, bv, bo, ga, sa, bi, bb, gf, sf, wq, wk, wv, wo, wi, wb, pstage, x_s, xT, q_s, k_s, v_s, p_s, pq_s, c_s, cT, n1, n2, r1, r2,
    ml, mlT, act_a, act_b, actT, tmp_a, tmp_b, gp, qg_s, pg_s, qo_s, po_s, ex, ex_f, vec, vecr, vecs, vecz, small_o, parts,
    g_s, rc, ra, rb, rz, rw, rw_mate, rw_far, rw_in,
    load_sem, out_sem, part_sem, ex_send, ex_recv, c_send, c_recv, a_send, a_recv, b_send, b_recv,
    z_send, z_recv, r_send, v_send, v_recv, credit,
):
    me = lax.axis_index("dp")
    core = lax.rem(me, 2)
    xx = lax.rem(lax.div(me, 2), 2)
    yy = lax.rem(lax.div(me, 4), 2)
    zz = lax.div(me, 8)
    chip = lax.div(me, 2)
    partner = me + 1 - 2 * core
    x_peer = me + 2 - 4 * xx
    y_peer = me + 4 - 8 * yy
    plane = lax.rem(me, 8)

    loads = {}

    def load(name, source, target):
        loads[name] = pltpu.make_async_copy(source, target, load_sem.at[len(loads)])
        loads[name].start()

    load("ptok", ptok, pstage)
    load("qtok", qtok, qo_s)
    load("wq", wq_h, wq)
    vectors = (
        (plen_h, plen), (pvalid_h, pvalid), (bq_h, bq), (bv_h, bv), (bo_h, bo), (ga_h, ga), (sa_h, sa), (bi_h, bi),
        (bb_h, bb), (gf_h, gf), (sf_h, sf),
    )
    for at, (source, target) in enumerate(vectors):
        load("vec" + str(at), source, target)
    load("wk", wk_h, wk)
    load("wv", wv_h, wv)

    barrier = pltpu.get_barrier_semaphore()
    for hop in range(1, 16):
        other = 2 * lax.rem(chip + hop, 16) + core
        pl.semaphore_signal(barrier, inc=1, device_id=(other,), device_id_type=MESH)
    pl.semaphore_signal(barrier, inc=1, device_id=(partner,), device_id_type=MESH)

    loads["ptok"].wait()
    loads["qtok"].wait()
    x_s[0:32, :] = qo_s[...]

    def copy_tokens(i, carry):
        x_s[pl.ds(pl.multiple_of(32 + i * 16, 16), 16), :] = pstage[pl.ds(pl.multiple_of(i * 16, 16), 16), :]
        return carry

    lax.fori_loop(0, 27, copy_tokens, 0)
    x_s[464:480, :] = jnp.concatenate(
        [pstage[432:440, :].astype(F32), jnp.zeros((8, D), F32)], axis=0
    ).astype(BF16)

    loads["wq"].wait()
    for at in range(len(vectors)):
        loads["vec" + str(at)].wait()
    load("wo", wo_h, wo)
    load("wi", wi_h, wi)

    def project_queries(start, stop):
        rows = pl.ds(start, stop - start)
        q_s[rows, :] = ((dot_nn(x_s[rows, :], wq[...]) + row_of(bq)).astype(BF16) * 0.125).astype(BF16)

    project_queries(0, 256)
    loads["wk"].wait()
    k_s[...] = dot_nn(x_s[...], wk[...]).astype(BF16)
    loads["wv"].wait()
    for h in range(3):
        load("wb" + str(h), wb_h.at[:, :, :, :, :, :, pl.ds(WIDE * h, WIDE)], wb.at[h])
    load("qg", qgrad, qg_s)
    load("pg", pgrad, pg_s)
    v_s[...] = (dot_nn(x_s[...], wv[...]) + row_of(bv)).astype(BF16)

    head_of = iota((12, 1, D), 2) // 64
    head_mask = (head_of == iota((12, 1, D), 0)).astype(F32)

    def spread(rows):
        return (rows.astype(F32)[None] * head_mask).astype(BF16).reshape(384, D)

    def gather_heads(stacked):
        return jnp.sum(stacked.reshape(12, 32, D) * head_mask, axis=0)

    raw = dot_nt(k_s[0:32, :], spread(q_s[0:32, :]))
    raw = jnp.where(iota((32, 384), 0) < qlen[0], raw, NEG)
    soft = jnp.exp(raw - jnp.max(raw, axis=0, keepdims=True))
    soft = (soft * (1.0 / jnp.sum(soft, axis=0, keepdims=True))).astype(BF16)
    pq_s[...] = soft
    c_s[0:32, :] = gather_heads(dot_tn(soft, v_s[0:32, :])).astype(BF16)

    by_head = (q_s[240:256, :].astype(F32)[None] * head_mask).astype(BF16).reshape(192, D)
    raw = dot_nt(by_head, k_s[240:480, :])
    key_lane = iota((1, WIN), 1)
    raw = jnp.where((key_lane >= 12) & (key_lane < 12 + item(plen, 1)), raw, NEG)
    soft = jnp.exp(raw - jnp.max(raw, axis=1, keepdims=True))
    soft = (soft * (1.0 / jnp.sum(soft, axis=1, keepdims=True))).astype(BF16)
    block = jnp.sum(dot_nn(soft, v_s[240:480, :]).reshape(12, 16, D) * head_mask, axis=0)

    lane = iota((1, 128), 1)
    half = ((lane < 64).astype(BF16), (lane >= 64).astype(BF16))
    key_at = iota((WIN, 1), 0)

    def attend(pair, slot):
        lanes = pl.ds(pl.multiple_of(pair * 128, 128), 128)
        low_at = 12 * slot
        first_row = 32 + 208 * slot
        rows = pl.ds(first_row, WIN)
        keys, queries = k_s[rows, lanes], q_s[rows, lanes]
        values_t = v_s[rows, lanes].T
        allowed = (key_at >= low_at) & (key_at < low_at + item(plen, slot))
        parts = []
        for h in range(2):
            scores = jnp.where(allowed, dot_nt(keys, queries * half[h]), NEG)
            e = jnp.exp(scores - jnp.max(scores, axis=0, keepdims=True))
            p = (e * (1.0 / jnp.sum(e, axis=0, keepdims=True))).astype(BF16)
            p_s[slot, 2 * pair + h] = p
            parts.append(dot_nn(values_t, p)[64 * h:64 * h + 64, :])
        context = jnp.concatenate(parts, axis=0).T
        if slot == 0:
            c_s[rows, lanes] = context.astype(BF16)
            return
        old = c_s[240:256, lanes].astype(F32)
        c_s[240:256, lanes] = jnp.where(iota((16, 128), 0) >= 12, context[0:16], old).astype(BF16)
        c_s[256:480, lanes] = context[16:240].astype(BF16)

    def attend_slot(slot):
        def two_pairs(i, carry):
            attend(2 * i, slot)
            attend(2 * i + 1, slot)
            return carry

        lax.fori_loop(0, 3, two_pairs, 0)

    attend_slot(0)
    old = c_s[240:256, :].astype(F32)
    c_s[240:256, :] = jnp.where(iota((16, 1), 0) >= 12, block, old).astype(BF16)

    loads["wo"].wait()
    gain1, shift1, bias1 = row_of(ga), row_of(sa), row_of(bo)
    gain2, shift2, bias2 = row_of(gf), row_of(sf), row_of(bb)

    def wb_tile(t):
        return jnp.concatenate([wb[h, t // 2, t % 2].reshape(D, WIDE) for h in range(3)], axis=1)

    def normalized(hidden):
        centered = hidden - jnp.mean(hidden, axis=-1, keepdims=True)
        inv = lax.rsqrt(jnp.mean(centered * centered, axis=-1, keepdims=True) + ln_eps)
        return centered * inv, inv

    def forward_rows(start, stop):
        size = stop - start
        every, own = pl.ds(start, size), pl.ds(0, size)
        tmp_a[own, :] = dot_nn(c_s[every, :], wo[...])
        for at, count in blocks(0, size, 32):
            rows, here = pl.ds(start + at, count), pl.ds(at, count)
            unit, inv = normalized(tmp_a[here, :] + x_s[rows, :].astype(F32) + bias1)
            n1[rows, :] = unit
            r1[rows, :] = inv
            ml[rows, :] = (unit * gain1 + shift1).astype(BF16)
        if start == 0:
            loads["wi"].wait()
            for h in range(3):
                loads["wb" + str(h)].wait()
        inner, acts = (tmp_a, tmp_b), (act_a, act_b)
        tmp_a[own, :] = dot_nn(ml[every, :], wi[:, 0:D])
        mlT[:, every] = ml[every, :].T
        xT[:, every] = x_s[every, :].T
        cT[:, every] = c_s[every, :].T

        def finish(t):
            act = acts[t % 2][own, :]
            if t == 0:
                n2[every, :] = dot_nn(act, wb_tile(t))
            else:
                n2[every, :] += dot_nn(act, wb_tile(t))
            actT[t * D:t * D + D, every] = act.T

        for t in range(4):
            if t < 3:
                inner[(t + 1) % 2][own, :] = dot_nn(ml[every, :], wi[:, t * D + D:t * D + 2 * D])
            bias_t = row_of(bi, t * D)
            for at, count in blocks(0, size, 16):
                here = pl.ds(at, count)
                u = inner[t % 2][here, :] + bias_t
                cdf = 0.5 * (1.0 + lax.erf(u * root_half))
                acts[t % 2][here, :] = (u * cdf).astype(BF16)
                gp[start + at:start + at + count, t * D:t * D + D] = (
                    cdf + u * inv_root_tau * jnp.exp(-0.5 * u * u)
                ).astype(BF16)
            if t > 0:
                finish(t - 1)
        finish(3)
        for at, count in blocks(start, stop, 32):
            rows = pl.ds(at, count)
            unit, inv = normalized(n2[rows, :] + (n1[rows, :] * gain1 + shift1) + bias2)
            n2[rows, :] = unit
            r2[rows, :] = inv
            out = (unit * gain2 + shift2).astype(BF16)
            if at == 0:
                qo_s[...] = out
            else:
                po_s[at - 32:min(at, 440), :] = out[0:min(count, 472 - at)]

    forward_rows(0, 256)

    slot_me = core * 16 + chip
    base = pl.multiple_of(slot_me * 32, 32)
    first_rows = (
        qo_s[0:16, :].astype(F32)[0:1],
        po_s[0:16, :].astype(F32)[0:1],
        po_s[208:224, :].astype(F32)[12:13],
    )
    lane_row = iota((1, 128), 1)
    meta = jnp.zeros((1, 128), F32)
    margin_0 = jnp.zeros((1, 128), F32) + margin[0]
    margin_1 = margin_0.astype(BF16).astype(F32)
    margin_2 = (margin_0 - margin_1).astype(BF16).astype(F32)
    for at, value in enumerate((
        item(pvalid, 0).astype(F32), item(pvalid, 1).astype(F32), pos[0].astype(F32), neg[0].astype(F32),
        margin_1, margin_2, margin_0 - margin_1 - margin_2,
    )):
        meta = jnp.where(lane_row == at, value, meta)
    pieces = [row[:, 128 * i:128 * i + 128] for row in first_rows for i in range(6)]
    ex[pl.ds(base, 32), :] = jnp.concatenate(pieces + [meta, jnp.zeros((13, 128), F32)], axis=0).astype(BF16)

    pl.semaphore_wait(barrier, 16)
    sends = []
    for hop in range(1, 16):
        block = ex.at[pl.ds(base, 32), :]
        sends.append(pltpu.make_async_remote_copy(
            src_ref=block, dst_ref=block, send_sem=ex_send.at[hop], recv_sem=ex_recv.at[hop],
            device_id=(2 * lax.rem(chip + hop, 16) + core,), device_id_type=MESH,
        ))
        sends[-1].start()

    project_queries(256, 480)
    attend_slot(1)
    forward_rows(256, 480)
    out_q = pltpu.make_async_copy(qo_s, qout_h, out_sem.at[0])
    out_p = pltpu.make_async_copy(po_s, pout_h, out_sem.at[1])
    out_q.start()
    out_p.start()
    loads["qg"].wait()
    loads["pg"].wait()

    def ffn_norm_back(r0, upstream, sums):
        rows = pl.ds(r0, upstream.shape[0])
        unit = n2[rows, :]
        scaled = upstream * gain2
        hidden_grad = r2[rows, :] * (
            scaled
            - jnp.mean(scaled, axis=-1, keepdims=True)
            - unit * jnp.mean(scaled * unit, axis=-1, keepdims=True)
        )
        n2[rows, :] = hidden_grad
        rounded = hidden_grad.astype(BF16)
        ml[rows, :] = rounded
        return (
            sums[0] + fold8(upstream * unit), sums[1] + fold8(upstream), sums[2] + fold8(rounded.astype(F32)),
        )

    zero8 = jnp.zeros((8, D), F32)
    sums = (zero8, zero8, zero8)

    for i in (1, 2, 3, 4, 5, 7, 8, 9, 10, 11, 12):
        sums = ffn_norm_back(32 + 32 * i, pg_s[32 * i:32 * i + 32, :].astype(F32), sums)
    last = jnp.concatenate([pg_s[416:440, :].astype(F32), jnp.zeros((8, D), F32)], axis=0)
    sums = ffn_norm_back(448, last, sums)

    for send in sends:
        send.wait()
    same_core = ex.at[pl.ds(pl.multiple_of(core * 512, 512), 512), :]
    across = pltpu.make_async_remote_copy(
        src_ref=same_core, dst_ref=same_core, send_sem=ex_send.at[0], recv_sem=ex_recv.at[0],
        device_id=(partner,), device_id_type=MESH,
    )
    across.start()
    across.wait()

    ex_f[...] = ex[...].astype(F32)

    def first(r):
        return ex_f[pl.ds(r, 32, stride=32), :]

    cls_q = jnp.concatenate([first(i) for i in range(6)], axis=1)
    cls_0 = jnp.concatenate([first(6 + i) for i in range(6)], axis=1).astype(BF16)
    cls_1 = jnp.concatenate([first(12 + i) for i in range(6)], axis=1).astype(BF16)
    metas = first(18)
    metas_t = metas.T
    s0 = score_scale * dot_nt(cls_q.astype(BF16), cls_0)
    s1 = score_scale * dot_nt(cls_q.astype(BF16), cls_1)
    col = iota((1, 32), 1)
    passage = (4 * lax.rem(col, 16) + 2 * lax.div(col, 16)).astype(F32)
    at_pos, at_neg, wanted = metas[:, 2:3], metas[:, 3:4], metas[:, 4:5] + metas[:, 5:6] + metas[:, 6:7]
    pos0, pos1 = at_pos == passage, at_pos == passage + 1.0
    neg0, neg1 = at_neg == passage, at_neg == passage + 1.0
    m0 = jnp.where((metas_t[0:1, :] > 0.5) | pos0, s0, -1e30)
    m1 = jnp.where((metas_t[1:2, :] > 0.5) | pos1, s1, -1e30)
    peak = jnp.maximum(jnp.max(m0, axis=1, keepdims=True), jnp.max(m1, axis=1, keepdims=True))
    total = jnp.sum(jnp.exp(m0 - peak), axis=1, keepdims=True) + jnp.sum(jnp.exp(m1 - peak), axis=1, keepdims=True)
    lse = peak + jnp.log(total)

    def picked(where0, where1):
        return jnp.sum(jnp.where(where0, s0, 0.0), axis=1, keepdims=True) + jnp.sum(
            jnp.where(where1, s1, 0.0), axis=1, keepdims=True
        )

    at_positive = picked(pos0, pos1)
    miss = at_positive - picked(neg0, neg1) - wanted
    losses = lse - at_positive + margin_weight * miss * miss
    pos0, pos1, neg0, neg1 = (hit.astype(F32) for hit in (pos0, pos1, neg0, neg1))
    ds0 = (jnp.exp(m0 - lse) - pos0 + 2.0 * margin_weight * miss * (pos0 - neg0)).astype(BF16)
    ds1 = (jnp.exp(m1 - lse) - pos1 + 2.0 * margin_weight * miss * (pos1 - neg1)).astype(BF16)
    mine = iota((32, 1), 0) == slot_me
    mine_col = iota((1, 32), 1) == slot_me
    small_o[9:10, :] = jnp.sum(jnp.where(mine, losses, 0.0), axis=0, keepdims=True) + jnp.zeros((1, 128), F32)
    dq_all = score_scale * (dot_nn(ds0, cls_0) + dot_nn(ds1, cls_1))
    d_query = jnp.sum(jnp.where(mine, dq_all, 0.0), axis=0, keepdims=True)

    def passage_grad_row(ds):
        column = jnp.sum(jnp.where(mine_col, ds.astype(F32), 0.0), axis=1, keepdims=True)
        return score_scale * jnp.sum(column * cls_q, axis=0, keepdims=True)

    d_first = (d_query, passage_grad_row(ds0), passage_grad_row(ds1))

    row32 = iota((32, 1), 0)
    for r0, at, source, add in (
        (0, 0, qg_s[...], d_first[0]), (32, 0, pg_s[0:32, :], d_first[1]), (224, 28, pg_s[192:224, :], d_first[2]),
    ):
        upstream = source.astype(F32) + jnp.where(row32 == at, add, 0.0)
        sums = ffn_norm_back(r0, upstream, sums)
    vec[...] = jnp.zeros_like(vec)
    vec[5:6, :] = jnp.sum(sums[2], axis=0, keepdims=True)
    vec[6:7, :] = jnp.sum(sums[0], axis=0, keepdims=True)
    vec[7:8, :] = jnp.sum(sums[1], axis=0, keepdims=True)

    def chunk(p, h):
        return g_s.at[p, h] if p < 4 else wb.at[h, p - 4]

    z_slot, r_slot = {}, {}
    for at, way in enumerate(ROUTE):
        for kind, slots in (("z", z_slot), ("r", r_slot)):
            if way[0] == kind:
                slots[(at // 3, at % 3)] = len(slots)
    inner = (zz == 1) | (zz == 2)
    mate = zz + 1 - 2 * lax.rem(zz, 2)
    far = 2 - 2 * lax.div(zz, 2)

    def route(p, h):
        return ROUTE[3 * p + h]

    def remote(source, target, send, recv, device):
        return pltpu.make_async_remote_copy(
            src_ref=source, dst_ref=target, send_sem=send, recv_sem=recv, device_id=(device,), device_id_type=MESH,
        )

    def step_c(p, h):
        return [remote(chunk(p, h).at[1 - core], rc.at[p % 2, h], c_send.at[p, h], c_recv.at[p, h], partner)]

    def along_z(p, h, pick, target):
        steps = []
        for hop in range(1, 4):
            to = lax.rem(zz + hop, 4)
            steps.append(remote(
                pick(to), target(hop - 1), z_send.at[p, h, hop - 1], z_recv.at[p, h, hop - 1], to * 8 + plane,
            ))
        return steps

    def step_1(p, h):
        mine, way = chunk(p, h), route(p, h)
        if way[0] == "z":
            return along_z(p, h, lambda to: mine.at[core, to], lambda i: rw.at[z_slot[(p, h)], i])
        away = mine.at[core, :, :, 1 - xx] if way == "xyz" else mine.at[core, :, 1 - yy]
        return [remote(away, ra.at[p, h], a_send.at[p, h], a_recv.at[p, h], x_peer if way == "xyz" else y_peer)]

    def step_2(p, h):
        mine, way = chunk(p, h), route(p, h)
        if way in ("zyx", "ryx"):
            away, target = mine.at[core, zz, 1 - yy], rb.at[p, h, 0:2]
        elif way in ("zxy", "rxy"):
            away, target = mine.at[core, zz, :, 1 - xx], rb.at[p, h, 0:2]
        elif way == "xyz":
            away, target = mine.at[core, :, 1 - yy, xx], rb.at[p, h]
        else:
            away, target = mine.at[core, :, yy, 1 - xx], rb.at[p, h]
        return [remote(away, target, b_send.at[p, h], b_recv.at[p, h], x_peer if way[1] == "x" else y_peer)]

    def step_3(p, h):
        mine = chunk(p, h)
        way = route(p, h)
        if way[0] in "zr":
            away = mine.at[core, zz, yy, 1 - xx] if way[2] == "x" else mine.at[core, zz, 1 - yy, xx]
            return [remote(
                away, rz.at[p, h, 0], a_send.at[p, h], a_recv.at[p, h], x_peer if way[2] == "x" else y_peer,
            )]
        return along_z(p, h, lambda to: mine.at[core, to, yy, xx], lambda i: rz.at[p, h, i])

    def begin(steps):
        for step in steps:
            step.start()

    def finish_steps(steps):
        for step in steps:
            step.wait()

    def mate_step(p, h):
        return remote(
            chunk(p, h).at[core, mate], rw_mate.at[r_slot[(p, h)]], z_send.at[p, h, 0], z_recv.at[p, h, 0],
            mate * 8 + plane,
        )

    def far_step(p, h):
        return remote(
            chunk(p, h).at[core, pl.ds(far, 2)], rw_far.at[r_slot[(p, h)]], z_send.at[p, h, 1], z_recv.at[p, h, 1],
            mate * 8 + plane,
        )

    def relay_step(p, h, i):
        return remote(
            chunk(p, h).at[core, far + i], rw_in.at[r_slot[(p, h)]], r_send.at[r_slot[(p, h)], i], z_recv.at[p, h, 2],
            (far + i) * 8 + plane,
        )

    def start_relay(p, h):
        mate_step(p, h).start()

        @pl.when(jnp.logical_not(inner))
        def _():
            far_step(p, h).start()

    def relay_on(p, h):
        @pl.when(inner)
        def _():
            far_step(p, h).wait_recv()

            def add(i, carry):
                for y in range(2):
                    for x in range(2):
                        chunk(p, h)[core, far + i, y, x] += rw_far[r_slot[(p, h)], i, y, x]
                return carry

            lax.fori_loop(0, 2, add, 0)
            for i in range(2):
                relay_step(p, h, i).start()

        @pl.when(jnp.logical_not(inner))
        def _():
            far_step(p, h).wait_send()

    def end_relay(p, h):
        mate_step(p, h).wait()
        relay_step(p, h, 0).wait_recv()

        @pl.when(inner)
        def _():
            for i in range(2):
                relay_step(p, h, i).wait_send()

        mine, at = chunk(p, h), r_slot[(p, h)]

        def add(y, carry):
            for x in range(2):
                total = mine[core, zz, y, x].astype(F32) + rw_mate[at, y, x].astype(F32) + rw_in[at, y, x].astype(F32)
                mine[core, zz, y, x] = total.astype(BF16)
            return carry

        lax.fori_loop(0, 2, add, 0)
        begin(step_2(p, h))

    def start_c(p, h):
        if p >= 2:
            pl.semaphore_wait(credit.at[p % 2, h], 1)
        begin(step_c(p, h))

    def end_c(p, h):
        finish_steps(step_c(p, h))

        def add(z, carry):
            for y in range(2):
                for x in range(2):
                    chunk(p, h)[core, z, y, x] += rc[p % 2, h, z, y, x]
            return carry

        lax.fori_loop(0, 4, add, 0)
        if route(p, h)[0] == "r":
            start_relay(p, h)
        else:
            begin(step_1(p, h))
        if p < 4:
            pl.semaphore_signal(credit.at[p % 2, h], inc=1, device_id=(partner,), device_id_type=MESH)

    def end_1(p, h):
        finish_steps(step_1(p, h))
        mine, way = chunk(p, h), route(p, h)
        if way[0] == "z":
            def add(y, carry):
                for x in range(2):
                    total = mine[core, zz, y, x].astype(F32)
                    for i in range(3):
                        total += rw[z_slot[(p, h)], i, y, x].astype(F32)
                    mine[core, zz, y, x] = total.astype(BF16)
                return carry

            lax.fori_loop(0, 2, add, 0)
        else:
            def add(z, carry):
                for i in range(2):
                    if way == "yxz":
                        mine[core, z, yy, i] += ra[p, h, z, i]
                    else:
                        mine[core, z, i, xx] += ra[p, h, z, i]
                return carry

            lax.fori_loop(0, 4, add, 0)
        begin(step_2(p, h))

    def end_2(p, h):
        finish_steps(step_2(p, h))
        mine = chunk(p, h)
        way = route(p, h)
        if way[0] in "zr":
            for i in range(2):
                if way[1] == "y":
                    mine[core, zz, yy, i] += rb[p, h, i]
                else:
                    mine[core, zz, i, xx] += rb[p, h, i]
        else:
            def add(z, carry):
                mine[core, z, yy, xx] += rb[p, h, z]
                return carry

            lax.fori_loop(0, 4, add, 0)
        begin(step_3(p, h))

    outs = []

    def end_3(p, h):
        finish_steps(step_3(p, h))
        total = chunk(p, h)[core, zz, yy, xx].astype(F32)
        for i in range(1 if route(p, h)[0] in "zr" else 3):
            total += rz[p, h, i].astype(F32)
        parts[p, h] = total
        at = WIDE * h
        if p < 2:
            targets = [wbg.at[pl.ds(48 * p, 48), pl.ds(at, WIDE)]]
        elif p < 4:
            at += (p - 2) * 2 * D
            targets = [wig.at[:, pl.ds(at, WIDE)], wig.at[:, pl.ds(at + D, WIDE)]]
        else:
            targets = [ref.at[:, pl.ds(at, WIDE)] for ref in ((wvg, wog) if p == 4 else (wqg, wkg))]
        rows = 48 // len(targets)
        for i, target in enumerate(targets):
            outs.append(pltpu.make_async_copy(parts.at[p, h, pl.ds(rows * i, rows)], target, part_sem.at[p, h, i]))
            outs[-1].start()

    def store_grad(p, h, grad):
        for i in range(32):
            chunk(p, h)[i % 2, i // 8, (i // 4) % 2, (i // 2) % 2] = grad[i]

    def back_grad(p, h):
        left = jnp.concatenate([actT[96 * i + 48 * p:96 * i + 48 * p + 48, :] for i in range(32)], axis=0)
        grad = dot_nn(left, ml[:, WIDE * h:WIDE * h + WIDE]).astype(BF16)
        store_grad(p, h, grad.reshape(32, 48, WIDE))

    def pair_grad(p, h, left_0, right_0, left_1, right_1):
        cols = pl.ds(WIDE * h, WIDE)
        grad_0 = dot_nn(left_0[...], right_0[:, cols]).reshape(32, 24, WIDE)
        grad_1 = dot_nn(left_1[...], right_1[:, cols]).reshape(32, 24, WIDE)
        store_grad(p, h, jnp.concatenate([grad_0, grad_1], axis=1).astype(BF16))

    def in_grad(p, h):
        at = (p - 2) * 2 * D
        pair_grad(p, h, mlT, gp.at[:, pl.ds(at, D)], mlT, gp.at[:, pl.ds(at + D, D)])

    def inner_grad(t):
        cols = pl.ds(t * D, D)
        weight = wb_tile(t)
        tmp_a[...] = dot_nt(ml[0:256, :], weight)
        tmp_b[0:224, :] = dot_nt(ml[256:480, :], weight)
        total = zero8
        for ref, start, size in ((tmp_a, 0, 256), (tmp_b, 256, 224)):
            for at, count in blocks(0, size, 16):
                rows = pl.ds(start + at, count)
                rounded = (ref[at:at + count, :] * gp[rows, cols].astype(F32)).astype(BF16)
                gp[rows, cols] = rounded
                total = total + fold8(rounded.astype(F32))
        vec[8 + t:9 + t, :] = jnp.sum(total, axis=0, keepdims=True)

    def middle_grad(t):
        cols = pl.ds(t * D, D)
        n2[...] += dot_nt(gp[:, cols], wi[:, cols])

    def attn_norm_back():
        def block(i, sums):
            rows = pl.ds(pl.multiple_of(i * 32, 32), 32)
            upstream, unit = n2[rows, :], n1[rows, :]
            scaled = upstream * gain1
            hidden_grad = r1[rows, :] * (
                scaled
                - jnp.mean(scaled, axis=-1, keepdims=True)
                - unit * jnp.mean(scaled * unit, axis=-1, keepdims=True)
            )
            n1[rows, :] = hidden_grad
            rounded = hidden_grad.astype(BF16)
            ml[rows, :] = rounded
            return (
                sums[0] + fold8(upstream * unit), sums[1] + fold8(upstream), sums[2] + fold8(rounded.astype(F32)),
            )

        sums = lax.fori_loop(0, 15, block, (zero8, zero8, zero8))
        vec[2:3, :] = jnp.sum(sums[2], axis=0, keepdims=True)
        vec[3:4, :] = jnp.sum(sums[0], axis=0, keepdims=True)
        vec[4:5, :] = jnp.sum(sums[1], axis=0, keepdims=True)

    def context_grad():
        c_s[...] = dot_nt(ml[...], wo[...]).astype(BF16)

    def query_slot_back():
        q_rows, k_rows, v_rows = spread(q_s[0:32, :]), k_s[0:32, :], v_s[0:32, :]
        dc_rows = spread(c_s[0:32, :])
        soft = pq_s[...]
        dp = dot_nt(v_rows, dc_rows)
        soft_f = soft.astype(F32)
        ds = (soft_f * (dp - jnp.sum(soft_f * dp, axis=0, keepdims=True))).astype(BF16)
        v_s[0:32, :] = dot_nn(soft, dc_rows).astype(BF16)
        k_s[0:32, :] = dot_nn(ds, q_rows).astype(BF16)
        q_s[0:32, :] = (0.125 * gather_heads(dot_tn(ds, k_rows))).astype(BF16)

    def attend_back_pair(pair):
        lanes = pl.ds(pl.multiple_of(pair * 128, 128), 128)
        for slot in range(2):
            low_at = 12 * slot
            rows = pl.ds(32 + 208 * slot, WIN)
            keys, queries, values = k_s[rows, lanes], q_s[rows, lanes], v_s[rows, lanes]
            inside = ((key_at >= low_at) & (key_at < low_at + SLOT)).astype(BF16)
            upstream = c_s[rows, lanes] * inside
            keys_t = keys.T
            parts, dv, dk = [], 0.0, 0.0
            for h in range(2):
                p = p_s[slot, 2 * pair + h]
                dc = upstream * half[h]
                dp = dot_nt(values, dc)
                pf = p.astype(F32)
                ds = (pf * (dp - jnp.sum(pf * dp, axis=0, keepdims=True))).astype(BF16)
                dv += dot_nn(p, dc)
                dk += dot_nn(ds, queries * half[h])
                parts.append(dot_nn(keys_t, ds)[64 * h:64 * h + 64, :])
            dq = 0.125 * jnp.concatenate(parts, axis=0).T
            for ref, new in ((q_s, dq), (k_s, dk), (v_s, dv)):
                if slot == 0:
                    ref[32:240, lanes] = new[0:208].astype(BF16)
                    old = ref[240:272, lanes].astype(F32)
                    ref[240:272, lanes] = jnp.where(iota((32, 128), 0) < 12, new[208:240], old).astype(BF16)
                else:
                    old = ref[240:256, lanes].astype(F32)
                    ref[240:256, lanes] = jnp.where(iota((16, 128), 0) >= 12, new[0:16], old).astype(BF16)
                    ref[256:480, lanes] = new[16:240].astype(BF16)

    def attend_back(first, count):
        def step(i, carry):
            attend_back_pair(first + i)
            return carry

        lax.fori_loop(0, count, step, 0)

    def column_sum(ref):
        def step(i, total):
            return total + fold8(ref[pl.ds(pl.multiple_of(i * 32, 32), 32), :].astype(F32))

        return jnp.sum(lax.fori_loop(0, 15, step, zero8), axis=0, keepdims=True)

    def column_sums():
        vec[0:1, :] = column_sum(q_s)
        vec[1:2, :] = column_sum(v_s)

    def token_grad(grads, weight):
        n1[...] += dot_nt(grads[...], weight[...])

    out_qg = pltpu.make_async_copy(n1.at[0:32, :], qtg_h, out_sem.at[2])
    out_pg = pltpu.make_async_copy(n1.at[32:472, :], ptg_h, out_sem.at[3])

    def send_tokens():
        out_qg.start()
        out_pg.start()

    def vec_step(i):
        return remote(vec, vecr.at[i], v_send.at[i], v_recv.at[i], (partner, x_peer, y_peer)[i])

    def vec_part(whole, to):
        device = to * 8 + plane
        narrow = pltpu.roll(whole[0:8], D - 24 * device, 1)[:, 0:128]
        wide = pltpu.roll(whole[8:16], D - 96 * plane, 1)[:, 0:128]
        wide = jnp.sum(jnp.where(iota((8, 128), 0) == to, wide, 0.0), axis=0, keepdims=True)
        return jnp.concatenate([narrow, wide, jnp.zeros((7, 128), F32)], axis=0)

    def vec_z():
        return [
            remote(
                vecs.at[hop - 1], vecz.at[hop - 1], v_send.at[2 + hop], v_recv.at[2 + hop],
                lax.rem(zz + hop, 4) * 8 + plane,
            )
            for hop in range(1, 4)
        ]

    def vec_on(i):
        if i > 0:
            vec_step(i - 1).wait()
            vec[...] += vecr[i - 1]
        if i < 3:
            vec_step(i).start()
        else:
            whole = vec[...]
            for hop in range(1, 4):
                vecs[hop - 1] = vec_part(whole, lax.rem(zz + hop, 4))
            begin(vec_z())

    def vec_end():
        finish_steps(vec_z())
        part = vec_part(vec[...], zz) + vecz[0] + vecz[1] + vecz[2]
        small_o[0:9, :] = part[0:9]
        outs.append(pltpu.make_async_copy(small_o, small_h, out_sem.at[4]))
        outs[-1].start()

    def serve(at, p, h):
        relayed = route(p, h)[0] == "r"
        ((relay_on, end_relay, end_2, end_3) if relayed else (end_1, end_2, end_3))[at](p, h)

    pieces_of = {
        "wback": back_grad, "dinner": inner_grad, "win": in_grad, "dmid": middle_grad, "lnback": attn_norm_back,
        "dctx": context_grad, "qslot": query_slot_back, "attn": attend_back, "sums": column_sums,
        "wvo": lambda h: pair_grad(4, h, xT, v_s, cT, ml), "wqk": lambda h: pair_grad(5, h, xT, q_s, xT, k_s),
        "tq": lambda: token_grad(q_s, wq), "tk": lambda: token_grad(k_s, wk), "tv": lambda: token_grad(v_s, wv),
        "tout": send_tokens, "vec": vec_on, "vecend": vec_end,
        "c": start_c, "ec": end_c, "e1": lambda p, h: serve(0, p, h), "e2": lambda p, h: serve(1, p, h),
        "e3": lambda p, h: serve(2, p, h), "e4": lambda p, h: serve(3, p, h),
    }
    for name, *operands in ORDER:
        pieces_of[name](*operands)

    out_q.wait()
    out_p.wait()
    out_qg.wait()
    out_pg.wait()
    for out in outs:
        out.wait()


def hand_on_kernel(*refs):
    count = 10
    sources, small = refs[:count], refs[count]
    targets, vectors = refs[count + 1:2 * count + 1], refs[2 * count + 1:2 * count + 11]
    held, rest = refs[2 * count + 11:3 * count + 11], refs[3 * count + 11:]
    small_v, lines, in_sem, out_sem = rest[0], rest[1:11], rest[11], rest[12]
    whole = [(i, None) for i in range(count) if i != 3]
    pieces = [(3, pl.ds(at, size)) for at, size in blocks(0, 440, 112)] + whole
    into, out = [], []
    for at, (i, rows) in enumerate(pieces):
        source, kept, target = (ref if rows is None else ref.at[rows, :] for ref in (sources[i], held[i], targets[i]))
        into.append(pltpu.make_async_copy(source, kept, in_sem.at[at]))
        out.append(pltpu.make_async_copy(kept, target, out_sem.at[at]))
    last = pltpu.make_async_copy(small, small_v, in_sem.at[len(pieces)])
    last.start()
    for copy in into:
        copy.start()
    last.wait()
    for at, ref in enumerate(lines[:8]):
        ref[...] = small_v[at:at + 1, 0:24].reshape(24)
    lines[8][...] = small_v[8:9, 0:96].reshape(96)
    lines[9][...] = small_v[9:10, 0:1].reshape(1)
    for at, (line, vector) in enumerate(zip(lines, vectors)):
        out.append(pltpu.make_async_copy(line, vector, out_sem.at[len(pieces) + at]))
        out[-1].start()
    for first, second in zip(into, out):
        first.wait()
        second.start()
    for copy in out:
        copy.wait()


def on_device_small(*operands):
    (
        query_tokens, passage_tokens, query_lengths, passage_lengths, passage_valid, positives, negatives,
        teacher_margins, query_grad, passage_grad, weight_query, bias_query, weight_key, weight_value, bias_value,
        weight_out, bias_out, gain_attn, shift_attn, weight_in, bias_in, weight_back, bias_back, gain_ffn, shift_ffn,
    ) = operands
    hbm, smem = (pl.BlockSpec(memory_space=space) for space in (pl.ANY, pltpu.SMEM))
    shape = jax.ShapeDtypeStruct
    slabs = (2, 2, 4, 2, 2, 48, D)
    large = (
        shape((32, D), BF16), shape((440, D), BF16), shape((32, D), F32), shape((440, D), F32), shape((24, D), F32),
        shape((24, D), F32), shape((24, D), F32), shape((24, D), F32), shape((24, FF), F32), shape((96, D), F32),
    )
    outs = pl.pallas_call(
        layer_kernel,
        out_shape=(
            *large, shape((16, 128), F32),
        ),
        in_specs=[
            hbm, hbm, smem, hbm, hbm, smem, smem, smem, hbm, hbm,
            *(hbm,) * 15,
        ],
        out_specs=(hbm,) * 11,
        scratch_shapes=[
            pltpu.VMEM((2,), jnp.int32), pltpu.VMEM((2,), jnp.int32),
            *(pltpu.VMEM((size,), BF16) for size in (D, D, D, D, D, FF, D, D, D)),
            pltpu.VMEM((D, D), BF16), pltpu.VMEM((D, D), BF16), pltpu.VMEM((D, D), BF16), pltpu.VMEM((D, D), BF16),
            pltpu.VMEM((D, FF), BF16), pltpu.VMEM((3, 2, 2, 4, 2, 2, 48, WIDE), BF16),
            pltpu.VMEM((440, D), BF16), pltpu.VMEM((ROWS, D), BF16), pltpu.VMEM((D, ROWS), BF16),
            pltpu.VMEM((ROWS, D), BF16), pltpu.VMEM((ROWS, D), BF16), pltpu.VMEM((ROWS, D), BF16),
            pltpu.VMEM((2, 12, WIN, WIN), BF16), pltpu.VMEM((32, 384), BF16),
            pltpu.VMEM((ROWS, D), BF16), pltpu.VMEM((D, ROWS), BF16),
            pltpu.VMEM((ROWS, D), F32), pltpu.VMEM((ROWS, D), F32), pltpu.VMEM((ROWS, 1), F32), pltpu.VMEM((ROWS, 1), F32),
            pltpu.VMEM((ROWS, D), BF16), pltpu.VMEM((D, ROWS), BF16),
            pltpu.VMEM((256, D), BF16), pltpu.VMEM((256, D), BF16), pltpu.VMEM((FF, ROWS), BF16),
            pltpu.VMEM((256, D), F32), pltpu.VMEM((256, D), F32),
            pltpu.VMEM((ROWS, FF), BF16),
            pltpu.VMEM((32, D), BF16), pltpu.VMEM((440, D), BF16), pltpu.VMEM((32, D), BF16), pltpu.VMEM((440, D), BF16),
            pltpu.VMEM((1024, 128), BF16), pltpu.VMEM((1024, 128), F32),
            pltpu.VMEM((16, D), F32), pltpu.VMEM((3, 16, D), F32), pltpu.VMEM((3, 16, 128), F32), pltpu.VMEM((3, 16, 128), F32),
            pltpu.VMEM((16, 128), F32), pltpu.VMEM((6, 3, 48, WIDE), F32),
            pltpu.VMEM((4, 3, 2, 4, 2, 2, 48, WIDE), BF16),
            pltpu.VMEM((2, 3, 4, 2, 2, 48, WIDE), BF16), pltpu.VMEM((6, 3, 4, 2, 48, WIDE), BF16),
            pltpu.VMEM((6, 3, 4, 48, WIDE), BF16), pltpu.VMEM((6, 3, 3, 48, WIDE), BF16),
            pltpu.VMEM((max(1, sum(way[0] == "z" for way in ROUTE)), 3, 2, 2, 48, WIDE), BF16),
            pltpu.VMEM((RELAYS, 2, 2, 48, WIDE), BF16), pltpu.VMEM((RELAYS, 2, 2, 2, 48, WIDE), BF16),
            pltpu.VMEM((RELAYS, 2, 2, 48, WIDE), BF16),
            pltpu.SemaphoreType.DMA((32,)), pltpu.SemaphoreType.DMA((5,)), pltpu.SemaphoreType.DMA((6, 3, 2)),
            pltpu.SemaphoreType.DMA((16,)), pltpu.SemaphoreType.DMA((16,)),
            pltpu.SemaphoreType.DMA((6, 3)), pltpu.SemaphoreType.DMA((6, 3)),
            pltpu.SemaphoreType.DMA((6, 3)), pltpu.SemaphoreType.DMA((6, 3)),
            pltpu.SemaphoreType.DMA((6, 3)), pltpu.SemaphoreType.DMA((6, 3)),
            pltpu.SemaphoreType.DMA((6, 3, 3)), pltpu.SemaphoreType.DMA((6, 3, 3)), pltpu.SemaphoreType.DMA((RELAYS, 2)),
            pltpu.SemaphoreType.DMA((6,)), pltpu.SemaphoreType.DMA((6,)),
            pltpu.SemaphoreType.REGULAR((2, 3)),
        ],
        compiler_params=pltpu.CompilerParams(
            collective_id=0, has_side_effects=True, vmem_limit_bytes=64 * 1024 * 1024 - 65536,
        ),
        name="encoder_layer",
    )(
        query_tokens, passage_tokens, query_lengths, passage_lengths, passage_valid, positives, negatives,
        teacher_margins, query_grad, passage_grad, weight_query, bias_query, weight_key, weight_value, bias_value,
        weight_out, bias_out, gain_attn, shift_attn, weight_in, bias_in, weight_back.reshape(slabs), bias_back,
        gain_ffn, shift_ffn,
    )
    done = pl.pallas_call(
        hand_on_kernel,
        out_shape=large + (shape((24,), F32),) * 8 + (shape((96,), F32), shape((1,), F32)),
        in_specs=[hbm] * 11,
        out_specs=(hbm,) * 20,
        scratch_shapes=[pltpu.VMEM(out.shape, out.dtype) for out in large]
        + [pltpu.VMEM((16, 128), F32)] + [pltpu.VMEM((size,), F32) for size in (24,) * 8 + (96, 1)]
        + [pltpu.SemaphoreType.DMA((24,)), pltpu.SemaphoreType.DMA((24,))],
        name="hand_on",
    )(*outs)
    qout, pout, qtg, ptg, wqg, wkg, wvg, wog, wig, wbg, bqg, bvg, bog, gag, sag, bbg, gfg, sfg, big, loss = done
    return (
        qout, pout, loss, qtg, ptg, wqg, bqg, wkg, wvg, bvg, wog, bog, gag, sag, wig, big, wbg, bbg, gfg, sfg,
    )


def solution(mesh):
    return jax.shard_map(
        on_device_small if mesh.shape["dp"] == 32 else on_device,
        mesh=mesh,
        in_specs=(
            P("dp", None),
            P("dp", None),
            P("dp"),
            P("dp"),
            P("dp"),
            P("dp"),
            P("dp"),
            P("dp"),
            P("dp", None),
            P("dp", None),
            P(),
            P(),
            P(),
            P(),
            P(),
            P(),
            P(),
            P(),
            P(),
            P(),
            P(),
            P(),
            P(),
            P(),
            P(),
        ),
        out_specs=(
            P("dp", None),
            P("dp", None),
            P("dp"),
            P("dp", None),
            P("dp", None),
            P("dp", None),
            P("dp"),
            P("dp", None),
            P("dp", None),
            P("dp"),
            P("dp", None),
            P("dp"),
            P("dp"),
            P("dp"),
            P("dp", None),
            P("dp"),
            P("dp", None),
            P("dp"),
            P("dp"),
            P("dp"),
        ),
        check_vma=False,
    )
```

```python
import jax
import jax.numpy as jnp
from jax import lax
from jax.experimental import pallas as pl
from jax.experimental.pallas import tpu as pltpu
from jax.sharding import PartitionSpec as P

D = 768
HEADS = 12
HEAD_DIM = 64


ln_eps = 1e-12
score_scale = 0.0625
margin_weight = 0.5
root_half = 0.7071067811865476
inv_root_tau = 0.3989422804014327


def matmul(left, right):
    return jnp.dot(left, right, preferred_element_type=jnp.float32)


def left_across(left, right):
    return lax.dot_general(
        left, right, (((0,), (0,)), ((), ())), preferred_element_type=jnp.float32
    )


def right_across(left, right):
    return lax.dot_general(
        left, right, (((1,), (1,)), ((), ())), preferred_element_type=jnp.float32
    )


def normalize(hidden, gain, shift):
    centered = hidden - jnp.mean(hidden, axis=-1, keepdims=True)
    inv_std = lax.rsqrt(jnp.mean(centered * centered, axis=-1, keepdims=True) + ln_eps)
    unit_rows = centered * inv_std
    return (unit_rows * gain.astype(jnp.float32) + shift.astype(jnp.float32), unit_rows, inv_std)


def normalize_back(upstream, unit_rows, inv_std, gain):
    scaled = upstream * gain.astype(jnp.float32)
    hidden_grad = inv_std * (
        scaled
        - jnp.mean(scaled, axis=-1, keepdims=True)
        - unit_rows * jnp.mean(scaled * unit_rows, axis=-1, keepdims=True)
    )
    return (hidden_grad, jnp.sum(upstream * unit_rows, axis=0), jnp.sum(upstream, axis=0))


def gelu_exact(inputs):
    return 0.5 * inputs * (1.0 + lax.erf(inputs * root_half))


def gelu_slope(inputs):
    return 0.5 * (1.0 + lax.erf(inputs * root_half)) + inputs * inv_root_tau * jnp.exp(
        -0.5 * inputs * inputs
    )


def head_scores(query_heads, key_heads, lengths):
    slot_length = query_heads.shape[1]
    allowed = (lax.iota(jnp.int32, slot_length)[None, :] < lengths[:, None])[:, None, None, :]
    raw_scores = 0.125 * jnp.einsum(
        "bqhd,bkhd->bhqk", query_heads, key_heads, preferred_element_type=jnp.float32
    )
    return jnp.where(allowed, raw_scores, -1000000000.0)


def encode_forward(tokens, lengths, params):
    (
        weight_query,
        bias_query,
        weight_key,
        weight_value,
        bias_value,
        weight_out,
        bias_out,
        gain_attn,
        shift_attn,
        weight_in,
        bias_in,
        weight_back,
        bias_back,
        gain_ffn,
        shift_ffn,
    ) = params
    slot_count = lengths.shape[0]
    row_count = tokens.shape[0]
    split_heads = (slot_count, row_count // slot_count, HEADS, HEAD_DIM)
    queries = (matmul(tokens, weight_query) + bias_query.astype(jnp.float32)).astype(jnp.bfloat16)
    keys_all = matmul(tokens, weight_key).astype(jnp.bfloat16)
    values_all = (matmul(tokens, weight_value) + bias_value.astype(jnp.float32)).astype(
        jnp.bfloat16
    )
    scores = head_scores(queries.reshape(split_heads), keys_all.reshape(split_heads), lengths)
    peak_score = jnp.max(scores, axis=-1, keepdims=True)
    exp_scores = jnp.exp(scores - peak_score)
    row_total = jnp.sum(exp_scores, axis=-1, keepdims=True)
    soft_low = (exp_scores / row_total).astype(jnp.bfloat16)
    log_total = peak_score + jnp.log(row_total)
    context = jnp.einsum(
        "bhqk,bkhd->bqhd",
        soft_low,
        values_all.reshape(split_heads),
        preferred_element_type=jnp.float32,
    )
    context = context.reshape(row_count, D).astype(jnp.bfloat16)
    attn_sum = (
        tokens.astype(jnp.float32) + matmul(context, weight_out) + bias_out.astype(jnp.float32)
    )
    middle, unit_attn, inv_attn = normalize(attn_sum, gain_attn, shift_attn)
    middle_low = middle.astype(jnp.bfloat16)
    inner_act = matmul(middle_low, weight_in) + bias_in.astype(jnp.float32)
    gelu_low = gelu_exact(inner_act).astype(jnp.bfloat16)
    ffn_sum = middle + matmul(gelu_low, weight_back) + bias_back.astype(jnp.float32)
    output, unit_ffn, inv_ffn = normalize(ffn_sum, gain_ffn, shift_ffn)
    kept = (
        queries,
        keys_all,
        values_all,
        log_total,
        context,
        unit_attn,
        inv_attn,
        middle_low,
        inner_act,
        gelu_low,
        unit_ffn,
        inv_ffn,
    )
    return (output.astype(jnp.bfloat16), kept)


def ffn_backward(upstream, kept, params):
    (
        queries,
        keys_all,
        values_all,
        log_total,
        context,
        unit_attn,
        inv_attn,
        middle_low,
        inner_act,
        gelu_low,
        unit_ffn,
        inv_ffn,
    ) = kept
    weight_in, weight_back, gain_ffn = (params[9], params[11], params[13])
    ffn_grad, gain_grad, shift_grad = normalize_back(upstream, unit_ffn, inv_ffn, gain_ffn)
    branch_low = ffn_grad.astype(jnp.bfloat16)
    back_weight_grad = left_across(gelu_low, branch_low)
    back_bias_grad = jnp.sum(branch_low, axis=0, dtype=jnp.float32)
    inner_low = (right_across(branch_low, weight_back) * gelu_slope(inner_act)).astype(jnp.bfloat16)
    in_weight_grad = left_across(middle_low, inner_low)
    in_bias_grad = jnp.sum(inner_low, axis=0, dtype=jnp.float32)
    middle_grad = ffn_grad + right_across(inner_low, weight_in)
    return (
        middle_grad,
        (in_weight_grad, in_bias_grad, back_weight_grad, back_bias_grad, gain_grad, shift_grad),
    )


def attention_backward(middle_grad, tokens, lengths, kept, params):
    (
        queries,
        keys_all,
        values_all,
        log_total,
        context,
        unit_attn,
        inv_attn,
        middle_low,
        inner_act,
        gelu_low,
        unit_ffn,
        inv_ffn,
    ) = kept
    weight_query, weight_key, weight_value, weight_out, gain_attn = (
        params[0],
        params[2],
        params[3],
        params[5],
        params[7],
    )
    slot_count = lengths.shape[0]
    row_count = tokens.shape[0]
    split_heads = (slot_count, row_count // slot_count, HEADS, HEAD_DIM)
    attn_grad, gain_grad, shift_grad = normalize_back(middle_grad, unit_attn, inv_attn, gain_attn)
    attn_low = attn_grad.astype(jnp.bfloat16)
    out_weight_grad = left_across(context, attn_low)
    out_bias_grad = jnp.sum(attn_low, axis=0, dtype=jnp.float32)
    context_grad = right_across(attn_low, weight_out).astype(jnp.bfloat16).reshape(split_heads)
    query_heads = queries.reshape(split_heads)
    key_heads = keys_all.reshape(split_heads)
    value_heads = values_all.reshape(split_heads)
    soft_full = jnp.exp(head_scores(query_heads, key_heads, lengths) - log_total)
    soft_grad = jnp.einsum(
        "bqhd,bkhd->bhqk", context_grad, value_heads, preferred_element_type=jnp.float32
    )
    value_grad = jnp.einsum(
        "bhqk,bqhd->bkhd",
        soft_full.astype(jnp.bfloat16),
        context_grad,
        preferred_element_type=jnp.float32,
    )
    value_grad = value_grad.reshape(row_count, D).astype(jnp.bfloat16)
    score_low = (
        soft_full * (soft_grad - jnp.sum(soft_full * soft_grad, axis=-1, keepdims=True))
    ).astype(jnp.bfloat16)
    query_grad_low = 0.125 * jnp.einsum(
        "bhqk,bkhd->bqhd", score_low, key_heads, preferred_element_type=jnp.float32
    )
    query_grad_low = query_grad_low.reshape(row_count, D).astype(jnp.bfloat16)
    key_grad_low = 0.125 * jnp.einsum(
        "bhqk,bqhd->bkhd", score_low, query_heads, preferred_element_type=jnp.float32
    )
    key_grad_low = key_grad_low.reshape(row_count, D).astype(jnp.bfloat16)
    token_grad = (
        attn_grad
        + right_across(query_grad_low, weight_query)
        + right_across(key_grad_low, weight_key)
        + right_across(value_grad, weight_value)
    )
    grads = (
        left_across(tokens, query_grad_low),
        jnp.sum(query_grad_low, axis=0, dtype=jnp.float32),
        left_across(tokens, key_grad_low),
        left_across(tokens, value_grad),
        jnp.sum(value_grad, axis=0, dtype=jnp.float32),
        out_weight_grad,
        out_bias_grad,
        gain_grad,
        shift_grad,
    )
    return (token_grad, grads)


def on_device(
    query_tokens,
    passage_tokens,
    query_lengths,
    passage_lengths,
    passage_valid,
    positives,
    negatives,
    teacher_margins,
    query_grad,
    passage_grad,
    weight_query,
    bias_query,
    weight_key,
    weight_value,
    bias_value,
    weight_out,
    bias_out,
    gain_attn,
    shift_attn,
    weight_in,
    bias_in,
    weight_back,
    bias_back,
    gain_ffn,
    shift_ffn,
):
    params = (
        weight_query,
        bias_query,
        weight_key,
        weight_value,
        bias_value,
        weight_out,
        bias_out,
        gain_attn,
        shift_attn,
        weight_in,
        bias_in,
        weight_back,
        bias_back,
        gain_ffn,
        shift_ffn,
    )
    query_out, query_kept = encode_forward(query_tokens, query_lengths, params)
    passage_out, passage_kept = encode_forward(passage_tokens, passage_lengths, params)
    query_slots = query_lengths.shape[0]
    passage_slots = passage_lengths.shape[0]
    cls_query = query_out.reshape(query_slots, -1, D)[:, 0]
    cls_passage = passage_out.reshape(passage_slots, -1, D)[:, 0]
    valid_low = passage_valid.astype(jnp.bfloat16)

    def score_piece(cls_piece, valid_piece):
        scores = score_scale * right_across(cls_query, cls_piece)
        position = lax.iota(jnp.int32, cls_piece.shape[0])
        is_positive = position[None, :] == positives[:, None]
        is_negative = position[None, :] == negatives[:, None]
        allowed = (valid_piece[None, :] > 0.5) | is_positive
        return (scores, allowed, is_positive, is_negative)

    peak_score = jnp.full((query_slots,), -1e30, jnp.float32)
    scores, allowed, is_positive, is_negative = score_piece(
        lax.all_gather(cls_passage, "dp", axis=0, tiled=True),
        lax.all_gather(valid_low, "dp", axis=0, tiled=True),
    )
    masked = jnp.where(allowed, scores, -1e30)
    new_peak = jnp.maximum(peak_score, jnp.max(masked, axis=1))
    row_total = jnp.sum(jnp.where(allowed, jnp.exp(masked - new_peak[:, None]), 0.0), axis=1)
    positive_score = jnp.sum(jnp.where(is_positive, scores, 0.0), axis=1)
    negative_score = jnp.sum(jnp.where(is_negative, scores, 0.0), axis=1)
    peak_score, row_total, positive_score, negative_score = (
        new_peak,
        row_total,
        positive_score,
        negative_score,
    )
    all_cls, all_valid = (
        lax.all_gather(cls_passage, "dp", axis=0, tiled=True),
        lax.all_gather(valid_low, "dp", axis=0, tiled=True),
    )
    log_total = peak_score + jnp.log(row_total)
    shortfall = positive_score - negative_score - teacher_margins
    query_loss = log_total - positive_score + margin_weight * shortfall * shortfall
    scores, allowed, is_positive, is_negative = score_piece(all_cls, all_valid)
    soft_scores = jnp.where(allowed, jnp.exp(scores - log_total[:, None]), 0.0)
    positive_hit = is_positive.astype(jnp.float32)
    negative_hit = is_negative.astype(jnp.float32)
    score_grad = (
        soft_scores
        - positive_hit
        + 2.0 * margin_weight * shortfall[:, None] * (positive_hit - negative_hit)
    ).astype(jnp.bfloat16)
    cls_query_grad = score_scale * matmul(score_grad, all_cls)
    cls_passage_grad = lax.psum_scatter(
        score_scale * left_across(score_grad, cls_query), "dp", scatter_dimension=0, tiled=True
    )
    query_upstream = (
        query_grad.astype(jnp.float32)
        .reshape(query_slots, -1, D)
        .at[:, 0]
        .add(cls_query_grad)
        .reshape(-1, D)
    )
    passage_upstream = (
        passage_grad.astype(jnp.float32)
        .reshape(passage_slots, -1, D)
        .at[:, 0]
        .add(cls_passage_grad)
        .reshape(-1, D)
    )
    query_middle_grad, query_ffn = ffn_backward(query_upstream, query_kept, params)
    passage_middle_grad, passage_ffn = ffn_backward(passage_upstream, passage_kept, params)
    (
        in_weight_grad,
        in_bias_grad,
        back_weight_grad,
        back_bias_grad,
        ffn_gain_grad,
        ffn_shift_grad,
    ) = tuple((first + second for first, second in zip(query_ffn, passage_ffn)))
    query_tokens_grad, query_attn = attention_backward(
        query_middle_grad, query_tokens, query_lengths, query_kept, params
    )
    passage_tokens_grad, passage_attn = attention_backward(
        passage_middle_grad, passage_tokens, passage_lengths, passage_kept, params
    )
    (
        query_weight_grad,
        query_bias_grad,
        key_weight_grad,
        value_weight_grad,
        value_bias_grad,
        out_weight_grad,
        out_bias_grad,
        attn_gain_grad,
        attn_shift_grad,
    ) = tuple((first + second for first, second in zip(query_attn, passage_attn)))
    (
        query_weight_grad,
        query_bias_grad,
        key_weight_grad,
        value_weight_grad,
        value_bias_grad,
        out_weight_grad,
        out_bias_grad,
        attn_gain_grad,
        attn_shift_grad,
        in_weight_grad,
        in_bias_grad,
        back_weight_grad,
        back_bias_grad,
        ffn_gain_grad,
        ffn_shift_grad,
    ) = (
        lax.psum_scatter(query_weight_grad, "dp", scatter_dimension=0, tiled=True),
        lax.psum_scatter(query_bias_grad, "dp", scatter_dimension=0, tiled=True),
        lax.psum_scatter(key_weight_grad, "dp", scatter_dimension=0, tiled=True),
        lax.psum_scatter(value_weight_grad, "dp", scatter_dimension=0, tiled=True),
        lax.psum_scatter(value_bias_grad, "dp", scatter_dimension=0, tiled=True),
        lax.psum_scatter(out_weight_grad, "dp", scatter_dimension=0, tiled=True),
        lax.psum_scatter(out_bias_grad, "dp", scatter_dimension=0, tiled=True),
        lax.psum_scatter(attn_gain_grad, "dp", scatter_dimension=0, tiled=True),
        lax.psum_scatter(attn_shift_grad, "dp", scatter_dimension=0, tiled=True),
        lax.psum_scatter(in_weight_grad, "dp", scatter_dimension=0, tiled=True),
        lax.psum_scatter(in_bias_grad, "dp", scatter_dimension=0, tiled=True),
        lax.psum_scatter(back_weight_grad, "dp", scatter_dimension=0, tiled=True),
        lax.psum_scatter(back_bias_grad, "dp", scatter_dimension=0, tiled=True),
        lax.psum_scatter(ffn_gain_grad, "dp", scatter_dimension=0, tiled=True),
        lax.psum_scatter(ffn_shift_grad, "dp", scatter_dimension=0, tiled=True),
    )
    return (
        query_out,
        passage_out,
        query_loss,
        query_tokens_grad,
        passage_tokens_grad,
        query_weight_grad,
        query_bias_grad,
        key_weight_grad,
        value_weight_grad,
        value_bias_grad,
        out_weight_grad,
        out_bias_grad,
        attn_gain_grad,
        attn_shift_grad,
        in_weight_grad,
        in_bias_grad,
        back_weight_grad,
        back_bias_grad,
        ffn_gain_grad,
        ffn_shift_grad,
    )


F32 = jnp.float32
BF16 = jnp.bfloat16
MESH = pl.DeviceIdType.MESH
FF = 3072
ROWS = 480
WIN = 240
SLOT = 220
NEG = -1000000000.0


def dot_nn(left, right):
    return jnp.dot(left, right, preferred_element_type=F32)


def dot_nt(left, right):
    return lax.dot_general(left, right, (((1,), (1,)), ((), ())), preferred_element_type=F32)


def dot_tn(left, right):
    return lax.dot_general(left, right, (((0,), (0,)), ((), ())), preferred_element_type=F32)


def row_of(ref, start=0, size=D):
    return ref[pl.ds(start, size)].astype(F32).reshape(1, size)


def item(ref, at):
    return ref[...].reshape(1, 2)[:, at:at + 1]


def blocks(start, stop, size):
    return [(at, min(size, stop - at)) for at in range(start, stop, size)]


def iota(shape, dim):
    return lax.broadcasted_iota(jnp.int32, shape, dim)


def fold8(block):
    return jnp.sum(block.reshape(-1, 8, block.shape[-1]), axis=0)


WIDE = 256
ROUTE = (
    "xyz", "yxz", "ryx", "xyz", "rxy", "ryx", "yxz", "xyz", "yxz", "xyz", "yxz", "xyz", "yxz", "xyz", "yxz", "xyz",
    "yxz", "xyz",
)
ORDER = (
    ("wback", 0, 0), ("c", 0, 0), ("wback", 0, 1), ("c", 0, 1), ("wback", 0, 2), ("c", 0, 2), ("wback", 1, 0),
    ("c", 1, 0), ("ec", 0, 0), ("wback", 1, 1), ("ec", 0, 1), ("c", 1, 1), ("wback", 1, 2), ("ec", 0, 2),
    ("c", 1, 2), ("dinner", 0), ("dinner", 1), ("win", 2, 0), ("c", 2, 0), ("ec", 1, 0), ("win", 2, 1), ("c", 2, 1),
    ("win", 2, 2), ("c", 2, 2), ("ec", 1, 1), ("ec", 2, 0), ("dinner", 2), ("dinner", 3), ("e1", 0, 1),
    ("win", 3, 0), ("c", 3, 0), ("win", 3, 1), ("e1", 0, 0), ("c", 3, 1), ("win", 3, 2), ("ec", 2, 1), ("ec", 1, 2),
    ("c", 3, 2), ("dmid", 0), ("dmid", 1), ("ec", 2, 2), ("ec", 3, 1), ("e1", 0, 2), ("ec", 3, 0), ("dmid", 2),
    ("dmid", 3), ("ec", 3, 2), ("lnback",), ("e2", 0, 1), ("dctx",), ("e1", 1, 0), ("e2", 0, 0), ("qslot",),
    ("attn", 0, 1), ("e1", 2, 0), ("e1", 1, 1), ("attn", 1, 2), ("e1", 2, 1), ("attn", 3, 3), ("sums",),
    ("e1", 3, 0), ("e1", 1, 2), ("wvo", 0), ("e1", 3, 1), ("c", 4, 0), ("vec", 0), ("wvo", 1), ("c", 4, 1),
    ("e1", 2, 2), ("wvo", 2), ("e1", 3, 2), ("c", 4, 2), ("wqk", 0), ("c", 5, 0), ("wqk", 1), ("ec", 4, 1),
    ("c", 5, 1), ("wqk", 2), ("e2", 2, 1), ("ec", 4, 2), ("e3", 0, 1), ("e2", 3, 0), ("e2", 2, 0), ("vec", 1),
    ("e2", 3, 1), ("ec", 5, 1), ("e2", 1, 0), ("e2", 3, 2), ("ec", 5, 0), ("e2", 2, 2), ("e1", 4, 1), ("e1", 4, 2),
    ("vec", 2), ("ec", 4, 0), ("c", 5, 2), ("tq",), ("e3", 3, 0), ("e1", 5, 1), ("ec", 5, 2), ("e2", 4, 1),
    ("e1", 5, 0), ("vec", 3), ("e3", 0, 0), ("e2", 0, 2), ("e2", 5, 1), ("tk",), ("e2", 1, 2), ("e1", 4, 0),
    ("e2", 4, 2), ("e3", 2, 0), ("e1", 5, 2), ("e2", 5, 0), ("e3", 3, 1), ("e2", 1, 1), ("e2", 4, 0), ("e3", 2, 2),
    ("e2", 5, 2), ("e3", 1, 2), ("e3", 1, 1), ("e3", 4, 2), ("e3", 0, 2), ("e3", 4, 1), ("e4", 1, 1), ("e3", 2, 1),
    ("vecend",), ("e3", 5, 1), ("e3", 5, 0), ("e3", 3, 2), ("tv",), ("tout",), ("e3", 4, 0), ("e3", 1, 0),
    ("e4", 0, 2), ("e4", 1, 2), ("e3", 5, 2),
)


RELAYS = max(1, sum(way[0] == "r" for way in ROUTE))


def layer_kernel(
    qtok, ptok, qlen, plen_h, pvalid_h, pos, neg, margin, qgrad, pgrad,
    wq_h, bq_h, wk_h, wv_h, bv_h, wo_h, bo_h, ga_h, sa_h, wi_h, bi_h, wb_h, bb_h, gf_h, sf_h,
    qout_h, pout_h, qtg_h, ptg_h, wqg, wkg, wvg, wog, wig, wbg, small_h,
    plen, pvalid, bq, bv, bo, ga, sa, bi, bb, gf, sf, wq, wk, wv, wo, wi, wb, pstage, x_s, xT, q_s, k_s, v_s, p_s, pq_s, c_s, cT, n1, n2, r1, r2,
    ml, mlT, act_a, act_b, actT, tmp_a, tmp_b, gp, qg_s, pg_s, qo_s, po_s, ex, ex_f, vec, vecr, vecs, vecz, small_o, parts,
    g_s, rc, ra, rb, rz, rw, rw_mate, rw_far, rw_in,
    load_sem, out_sem, part_sem, ex_send, ex_recv, c_send, c_recv, a_send, a_recv, b_send, b_recv,
    z_send, z_recv, r_send, v_send, v_recv, credit,
):
    me = lax.axis_index("dp")
    core = lax.rem(me, 2)
    xx = lax.rem(lax.div(me, 2), 2)
    yy = lax.rem(lax.div(me, 4), 2)
    zz = lax.div(me, 8)
    chip = lax.div(me, 2)
    partner = me + 1 - 2 * core
    x_peer = me + 2 - 4 * xx
    y_peer = me + 4 - 8 * yy
    plane = lax.rem(me, 8)

    loads = {}

    def load(name, source, target):
        loads[name] = pltpu.make_async_copy(source, target, load_sem.at[len(loads)])
        loads[name].start()

    load("ptok", ptok, pstage)
    load("qtok", qtok, qo_s)
    load("wq", wq_h, wq)
    vectors = (
        (plen_h, plen), (pvalid_h, pvalid), (bq_h, bq), (bv_h, bv), (bo_h, bo), (ga_h, ga), (sa_h, sa), (bi_h, bi),
        (bb_h, bb), (gf_h, gf), (sf_h, sf),
    )
    for at, (source, target) in enumerate(vectors):
        load("vec" + str(at), source, target)
    load("wk", wk_h, wk)
    load("wv", wv_h, wv)

    barrier = pltpu.get_barrier_semaphore()
    for hop in range(1, 16):
        other = 2 * lax.rem(chip + hop, 16) + core
        pl.semaphore_signal(barrier, inc=1, device_id=(other,), device_id_type=MESH)
    pl.semaphore_signal(barrier, inc=1, device_id=(partner,), device_id_type=MESH)

    loads["ptok"].wait()
    loads["qtok"].wait()
    x_s[0:32, :] = qo_s[...]

    def copy_tokens(i, carry):
        x_s[pl.ds(pl.multiple_of(32 + i * 16, 16), 16), :] = pstage[pl.ds(pl.multiple_of(i * 16, 16), 16), :]
        return carry

    lax.fori_loop(0, 27, copy_tokens, 0)
    x_s[464:480, :] = jnp.concatenate(
        [pstage[432:440, :].astype(F32), jnp.zeros((8, D), F32)], axis=0
    ).astype(BF16)

    loads["wq"].wait()
    for at in range(len(vectors)):
        loads["vec" + str(at)].wait()
    load("wo", wo_h, wo)
    load("wi", wi_h, wi)

    def project_queries(start, stop):
        rows = pl.ds(start, stop - start)
        q_s[rows, :] = ((dot_nn(x_s[rows, :], wq[...]) + row_of(bq)).astype(BF16) * 0.125).astype(BF16)

    project_queries(0, 256)
    loads["wk"].wait()
    k_s[...] = dot_nn(x_s[...], wk[...]).astype(BF16)
    loads["wv"].wait()
    for h in range(3):
        load("wb" + str(h), wb_h.at[:, :, :, :, :, :, pl.ds(WIDE * h, WIDE)], wb.at[h])
    load("qg", qgrad, qg_s)
    load("pg", pgrad, pg_s)
    v_s[...] = (dot_nn(x_s[...], wv[...]) + row_of(bv)).astype(BF16)

    head_of = iota((12, 1, D), 2) // 64
    head_mask = (head_of == iota((12, 1, D), 0)).astype(F32)

    def spread(rows):
        return (rows.astype(F32)[None] * head_mask).astype(BF16).reshape(384, D)

    def gather_heads(stacked):
        return jnp.sum(stacked.reshape(12, 32, D) * head_mask, axis=0)

    raw = dot_nt(k_s[0:32, :], spread(q_s[0:32, :]))
    raw = jnp.where(iota((32, 384), 0) < qlen[0], raw, NEG)
    soft = jnp.exp(raw - jnp.max(raw, axis=0, keepdims=True))
    soft = (soft * (1.0 / jnp.sum(soft, axis=0, keepdims=True))).astype(BF16)
    pq_s[...] = soft
    c_s[0:32, :] = gather_heads(dot_tn(soft, v_s[0:32, :])).astype(BF16)

    by_head = (q_s[240:256, :].astype(F32)[None] * head_mask).astype(BF16).reshape(192, D)
    raw = dot_nt(by_head, k_s[240:480, :])
    key_lane = iota((1, WIN), 1)
    raw = jnp.where((key_lane >= 12) & (key_lane < 12 + item(plen, 1)), raw, NEG)
    soft = jnp.exp(raw - jnp.max(raw, axis=1, keepdims=True))
    soft = (soft * (1.0 / jnp.sum(soft, axis=1, keepdims=True))).astype(BF16)
    block = jnp.sum(dot_nn(soft, v_s[240:480, :]).reshape(12, 16, D) * head_mask, axis=0)

    lane = iota((1, 128), 1)
    half = ((lane < 64).astype(BF16), (lane >= 64).astype(BF16))
    key_at = iota((WIN, 1), 0)

    def attend(pair, slot):
        lanes = pl.ds(pl.multiple_of(pair * 128, 128), 128)
        low_at = 12 * slot
        first_row = 32 + 208 * slot
        rows = pl.ds(first_row, WIN)
        keys, queries = k_s[rows, lanes], q_s[rows, lanes]
        values_t = v_s[rows, lanes].T
        allowed = (key_at >= low_at) & (key_at < low_at + item(plen, slot))
        parts = []
        for h in range(2):
            scores = jnp.where(allowed, dot_nt(keys, queries * half[h]), NEG)
            e = jnp.exp(scores - jnp.max(scores, axis=0, keepdims=True))
            p = (e * (1.0 / jnp.sum(e, axis=0, keepdims=True))).astype(BF16)
            p_s[slot, 2 * pair + h] = p
            parts.append(dot_nn(values_t, p)[64 * h:64 * h + 64, :])
        context = jnp.concatenate(parts, axis=0).T
        if slot == 0:
            c_s[rows, lanes] = context.astype(BF16)
            return
        old = c_s[240:256, lanes].astype(F32)
        c_s[240:256, lanes] = jnp.where(iota((16, 128), 0) >= 12, context[0:16], old).astype(BF16)
        c_s[256:480, lanes] = context[16:240].astype(BF16)

    def attend_slot(slot):
        def two_pairs(i, carry):
            attend(2 * i, slot)
            attend(2 * i + 1, slot)
            return carry

        lax.fori_loop(0, 3, two_pairs, 0)

    attend_slot(0)
    old = c_s[240:256, :].astype(F32)
    c_s[240:256, :] = jnp.where(iota((16, 1), 0) >= 12, block, old).astype(BF16)

    loads["wo"].wait()
    gain1, shift1, bias1 = row_of(ga), row_of(sa), row_of(bo)
    gain2, shift2, bias2 = row_of(gf), row_of(sf), row_of(bb)

    def wb_tile(t):
        return jnp.concatenate([wb[h, t // 2, t % 2].reshape(D, WIDE) for h in range(3)], axis=1)

    def normalized(hidden):
        centered = hidden - jnp.mean(hidden, axis=-1, keepdims=True)
        inv = lax.rsqrt(jnp.mean(centered * centered, axis=-1, keepdims=True) + ln_eps)
        return centered * inv, inv

    def forward_rows(start, stop):
        size = stop - start
        every, own = pl.ds(start, size), pl.ds(0, size)
        tmp_a[own, :] = dot_nn(c_s[every, :], wo[...])
        for at, count in blocks(0, size, 32):
            rows, here = pl.ds(start + at, count), pl.ds(at, count)
            unit, inv = normalized(tmp_a[here, :] + x_s[rows, :].astype(F32) + bias1)
            n1[rows, :] = unit
            r1[rows, :] = inv
            ml[rows, :] = (unit * gain1 + shift1).astype(BF16)
        if start == 0:
            loads["wi"].wait()
            for h in range(3):
                loads["wb" + str(h)].wait()
        inner, acts = (tmp_a, tmp_b), (act_a, act_b)
        tmp_a[own, :] = dot_nn(ml[every, :], wi[:, 0:D])
        mlT[:, every] = ml[every, :].T
        xT[:, every] = x_s[every, :].T
        cT[:, every] = c_s[every, :].T

        def finish(t):
            act = acts[t % 2][own, :]
            if t == 0:
                n2[every, :] = dot_nn(act, wb_tile(t))
            else:
                n2[every, :] += dot_nn(act, wb_tile(t))
            actT[t * D:t * D + D, every] = act.T

        for t in range(4):
            if t < 3:
                inner[(t + 1) % 2][own, :] = dot_nn(ml[every, :], wi[:, t * D + D:t * D + 2 * D])
            bias_t = row_of(bi, t * D)
            for at, count in blocks(0, size, 16):
                here = pl.ds(at, count)
                u = inner[t % 2][here, :] + bias_t
                cdf = 0.5 * (1.0 + lax.erf(u * root_half))
                acts[t % 2][here, :] = (u * cdf).astype(BF16)
                gp[start + at:start + at + count, t * D:t * D + D] = (
                    cdf + u * inv_root_tau * jnp.exp(-0.5 * u * u)
                ).astype(BF16)
            if t > 0:
                finish(t - 1)
        finish(3)
        for at, count in blocks(start, stop, 32):
            rows = pl.ds(at, count)
            unit, inv = normalized(n2[rows, :] + (n1[rows, :] * gain1 + shift1) + bias2)
            n2[rows, :] = unit
            r2[rows, :] = inv
            out = (unit * gain2 + shift2).astype(BF16)
            if at == 0:
                qo_s[...] = out
            else:
                po_s[at - 32:min(at, 440), :] = out[0:min(count, 472 - at)]

    forward_rows(0, 256)

    slot_me = core * 16 + chip
    base = pl.multiple_of(slot_me * 32, 32)
    first_rows = (
        qo_s[0:16, :].astype(F32)[0:1],
        po_s[0:16, :].astype(F32)[0:1],
        po_s[208:224, :].astype(F32)[12:13],
    )
    lane_row = iota((1, 128), 1)
    meta = jnp.zeros((1, 128), F32)
    margin_0 = jnp.zeros((1, 128), F32) + margin[0]
    margin_1 = margin_0.astype(BF16).astype(F32)
    margin_2 = (margin_0 - margin_1).astype(BF16).astype(F32)
    for at, value in enumerate((
        item(pvalid, 0).astype(F32), item(pvalid, 1).astype(F32), pos[0].astype(F32), neg[0].astype(F32),
        margin_1, margin_2, margin_0 - margin_1 - margin_2,
    )):
        meta = jnp.where(lane_row == at, value, meta)
    pieces = [row[:, 128 * i:128 * i + 128] for row in first_rows for i in range(6)]
    ex[pl.ds(base, 32), :] = jnp.concatenate(pieces + [meta, jnp.zeros((13, 128), F32)], axis=0).astype(BF16)

    pl.semaphore_wait(barrier, 16)
    sends = []
    for hop in range(1, 16):
        block = ex.at[pl.ds(base, 32), :]
        sends.append(pltpu.make_async_remote_copy(
            src_ref=block, dst_ref=block, send_sem=ex_send.at[hop], recv_sem=ex_recv.at[hop],
            device_id=(2 * lax.rem(chip + hop, 16) + core,), device_id_type=MESH,
        ))
        sends[-1].start()

    project_queries(256, 480)
    attend_slot(1)
    forward_rows(256, 480)
    out_q = pltpu.make_async_copy(qo_s, qout_h, out_sem.at[0])
    out_p = pltpu.make_async_copy(po_s, pout_h, out_sem.at[1])
    out_q.start()
    out_p.start()
    loads["qg"].wait()
    loads["pg"].wait()

    def ffn_norm_back(r0, upstream, sums):
        rows = pl.ds(r0, upstream.shape[0])
        unit = n2[rows, :]
        scaled = upstream * gain2
        hidden_grad = r2[rows, :] * (
            scaled
            - jnp.mean(scaled, axis=-1, keepdims=True)
            - unit * jnp.mean(scaled * unit, axis=-1, keepdims=True)
        )
        n2[rows, :] = hidden_grad
        rounded = hidden_grad.astype(BF16)
        ml[rows, :] = rounded
        return (
            sums[0] + fold8(upstream * unit), sums[1] + fold8(upstream), sums[2] + fold8(rounded.astype(F32)),
        )

    zero8 = jnp.zeros((8, D), F32)
    sums = (zero8, zero8, zero8)

    for i in (1, 2, 3, 4, 5, 7, 8, 9, 10, 11, 12):
        sums = ffn_norm_back(32 + 32 * i, pg_s[32 * i:32 * i + 32, :].astype(F32), sums)
    last = jnp.concatenate([pg_s[416:440, :].astype(F32), jnp.zeros((8, D), F32)], axis=0)
    sums = ffn_norm_back(448, last, sums)

    for send in sends:
        send.wait()
    same_core = ex.at[pl.ds(pl.multiple_of(core * 512, 512), 512), :]
    across = pltpu.make_async_remote_copy(
        src_ref=same_core, dst_ref=same_core, send_sem=ex_send.at[0], recv_sem=ex_recv.at[0],
        device_id=(partner,), device_id_type=MESH,
    )
    across.start()
    across.wait()

    ex_f[0:1024, :] = ex[...].astype(F32)

    def first(r):
        return ex_f[pl.ds(r, 32, stride=32), :]

    cls_q = jnp.concatenate([first(i) for i in range(6)], axis=1)
    cls_0 = jnp.concatenate([first(6 + i) for i in range(6)], axis=1).astype(BF16)
    cls_1 = jnp.concatenate([first(12 + i) for i in range(6)], axis=1).astype(BF16)
    metas = first(18)
    metas_t = metas.T
    s0 = score_scale * dot_nt(cls_q.astype(BF16), cls_0)
    s1 = score_scale * dot_nt(cls_q.astype(BF16), cls_1)
    col = iota((1, 32), 1)
    passage = (4 * lax.rem(col, 16) + 2 * lax.div(col, 16)).astype(F32)
    at_pos, at_neg, wanted = metas[:, 2:3], metas[:, 3:4], metas[:, 4:5] + metas[:, 5:6] + metas[:, 6:7]
    pos0, pos1 = at_pos == passage, at_pos == passage + 1.0
    neg0, neg1 = at_neg == passage, at_neg == passage + 1.0
    m0 = jnp.where((metas_t[0:1, :] > 0.5) | pos0, s0, -1e30)
    m1 = jnp.where((metas_t[1:2, :] > 0.5) | pos1, s1, -1e30)
    peak = jnp.maximum(jnp.max(m0, axis=1, keepdims=True), jnp.max(m1, axis=1, keepdims=True))
    total = jnp.sum(jnp.exp(m0 - peak), axis=1, keepdims=True) + jnp.sum(jnp.exp(m1 - peak), axis=1, keepdims=True)
    lse = peak + jnp.log(total)

    def picked(where0, where1):
        return jnp.sum(jnp.where(where0, s0, 0.0), axis=1, keepdims=True) + jnp.sum(
            jnp.where(where1, s1, 0.0), axis=1, keepdims=True
        )

    at_positive = picked(pos0, pos1)
    miss = at_positive - picked(neg0, neg1) - wanted
    losses = lse - at_positive + margin_weight * miss * miss
    pos0, pos1, neg0, neg1 = (hit.astype(F32) for hit in (pos0, pos1, neg0, neg1))
    ds0 = (jnp.exp(m0 - lse) - pos0 + 2.0 * margin_weight * miss * (pos0 - neg0)).astype(BF16)
    ds1 = (jnp.exp(m1 - lse) - pos1 + 2.0 * margin_weight * miss * (pos1 - neg1)).astype(BF16)
    mine = iota((32, 1), 0) == slot_me
    mine_col = iota((1, 32), 1) == slot_me
    small_o[9:10, :] = jnp.sum(jnp.where(mine, losses, 0.0), axis=0, keepdims=True) + jnp.zeros((1, 128), F32)
    dq_all = score_scale * (dot_nn(ds0, cls_0) + dot_nn(ds1, cls_1))
    d_query = jnp.sum(jnp.where(mine, dq_all, 0.0), axis=0, keepdims=True)

    def passage_grad_row(ds):
        column = jnp.sum(jnp.where(mine_col, ds.astype(F32), 0.0), axis=1, keepdims=True)
        return score_scale * jnp.sum(column * cls_q, axis=0, keepdims=True)

    d_first = (d_query, passage_grad_row(ds0), passage_grad_row(ds1))

    row32 = iota((32, 1), 0)
    for r0, at, source, add in (
        (0, 0, qg_s[...], d_first[0]), (32, 0, pg_s[0:32, :], d_first[1]), (224, 28, pg_s[192:224, :], d_first[2]),
    ):
        upstream = source.astype(F32) + jnp.where(row32 == at, add, 0.0)
        sums = ffn_norm_back(r0, upstream, sums)
    vec[...] = jnp.zeros_like(vec)
    vec[5:6, :] = jnp.sum(sums[2], axis=0, keepdims=True)
    vec[6:7, :] = jnp.sum(sums[0], axis=0, keepdims=True)
    vec[7:8, :] = jnp.sum(sums[1], axis=0, keepdims=True)

    def chunk(p, h):
        return g_s.at[p, h] if p < 4 else wb.at[h, p - 4]

    z_slot, r_slot = {}, {}
    for at, way in enumerate(ROUTE):
        for kind, slots in (("z", z_slot), ("r", r_slot)):
            if way[0] == kind:
                slots[(at // 3, at % 3)] = len(slots)
    inner = (zz == 1) | (zz == 2)
    mate = zz + 1 - 2 * lax.rem(zz, 2)
    far = 2 - 2 * lax.div(zz, 2)

    def route(p, h):
        return ROUTE[3 * p + h]

    def remote(source, target, send, recv, device):
        return pltpu.make_async_remote_copy(
            src_ref=source, dst_ref=target, send_sem=send, recv_sem=recv, device_id=(device,), device_id_type=MESH,
        )

    def step_c(p, h):
        return [remote(chunk(p, h).at[1 - core], rc.at[p % 2, h], c_send.at[p, h], c_recv.at[p, h], partner)]

    def along_z(p, h, pick, target):
        steps = []
        for hop in range(1, 4):
            to = lax.rem(zz + hop, 4)
            steps.append(remote(
                pick(to), target(hop - 1), z_send.at[p, h, hop - 1], z_recv.at[p, h, hop - 1], to * 8 + plane,
            ))
        return steps

    def step_1(p, h):
        mine, way = chunk(p, h), route(p, h)
        if way[0] == "z":
            return along_z(p, h, lambda to: mine.at[core, to], lambda i: rw.at[z_slot[(p, h)], i])
        away = mine.at[core, :, :, 1 - xx] if way == "xyz" else mine.at[core, :, 1 - yy]
        return [remote(away, ra.at[p, h], a_send.at[p, h], a_recv.at[p, h], x_peer if way == "xyz" else y_peer)]

    def step_2(p, h):
        mine, way = chunk(p, h), route(p, h)
        if way in ("zyx", "ryx"):
            away, target = mine.at[core, zz, 1 - yy], rb.at[p, h, 0:2]
        elif way in ("zxy", "rxy"):
            away, target = mine.at[core, zz, :, 1 - xx], rb.at[p, h, 0:2]
        elif way == "xyz":
            away, target = mine.at[core, :, 1 - yy, xx], rb.at[p, h]
        else:
            away, target = mine.at[core, :, yy, 1 - xx], rb.at[p, h]
        return [remote(away, target, b_send.at[p, h], b_recv.at[p, h], x_peer if way[1] == "x" else y_peer)]

    def step_3(p, h):
        mine = chunk(p, h)
        way = route(p, h)
        if way[0] in "zr":
            away = mine.at[core, zz, yy, 1 - xx] if way[2] == "x" else mine.at[core, zz, 1 - yy, xx]
            return [remote(
                away, rz.at[p, h, 0], a_send.at[p, h], a_recv.at[p, h], x_peer if way[2] == "x" else y_peer,
            )]
        return along_z(p, h, lambda to: mine.at[core, to, yy, xx], lambda i: rz.at[p, h, i])

    def begin(steps):
        for step in steps:
            step.start()

    def finish_steps(steps):
        for step in steps:
            step.wait()

    def mate_step(p, h):
        return remote(
            chunk(p, h).at[core, mate], rw_mate.at[r_slot[(p, h)]], z_send.at[p, h, 0], z_recv.at[p, h, 0],
            mate * 8 + plane,
        )

    def far_step(p, h):
        return remote(
            chunk(p, h).at[core, pl.ds(far, 2)], rw_far.at[r_slot[(p, h)]], z_send.at[p, h, 1], z_recv.at[p, h, 1],
            mate * 8 + plane,
        )

    def relay_step(p, h, i):
        return remote(
            chunk(p, h).at[core, far + i], rw_in.at[r_slot[(p, h)]], r_send.at[r_slot[(p, h)], i], z_recv.at[p, h, 2],
            (far + i) * 8 + plane,
        )

    def start_relay(p, h):
        mate_step(p, h).start()

        @pl.when(jnp.logical_not(inner))
        def _():
            far_step(p, h).start()

    def relay_on(p, h):
        @pl.when(inner)
        def _():
            far_step(p, h).wait_recv()

            def add(i, carry):
                for y in range(2):
                    for x in range(2):
                        chunk(p, h)[core, far + i, y, x] += rw_far[r_slot[(p, h)], i, y, x]
                return carry

            lax.fori_loop(0, 2, add, 0)
            for i in range(2):
                relay_step(p, h, i).start()

        @pl.when(jnp.logical_not(inner))
        def _():
            far_step(p, h).wait_send()

    def end_relay(p, h):
        mate_step(p, h).wait()
        relay_step(p, h, 0).wait_recv()

        @pl.when(inner)
        def _():
            for i in range(2):
                relay_step(p, h, i).wait_send()

        mine, at = chunk(p, h), r_slot[(p, h)]

        def add(y, carry):
            for x in range(2):
                total = mine[core, zz, y, x].astype(F32) + rw_mate[at, y, x].astype(F32) + rw_in[at, y, x].astype(F32)
                mine[core, zz, y, x] = total.astype(BF16)
            return carry

        lax.fori_loop(0, 2, add, 0)
        begin(step_2(p, h))

    def start_c(p, h):
        if p >= 2:
            pl.semaphore_wait(credit.at[p % 2, h], 1)
        begin(step_c(p, h))

    def end_c(p, h):
        finish_steps(step_c(p, h))

        def add(z, carry):
            for y in range(2):
                for x in range(2):
                    chunk(p, h)[core, z, y, x] += rc[p % 2, h, z, y, x]
            return carry

        lax.fori_loop(0, 4, add, 0)
        if route(p, h)[0] == "r":
            start_relay(p, h)
        else:
            begin(step_1(p, h))
        if p < 4:
            pl.semaphore_signal(credit.at[p % 2, h], inc=1, device_id=(partner,), device_id_type=MESH)

    def end_1(p, h):
        finish_steps(step_1(p, h))
        mine, way = chunk(p, h), route(p, h)
        if way[0] == "z":
            def add(y, carry):
                for x in range(2):
                    total = mine[core, zz, y, x].astype(F32)
                    for i in range(3):
                        total += rw[z_slot[(p, h)], i, y, x].astype(F32)
                    mine[core, zz, y, x] = total.astype(BF16)
                return carry

            lax.fori_loop(0, 2, add, 0)
        else:
            def add(z, carry):
                for i in range(2):
                    if way == "yxz":
                        mine[core, z, yy, i] += ra[p, h, z, i]
                    else:
                        mine[core, z, i, xx] += ra[p, h, z, i]
                return carry

            lax.fori_loop(0, 4, add, 0)
        begin(step_2(p, h))

    def end_2(p, h):
        finish_steps(step_2(p, h))
        mine = chunk(p, h)
        way = route(p, h)
        if way[0] in "zr":
            for i in range(2):
                if way[1] == "y":
                    mine[core, zz, yy, i] += rb[p, h, i]
                else:
                    mine[core, zz, i, xx] += rb[p, h, i]
        else:
            def add(z, carry):
                mine[core, z, yy, xx] += rb[p, h, z]
                return carry

            lax.fori_loop(0, 4, add, 0)
        begin(step_3(p, h))

    outs = []

    def end_3(p, h):
        finish_steps(step_3(p, h))
        total = chunk(p, h)[core, zz, yy, xx].astype(F32)
        for i in range(1 if route(p, h)[0] in "zr" else 3):
            total += rz[p, h, i].astype(F32)
        parts[p, h] = total
        at = WIDE * h
        if p < 2:
            targets = [wbg.at[pl.ds(48 * p, 48), pl.ds(at, WIDE)]]
        elif p < 4:
            at += (p - 2) * 2 * D
            targets = [wig.at[:, pl.ds(at, WIDE)], wig.at[:, pl.ds(at + D, WIDE)]]
        else:
            targets = [ref.at[:, pl.ds(at, WIDE)] for ref in ((wvg, wog) if p == 4 else (wqg, wkg))]
        rows = 48 // len(targets)
        for i, target in enumerate(targets):
            outs.append(pltpu.make_async_copy(parts.at[p, h, pl.ds(rows * i, rows)], target, part_sem.at[p, h, i]))
            outs[-1].start()

    def store_grad(p, h, grad):
        for i in range(32):
            chunk(p, h)[i % 2, i // 8, (i // 4) % 2, (i // 2) % 2] = grad[i]

    def back_grad(p, h):
        left = jnp.concatenate([actT[96 * i + 48 * p:96 * i + 48 * p + 48, :] for i in range(32)], axis=0)
        grad = dot_nn(left, ml[:, WIDE * h:WIDE * h + WIDE]).astype(BF16)
        store_grad(p, h, grad.reshape(32, 48, WIDE))

    def pair_grad(p, h, left_0, right_0, left_1, right_1):
        cols = pl.ds(WIDE * h, WIDE)
        grad_0 = dot_nn(left_0[...], right_0[:, cols]).reshape(32, 24, WIDE)
        grad_1 = dot_nn(left_1[...], right_1[:, cols]).reshape(32, 24, WIDE)
        store_grad(p, h, jnp.concatenate([grad_0, grad_1], axis=1).astype(BF16))

    def in_grad(p, h):
        at = (p - 2) * 2 * D
        pair_grad(p, h, mlT, gp.at[:, pl.ds(at, D)], mlT, gp.at[:, pl.ds(at + D, D)])

    def inner_grad(t):
        cols = pl.ds(t * D, D)
        weight = wb_tile(t)
        tmp_a[...] = dot_nt(ml[0:256, :], weight)
        tmp_b[0:224, :] = dot_nt(ml[256:480, :], weight)
        total = zero8
        for ref, start, size in ((tmp_a, 0, 256), (tmp_b, 256, 224)):
            for at, count in blocks(0, size, 16):
                rows = pl.ds(start + at, count)
                rounded = (ref[at:at + count, :] * gp[rows, cols].astype(F32)).astype(BF16)
                gp[rows, cols] = rounded
                total = total + fold8(rounded.astype(F32))
        vec[8 + t:9 + t, :] = jnp.sum(total, axis=0, keepdims=True)

    def middle_grad(t):
        cols = pl.ds(t * D, D)
        n2[...] += dot_nt(gp[:, cols], wi[:, cols])

    def attn_norm_back():
        def block(i, sums):
            rows = pl.ds(pl.multiple_of(i * 32, 32), 32)
            upstream, unit = n2[rows, :], n1[rows, :]
            scaled = upstream * gain1
            hidden_grad = r1[rows, :] * (
                scaled
                - jnp.mean(scaled, axis=-1, keepdims=True)
                - unit * jnp.mean(scaled * unit, axis=-1, keepdims=True)
            )
            n1[rows, :] = hidden_grad
            rounded = hidden_grad.astype(BF16)
            ml[rows, :] = rounded
            return (
                sums[0] + fold8(upstream * unit), sums[1] + fold8(upstream), sums[2] + fold8(rounded.astype(F32)),
            )

        sums = lax.fori_loop(0, 15, block, (zero8, zero8, zero8))
        vec[2:3, :] = jnp.sum(sums[2], axis=0, keepdims=True)
        vec[3:4, :] = jnp.sum(sums[0], axis=0, keepdims=True)
        vec[4:5, :] = jnp.sum(sums[1], axis=0, keepdims=True)

    def context_grad():
        c_s[...] = dot_nt(ml[...], wo[...]).astype(BF16)

    def query_slot_back():
        q_rows, k_rows, v_rows = spread(q_s[0:32, :]), k_s[0:32, :], v_s[0:32, :]
        dc_rows = spread(c_s[0:32, :])
        soft = pq_s[...]
        dp = dot_nt(v_rows, dc_rows)
        soft_f = soft.astype(F32)
        ds = (soft_f * (dp - jnp.sum(soft_f * dp, axis=0, keepdims=True))).astype(BF16)
        v_s[0:32, :] = dot_nn(soft, dc_rows).astype(BF16)
        k_s[0:32, :] = dot_nn(ds, q_rows).astype(BF16)
        q_s[0:32, :] = (0.125 * gather_heads(dot_tn(ds, k_rows))).astype(BF16)

    def attend_back_pair(pair):
        lanes = pl.ds(pl.multiple_of(pair * 128, 128), 128)
        for slot in range(2):
            low_at = 12 * slot
            rows = pl.ds(32 + 208 * slot, WIN)
            keys, queries, values = k_s[rows, lanes], q_s[rows, lanes], v_s[rows, lanes]
            inside = ((key_at >= low_at) & (key_at < low_at + SLOT)).astype(BF16)
            upstream = c_s[rows, lanes] * inside
            keys_t = keys.T
            parts, dv, dk = [], 0.0, 0.0
            for h in range(2):
                p = p_s[slot, 2 * pair + h]
                dc = upstream * half[h]
                dp = dot_nt(values, dc)
                pf = p.astype(F32)
                ds = (pf * (dp - jnp.sum(pf * dp, axis=0, keepdims=True))).astype(BF16)
                dv += dot_nn(p, dc)
                dk += dot_nn(ds, queries * half[h])
                parts.append(dot_nn(keys_t, ds)[64 * h:64 * h + 64, :])
            dq = 0.125 * jnp.concatenate(parts, axis=0).T
            for ref, new in ((q_s, dq), (k_s, dk), (v_s, dv)):
                if slot == 0:
                    ref[32:240, lanes] = new[0:208].astype(BF16)
                    old = ref[240:272, lanes].astype(F32)
                    ref[240:272, lanes] = jnp.where(iota((32, 128), 0) < 12, new[208:240], old).astype(BF16)
                else:
                    old = ref[240:256, lanes].astype(F32)
                    ref[240:256, lanes] = jnp.where(iota((16, 128), 0) >= 12, new[0:16], old).astype(BF16)
                    ref[256:480, lanes] = new[16:240].astype(BF16)

    def attend_back(first, count):
        def step(i, carry):
            attend_back_pair(first + i)
            return carry

        lax.fori_loop(0, count, step, 0)

    def column_sum(ref):
        def step(i, total):
            return total + fold8(ref[pl.ds(pl.multiple_of(i * 32, 32), 32), :].astype(F32))

        return jnp.sum(lax.fori_loop(0, 15, step, zero8), axis=0, keepdims=True)

    def column_sums():
        vec[0:1, :] = column_sum(q_s)
        vec[1:2, :] = column_sum(v_s)

    def token_grad(grads, weight):
        n1[...] += dot_nt(grads[...], weight[...])

    out_qg = pltpu.make_async_copy(n1.at[0:32, :], qtg_h, out_sem.at[2])
    out_pg = pltpu.make_async_copy(n1.at[32:472, :], ptg_h, out_sem.at[3])

    def send_tokens():
        out_qg.start()
        out_pg.start()

    def vec_step(i):
        return remote(vec, vecr.at[i], v_send.at[i], v_recv.at[i], (partner, x_peer, y_peer)[i])

    def vec_part(whole, to):
        device = to * 8 + plane
        narrow = pltpu.roll(whole[0:8], lax.rem(D - 24 * device, D), 1)[:, 0:128]
        wide = pltpu.roll(whole[8:16], lax.rem(D - 96 * plane, D), 1)[:, 0:128]
        wide = jnp.sum(jnp.where(iota((8, 128), 0) == to, wide, 0.0), axis=0, keepdims=True)
        return jnp.concatenate([narrow, wide, jnp.zeros((7, 128), F32)], axis=0)

    def vec_z():
        return [
            remote(
                vecs.at[hop - 1], vecz.at[hop - 1], v_send.at[2 + hop], v_recv.at[2 + hop],
                lax.rem(zz + hop, 4) * 8 + plane,
            )
            for hop in range(1, 4)
        ]

    def vec_on(i):
        if i > 0:
            vec_step(i - 1).wait()
            vec[...] += vecr[i - 1]
        if i < 3:
            vec_step(i).start()
        else:
            whole = vec[...]
            for hop in range(1, 4):
                vecs[hop - 1] = vec_part(whole, lax.rem(zz + hop, 4))
            begin(vec_z())

    def vec_end():
        finish_steps(vec_z())
        part = vec_part(vec[...], zz) + vecz[0] + vecz[1] + vecz[2]
        small_o[0:9, :] = part[0:9]
        outs.append(pltpu.make_async_copy(small_o, small_h, out_sem.at[4]))
        outs[-1].start()

    def serve(at, p, h):
        relayed = route(p, h)[0] == "r"
        ((relay_on, end_relay, end_2, end_3) if relayed else (end_1, end_2, end_3))[at](p, h)

    pieces_of = {
        "wback": back_grad, "dinner": inner_grad, "win": in_grad, "dmid": middle_grad, "lnback": attn_norm_back,
        "dctx": context_grad, "qslot": query_slot_back, "attn": attend_back, "sums": column_sums,
        "wvo": lambda h: pair_grad(4, h, xT, v_s, cT, ml), "wqk": lambda h: pair_grad(5, h, xT, q_s, xT, k_s),
        "tq": lambda: token_grad(q_s, wq), "tk": lambda: token_grad(k_s, wk), "tv": lambda: token_grad(v_s, wv),
        "tout": send_tokens, "vec": vec_on, "vecend": vec_end,
        "c": start_c, "ec": end_c, "e1": lambda p, h: serve(0, p, h), "e2": lambda p, h: serve(1, p, h),
        "e3": lambda p, h: serve(2, p, h), "e4": lambda p, h: serve(3, p, h),
    }
    for name, *operands in ORDER:
        pieces_of[name](*operands)

    out_q.wait()
    out_p.wait()
    out_qg.wait()
    out_pg.wait()
    for out in outs:
        out.wait()


def hand_on_kernel(*refs):
    count = 10
    sources, small = refs[:count], refs[count]
    targets, vectors = refs[count + 1:2 * count + 1], refs[2 * count + 1:2 * count + 11]
    held, rest = refs[2 * count + 11:3 * count + 11], refs[3 * count + 11:]
    small_v, lines, in_sem, out_sem = rest[0], rest[1:11], rest[11], rest[12]
    whole = [(i, None) for i in range(count) if i != 3]
    pieces = [(3, pl.ds(at, size)) for at, size in blocks(0, 440, 112)] + whole
    into, out = [], []
    for at, (i, rows) in enumerate(pieces):
        source, kept, target = (ref if rows is None else ref.at[rows, :] for ref in (sources[i], held[i], targets[i]))
        into.append(pltpu.make_async_copy(source, kept, in_sem.at[at]))
        out.append(pltpu.make_async_copy(kept, target, out_sem.at[at]))
    last = pltpu.make_async_copy(small, small_v, in_sem.at[len(pieces)])
    last.start()
    for copy in into:
        copy.start()
    last.wait()
    for at, ref in enumerate(lines[:8]):
        ref[...] = small_v[at:at + 1, 0:24].reshape(24)
    lines[8][...] = small_v[8:9, 0:96].reshape(96)
    lines[9][...] = small_v[9:10, 0:1].reshape(1)
    for at, (line, vector) in enumerate(zip(lines, vectors)):
        out.append(pltpu.make_async_copy(line, vector, out_sem.at[len(pieces) + at]))
        out[-1].start()
    for first, second in zip(into, out):
        first.wait()
        second.start()
    for copy in out:
        copy.wait()


def on_device_small(*operands):
    (
        query_tokens, passage_tokens, query_lengths, passage_lengths, passage_valid, positives, negatives,
        teacher_margins, query_grad, passage_grad, weight_query, bias_query, weight_key, weight_value, bias_value,
        weight_out, bias_out, gain_attn, shift_attn, weight_in, bias_in, weight_back, bias_back, gain_ffn, shift_ffn,
    ) = operands
    hbm, smem = (pl.BlockSpec(memory_space=space) for space in (pl.ANY, pltpu.SMEM))
    shape = jax.ShapeDtypeStruct
    slabs = (2, 2, 4, 2, 2, 48, D)
    large = (
        shape((32, D), BF16), shape((440, D), BF16), shape((32, D), F32), shape((440, D), F32), shape((24, D), F32),
        shape((24, D), F32), shape((24, D), F32), shape((24, D), F32), shape((24, FF), F32), shape((96, D), F32),
    )
    outs = pl.pallas_call(
        layer_kernel,
        out_shape=(
            *large, shape((16, 128), F32),
        ),
        in_specs=[
            hbm, hbm, smem, hbm, hbm, smem, smem, smem, hbm, hbm,
            *(hbm,) * 15,
        ],
        out_specs=(hbm,) * 11,
        scratch_shapes=[
            pltpu.VMEM((2,), jnp.int32), pltpu.VMEM((2,), jnp.int32),
            *(pltpu.VMEM((size,), BF16) for size in (D, D, D, D, D, FF, D, D, D)),
            pltpu.VMEM((D, D), BF16), pltpu.VMEM((D, D), BF16), pltpu.VMEM((D, D), BF16), pltpu.VMEM((D, D), BF16),
            pltpu.VMEM((D, FF), BF16), pltpu.VMEM((3, 2, 2, 4, 2, 2, 48, WIDE), BF16),
            pltpu.VMEM((440, D), BF16), pltpu.VMEM((ROWS, D), BF16), pltpu.VMEM((D, ROWS), BF16),
            pltpu.VMEM((ROWS, D), BF16), pltpu.VMEM((ROWS, D), BF16), pltpu.VMEM((ROWS, D), BF16),
            pltpu.VMEM((2, 12, WIN, WIN), BF16), pltpu.VMEM((32, 384), BF16),
            pltpu.VMEM((ROWS, D), BF16), pltpu.VMEM((D, ROWS), BF16),
            pltpu.VMEM((ROWS, D), F32), pltpu.VMEM((ROWS, D), F32), pltpu.VMEM((ROWS, 1), F32), pltpu.VMEM((ROWS, 1), F32),
            pltpu.VMEM((ROWS, D), BF16), pltpu.VMEM((D, ROWS), BF16),
            pltpu.VMEM((256, D), BF16), pltpu.VMEM((256, D), BF16), pltpu.VMEM((FF, ROWS), BF16),
            pltpu.VMEM((256, D), F32), pltpu.VMEM((256, D), F32),
            pltpu.VMEM((ROWS, FF), BF16),
            pltpu.VMEM((32, D), BF16), pltpu.VMEM((440, D), BF16), pltpu.VMEM((32, D), BF16), pltpu.VMEM((440, D), BF16),
            pltpu.VMEM((1024, 128), BF16), pltpu.VMEM((1056, 128), F32),
            pltpu.VMEM((16, D), F32), pltpu.VMEM((3, 16, D), F32), pltpu.VMEM((3, 16, 128), F32), pltpu.VMEM((3, 16, 128), F32),
            pltpu.VMEM((16, 128), F32), pltpu.VMEM((6, 3, 48, WIDE), F32),
            pltpu.VMEM((4, 3, 2, 4, 2, 2, 48, WIDE), BF16),
            pltpu.VMEM((2, 3, 4, 2, 2, 48, WIDE), BF16), pltpu.VMEM((6, 3, 4, 2, 48, WIDE), BF16),
            pltpu.VMEM((6, 3, 4, 48, WIDE), BF16), pltpu.VMEM((6, 3, 3, 48, WIDE), BF16),
            pltpu.VMEM((max(1, sum(way[0] == "z" for way in ROUTE)), 3, 2, 2, 48, WIDE), BF16),
            pltpu.VMEM((RELAYS, 2, 2, 48, WIDE), BF16), pltpu.VMEM((RELAYS, 2, 2, 2, 48, WIDE), BF16),
            pltpu.VMEM((RELAYS, 2, 2, 48, WIDE), BF16),
            pltpu.SemaphoreType.DMA((32,)), pltpu.SemaphoreType.DMA((5,)), pltpu.SemaphoreType.DMA((6, 3, 2)),
            pltpu.SemaphoreType.DMA((16,)), pltpu.SemaphoreType.DMA((16,)),
            pltpu.SemaphoreType.DMA((6, 3)), pltpu.SemaphoreType.DMA((6, 3)),
            pltpu.SemaphoreType.DMA((6, 3)), pltpu.SemaphoreType.DMA((6, 3)),
            pltpu.SemaphoreType.DMA((6, 3)), pltpu.SemaphoreType.DMA((6, 3)),
            pltpu.SemaphoreType.DMA((6, 3, 3)), pltpu.SemaphoreType.DMA((6, 3, 3)), pltpu.SemaphoreType.DMA((RELAYS, 2)),
            pltpu.SemaphoreType.DMA((6,)), pltpu.SemaphoreType.DMA((6,)),
            pltpu.SemaphoreType.REGULAR((2, 3)),
        ],
        compiler_params=pltpu.CompilerParams(
            collective_id=0, has_side_effects=True, vmem_limit_bytes=64 * 1024 * 1024 - 65536,
        ),
        name="encoder_layer",
    )(
        query_tokens, passage_tokens, query_lengths, passage_lengths, passage_valid, positives, negatives,
        teacher_margins, query_grad, passage_grad, weight_query, bias_query, weight_key, weight_value, bias_value,
        weight_out, bias_out, gain_attn, shift_attn, weight_in, bias_in, weight_back.reshape(slabs), bias_back,
        gain_ffn, shift_ffn,
    )
    done = pl.pallas_call(
        hand_on_kernel,
        out_shape=large + (shape((24,), F32),) * 8 + (shape((96,), F32), shape((1,), F32)),
        in_specs=[hbm] * 11,
        out_specs=(hbm,) * 20,
        scratch_shapes=[pltpu.VMEM(out.shape, out.dtype) for out in large]
        + [pltpu.VMEM((16, 128), F32)] + [pltpu.VMEM((size,), F32) for size in (24,) * 8 + (96, 1)]
        + [pltpu.SemaphoreType.DMA((24,)), pltpu.SemaphoreType.DMA((24,))],
        name="hand_on",
    )(*outs)
    qout, pout, qtg, ptg, wqg, wkg, wvg, wog, wig, wbg, bqg, bvg, bog, gag, sag, bbg, gfg, sfg, big, loss = done
    return (
        qout, pout, loss, qtg, ptg, wqg, bqg, wkg, wvg, bvg, wog, bog, gag, sag, wig, big, wbg, bbg, gfg, sfg,
    )


def solution(mesh):
    return jax.shard_map(
        on_device_small if mesh.shape["dp"] == 32 else on_device,
        mesh=mesh,
        in_specs=(
            P("dp", None),
            P("dp", None),
            P("dp"),
            P("dp"),
            P("dp"),
            P("dp"),
            P("dp"),
            P("dp"),
            P("dp", None),
            P("dp", None),
            P(),
            P(),
            P(),
            P(),
            P(),
            P(),
            P(),
            P(),
            P(),
            P(),
            P(),
            P(),
            P(),
            P(),
            P(),
        ),
        out_specs=(
            P("dp", None),
            P("dp", None),
            P("dp"),
            P("dp", None),
            P("dp", None),
            P("dp", None),
            P("dp"),
            P("dp", None),
            P("dp", None),
            P("dp"),
            P("dp", None),
            P("dp"),
            P("dp"),
            P("dp"),
            P("dp", None),
            P("dp"),
            P("dp", None),
            P("dp"),
            P("dp"),
            P("dp"),
        ),
        check_vma=False,
    )
```
